32 devices in a mesh: cuts: 16 (over z, y, core), chan: 2 (over x).
Axes of the slice: x: 2, y: 2, z: 4, core: 2. Of those that a mesh axis runs over, the one named last changes fastest.
Arguments:
- data: bfloat16 [128, 384, 1024], P('cuts', None, 'chan'), may hold values from -6 to 6
- order: int32 [128], P('cuts'), may hold values from 0 to 127, as said below
- chan_factor: bfloat16 [1024, 64], P('chan'), may hold values from -0.1875 to 0.1875
- slice_weights: float32 [128, 64], P('cuts'), may hold values from 0.5 to 2
- smooth_aux: float32 [128, 384, 64], P('cuts', 'chan'), may hold values from -6 to 6
- coupled: float32 [128, 384, 64], P('cuts', 'chan'), may hold values from -6 to 6
- smooth_dual: float32 [128, 384, 64], P('cuts', 'chan'), may hold values from -2 to 2
- coupling_dual: float32 [128, 384, 64], P('cuts', 'chan'), may hold values from -2 to 2
- delta: float32 [64, 64], replicated, may hold values from -0.1125 to 1.1125, as said below
Outputs:
- evolving: float32 [128, 384, 64], P('cuts', 'chan')
- coupled_out: float32 [128, 384, 64], P('cuts', 'chan')
- delta_out: float32 [64, 64], replicated
The draws below stay inside these ranges and needn't reach their ends.
Inputs may be any that keep to these rules, and one draw needn't show every extreme that they name: `order`: within each aligned block of 8 entries (the slices of one index of cuts) the entries are a permutation of that block's own slice indices; entry k names the stored slice of phase bin k. `delta`: A full-rank matrix.
All inputs are finite; a program needn't handle non-finite values.
Results may differ from the reference program's by a relative error of at most 0.0003.
Values sent between devices are 32-bit elements; how exact they have to be, the bound alone decides.
No kernel may reach another device: no remote copies, remote signals or barrier semaphores. Data moves between devices by JAX's collectives and lax.ppermute only.
A program may use at most 64 MiB of HBM per device.

```python
import math
import jax
import jax.numpy as jnp
from jax import lax

SLICE_DEV = 8
ROWS = 384
CHANNELS = 1024
RANK = 64
INNER = 3
SWEEPS = 4
POLAR = 8
SLICES = 128


def draw_order(key, part):
    blocks = SLICES // SLICE_DEV
    block_keys = jax.random.split(key, blocks)
    shuffled = jax.vmap(lambda sub_key: jax.random.permutation(sub_key, SLICE_DEV))(block_keys)
    offsets = jnp.arange(blocks, dtype=jnp.int32)[:, None] * SLICE_DEV
    return (shuffled.astype(jnp.int32) + offsets).reshape(SLICES)


def draw_delta(key, part):
    noise = jax.random.truncated_normal(key, -3.0, 3.0, (RANK, RANK), jnp.float32)
    return jnp.eye(RANK, dtype=jnp.float32) + 0.3 * RANK ** (-0.5) * noise


def shard_levels(rng, shape, shards, least, largest):
    level, own = 1.0, jax.random.fold_in(rng, 6)
    for axis_at, parts in shards:
        steps = jnp.exp(jax.random.uniform(jax.random.fold_in(own, axis_at), (parts,), jnp.float32, least / len(shards), largest / len(shards)))
        level = level * jnp.repeat(steps, shape[axis_at] // parts).reshape([-1 if axis == axis_at else 1 for axis in range(len(shape))])
    return level


def centred(rng, dims, scale, reach, cuts=(), kind=jnp.bfloat16):
    entries = jax.random.normal(rng, dims, jnp.float32) * scale
    if len(cuts) > 0:
        entries = shard_levels(rng, dims, cuts, -0.22, 0.18) * entries
    return jnp.clip(entries, min=-reach, max=reach).astype(kind)


def setup_inputs(seed: int = 0) -> dict:
    key_of = jax.random.split(jax.random.key(seed), 10)
    data = centred(key_of[0], (SLICES, ROWS, CHANNELS), 1.0, 6.0, ((0, 16), (2, 2)))
    order = draw_order(jax.random.fold_in(key_of[9], 71), 0)
    chan_factor = centred(key_of[2], (CHANNELS, RANK), CHANNELS ** -0.5, 0.1875, ((0, 2),))
    slice_weights = jnp.clip(jnp.exp(math.log(2.0) - 1.3862944 * jax.random.uniform(key_of[3], (SLICES, RANK), jnp.float32) ** shard_levels(key_of[3], (SLICES, RANK), ((0, 16),), -0.2, 0.2)), 0.5, 2.0)
    smooth_aux = centred(key_of[4], (SLICES, ROWS, RANK), 1.0, 6.0, ((0, 16), (1, 2)), jnp.float32)
    coupled = centred(key_of[5], (SLICES, ROWS, RANK), 1.0, 6.0, ((0, 16), (1, 2)), jnp.float32)
    smooth_dual = centred(key_of[6], (SLICES, ROWS, RANK), 0.3, 2.0, ((0, 16), (1, 2)), jnp.float32)
    coupling_dual = centred(key_of[7], (SLICES, ROWS, RANK), 0.3, 2.0, ((0, 16), (1, 2)), jnp.float32)
    delta = draw_delta(jax.random.fold_in(key_of[9], 71), 0)
    return dict(data=data, order=order, chan_factor=chan_factor, slice_weights=slice_weights, smooth_aux=smooth_aux, coupled=coupled, smooth_dual=smooth_dual, coupling_dual=coupling_dual, delta=delta)


smooth_weight = 1.0
eps_trace = 1e-06
highest = lax.Precision.HIGHEST

def setup_system(slice_weights, factor_gram):
    rank = factor_gram.shape[0]
    identity = jnp.eye(rank, dtype=jnp.float32)
    diagonal_gram = jnp.diagonal(factor_gram)
    rho = lax.optimization_barrier(jnp.sum(slice_weights * slice_weights * diagonal_gram[None, :], axis=1)) / rank
    system = slice_weights[:, :, None] * factor_gram[None] * slice_weights[:, None, :]
    system = system + 2.0 * rho[:, None, None] * identity
    factors = jax.vmap(jnp.linalg.cholesky)(system)
    inverse = jax.vmap(lambda lower: jax.scipy.linalg.cho_solve((lower, True), identity))(factors)
    return (rho, inverse)

def polar_terms(gram, delta_now):
    rank = gram.shape[1]
    identity = jnp.eye(rank, dtype=jnp.float32)
    left = jnp.einsum('rs,kst->krt', delta_now, gram, precision=highest)
    normal = jnp.einsum('krt,ut->kru', left, delta_now, precision=highest)
    trace = jnp.trace(normal, axis1=1, axis2=2) + eps_trace
    current = normal / trace[:, None, None]
    root = jnp.broadcast_to(identity, normal.shape)
    for step in range(POLAR):
        bracket = 1.5 * identity - 0.5 * jnp.einsum('krs,kst->krt', root, current, precision=highest)
        current = jnp.einsum('krs,kst->krt', current, bracket, precision=highest)
        root = jnp.einsum('krs,kst->krt', bracket, root, precision=highest)
    scale = 1.0 / jnp.sqrt(trace)
    partial_value = jnp.einsum('ksr,st->krt', root, delta_now, precision=highest)
    partial_value = jnp.einsum('krt,ktu->kru', partial_value, gram, precision=highest) * scale[:, None, None]
    return (root, scale, partial_value)

def coupled_update(tall, root, scale, delta_now, delta_new):
    mixer = jnp.einsum('sr,kst->krt', delta_now, root, precision=highest)
    mixer = jnp.einsum('krt,tu->kru', mixer, delta_new, precision=highest) * scale[:, None, None]
    return jnp.einsum('kir,kru->kiu', tall, mixer, precision=highest)

def reference(data, order, chan_factor, slice_weights, smooth_aux, coupled, smooth_dual, coupling_dual, delta):
    flat = data.reshape(SLICES * ROWS, CHANNELS)
    projected = jnp.dot(flat.astype(jnp.float32), chan_factor.astype(jnp.float32), preferred_element_type=jnp.float32).reshape(SLICES, ROWS, RANK)
    projected = jnp.take(projected, order, axis=0)
    factor_gram = jnp.dot(chan_factor.T.astype(jnp.float32), chan_factor.astype(jnp.float32), preferred_element_type=jnp.float32)
    rho, inverse = setup_system(slice_weights, factor_gram)
    data_side = projected * slice_weights[:, None, :]
    rho_cols = rho[:, None, None]
    aux = smooth_aux
    coup = coupled
    dual_s = smooth_dual
    dual_c = coupling_dual
    delta_now = delta
    evolving = aux
    for inner in range(INNER):
        rhs = data_side + rho_cols * (aux - dual_s + coup - dual_c)
        evolving = jnp.einsum('kir,krs->kis', rhs, inverse, precision=highest)
        target = evolving + dual_s
        for sweep in range(SWEEPS):
            beside = jnp.roll(aux, 1, 0) + jnp.roll(aux, -1, 0)
            aux = (rho_cols * target + 2.0 * smooth_weight * beside) / (rho_cols + 4.0 * smooth_weight)
        tall = evolving + dual_c
        gram = jnp.einsum('kir,kis->krs', tall, tall, precision=highest)
        root, scale, partial_value = polar_terms(gram, delta_now)
        delta_new = lax.optimization_barrier(jnp.sum(partial_value, axis=0)) / SLICES
        coup = coupled_update(tall, root, scale, delta_now, delta_new)
        dual_s = dual_s + evolving - aux
        dual_c = dual_c + evolving - coup
        delta_now = delta_new
    return (evolving, coup, delta_now)
```

```python
import functools

import jax
import jax.numpy as jnp
from jax import lax
from jax.experimental import pallas as pl
from jax.experimental.pallas import tpu as pltpu
from jax.sharding import PartitionSpec as P

INNER = 3
SWEEPS = 4
POLAR = 8

smooth_weight = 1.0
eps_trace = 1e-06
f32 = jnp.float32
bf16 = jnp.bfloat16
NN = (((1,), (0,)), ((), ()))
NT = (((1,), (1,)), ((), ()))


def dot(left, right, dims=NN):
    return lax.dot_general(left, right, dims, preferred_element_type=f32)


def split(value):
    high = value.astype(bf16)
    low = (value - high.astype(f32)).astype(bf16)
    return high, low


def left_triple(value):
    high, low = split(value)
    return jnp.concatenate([high, high, low], axis=1)


def right_triple(value):
    high, low = split(value)
    return jnp.concatenate([high, low, high], axis=0)


def block_mask(rank, group):
    wide = rank * group
    rows = lax.div(lax.broadcasted_iota(jnp.int32, (wide, wide), 0), rank)
    cols = lax.div(lax.broadcasted_iota(jnp.int32, (wide, wide), 1), rank)
    return jnp.where(rows == cols, 1.0, 0.0).astype(bf16)


def wide_eye(rank, group):
    rows = lax.broadcasted_iota(jnp.int32, (rank, rank * group), 0)
    cols = lax.broadcasted_iota(jnp.int32, (rank, rank * group), 1)
    return jnp.where(rows == lax.rem(cols, rank), 1.0, 0.0).astype(f32)


def block_diagonal(value, mask, group):
    high, low = split(value)
    return (
        jnp.concatenate([high] * group, axis=0) * mask,
        jnp.concatenate([low] * group, axis=0) * mask,
    )


def times_blocks(values, blocks, dims=NN):
    rank = values[0].shape[0]
    count = len(values)
    pieces = [split(value) for value in values]
    high = jnp.concatenate([piece[0] for piece in pieces], axis=0)
    both = jnp.concatenate([high] + [piece[1] for piece in pieces], axis=0)
    first = dot(both, blocks[0], dims)
    total = first[: count * rank] + first[count * rank :] + dot(high, blocks[1], dims)
    return [total[at * rank : (at + 1) * rank] for at in range(count)]


def diagonal_blocks(value, rank, group):
    at = lax.div(lax.broadcasted_iota(jnp.int32, (rank, rank * group), 1), rank)
    total = value[:rank]
    for block in range(1, group):
        total = jnp.where(at == block, value[block * rank : (block + 1) * rank], total)
    return total


def group_size(count, rank):
    group = max(1, 256 // rank)
    while count % group:
        group -= 1
    return group


def project_kernel(order_ref, me_ref, first_ref, second_ref, factor_ref, *outs):
    parts = len(outs)
    rows = outs[0].shape[2] // 2
    factor = factor_ref[...]
    for part in range(parts):
        start = pl.multiple_of(lax.rem(me_ref[0] + part, parts) * rows, 16)
        both = jnp.concatenate(
            [first_ref[0, pl.ds(start, rows), :], second_ref[0, pl.ds(start, rows), :]], axis=0
        )
        outs[part][0] = dot(factor, both, NT)


def setup_kernel(grams, group, *refs):
    gram_refs, refs = refs[:grams], refs[grams:]
    (left_ref, own_ref, right_ref, weights_ref, projected_ref) = refs[:5]
    (aux_ref, coupled_ref, dual_s_ref, dual_c_ref) = refs[5:9]
    (inverse_ref, rho_ref, base_ref) = refs[9:]
    count, rank = own_ref.shape
    rows = aux_ref.shape[2]
    gram = gram_refs[0][...]
    for ref in gram_refs[1:]:
        gram = gram + ref[...]
    eye = wide_eye(rank, 1)
    diagonal = jnp.sum(gram * eye, axis=0, keepdims=True)
    weights = jnp.concatenate([left_ref[...], own_ref[...], right_ref[...]], axis=0)
    rho = jnp.sum(weights * weights * diagonal, axis=1, keepdims=True) / rank
    rho_ref[...] = jnp.broadcast_to(rho, rho_ref.shape)
    width = left_ref.shape[0]

    edge = 34.0 / 32.0
    lead = 4.0 * edge**3 / (4.0 * edge**3 - 3.0 * edge)
    mask = block_mask(rank, group)
    wide = wide_eye(rank, group)
    for first in range(0, count, group):
        scaled = []
        for k in range(first, first + group):
            unit = 1.0 / (34.0 * rho[width + k : width + k + 1, :])
            column = weights_ref[:, k : k + 1]
            scaled.append(
                column * gram * own_ref[k : k + 1, :] * unit + (2.0 / 34.0) * eye
            )
        system = jnp.concatenate(scaled, axis=1)
        rest = wide - system
        blocks = block_diagonal(rest, mask, group)
        (square,) = times_blocks([rest], blocks)
        (cube,) = times_blocks([square], blocks)
        inverse = wide + lead * (rest + square)
        rest = lead * cube - (lead - 1.0) * rest
        for step in range(4):
            blocks = block_diagonal(rest, mask, group)
            more, rest = times_blocks([inverse, rest], blocks)
            inverse = inverse + more
        system_blocks = block_diagonal(system, mask, group)
        for step in range(2):
            (product,) = times_blocks([inverse], system_blocks)
            blocks = block_diagonal(wide - product, mask, group)
            (more,) = times_blocks([inverse], blocks)
            inverse = inverse + more
        for k in range(first, first + group):
            unit = 1.0 / (34.0 * rho[width + k : width + k + 1, :])
            place = (k - first) * rank
            inverse_ref[k] = left_triple(inverse[:, place : place + rank] * unit)
    for k in range(count):
        column = weights_ref[:, k : k + 1]
        half = (k % 2) * rows
        base_ref[k] = column * projected_ref[k // 2, :, half : half + rows] + rho[
            width + k : width + k + 1, :
        ] * (aux_ref[k] - dual_s_ref[k] + coupled_ref[k] - dual_c_ref[k])


def gram_blocks(talls, rank):
    group = len(talls)
    pieces = [split(tall) for tall in talls]
    high = jnp.concatenate([piece[0] for piece in pieces], axis=0)
    low = jnp.concatenate([piece[1] for piece in pieces], axis=0)
    wide = group * rank
    first = dot(jnp.concatenate([high, low], axis=0), high, NT)
    return diagonal_blocks(first[:wide] + first[wide:] + dot(high, low, NT), rank, group)


def first_kernel(parts, group, *refs):
    base_ref, weights_ref, inverse_ref, dual_s_ref, dual_c_ref = refs[:5]
    recv_refs = refs[5 : 5 + parts]
    tall_ref, target_ref, gram_ref = refs[5 + parts :]
    count, rank, rows = base_ref.shape
    for first in range(0, count, group):
        talls = []
        for k in range(first, first + group):
            half = (k % 2) * rows
            right = base_ref[k]
            if recv_refs:
                more = recv_refs[0][k // 2, :, half : half + rows]
                for ref in recv_refs[1:]:
                    more = more + ref[k // 2, :, half : half + rows]
                right = right + weights_ref[:, k : k + 1] * more
            evolving = dot(inverse_ref[k], right_triple(right))
            target_ref[k] = evolving + dual_s_ref[k]
            tall = evolving + dual_c_ref[k]
            tall_ref[k] = tall
            talls.append(tall)
        gram_ref[first // group] = gram_blocks(talls, rank)


def smooth_kernel(parts, aux_ref, target_ref, rho_ref, *refs):
    inside_ref, left_ref, right_ref = refs[-3:]
    count, rank, rows = aux_ref.shape
    if parts:
        weights_ref, projected_refs, side_ref = refs[0], refs[1 : 1 + parts], refs[1 + parts]
        for k in range(count):
            half = (k % 2) * rows
            side = projected_refs[0][k // 2, :, half : half + rows]
            for ref in projected_refs[1:]:
                side = side + ref[k // 2, :, half : half + rows]
            side_ref[k] = weights_ref[:, k : k + 1] * side
    width = SWEEPS
    rho = {j: rho_ref[width + j : width + j + 1, 0:1] for j in range(-width, count + width)}
    near = {j: 2.0 * smooth_weight / (rho[j] + 4.0 * smooth_weight) for j in rho}
    pull = {j: (rho[j] / (rho[j] + 4.0 * smooth_weight)) * target_ref[j] for j in range(count)}
    now = {j: aux_ref[j] for j in range(count)}
    for sweep in range(width):
        later = {}
        for j in range(-sweep - 1, count + sweep + 1):
            beside = [now[i] for i in (j - 1, j + 1) if i in now]
            total = beside[0] if len(beside) == 1 else beside[0] + beside[1]
            total = near[j] * total
            later[j] = total + pull[j] if j in pull else total
        now = later
    for j in range(count):
        inside_ref[j] = now[j]
    for j in range(width):
        left_ref[j] = now[j - width]
        right_ref[j] = now[count + j]


def polar_kernel(grams, delta_ref, *refs):
    gram_refs = refs[:grams]
    mixed_ref, partial_ref = refs[grams:]
    groups, rank, wide = mixed_ref.shape
    group = wide // rank
    delta = delta_ref[...]
    mask = block_mask(rank, group)
    eye = wide_eye(rank, group)
    delta_left = left_triple(delta)
    delta_blocks = block_diagonal(jnp.concatenate([delta] * group, axis=1), mask, group)
    sums, currents, roots, scales = [], [], [], []
    for at in range(groups):
        gram = gram_refs[0][at]
        for ref in gram_refs[1:]:
            gram = gram + ref[at]
        sums.append(gram)
        left = dot(delta_left, right_triple(gram))
        (normal,) = times_blocks([left], delta_blocks, NT)
        line = jnp.broadcast_to(jnp.sum(normal * eye, axis=0, keepdims=True), (16, wide))
        high, low = split(line)
        rest = (line - high.astype(f32) - low.astype(f32)).astype(bf16)
        line = dot(high, mask) + dot(low, mask) + dot(rest, mask)
        trace = line[0:1] + eps_trace
        currents.append(normal / trace)
        scales.append(1.0 / jnp.sqrt(trace))
    for step in range(POLAR):
        for at in range(groups):
            product = currents[at]
            if step == 0:
                roots.append(1.5 * eye - 0.5 * product)
                blocks = block_diagonal(product, mask, group)
                (square,) = times_blocks([product], blocks)
            elif step < POLAR - 1:
                blocks = block_diagonal(product, mask, group)
                square, more = times_blocks([product, roots[at]], blocks)
                roots[at] = 1.5 * roots[at] - 0.5 * more
            else:
                blocks = block_diagonal(product, mask, group)
                (more,) = times_blocks([roots[at]], blocks)
                roots[at] = 1.5 * roots[at] - 0.5 * more
            if step < POLAR - 1:
                half = 1.5 * product - 0.5 * square
                (more,) = times_blocks([half], blocks)
                currents[at] = 1.5 * half - 0.5 * more
    left, right = [], []
    for at in range(groups):
        (mixed,) = times_blocks([roots[at]], delta_blocks)
        mixed = mixed * scales[at]
        mixed_ref[at] = mixed
        high, low = split(mixed)
        left += [high, high, low]
        high, low = split(sums[at])
        right += [high, low, high]
    partial = dot(jnp.concatenate(left, axis=1), jnp.concatenate(right, axis=1), NT)
    half = rank // 2
    partial_ref[...] = jnp.concatenate([partial[:half], partial[half:]], axis=1)


def ahead_kernel(
    inside_ref, left_ref, right_ref, target_ref, tall_ref, base_ref, rho_ref, inverse_ref,
    aux_ref, dual_ref, known_ref,
):
    count = inside_ref.shape[0]
    width = SWEEPS
    for k in range(count):
        aux = inside_ref[k]
        if k < width:
            aux = aux + left_ref[k]
        if k >= count - width:
            aux = aux + right_ref[k - count + width]
        target = target_ref[k]
        rho = rho_ref[width + k : width + k + 1, 0:1]
        aux_ref[k] = aux
        dual_ref[k] = target - aux
        known_ref[k] = dot(
            inverse_ref[k], right_triple(base_ref[k] + rho * (2.0 * aux - target - tall_ref[k]))
        )


def new_delta(sums, total, rank):
    packed = sums[0][...]
    for ref in sums[1:]:
        packed = packed + ref[...]
    packed = packed / total
    return jnp.concatenate([packed[:, :rank], packed[:, rank:]], axis=0)


def step_kernel(sums, total, last, *refs):
    sum_refs, refs = refs[:sums], refs[sums:]
    mixed_ref, tall_ref, known_ref, dual_ref, inverse_ref, rho_ref = refs[:6]
    next_ref, target_ref, gram_ref, delta_ref = refs[6:]
    groups, rank, wide = mixed_ref.shape
    group = wide // rank
    delta = new_delta(sum_refs, total, rank)
    delta_ref[...] = delta
    delta_left = left_triple(delta.T)
    width = SWEEPS
    for at in range(groups):
        mixer = dot(delta_left, right_triple(mixed_ref[at]))
        inverses = jnp.concatenate(
            [inverse_ref[k] for k in range(at * group, (at + 1) * group)], axis=0
        )
        onward = diagonal_blocks(dot(inverses, right_triple(mixer)), rank, group)
        talls = []
        for k in range(at * group, (at + 1) * group):
            place = (k - at * group) * rank
            rho = rho_ref[width + k : width + k + 1, 0:1]
            forward = 2.0 * rho * onward[:, place : place + rank]
            change = forward - mixer[:, place : place + rank]
            tall = tall_ref[k]
            left = jnp.concatenate([left_triple(change), left_triple(forward)], axis=0)
            both = dot(left, right_triple(tall))
            known = known_ref[k]
            later = known + tall + both[:rank]
            next_ref[k] = later
            evolving = known + both[rank:]
            target_ref[k] = evolving if last else evolving + dual_ref[k]
            talls.append(later)
        gram_ref[at] = gram_blocks(talls, rank)


def last_kernel(sums, total, *refs):
    sum_refs, refs = refs[:sums], refs[sums:]
    mixed_ref, tall_ref, coupled_ref, delta_ref = refs
    groups, rank, wide = mixed_ref.shape
    group = wide // rank
    delta = new_delta(sum_refs, total, rank)
    delta_ref[...] = delta
    delta_left = left_triple(delta.T)
    for at in range(groups):
        mixer = dot(delta_left, right_triple(mixed_ref[at]))
        for k in range(at * group, (at + 1) * group):
            place = (k - at * group) * rank
            coupled_ref[k] = dot(
                left_triple(mixer[:, place : place + rank]), right_triple(tall_ref[k])
            )


def call(kernel, name, outs, *args, flops=50_000_000):
    shapes = [jax.ShapeDtypeStruct(shape, dtype) for shape, dtype in outs]
    moved = sum(arg.size * arg.dtype.itemsize for arg in args)
    moved += sum(shape.size * shape.dtype.itemsize for shape in shapes)
    return pl.pallas_call(
        kernel,
        out_shape=shapes,
        in_specs=[pl.BlockSpec(memory_space=pltpu.VMEM)] * len(args),
        out_specs=[pl.BlockSpec(memory_space=pltpu.VMEM)] * len(shapes),
        compiler_params=pltpu.CompilerParams(vmem_limit_bytes=40 * 1024 * 1024),
        cost_estimate=pl.CostEstimate(flops=flops, bytes_accessed=moved, transcendentals=0),
        name=name,
    )(*args)


def rotated(value, axis, shift):
    count = lax.axis_size(axis)
    return lax.ppermute(value, axis, [(i, (i + shift) % count) for i in range(count)])


def from_others(value, axis):
    return [rotated(value, axis, shift) for shift in range(1, lax.axis_size(axis))]


def stage_sizes(count):
    sizes = []
    while count > 1:
        size = next(size for size in (4, 2, 3, 5, 7, count) if count % size == 0)
        sizes.append(size)
        count //= size
    return sizes


def in_stages(value, axis):
    count = lax.axis_size(axis)
    stride = 1
    terms = [value]
    for size in stage_sizes(count):
        value = terms[0]
        for term in terms[1:]:
            value = value + term
        terms = [value]
        for shift in range(1, size):
            moves = []
            for i in range(count):
                digit = (i // stride) % size
                moves.append((i, i + ((digit + shift) % size - digit) * stride))
            terms.append(lax.ppermute(value, axis, moves))
        stride *= size
    return terms


def body(
    data, order, chan_factor, slice_weights, smooth_aux, coupled, smooth_dual, coupling_dual, delta
):
    count, all_rows, channels = data.shape
    rank = chan_factor.shape[1]
    rows = smooth_aux.shape[1]
    parts = lax.axis_size("chan")
    total = count * lax.axis_size("cuts")
    group = group_size(count, rank)
    groups = count // group
    wide = group * rank
    flip = lambda value: jnp.swapaxes(value, 1, 2)
    aux, coup, dual_s, dual_c = map(flip, (smooth_aux, coupled, smooth_dual, coupling_dual))
    factor = chan_factor.T
    state = ((count, rank, rows), f32)

    gram_part = dot(factor, factor, NT)
    grams = [gram_part] + from_others(gram_part, "chan")
    before = rotated(slice_weights[count - SWEEPS :], "cuts", 1)
    after = rotated(slice_weights[:SWEEPS], "cuts", -1)

    me = lax.axis_index("chan").astype(jnp.int32).reshape(1)
    block = pl.BlockSpec((1, rank, 2 * rows), lambda i, order, me: (i, 0, 0))
    spec = lambda odd: pl.BlockSpec(
        (1, all_rows, channels), lambda i, order, me: (lax.rem(order[2 * i + odd], count), 0, 0)
    )
    projected = pl.pallas_call(
        project_kernel,
        out_shape=[jax.ShapeDtypeStruct((count // 2, rank, 2 * rows), f32)] * parts,
        grid_spec=pltpu.PrefetchScalarGridSpec(
            num_scalar_prefetch=2,
            grid=(count // 2,),
            in_specs=[
                spec(0),
                spec(1),
                pl.BlockSpec((rank, channels), lambda i, order, me: (0, 0)),
            ],
            out_specs=[block] * parts,
        ),
        cost_estimate=pl.CostEstimate(
            flops=2 * data.size * rank, bytes_accessed=2 * data.size, transcendentals=0
        ),
        name="project",
    )(order, me, data, data, factor)
    arrived = [rotated(projected[shift], "chan", shift) for shift in range(1, parts)]

    weights = slice_weights.T
    inverse, rho, base = call(
        functools.partial(setup_kernel, len(grams), group),
        "setup",
        [((count, rank, 3 * rank), bf16), ((count + 2 * SWEEPS, 128), f32), state],
        *grams, before, slice_weights, after, weights, projected[0],
        aux, coup, dual_s, dual_c,
    )
    tall, target, gram = call(
        functools.partial(first_kernel, parts - 1, group),
        "first",
        [state, state, ((groups, rank, wide), f32)],
        base, weights, inverse, dual_s, dual_c, *arrived,
    )

    halo = ((SWEEPS, rank, rows), f32)
    for inner in range(INNER):
        others = from_others(gram, "chan")
        last = inner == INNER - 1
        if not last:
            if inner == 0:
                data_side, inside, to_left, to_right = call(
                    functools.partial(smooth_kernel, parts),
                    "smooth",
                    [state, state, halo, halo],
                    aux, target, rho, weights, projected[0], *arrived,
                )
            else:
                inside, to_left, to_right = call(
                    functools.partial(smooth_kernel, 0),
                    "smooth",
                    [state, halo, halo],
                    aux, target, rho,
                )
            from_left = rotated(to_right, "cuts", 1)
            from_right = rotated(to_left, "cuts", -1)
        mixed, partial = call(
            functools.partial(polar_kernel, parts),
            "polar",
            [((groups, rank, wide), f32), ((rank // 2, 2 * rank), f32)],
            delta, gram, *others,
        )
        sums = in_stages(partial, "cuts")
        if last:
            coup, delta = call(
                functools.partial(last_kernel, len(sums), total),
                "last",
                [state, ((rank, rank), f32)],
                *sums, mixed, tall,
            )
        else:
            aux, dual, known = call(
                ahead_kernel, "ahead", [state, state, state],
                inside, from_left, from_right, target, tall, data_side, rho, inverse,
            )
            tall, target, gram, delta = call(
                functools.partial(step_kernel, len(sums), total, inner == INNER - 2),
                "step",
                [state, state, ((groups, rank, wide), f32), ((rank, rank), f32)],
                *sums, mixed, tall, known, dual, inverse, rho,
            )
    return (flip(target), flip(coup), delta)


def solution(mesh):
    return jax.shard_map(
        body,
        mesh=mesh,
        in_specs=(
            P("cuts", None, "chan"),
            P("cuts"),
            P("chan", None),
            P("cuts", None),
            P("cuts", "chan", None),
            P("cuts", "chan", None),
            P("cuts", "chan", None),
            P("cuts", "chan", None),
            P(),
        ),
        out_specs=(P("cuts", "chan", None), P("cuts", "chan", None), P()),
        check_vma=False,
    )
```

```python
import functools

import jax
import jax.numpy as jnp
from jax import lax
from jax.experimental import pallas as pl
from jax.experimental.pallas import tpu as pltpu
from jax.sharding import PartitionSpec as P

INNER = 3
SWEEPS = 4
POLAR = 8

smooth_weight = 1.0
eps_trace = 1e-06
f32 = jnp.float32
bf16 = jnp.bfloat16
NN = (((1,), (0,)), ((), ()))
NT = (((1,), (1,)), ((), ()))


def dot(left, right, dims=NN):
    return lax.dot_general(left, right, dims, preferred_element_type=f32)


def split(value):
    high = value.astype(bf16)
    low = (value - high.astype(f32)).astype(bf16)
    return high, low


def left_triple(value):
    high, low = split(value)
    return jnp.concatenate([high, high, low], axis=1)


def right_triple(value):
    high, low = split(value)
    return jnp.concatenate([high, low, high], axis=0)


def block_mask(rank, group):
    wide = rank * group
    rows = lax.div(lax.broadcasted_iota(jnp.int32, (wide, wide), 0), rank)
    cols = lax.div(lax.broadcasted_iota(jnp.int32, (wide, wide), 1), rank)
    return jnp.where(rows == cols, 1.0, 0.0).astype(bf16)


def wide_eye(rank, group):
    rows = lax.broadcasted_iota(jnp.int32, (rank, rank * group), 0)
    cols = lax.broadcasted_iota(jnp.int32, (rank, rank * group), 1)
    return jnp.where(rows == lax.rem(cols, rank), 1.0, 0.0).astype(f32)


def block_diagonal(value, mask, group):
    high, low = split(value)
    return (
        jnp.concatenate([high] * group, axis=0) * mask,
        jnp.concatenate([low] * group, axis=0) * mask,
    )


def times_blocks(values, blocks, dims=NN):
    rank = values[0].shape[0]
    count = len(values)
    pieces = [split(value) for value in values]
    high = jnp.concatenate([piece[0] for piece in pieces], axis=0)
    both = jnp.concatenate([high] + [piece[1] for piece in pieces], axis=0)
    first = dot(both, blocks[0], dims)
    total = first[: count * rank] + first[count * rank :] + dot(high, blocks[1], dims)
    return [total[at * rank : (at + 1) * rank] for at in range(count)]


def diagonal_blocks(value, rank, group):
    at = lax.div(lax.broadcasted_iota(jnp.int32, (rank, rank * group), 1), rank)
    total = value[:rank]
    for block in range(1, group):
        total = jnp.where(at == block, value[block * rank : (block + 1) * rank], total)
    return total


def group_size(count, rank):
    group = max(1, 256 // rank)
    while count % group:
        group -= 1
    return group


def project_kernel(order_ref, me_ref, first_ref, second_ref, factor_ref, after_ref, *outs):
    parts = len(outs)
    rows = outs[0].shape[2] // 2
    factor = factor_ref[...]
    for part in reversed(range(parts)):
        start = pl.multiple_of(lax.rem(me_ref[0] + part, parts) * rows, 16)
        both = jnp.concatenate(
            [first_ref[0, pl.ds(start, rows), :], second_ref[0, pl.ds(start, rows), :]], axis=0
        )
        outs[part][0] = dot(both, factor, NT).T


def setup_kernel(grams, group, *refs):
    gram_refs, refs = refs[:grams], refs[grams:]
    (left_ref, own_ref, right_ref, weights_ref, projected_ref) = refs[:5]
    (aux_ref, coupled_ref, dual_s_ref, dual_c_ref) = refs[5:9]
    (inverse_ref, rho_ref, base_ref) = refs[9:]
    count, rank = own_ref.shape
    rows = aux_ref.shape[2]
    gram = gram_refs[0][...]
    for ref in gram_refs[1:]:
        gram = gram + ref[...]
    eye = wide_eye(rank, 1)
    diagonal = jnp.sum(gram * eye, axis=0, keepdims=True)
    weights = jnp.concatenate([left_ref[...], own_ref[...], right_ref[...]], axis=0)
    rho = jnp.sum(weights * weights * diagonal, axis=1, keepdims=True) / rank
    rho_ref[...] = jnp.broadcast_to(rho, rho_ref.shape)
    width = left_ref.shape[0]

    edge = 34.0 / 32.0
    lead = 4.0 * edge**3 / (4.0 * edge**3 - 3.0 * edge)
    mask = block_mask(rank, group)
    wide = wide_eye(rank, group)
    for first in range(0, count, group):
        scaled = []
        for k in range(first, first + group):
            unit = 1.0 / (34.0 * rho[width + k : width + k + 1, :])
            column = weights_ref[:, k : k + 1]
            scaled.append(
                column * gram * own_ref[k : k + 1, :] * unit + (2.0 / 34.0) * eye
            )
        system = jnp.concatenate(scaled, axis=1)
        rest = wide - system
        blocks = block_diagonal(rest, mask, group)
        (square,) = times_blocks([rest], blocks)
        (cube,) = times_blocks([square], blocks)
        inverse = wide + lead * (rest + square)
        rest = lead * cube - (lead - 1.0) * rest
        for step in range(4):
            blocks = block_diagonal(rest, mask, group)
            more, rest = times_blocks([inverse, rest], blocks)
            inverse = inverse + more
        system_blocks = block_diagonal(system, mask, group)
        for step in range(2):
            (product,) = times_blocks([inverse], system_blocks)
            blocks = block_diagonal(wide - product, mask, group)
            (more,) = times_blocks([inverse], blocks)
            inverse = inverse + more
        for k in range(first, first + group):
            unit = 1.0 / (34.0 * rho[width + k : width + k + 1, :])
            place = (k - first) * rank
            inverse_ref[k] = left_triple(inverse[:, place : place + rank] * unit)
    for k in range(count):
        column = weights_ref[:, k : k + 1]
        half = (k % 2) * rows
        base_ref[k] = column * projected_ref[k // 2, :, half : half + rows] + rho[
            width + k : width + k + 1, :
        ] * (aux_ref[k] - dual_s_ref[k] + coupled_ref[k] - dual_c_ref[k])


def gram_blocks(talls, rank):
    group = len(talls)
    pieces = [split(tall) for tall in talls]
    high = jnp.concatenate([piece[0] for piece in pieces], axis=0)
    low = jnp.concatenate([piece[1] for piece in pieces], axis=0)
    wide = group * rank
    first = dot(jnp.concatenate([high, low], axis=0), high, NT)
    return diagonal_blocks(first[:wide] + first[wide:] + dot(high, low, NT), rank, group)


def first_kernel(parts, group, *refs):
    base_ref, weights_ref, inverse_ref, dual_s_ref, dual_c_ref = refs[:5]
    recv_refs = refs[5 : 5 + parts]
    tall_ref, target_ref, gram_ref = refs[5 + parts :]
    count, rank, rows = base_ref.shape
    for first in range(0, count, group):
        talls = []
        for k in range(first, first + group):
            half = (k % 2) * rows
            right = base_ref[k]
            if recv_refs:
                more = recv_refs[0][k // 2, :, half : half + rows]
                for ref in recv_refs[1:]:
                    more = more + ref[k // 2, :, half : half + rows]
                right = right + weights_ref[:, k : k + 1] * more
            evolving = dot(inverse_ref[k], right_triple(right))
            target_ref[k] = evolving + dual_s_ref[k]
            tall = evolving + dual_c_ref[k]
            tall_ref[k] = tall
            talls.append(tall)
        gram_ref[first // group] = gram_blocks(talls, rank)


def smooth_kernel(parts, odd_ref, aux_ref, target_ref, rho_ref, *refs):
    inside_ref, near_ref, far_ref = refs[-3:]
    count, rank, rows = aux_ref.shape
    if parts:
        weights_ref, projected_refs, side_ref = refs[0], refs[1 : 1 + parts], refs[1 + parts]
        for k in range(count):
            half = (k % 2) * rows
            side = projected_refs[0][k // 2, :, half : half + rows]
            for ref in projected_refs[1:]:
                side = side + ref[k // 2, :, half : half + rows]
            side_ref[k] = weights_ref[:, k : k + 1] * side
    width = SWEEPS
    rho = {j: rho_ref[width + j : width + j + 1, 0:1] for j in range(-width, count + width)}
    share = {j: 2.0 * smooth_weight / (rho[j] + 4.0 * smooth_weight) for j in rho}
    pull = {j: (rho[j] / (rho[j] + 4.0 * smooth_weight)) * target_ref[j] for j in range(count)}
    now = {j: aux_ref[j] for j in range(count)}
    for sweep in range(width):
        later = {}
        for j in range(-sweep - 1, count + sweep + 1):
            beside = [now[i] for i in (j - 1, j + 1) if i in now]
            total = beside[0] if len(beside) == 1 else beside[0] + beside[1]
            total = share[j] * total
            later[j] = total + pull[j] if j in pull else total
        now = later
    for j in range(count):
        inside_ref[j] = now[j]
    for j in range(width):
        near_ref[j] = jnp.where(odd_ref[0] == 1, now[j - width], now[count + j])
        far_ref[j] = jnp.where(odd_ref[0] == 1, now[count + j], now[j - width])


def polar_kernel(grams, after_ref, delta_ref, *refs):
    gram_refs = refs[:grams]
    mixed_ref, partial_ref = refs[grams:]
    groups, rank, wide = mixed_ref.shape
    group = wide // rank
    delta = delta_ref[...]
    mask = block_mask(rank, group)
    eye = wide_eye(rank, group)
    delta_left = left_triple(delta)
    delta_blocks = block_diagonal(jnp.concatenate([delta] * group, axis=1), mask, group)
    sums, currents, roots, scales = [], [], [], []
    for at in range(groups):
        gram = gram_refs[0][at]
        for ref in gram_refs[1:]:
            gram = gram + ref[at]
        sums.append(gram)
        left = dot(delta_left, right_triple(gram))
        (normal,) = times_blocks([left], delta_blocks, NT)
        line = jnp.broadcast_to(jnp.sum(normal * eye, axis=0, keepdims=True), (16, wide))
        high, low = split(line)
        rest = (line - high.astype(f32) - low.astype(f32)).astype(bf16)
        line = dot(high, mask) + dot(low, mask) + dot(rest, mask)
        trace = line[0:1] + eps_trace
        currents.append(normal / trace)
        scales.append(1.0 / jnp.sqrt(trace))
    for step in range(POLAR):
        for at in range(groups):
            product = currents[at]
            if step == 0:
                roots.append(1.5 * eye - 0.5 * product)
                blocks = block_diagonal(product, mask, group)
                (square,) = times_blocks([product], blocks)
            elif step < POLAR - 1:
                blocks = block_diagonal(product, mask, group)
                square, more = times_blocks([product, roots[at]], blocks)
                roots[at] = 1.5 * roots[at] - 0.5 * more
            else:
                blocks = block_diagonal(product, mask, group)
                (more,) = times_blocks([roots[at]], blocks)
                roots[at] = 1.5 * roots[at] - 0.5 * more
            if step < POLAR - 1:
                half = 1.5 * product - 0.5 * square
                (more,) = times_blocks([half], blocks)
                currents[at] = 1.5 * half - 0.5 * more
    left, right = [], []
    for at in range(groups):
        (mixed,) = times_blocks([roots[at]], delta_blocks)
        mixed = mixed * scales[at]
        mixed_ref[at] = mixed
        high, low = split(mixed)
        left += [high, high, low]
        high, low = split(sums[at])
        right += [high, low, high]
    partial = dot(jnp.concatenate(left, axis=1), jnp.concatenate(right, axis=1), NT)
    half = rank // 2
    partial_ref[...] = jnp.concatenate([partial[:half], partial[half:]], axis=1)


def ahead_kernel(
    odd_ref, inside_ref, near_ref, far_ref, target_ref, tall_ref, base_ref, rho_ref, inverse_ref,
    aux_ref, dual_ref, known_ref,
):
    count = inside_ref.shape[0]
    width = SWEEPS
    for k in range(count):
        aux = inside_ref[k]
        if k < width:
            aux = aux + jnp.where(odd_ref[0] == 1, near_ref[k], far_ref[k])
        if k >= count - width:
            at = k - count + width
            aux = aux + jnp.where(odd_ref[0] == 1, far_ref[at], near_ref[at])
        target = target_ref[k]
        rho = rho_ref[width + k : width + k + 1, 0:1]
        aux_ref[k] = aux
        dual_ref[k] = target - aux
        known_ref[k] = dot(
            inverse_ref[k], right_triple(base_ref[k] + rho * (2.0 * aux - target - tall_ref[k]))
        )


def new_delta(sums, total, rank):
    packed = sums[0][...]
    for ref in sums[1:]:
        packed = packed + ref[...]
    packed = packed / total
    return jnp.concatenate([packed[:, :rank], packed[:, rank:]], axis=0)


def step_kernel(sums, total, last, *refs):
    sum_refs, refs = refs[:sums], refs[sums:]
    mixed_ref, tall_ref, known_ref, dual_ref, inverse_ref, rho_ref = refs[:6]
    next_ref, target_ref, gram_ref, delta_ref = refs[6:]
    groups, rank, wide = mixed_ref.shape
    group = wide // rank
    delta = new_delta(sum_refs, total, rank)
    delta_ref[...] = delta
    delta_left = left_triple(delta.T)
    width = SWEEPS
    for at in range(groups):
        mixer = dot(delta_left, right_triple(mixed_ref[at]))
        inverses = jnp.concatenate(
            [inverse_ref[k] for k in range(at * group, (at + 1) * group)], axis=0
        )
        onward = diagonal_blocks(dot(inverses, right_triple(mixer)), rank, group)
        talls = []
        for k in range(at * group, (at + 1) * group):
            place = (k - at * group) * rank
            rho = rho_ref[width + k : width + k + 1, 0:1]
            forward = 2.0 * rho * onward[:, place : place + rank]
            change = forward - mixer[:, place : place + rank]
            tall = tall_ref[k]
            left = jnp.concatenate([left_triple(change), left_triple(forward)], axis=0)
            both = dot(left, right_triple(tall))
            known = known_ref[k]
            later = known + tall + both[:rank]
            next_ref[k] = later
            evolving = known + both[rank:]
            target_ref[k] = evolving if last else evolving + dual_ref[k]
            talls.append(later)
        gram_ref[at] = gram_blocks(talls, rank)


def last_kernel(sums, total, *refs):
    sum_refs, refs = refs[:sums], refs[sums:]
    mixed_ref, tall_ref, coupled_ref, delta_ref = refs
    groups, rank, wide = mixed_ref.shape
    group = wide // rank
    delta = new_delta(sum_refs, total, rank)
    delta_ref[...] = delta
    delta_left = left_triple(delta.T)
    for at in range(groups):
        mixer = dot(delta_left, right_triple(mixed_ref[at]))
        for k in range(at * group, (at + 1) * group):
            place = (k - at * group) * rank
            coupled_ref[k] = dot(
                left_triple(mixer[:, place : place + rank]), right_triple(tall_ref[k])
            )


per_microsecond = 1_100_000_000


def call(kernel, name, outs, *args, scalars=0, unread=0, microseconds=1):
    flops = microseconds * per_microsecond
    specs = [pl.BlockSpec(memory_space=pltpu.SMEM)] * scalars
    specs += [pl.BlockSpec(memory_space=pl.ANY)] * unread
    specs += [pl.BlockSpec(memory_space=pltpu.VMEM)] * (len(args) - len(specs))
    shapes = [jax.ShapeDtypeStruct(shape, dtype) for shape, dtype in outs]
    moved = sum(arg.size * arg.dtype.itemsize for arg in args)
    moved += sum(shape.size * shape.dtype.itemsize for shape in shapes)
    return pl.pallas_call(
        kernel,
        out_shape=shapes,
        in_specs=specs,
        out_specs=[pl.BlockSpec(memory_space=pltpu.VMEM)] * len(shapes),
        compiler_params=pltpu.CompilerParams(vmem_limit_bytes=40 * 1024 * 1024),
        cost_estimate=pl.CostEstimate(flops=flops, bytes_accessed=moved, transcendentals=0),
        name=name,
    )(*args)


def rotated(value, axis, shift):
    count = lax.axis_size(axis)
    return lax.ppermute(value, axis, [(i, (i + shift) % count) for i in range(count)])


def swapped(value, axis, first):
    count = lax.axis_size(axis)
    pairs = [((i + first) % count, (i + first + 1) % count) for i in range(0, count, 2)]
    return lax.ppermute(value, axis, pairs + [(b, a) for a, b in pairs])


def from_others(value, axis):
    return [rotated(value, axis, shift) for shift in range(1, lax.axis_size(axis))]


def stage_sizes(count):
    sizes = []
    while count > 1:
        size = next(size for size in (4, 2, 3, 5, 7, count) if count % size == 0)
        sizes.append(size)
        count //= size
    return sizes


def in_stages(value, axis):
    count = lax.axis_size(axis)
    stride = 1
    terms = [value]
    for size in stage_sizes(count):
        value = terms[0]
        for term in terms[1:]:
            value = value + term
        terms = [value]
        for shift in range(1, size):
            moves = []
            for i in range(count):
                digit = (i // stride) % size
                moves.append((i, i + ((digit + shift) % size - digit) * stride))
            terms.append(lax.ppermute(value, axis, moves))
        stride *= size
    return terms


def body(
    data, order, chan_factor, slice_weights, smooth_aux, coupled, smooth_dual, coupling_dual, delta
):
    count, all_rows, channels = data.shape
    rank = chan_factor.shape[1]
    rows = smooth_aux.shape[1]
    parts = lax.axis_size("chan")
    total = count * lax.axis_size("cuts")
    group = group_size(count, rank)
    groups = count // group
    wide = group * rank
    flip = lambda value: jnp.swapaxes(value, 1, 2)
    aux, coup, dual_s, dual_c = map(flip, (smooth_aux, coupled, smooth_dual, coupling_dual))
    factor = chan_factor.T
    state = ((count, rank, rows), f32)

    gram_part = dot(factor, factor, NT)
    grams = [gram_part] + from_others(gram_part, "chan")
    before = rotated(slice_weights[count - SWEEPS :], "cuts", 1)
    after = rotated(slice_weights[:SWEEPS], "cuts", -1)

    me = lax.axis_index("chan").astype(jnp.int32).reshape(1)
    block = pl.BlockSpec((1, rank, 2 * rows), lambda i, order, me: (i, 0, 0))
    spec = lambda odd: pl.BlockSpec(
        (1, all_rows, channels), lambda i, order, me: (lax.rem(order[2 * i + odd], count), 0, 0)
    )
    projected = pl.pallas_call(
        project_kernel,
        out_shape=[jax.ShapeDtypeStruct((count // 2, rank, 2 * rows), f32)] * parts,
        grid_spec=pltpu.PrefetchScalarGridSpec(
            num_scalar_prefetch=2,
            grid=(count // 2,),
            in_specs=[
                spec(0),
                spec(1),
                pl.BlockSpec((rank, channels), lambda i, order, me: (0, 0)),
                pl.BlockSpec(memory_space=pl.ANY),
            ],
            out_specs=[block] * parts,
        ),
        cost_estimate=pl.CostEstimate(
            flops=3 * per_microsecond, bytes_accessed=2 * data.size, transcendentals=0
        ),
        name="project",
    )(order, me, data, data, factor, gram_part)
    arrived = [rotated(projected[shift], "chan", shift) for shift in range(1, parts)]

    weights = slice_weights.T
    inverse, rho, base = call(
        functools.partial(setup_kernel, len(grams), group),
        "setup",
        [((count, rank, 3 * rank), bf16), ((count + 2 * SWEEPS, 128), f32), state],
        *grams, before, slice_weights, after, weights, projected[0],
        aux, coup, dual_s, dual_c,
        microseconds=4,
    )
    tall, target, gram = call(
        functools.partial(first_kernel, parts - 1, group),
        "first",
        [state, state, ((groups, rank, wide), f32)],
        base, weights, inverse, dual_s, dual_c, *arrived,
    )

    halo = ((SWEEPS, rank, rows), f32)
    odd = lax.rem(lax.axis_index("cuts"), 2).astype(jnp.int32).reshape(1)
    for inner in range(INNER):
        others = from_others(gram, "chan")
        last = inner == INNER - 1
        if not last:
            if inner == 0:
                data_side, inside, to_near, to_far = call(
                    functools.partial(smooth_kernel, parts),
                    "smooth",
                    [state, state, halo, halo],
                    odd, aux, target, rho, weights, projected[0], *arrived,
                    scalars=1,
                )
            else:
                inside, to_near, to_far = call(
                    functools.partial(smooth_kernel, 0),
                    "smooth",
                    [state, halo, halo],
                    odd, aux, target, rho,
                    scalars=1,
                )
            near = swapped(to_near, "cuts", 0)
            far = swapped(to_far, "cuts", 1)
        mixed, partial = call(
            functools.partial(polar_kernel, parts),
            "polar",
            [((groups, rank, wide), f32), ((rank // 2, 2 * rank), f32)],
            inside, delta, gram, *others,
            unread=1, microseconds=5,
        )
        sums = in_stages(partial, "cuts")
        if last:
            coup, delta = call(
                functools.partial(last_kernel, len(sums), total),
                "last",
                [state, ((rank, rank), f32)],
                *sums, mixed, tall,
            )
        else:
            aux, dual, known = call(
                ahead_kernel, "ahead", [state, state, state],
                odd, inside, near, far, target, tall, data_side, rho, inverse,
                scalars=1,
            )
            tall, target, gram, delta = call(
                functools.partial(step_kernel, len(sums), total, inner == INNER - 2),
                "step",
                [state, state, ((groups, rank, wide), f32), ((rank, rank), f32)],
                *sums, mixed, tall, known, dual, inverse, rho,
            )
    return (flip(target), flip(coup), delta)


def solution(mesh):
    return jax.shard_map(
        body,
        mesh=mesh,
        in_specs=(
            P("cuts", None, "chan"),
            P("cuts"),
            P("chan", None),
            P("cuts", None),
            P("cuts", "chan", None),
            P("cuts", "chan", None),
            P("cuts", "chan", None),
            P("cuts", "chan", None),
            P(),
        ),
        out_specs=(P("cuts", "chan", None), P("cuts", "chan", None), P()),
        check_vma=False,
    )
```

```python
import functools

import jax
import jax.numpy as jnp
from jax import lax
from jax.experimental import pallas as pl
from jax.experimental.pallas import tpu as pltpu
from jax.sharding import PartitionSpec as P

INNER = 3
SWEEPS = 4
POLAR = 8

smooth_weight = 1.0
eps_trace = 1e-06
f32 = jnp.float32
bf16 = jnp.bfloat16
NN = (((1,), (0,)), ((), ()))
NT = (((1,), (1,)), ((), ()))


def dot(left, right, dims=NN):
    return lax.dot_general(left, right, dims, preferred_element_type=f32)


def split(value):
    high = value.astype(bf16)
    low = (value - high.astype(f32)).astype(bf16)
    return high, low


def left_triple(value):
    high, low = split(value)
    return jnp.concatenate([high, high, low], axis=1)


def right_triple(value):
    high, low = split(value)
    return jnp.concatenate([high, low, high], axis=0)


def block_mask(rank, group):
    wide = rank * group
    rows = lax.div(lax.broadcasted_iota(jnp.int32, (wide, wide), 0), rank)
    cols = lax.div(lax.broadcasted_iota(jnp.int32, (wide, wide), 1), rank)
    return jnp.where(rows == cols, 1.0, 0.0).astype(bf16)


def wide_eye(rank, group):
    rows = lax.broadcasted_iota(jnp.int32, (rank, rank * group), 0)
    cols = lax.broadcasted_iota(jnp.int32, (rank, rank * group), 1)
    return jnp.where(rows == lax.rem(cols, rank), 1.0, 0.0).astype(f32)


def block_diagonal(value, mask, group):
    high, low = split(value)
    return (
        jnp.concatenate([high] * group, axis=0) * mask,
        jnp.concatenate([low] * group, axis=0) * mask,
    )


def times_blocks(values, blocks, dims=NN):
    rank = values[0].shape[0]
    count = len(values)
    pieces = [split(value) for value in values]
    high = jnp.concatenate([piece[0] for piece in pieces], axis=0)
    both = jnp.concatenate([high] + [piece[1] for piece in pieces], axis=0)
    first = dot(both, blocks[0], dims)
    total = first[: count * rank] + first[count * rank :] + dot(high, blocks[1], dims)
    return [total[at * rank : (at + 1) * rank] for at in range(count)]


def diagonal_blocks(value, rank, group):
    at = lax.div(lax.broadcasted_iota(jnp.int32, (rank, rank * group), 1), rank)
    total = value[:rank]
    for block in range(1, group):
        total = jnp.where(at == block, value[block * rank : (block + 1) * rank], total)
    return total


def group_size(count, rank):
    group = max(1, 256 // rank)
    while count % group:
        group -= 1
    return group


def project_kernel(order_ref, me_ref, first_ref, second_ref, factor_ref, after_ref, *outs):
    parts = len(outs)
    rows = outs[0].shape[2] // 2
    factor = factor_ref[...]
    for part in reversed(range(parts)):
        start = pl.multiple_of(lax.rem(me_ref[0] + part, parts) * rows, 16)
        both = jnp.concatenate(
            [first_ref[0, pl.ds(start, rows), :], second_ref[0, pl.ds(start, rows), :]], axis=0
        )
        outs[part][0] = dot(both, factor, NT).T


def setup_kernel(grams, group, *refs):
    gram_refs, refs = refs[:grams], refs[grams:]
    (left_ref, own_ref, right_ref, weights_ref, projected_ref) = refs[:5]
    (aux_ref, coupled_ref, dual_s_ref, dual_c_ref) = refs[5:9]
    (inverse_ref, rho_ref, base_ref) = refs[9:]
    count, rank = own_ref.shape
    rows = aux_ref.shape[2]
    gram = gram_refs[0][...]
    for ref in gram_refs[1:]:
        gram = gram + ref[...]
    eye = wide_eye(rank, 1)
    diagonal = jnp.sum(gram * eye, axis=0, keepdims=True)
    weights = jnp.concatenate([left_ref[...], own_ref[...], right_ref[...]], axis=0)
    rho = jnp.sum(weights * weights * diagonal, axis=1, keepdims=True) / rank
    rho_ref[...] = jnp.broadcast_to(rho, rho_ref.shape)
    width = left_ref.shape[0]

    edge = 34.0 / 32.0
    lead = 4.0 * edge**3 / (4.0 * edge**3 - 3.0 * edge)
    mask = block_mask(rank, group)
    wide = wide_eye(rank, group)
    for first in range(0, count, group):
        scaled = []
        for k in range(first, first + group):
            unit = 1.0 / (34.0 * rho[width + k : width + k + 1, :])
            column = weights_ref[:, k : k + 1]
            scaled.append(
                column * gram * own_ref[k : k + 1, :] * unit + (2.0 / 34.0) * eye
            )
        system = jnp.concatenate(scaled, axis=1)
        rest = wide - system
        blocks = block_diagonal(rest, mask, group)
        (square,) = times_blocks([rest], blocks)
        (cube,) = times_blocks([square], blocks)
        inverse = wide + lead * (rest + square)
        rest = lead * cube - (lead - 1.0) * rest
        for step in range(4):
            blocks = block_diagonal(rest, mask, group)
            more, rest = times_blocks([inverse, rest], blocks)
            inverse = inverse + more
        system_blocks = block_diagonal(system, mask, group)
        for step in range(2):
            (product,) = times_blocks([inverse], system_blocks)
            blocks = block_diagonal(wide - product, mask, group)
            (more,) = times_blocks([inverse], blocks)
            inverse = inverse + more
        for k in range(first, first + group):
            unit = 1.0 / (34.0 * rho[width + k : width + k + 1, :])
            place = (k - first) * rank
            inverse_ref[k] = left_triple(inverse[:, place : place + rank] * unit)
    for k in range(count):
        column = weights_ref[:, k : k + 1]
        half = (k % 2) * rows
        base_ref[k] = column * projected_ref[k // 2, :, half : half + rows] + rho[
            width + k : width + k + 1, :
        ] * (aux_ref[k] - dual_s_ref[k] + coupled_ref[k] - dual_c_ref[k])


def gram_blocks(talls, rank):
    group = len(talls)
    pieces = [split(tall) for tall in talls]
    high = jnp.concatenate([piece[0] for piece in pieces], axis=0)
    low = jnp.concatenate([piece[1] for piece in pieces], axis=0)
    wide = group * rank
    first = dot(jnp.concatenate([high, low], axis=0), high, NT)
    return diagonal_blocks(first[:wide] + first[wide:] + dot(high, low, NT), rank, group)


def first_kernel(parts, group, *refs):
    base_ref, weights_ref, inverse_ref, dual_s_ref, dual_c_ref = refs[:5]
    recv_refs = refs[5 : 5 + parts]
    tall_ref, target_ref, gram_ref = refs[5 + parts :]
    count, rank, rows = base_ref.shape
    for first in range(0, count, group):
        talls = []
        for k in range(first, first + group):
            half = (k % 2) * rows
            right = base_ref[k]
            if recv_refs:
                more = recv_refs[0][k // 2, :, half : half + rows]
                for ref in recv_refs[1:]:
                    more = more + ref[k // 2, :, half : half + rows]
                right = right + weights_ref[:, k : k + 1] * more
            evolving = dot(inverse_ref[k], right_triple(right))
            target_ref[k] = evolving + dual_s_ref[k]
            tall = evolving + dual_c_ref[k]
            tall_ref[k] = tall
            talls.append(tall)
        gram_ref[first // group] = gram_blocks(talls, rank)


def smooth_kernel(parts, odd_ref, aux_ref, target_ref, rho_ref, *refs):
    inside_ref, near_ref, far_ref = refs[-3:]
    count, rank, rows = aux_ref.shape
    if parts:
        weights_ref, projected_refs, side_ref = refs[0], refs[1 : 1 + parts], refs[1 + parts]
        for k in range(count):
            half = (k % 2) * rows
            side = projected_refs[0][k // 2, :, half : half + rows]
            for ref in projected_refs[1:]:
                side = side + ref[k // 2, :, half : half + rows]
            side_ref[k] = weights_ref[:, k : k + 1] * side
    width = SWEEPS
    rho = {j: rho_ref[width + j : width + j + 1, 0:1] for j in range(-width, count + width)}
    share = {j: 2.0 * smooth_weight / (rho[j] + 4.0 * smooth_weight) for j in rho}
    pull = {j: (rho[j] / (rho[j] + 4.0 * smooth_weight)) * target_ref[j] for j in range(count)}
    now = {j: aux_ref[j] for j in range(count)}
    for sweep in range(width):
        later = {}
        for j in range(-sweep - 1, count + sweep + 1):
            beside = [now[i] for i in (j - 1, j + 1) if i in now]
            total = beside[0] if len(beside) == 1 else beside[0] + beside[1]
            total = share[j] * total
            later[j] = total + pull[j] if j in pull else total
        now = later
    for j in range(count):
        inside_ref[j] = now[j]
    for j in range(width):
        near_ref[j] = jnp.where(odd_ref[0] == 1, now[j - width], now[count + j])
        far_ref[j] = jnp.where(odd_ref[0] == 1, now[count + j], now[j - width])


def polar_kernel(grams, after_ref, delta_ref, *refs):
    gram_refs = refs[:grams]
    mixed_ref, partial_ref = refs[grams:]
    groups, rank, wide = mixed_ref.shape
    group = wide // rank
    delta = delta_ref[...]
    mask = block_mask(rank, group)
    eye = wide_eye(rank, group)
    delta_left = left_triple(delta)
    delta_blocks = block_diagonal(jnp.concatenate([delta] * group, axis=1), mask, group)
    sums, currents, roots, scales = [], [], [], []
    for at in range(groups):
        gram = gram_refs[0][at]
        for ref in gram_refs[1:]:
            gram = gram + ref[at]
        sums.append(gram)
        left = dot(delta_left, right_triple(gram))
        (normal,) = times_blocks([left], delta_blocks, NT)
        line = jnp.broadcast_to(jnp.sum(normal * eye, axis=0, keepdims=True), (16, wide))
        high, low = split(line)
        rest = (line - high.astype(f32) - low.astype(f32)).astype(bf16)
        line = dot(high, mask) + dot(low, mask) + dot(rest, mask)
        trace = line[0:1] + eps_trace
        currents.append(normal / trace)
        scales.append(1.0 / jnp.sqrt(trace))
    for step in range(POLAR):
        for at in range(groups):
            product = currents[at]
            if step == 0:
                roots.append(1.5 * eye - 0.5 * product)
                blocks = block_diagonal(product, mask, group)
                (square,) = times_blocks([product], blocks)
            elif step < POLAR - 1:
                blocks = block_diagonal(product, mask, group)
                square, more = times_blocks([product, roots[at]], blocks)
                roots[at] = 1.5 * roots[at] - 0.5 * more
            else:
                blocks = block_diagonal(product, mask, group)
                (more,) = times_blocks([roots[at]], blocks)
                roots[at] = 1.5 * roots[at] - 0.5 * more
            if step < POLAR - 1:
                half = 1.5 * product - 0.5 * square
                (more,) = times_blocks([half], blocks)
                currents[at] = 1.5 * half - 0.5 * more
    left, right = [], []
    for at in range(groups):
        (mixed,) = times_blocks([roots[at]], delta_blocks)
        mixed = mixed * scales[at]
        mixed_ref[at] = mixed
        high, low = split(mixed)
        left += [high, high, low]
        high, low = split(sums[at])
        right += [high, low, high]
    partial = dot(jnp.concatenate(left, axis=1), jnp.concatenate(right, axis=1), NT)
    half = rank // 2
    partial = jnp.concatenate([partial[:half], partial[half:]], axis=1)
    for at in range(partial_ref.shape[0]):
        partial_ref[at] = partial


def ahead_kernel(
    odd_ref, inside_ref, near_ref, far_ref, target_ref, tall_ref, base_ref, rho_ref, inverse_ref,
    aux_ref, dual_ref, known_ref,
):
    count = inside_ref.shape[0]
    width = SWEEPS
    for k in range(count):
        aux = inside_ref[k]
        if k < width:
            aux = aux + jnp.where(odd_ref[0] == 1, near_ref[k], far_ref[k])
        if k >= count - width:
            at = k - count + width
            aux = aux + jnp.where(odd_ref[0] == 1, far_ref[at], near_ref[at])
        target = target_ref[k]
        rho = rho_ref[width + k : width + k + 1, 0:1]
        aux_ref[k] = aux
        dual_ref[k] = target - aux
        known_ref[k] = dot(
            inverse_ref[k], right_triple(base_ref[k] + rho * (2.0 * aux - target - tall_ref[k]))
        )


def new_delta(sums, total, rank):
    packed = sums[0][0]
    for at in range(1, sums[0].shape[0]):
        packed = packed + sums[0][at]
    packed = packed / total
    return jnp.concatenate([packed[:, :rank], packed[:, rank:]], axis=0)


def step_kernel(sums, total, last, *refs):
    sum_refs, refs = refs[:sums], refs[sums:]
    mixed_ref, tall_ref, known_ref, dual_ref, inverse_ref, rho_ref = refs[:6]
    next_ref, target_ref, gram_ref, delta_ref = refs[6:]
    groups, rank, wide = mixed_ref.shape
    group = wide // rank
    delta = new_delta(sum_refs, total, rank)
    delta_ref[...] = delta
    delta_left = left_triple(delta.T)
    width = SWEEPS
    for at in range(groups):
        mixer = dot(delta_left, right_triple(mixed_ref[at]))
        inverses = jnp.concatenate(
            [inverse_ref[k] for k in range(at * group, (at + 1) * group)], axis=0
        )
        onward = diagonal_blocks(dot(inverses, right_triple(mixer)), rank, group)
        talls = []
        for k in range(at * group, (at + 1) * group):
            place = (k - at * group) * rank
            rho = rho_ref[width + k : width + k + 1, 0:1]
            forward = 2.0 * rho * onward[:, place : place + rank]
            change = forward - mixer[:, place : place + rank]
            tall = tall_ref[k]
            left = jnp.concatenate([left_triple(change), left_triple(forward)], axis=0)
            both = dot(left, right_triple(tall))
            known = known_ref[k]
            later = known + tall + both[:rank]
            next_ref[k] = later
            evolving = known + both[rank:]
            target_ref[k] = evolving if last else evolving + dual_ref[k]
            talls.append(later)
        gram_ref[at] = gram_blocks(talls, rank)


def last_kernel(sums, total, *refs):
    sum_refs, refs = refs[:sums], refs[sums:]
    mixed_ref, tall_ref, coupled_ref, delta_ref = refs
    groups, rank, wide = mixed_ref.shape
    group = wide // rank
    delta = new_delta(sum_refs, total, rank)
    delta_ref[...] = delta
    delta_left = left_triple(delta.T)
    for at in range(groups):
        mixer = dot(delta_left, right_triple(mixed_ref[at]))
        for k in range(at * group, (at + 1) * group):
            place = (k - at * group) * rank
            coupled_ref[k] = dot(
                left_triple(mixer[:, place : place + rank]), right_triple(tall_ref[k])
            )


per_microsecond = 1_100_000_000


def call(kernel, name, outs, *args, scalars=0, unread=0, microseconds=1):
    flops = microseconds * per_microsecond
    specs = [pl.BlockSpec(memory_space=pltpu.SMEM)] * scalars
    specs += [pl.BlockSpec(memory_space=pl.ANY)] * unread
    specs += [pl.BlockSpec(memory_space=pltpu.VMEM)] * (len(args) - len(specs))
    shapes = [jax.ShapeDtypeStruct(shape, dtype) for shape, dtype in outs]
    moved = sum(arg.size * arg.dtype.itemsize for arg in args)
    moved += sum(shape.size * shape.dtype.itemsize for shape in shapes)
    return pl.pallas_call(
        kernel,
        out_shape=shapes,
        in_specs=specs,
        out_specs=[pl.BlockSpec(memory_space=pltpu.VMEM)] * len(shapes),
        compiler_params=pltpu.CompilerParams(vmem_limit_bytes=40 * 1024 * 1024),
        cost_estimate=pl.CostEstimate(flops=flops, bytes_accessed=moved, transcendentals=0),
        name=name,
    )(*args)


def rotated(value, axis, shift):
    count = lax.axis_size(axis)
    return lax.ppermute(value, axis, [(i, (i + shift) % count) for i in range(count)])


def swapped(value, axis, first):
    count = lax.axis_size(axis)
    pairs = [((i + first) % count, (i + first + 1) % count) for i in range(0, count, 2)]
    return lax.ppermute(value, axis, pairs + [(b, a) for a, b in pairs])


def from_others(value, axis):
    return [rotated(value, axis, shift) for shift in range(1, lax.axis_size(axis))]


def stage_sizes(count):
    sizes = []
    while count > 1:
        size = next(size for size in (4, 2, 3, 5, 7, count) if count % size == 0)
        sizes.append(size)
        count //= size
    return sizes


def in_stages(value, axis):
    count = lax.axis_size(axis)
    stride = 1
    terms = [value]
    for size in stage_sizes(count):
        value = terms[0]
        for term in terms[1:]:
            value = value + term
        terms = [value]
        for shift in range(1, size):
            moves = []
            for i in range(count):
                digit = (i // stride) % size
                moves.append((i, i + ((digit + shift) % size - digit) * stride))
            terms.append(lax.ppermute(value, axis, moves))
        stride *= size
    return terms


def body(
    data, order, chan_factor, slice_weights, smooth_aux, coupled, smooth_dual, coupling_dual, delta
):
    count, all_rows, channels = data.shape
    rank = chan_factor.shape[1]
    rows = smooth_aux.shape[1]
    parts = lax.axis_size("chan")
    total = count * lax.axis_size("cuts")
    group = group_size(count, rank)
    groups = count // group
    wide = group * rank
    flip = lambda value: jnp.swapaxes(value, 1, 2)
    aux, coup, dual_s, dual_c = map(flip, (smooth_aux, coupled, smooth_dual, coupling_dual))
    factor = chan_factor.T
    state = ((count, rank, rows), f32)

    gram_part = dot(factor, factor, NT)
    grams = [gram_part] + from_others(gram_part, "chan")
    before = rotated(slice_weights[count - SWEEPS :], "cuts", 1)
    after = rotated(slice_weights[:SWEEPS], "cuts", -1)

    me = lax.axis_index("chan").astype(jnp.int32).reshape(1)
    block = pl.BlockSpec((1, rank, 2 * rows), lambda i, order, me: (i, 0, 0))
    spec = lambda odd: pl.BlockSpec(
        (1, all_rows, channels), lambda i, order, me: (lax.rem(order[2 * i + odd], count), 0, 0)
    )
    projected = pl.pallas_call(
        project_kernel,
        out_shape=[jax.ShapeDtypeStruct((count // 2, rank, 2 * rows), f32)] * parts,
        grid_spec=pltpu.PrefetchScalarGridSpec(
            num_scalar_prefetch=2,
            grid=(count // 2,),
            in_specs=[
                spec(0),
                spec(1),
                pl.BlockSpec((rank, channels), lambda i, order, me: (0, 0)),
                pl.BlockSpec(memory_space=pl.ANY),
            ],
            out_specs=[block] * parts,
        ),
        cost_estimate=pl.CostEstimate(
            flops=3 * per_microsecond, bytes_accessed=2 * data.size, transcendentals=0
        ),
        name="project",
    )(order, me, data, data, factor, gram_part)
    arrived = [rotated(projected[shift], "chan", shift) for shift in range(1, parts)]

    weights = slice_weights.T
    inverse, rho, base = call(
        functools.partial(setup_kernel, len(grams), group),
        "setup",
        [((count, rank, 3 * rank), bf16), ((count + 2 * SWEEPS, 128), f32), state],
        *grams, before, slice_weights, after, weights, projected[0],
        aux, coup, dual_s, dual_c,
        microseconds=4,
    )
    tall, target, gram = call(
        functools.partial(first_kernel, parts - 1, group),
        "first",
        [state, state, ((groups, rank, wide), f32)],
        base, weights, inverse, dual_s, dual_c, *arrived,
    )

    halo = ((SWEEPS, rank, rows), f32)
    odd = lax.rem(lax.axis_index("cuts"), 2).astype(jnp.int32).reshape(1)
    for inner in range(INNER):
        others = from_others(gram, "chan")
        last = inner == INNER - 1
        if not last:
            if inner == 0:
                data_side, inside, to_near, to_far = call(
                    functools.partial(smooth_kernel, parts),
                    "smooth",
                    [state, state, halo, halo],
                    odd, aux, target, rho, weights, projected[0], *arrived,
                    scalars=1,
                )
            else:
                inside, to_near, to_far = call(
                    functools.partial(smooth_kernel, 0),
                    "smooth",
                    [state, halo, halo],
                    odd, aux, target, rho,
                    scalars=1,
                )
            near = swapped(to_near, "cuts", 0)
            far = swapped(to_far, "cuts", 1)
        mixed, partial = call(
            functools.partial(polar_kernel, parts),
            "polar",
            [((groups, rank, wide), f32), ((lax.axis_size("cuts"), rank // 2, 2 * rank), f32)],
            inside, delta, gram, *others,
            unread=1, microseconds=5,
        )
        sums = [lax.all_to_all(partial, "cuts", 0, 0, tiled=True)]
        if last:
            coup, delta = call(
                functools.partial(last_kernel, len(sums), total),
                "last",
                [state, ((rank, rank), f32)],
                *sums, mixed, tall,
            )
        else:
            aux, dual, known = call(
                ahead_kernel, "ahead", [state, state, state],
                odd, inside, near, far, target, tall, data_side, rho, inverse,
                scalars=1,
            )
            tall, target, gram, delta = call(
                functools.partial(step_kernel, len(sums), total, inner == INNER - 2),
                "step",
                [state, state, ((groups, rank, wide), f32), ((rank, rank), f32)],
                *sums, mixed, tall, known, dual, inverse, rho,
            )
    return (flip(target), flip(coup), delta)


def solution(mesh):
    return jax.shard_map(
        body,
        mesh=mesh,
        in_specs=(
            P("cuts", None, "chan"),
            P("cuts"),
            P("chan", None),
            P("cuts", None),
            P("cuts", "chan", None),
            P("cuts", "chan", None),
            P("cuts", "chan", None),
            P("cuts", "chan", None),
            P(),
        ),
        out_specs=(P("cuts", "chan", None), P("cuts", "chan", None), P()),
        check_vma=False,
    )
```

```python
import functools

import jax
import jax.numpy as jnp
from jax import lax
from jax.experimental import pallas as pl
from jax.experimental.pallas import tpu as pltpu
from jax.sharding import PartitionSpec as P

INNER = 3
SWEEPS = 4
POLAR = 8

smooth_weight = 1.0
eps_trace = 1e-06
f32 = jnp.float32
bf16 = jnp.bfloat16
NN = (((1,), (0,)), ((), ()))
NT = (((1,), (1,)), ((), ()))


def dot(left, right, dims=NN):
    return lax.dot_general(left, right, dims, preferred_element_type=f32)


def split(value):
    high = value.astype(bf16)
    low = (value - high.astype(f32)).astype(bf16)
    return high, low


def left_triple(value):
    high, low = split(value)
    return jnp.concatenate([high, high, low], axis=1)


def right_triple(value):
    high, low = split(value)
    return jnp.concatenate([high, low, high], axis=0)


def block_mask(rank, group):
    wide = rank * group
    rows = lax.div(lax.broadcasted_iota(jnp.int32, (wide, wide), 0), rank)
    cols = lax.div(lax.broadcasted_iota(jnp.int32, (wide, wide), 1), rank)
    return jnp.where(rows == cols, 1.0, 0.0).astype(bf16)


def wide_eye(rank, group):
    rows = lax.broadcasted_iota(jnp.int32, (rank, rank * group), 0)
    cols = lax.broadcasted_iota(jnp.int32, (rank, rank * group), 1)
    return jnp.where(rows == lax.rem(cols, rank), 1.0, 0.0).astype(f32)


def block_diagonal(value, mask, group):
    high, low = split(value)
    return (
        jnp.concatenate([high] * group, axis=0) * mask,
        jnp.concatenate([low] * group, axis=0) * mask,
    )


def times_blocks(values, blocks, dims=NN):
    rank = values[0].shape[0]
    count = len(values)
    pieces = [split(value) for value in values]
    high = jnp.concatenate([piece[0] for piece in pieces], axis=0)
    both = jnp.concatenate([high] + [piece[1] for piece in pieces], axis=0)
    first = dot(both, blocks[0], dims)
    total = first[: count * rank] + first[count * rank :] + dot(high, blocks[1], dims)
    return [total[at * rank : (at + 1) * rank] for at in range(count)]


def diagonal_blocks(value, rank, group):
    at = lax.div(lax.broadcasted_iota(jnp.int32, (rank, rank * group), 1), rank)
    total = value[:rank]
    for block in range(1, group):
        total = jnp.where(at == block, value[block * rank : (block + 1) * rank], total)
    return total


def group_size(count, rank):
    group = max(1, 256 // rank)
    while count % group:
        group -= 1
    return group


def project_kernel(first, order_ref, me_ref, data_ref, factor_ref, *refs):
    (gram_ref, *outs), held, arrived = refs[:-2], refs[-2], refs[-1]
    parts = len(outs)
    pairs = outs[0].shape[0]
    rows = outs[0].shape[2] // 2
    count = data_ref.shape[0]
    copies = []
    for at in range(2 * pairs):
        stored = lax.rem(order_ref[2 * first + at], count)
        copy = pltpu.make_async_copy(data_ref.at[stored], held.at[at], arrived.at[at])
        copy.start()
        copies.append(copy)
    factor = factor_ref[...]
    gram_ref[...] = dot(factor, factor, NT)
    for pair in range(pairs):
        copies[2 * pair].wait()
        copies[2 * pair + 1].wait()
        for part in reversed(range(parts)):
            start = pl.multiple_of(lax.rem(me_ref[0] + part, parts) * rows, 16)
            both = jnp.concatenate(
                [held[2 * pair, pl.ds(start, rows), :], held[2 * pair + 1, pl.ds(start, rows), :]],
                axis=0,
            )
            outs[part][pair] = dot(both, factor, NT).T


def setup_kernel(grams, chunks, group, *refs):
    gram_refs, refs = refs[:grams], refs[grams:]
    projected_refs, refs = refs[:chunks], refs[chunks:]
    (own_ref, weights_ref, aux_ref, coupled_ref, dual_s_ref, dual_c_ref) = refs[:6]
    (inverse_ref, rho_ref, head_ref, tail_ref, base_ref) = refs[6:]
    count, rank = own_ref.shape
    rows = aux_ref.shape[2]
    pairs = projected_refs[0].shape[0]
    gram = gram_refs[0][...]
    for ref in gram_refs[1:]:
        gram = gram + ref[...]
    eye = wide_eye(rank, 1)
    diagonal = jnp.sum(gram * eye, axis=0, keepdims=True)
    weights = own_ref[...]
    rho = jnp.sum(weights * weights * diagonal, axis=1, keepdims=True) / rank
    rho_lanes = jnp.broadcast_to(rho, rho_ref.shape)
    rho_ref[...] = rho_lanes
    head_ref[...] = rho_lanes[:SWEEPS]
    tail_ref[...] = rho_lanes[count - SWEEPS :]

    edge = 34.0 / 32.0
    lead = 4.0 * edge**3 / (4.0 * edge**3 - 3.0 * edge)
    mask = block_mask(rank, group)
    wide = wide_eye(rank, group)
    starts = range(0, count, group)
    systems = []
    for first in starts:
        scaled = []
        for k in range(first, first + group):
            unit = 1.0 / (34.0 * rho[k : k + 1, :])
            column = weights_ref[:, k : k + 1]
            scaled.append(column * gram * own_ref[k : k + 1, :] * unit + (2.0 / 34.0) * eye)
        systems.append(jnp.concatenate(scaled, axis=1))
    inverses, rests = [], []
    for system in systems:
        rest = wide - system
        blocks = block_diagonal(rest, mask, group)
        (square,) = times_blocks([rest], blocks)
        (cube,) = times_blocks([square], blocks)
        inverses.append(wide + lead * (rest + square))
        rests.append(lead * cube - (lead - 1.0) * rest)
    for step in range(4):
        for at in range(len(systems)):
            blocks = block_diagonal(rests[at], mask, group)
            more, rests[at] = times_blocks([inverses[at], rests[at]], blocks)
            inverses[at] = inverses[at] + more
    for step in range(2):
        for at in range(len(systems)):
            (product,) = times_blocks([inverses[at]], block_diagonal(systems[at], mask, group))
            blocks = block_diagonal(wide - product, mask, group)
            (more,) = times_blocks([inverses[at]], blocks)
            inverses[at] = inverses[at] + more
    for k in range(count):
        unit = 1.0 / (34.0 * rho[k : k + 1, :])
        place = (k % group) * rank
        inverse_ref[k] = left_triple(inverses[k // group][:, place : place + rank] * unit)
    for k in range(count):
        half = (k % 2) * rows
        chunk, pair = divmod(k // 2, pairs)
        own = projected_refs[chunk][pair, :, half : half + rows]
        base_ref[k] = weights_ref[:, k : k + 1] * own + rho[k : k + 1, :] * (
            aux_ref[k] - dual_s_ref[k] + coupled_ref[k] - dual_c_ref[k]
        )


def cross_blocks(lefts, rights, rank):
    group = len(lefts)
    wide = group * rank
    left = [split(value) for value in lefts]
    high = jnp.concatenate([piece[0] for piece in left], axis=0)
    both = jnp.concatenate([high] + [piece[1] for piece in left], axis=0)
    right = left if rights is lefts else [split(value) for value in rights]
    first = dot(both, jnp.concatenate([piece[0] for piece in right], axis=0), NT)
    second = dot(high, jnp.concatenate([piece[1] for piece in right], axis=0), NT)
    return diagonal_blocks(first[:wide] + first[wide:] + second, rank, group)


def summed(refs, chunks, k, rows):
    half = (k % 2) * rows
    chunk, pair = divmod(k // 2, refs[0].shape[0])
    total = None
    for ref in refs[chunk::chunks]:
        piece = ref[pair, :, half : half + rows]
        total = piece if total is None else total + piece
    return total


def first_kernel(chunks, group, *refs):
    base_ref, weights_ref, inverse_ref, dual_s_ref, dual_c_ref = refs[:5]
    recv_refs = refs[5:-3]
    tall_ref, target_ref, gram_ref = refs[-3:]
    count, rank, rows = base_ref.shape
    for first in range(0, count, group):
        talls = []
        for k in range(first, first + group):
            right = base_ref[k]
            if recv_refs:
                right = right + weights_ref[:, k : k + 1] * summed(recv_refs, chunks, k, rows)
            evolving = dot(inverse_ref[k], right_triple(right))
            target_ref[k] = evolving + dual_s_ref[k]
            tall = evolving + dual_c_ref[k]
            tall_ref[k] = tall
            talls.append(tall)
        gram_ref[first // group] = cross_blocks(talls, talls, rank)


def smooth(odd, now, targets, rho, inside_ref, near_ref, far_ref):
    count = len(targets)
    width = SWEEPS
    share = {j: 2.0 * smooth_weight / (rho[j] + 4.0 * smooth_weight) for j in rho}
    pull = {j: (rho[j] / (rho[j] + 4.0 * smooth_weight)) * targets[j] for j in range(count)}
    now = {j: now[j] for j in range(count)}
    for sweep in range(width):
        later = {}
        for j in range(-sweep - 1, count + sweep + 1):
            beside = [now[i] for i in (j - 1, j + 1) if i in now]
            total = beside[0] if len(beside) == 1 else beside[0] + beside[1]
            total = share[j] * total
            later[j] = total + pull[j] if j in pull else total
        now = later
    for j in range(count):
        inside_ref[j] = now[j]
    for j in range(width):
        near_ref[j] = jnp.where(odd == 1, now[j - width], now[count + j])
        far_ref[j] = jnp.where(odd == 1, now[count + j], now[j - width])


def all_rho(before_ref, rho_ref, after_ref):
    count = rho_ref.shape[0]
    rho = {j: rho_ref[j : j + 1, 0:1] for j in range(count)}
    for j in range(SWEEPS):
        rho[j - SWEEPS] = before_ref[j : j + 1, 0:1]
        rho[count + j] = after_ref[j : j + 1, 0:1]
    return rho


def smooth_kernel(
    chunks, odd_ref, aux_ref, target_ref, before_ref, rho_ref, after_ref, weights_ref, *refs
):
    *projected_refs, side_ref, inside_ref, near_ref, far_ref = refs
    count, rank, rows = aux_ref.shape
    for k in range(count):
        side_ref[k] = weights_ref[:, k : k + 1] * summed(projected_refs, chunks, k, rows)
    rho = all_rho(before_ref, rho_ref, after_ref)
    slices = range(count)
    smooth(
        odd_ref[0], [aux_ref[k] for k in slices], [target_ref[k] for k in slices], rho,
        inside_ref, near_ref, far_ref,
    )


def polar(grams, delta):
    rank, wide = grams[0].shape
    group = wide // rank
    mask = block_mask(rank, group)
    eye = wide_eye(rank, group)
    delta_left = left_triple(delta)
    delta_blocks = block_diagonal(jnp.concatenate([delta] * group, axis=1), mask, group)
    currents, roots, scales = [], [], []
    for gram in grams:
        left = dot(delta_left, right_triple(gram))
        (normal,) = times_blocks([left], delta_blocks, NT)
        line = jnp.broadcast_to(jnp.sum(normal * eye, axis=0, keepdims=True), (16, wide))
        high, low = split(line)
        rest = (line - high.astype(f32) - low.astype(f32)).astype(bf16)
        line = dot(high, mask) + dot(low, mask) + dot(rest, mask)
        trace = line[0:1] + eps_trace
        currents.append(normal / trace)
        scales.append(1.0 / jnp.sqrt(trace))
    for step in range(POLAR):
        for at in range(len(grams)):
            product = currents[at]
            blocks = block_diagonal(product, mask, group)
            if step == 0:
                roots.append(1.5 * eye - 0.5 * product)
                (square,) = times_blocks([product], blocks)
            elif step < POLAR - 1:
                square, more = times_blocks([product, roots[at]], blocks)
                roots[at] = 1.5 * roots[at] - 0.5 * more
            else:
                (more,) = times_blocks([roots[at]], blocks)
                roots[at] = 1.5 * roots[at] - 0.5 * more
            if step < POLAR - 1:
                half = 1.5 * product - 0.5 * square
                (more,) = times_blocks([half], blocks)
                currents[at] = 1.5 * half - 0.5 * more
    return roots, scales


def mix(roots, scales, grams, delta, mixed_ref, partial_ref):
    rank, wide = roots[0].shape
    group = wide // rank
    mask = block_mask(rank, group)
    delta_blocks = block_diagonal(jnp.concatenate([delta] * group, axis=1), mask, group)
    left, right = [], []
    for at in range(len(roots)):
        (mixed,) = times_blocks([roots[at]], delta_blocks)
        mixed = mixed * scales[at]
        mixed_ref[at] = mixed
        high, low = split(mixed)
        left += [high, high, low]
        high, low = split(grams[at])
        right += [high, low, high]
    partial = dot(jnp.concatenate(left, axis=1), jnp.concatenate(right, axis=1), NT)
    half = rank // 2
    partial_ref[...] = jnp.concatenate([partial[:half], partial[half:]], axis=1)


def first_polar_kernel(after_ref, delta_ref, *refs):
    *gram_refs, root_ref, scale_ref, gram_ref = refs
    grams = []
    for at in range(gram_ref.shape[0]):
        gram = gram_refs[0][at]
        for ref in gram_refs[1:]:
            gram = gram + ref[at]
        gram_ref[at] = gram
        grams.append(gram)
    roots, scales = polar(grams, delta_ref[...])
    for at in range(len(grams)):
        root_ref[at] = roots[at]
        scale_ref[at] = jnp.broadcast_to(scales[at], scale_ref.shape[1:])


def later_polar_kernel(last, after_ref, delta_ref, change_ref, old_ref, *refs):
    if last:
        *cross_refs, mixed_ref, partial_ref = refs
    else:
        *cross_refs, root_ref, scale_ref, gram_ref = refs
    groups, rank, wide = old_ref.shape
    group = wide // rank
    mask = block_mask(rank, group)
    grams = []
    for at in range(groups):
        cross = cross_refs[0][at]
        for ref in cross_refs[1:]:
            cross = cross + ref[at]
        change = change_ref[at]
        (onward,) = times_blocks([change], block_diagonal(old_ref[at], mask, group))
        onward = cross[:, :wide] + 0.5 * onward
        (one,) = times_blocks([onward], block_diagonal(change, mask, group), NT)
        (other,) = times_blocks([change], block_diagonal(onward, mask, group), NT)
        grams.append(cross[:, wide:] + one + other)
    delta = delta_ref[...]
    roots, scales = polar(grams, delta)
    if last:
        mix(roots, scales, grams, delta, mixed_ref, partial_ref)
    else:
        for at in range(groups):
            gram_ref[at] = grams[at]
            root_ref[at] = roots[at]
            scale_ref[at] = jnp.broadcast_to(scales[at], scale_ref.shape[1:])


def mix_kernel(near_ref, far_ref, delta_ref, root_ref, scale_ref, gram_ref, mixed_ref, partial_ref):
    groups = range(root_ref.shape[0])
    mix(
        [root_ref[at] for at in groups],
        [scale_ref[at, 0:1] for at in groups],
        [gram_ref[at] for at in groups],
        delta_ref[...], mixed_ref, partial_ref,
    )


def ahead_kernel(
    group, odd_ref, after_ref, inside_ref, near_ref, far_ref, target_ref, tall_ref, side_ref, rho_ref,
    inverse_ref, aux_ref, dual_ref, known_ref, cross_ref,
):
    count, rank, _ = inside_ref.shape
    width = SWEEPS
    knowns, talls = [], []
    for k in range(count):
        aux = inside_ref[k]
        if k < width:
            aux = aux + jnp.where(odd_ref[0] == 1, near_ref[k], far_ref[k])
        if k >= count - width:
            at = k - count + width
            aux = aux + jnp.where(odd_ref[0] == 1, far_ref[at], near_ref[at])
        target, tall = target_ref[k], tall_ref[k]
        aux_ref[k] = aux
        dual_ref[k] = target - aux
        known = dot(
            inverse_ref[k],
            right_triple(side_ref[k] + rho_ref[k : k + 1, 0:1] * (2.0 * aux - target - tall)),
        )
        known_ref[k] = known
        talls.append(tall)
        knowns.append(known + tall)
        if len(talls) == group:
            cross_ref[k // group] = jnp.concatenate(
                [cross_blocks(knowns, talls, rank), cross_blocks(knowns, knowns, rank)], axis=1
            )
            knowns, talls = [], []


def new_delta(sum_refs, total, rank):
    packed = sum_refs[0][...]
    for ref in sum_refs[1:]:
        packed = packed + ref[...]
    packed = packed / total
    return jnp.concatenate([packed[:, :rank], packed[:, rank:]], axis=0)


def mixer_kernel(total, mixed_ref, inverse_ref, rho_ref, *refs):
    *sum_refs, delta_ref, change_ref, forward_ref = refs
    groups, rank, wide = mixed_ref.shape
    group = wide // rank
    delta = new_delta(sum_refs, total, rank)
    delta_ref[...] = delta
    delta_left = left_triple(delta.T)
    place = lax.div(lax.broadcasted_iota(jnp.int32, (1, wide), 1), rank)
    for at in range(groups):
        mixer = dot(delta_left, right_triple(mixed_ref[at]))
        slices = range(at * group, (at + 1) * group)
        inverses = jnp.concatenate([inverse_ref[k] for k in slices], axis=0)
        onward = diagonal_blocks(dot(inverses, right_triple(mixer)), rank, group)
        rho = rho_ref[at * group : at * group + 1, 0:1]
        for k in slices[1:]:
            rho = jnp.where(place == k - at * group, rho_ref[k : k + 1, 0:1], rho)
        forward = 2.0 * rho * onward
        forward_ref[at] = forward
        change_ref[at] = forward - mixer


def rows_kernel(odd_ref, aux_ref, before_ref, rho_ref, after_ref, *refs):
    (change_ref, forward_ref, tall_ref, known_ref, dual_ref) = refs[:5]
    (next_ref, target_ref, inside_ref, near_ref, far_ref) = refs[5:]
    targets = new_rows(change_ref, forward_ref, tall_ref, known_ref, next_ref)
    count = len(targets)
    for k in range(count):
        targets[k] = targets[k] + dual_ref[k]
        target_ref[k] = targets[k]
    rho = all_rho(before_ref, rho_ref, after_ref)
    smooth(
        odd_ref[0], [aux_ref[k] for k in range(count)], targets, rho,
        inside_ref, near_ref, far_ref,
    )


def last_rows_kernel(
    after_ref, change_ref, forward_ref, tall_ref, known_ref, next_ref, evolving_ref
):
    evolvings = new_rows(change_ref, forward_ref, tall_ref, known_ref, next_ref)
    for k in range(len(evolvings)):
        evolving_ref[k] = evolvings[k]


def new_rows(change_ref, forward_ref, tall_ref, known_ref, next_ref):
    groups, rank, wide = change_ref.shape
    group = wide // rank
    evolvings = []
    for k in range(groups * group):
        lanes = slice((k % group) * rank, (k % group + 1) * rank)
        change, forward = change_ref[k // group][:, lanes], forward_ref[k // group][:, lanes]
        left = jnp.concatenate([left_triple(change), left_triple(forward)], axis=0)
        tall, known = tall_ref[k], known_ref[k]
        both = dot(left, right_triple(tall))
        next_ref[k] = known + tall + both[:rank]
        evolvings.append(known + both[rank:])
    return evolvings


def last_kernel(total, mixed_ref, tall_ref, *refs):
    *sum_refs, coupled_ref, delta_ref = refs
    groups, rank, wide = mixed_ref.shape
    group = wide // rank
    delta = new_delta(sum_refs, total, rank)
    delta_ref[...] = delta
    delta_left = left_triple(delta.T)
    for at in range(groups):
        mixer = dot(delta_left, right_triple(mixed_ref[at]))
        for k in range(at * group, (at + 1) * group):
            place = (k - at * group) * rank
            coupled_ref[k] = dot(
                left_triple(mixer[:, place : place + rank]), right_triple(tall_ref[k])
            )


per_microsecond = 1_100_000_000


def call(kernel, name, outs, *args, scalars=0, unread=0, microseconds=1, scratch=()):
    flops = int(microseconds * per_microsecond)
    specs = [pl.BlockSpec(memory_space=pltpu.SMEM)] * scalars
    specs += [pl.BlockSpec(memory_space=pl.ANY)] * unread
    specs += [pl.BlockSpec(memory_space=pltpu.VMEM)] * (len(args) - len(specs))
    shapes = [jax.ShapeDtypeStruct(shape, dtype) for shape, dtype in outs]
    moved = sum(arg.size * arg.dtype.itemsize for arg in args)
    moved += sum(shape.size * shape.dtype.itemsize for shape in shapes)
    return pl.pallas_call(
        kernel,
        out_shape=shapes,
        in_specs=specs,
        out_specs=[pl.BlockSpec(memory_space=pltpu.VMEM)] * len(shapes),
        scratch_shapes=list(scratch),
        compiler_params=pltpu.CompilerParams(vmem_limit_bytes=16 * 1024 * 1024),
        cost_estimate=pl.CostEstimate(flops=flops, bytes_accessed=moved, transcendentals=0),
        name=name,
    )(*args)


def rotated(value, axis, shift):
    count = lax.axis_size(axis)
    return lax.ppermute(value, axis, [(i, (i + shift) % count) for i in range(count)])


def swapped(value, axis, first):
    count = lax.axis_size(axis)
    pairs = [((i + first) % count, (i + first + 1) % count) for i in range(0, count, 2)]
    return lax.ppermute(value, axis, pairs + [(b, a) for a, b in pairs])


def from_others(value, axis):
    return [rotated(value, axis, shift) for shift in range(1, lax.axis_size(axis))]


def stage_sizes(count):
    sizes = []
    while count > 1:
        choices = (2, 3, 5, 7, count) if len(sizes) < 2 else (4, 2, 3, 5, 7, count)
        sizes.append(next(size for size in choices if count % size == 0))
        count //= sizes[-1]
    return sizes


def in_stages(value, axis, beside=None):
    count = lax.axis_size(axis)
    stride = 1
    terms = [value]
    for size in stage_sizes(count):
        value = terms[0]
        for term in terms[1:]:
            value = value + term
        if stride > 1 and beside is not None:
            value, beside = lax.optimization_barrier((value, beside))
        terms = [value]
        for shift in range(1, size):
            moves = []
            for i in range(count):
                digit = (i // stride) % size
                other = digit ^ shift if size in (2, 4) else (digit + shift) % size
                moves.append((i, i + (other - digit) * stride))
            terms.append(lax.ppermute(value, axis, moves))
        stride *= size
    return terms if beside is None else (terms, beside)


def body(
    data, order, chan_factor, slice_weights, smooth_aux, coupled, smooth_dual, coupling_dual, delta
):
    count, all_rows, channels = data.shape
    rank = chan_factor.shape[1]
    rows = smooth_aux.shape[1]
    parts = lax.axis_size("chan")
    total = count * lax.axis_size("cuts")
    group = group_size(count, rank)
    groups = count // group
    wide = group * rank
    flip = lambda value: jnp.swapaxes(value, 1, 2)
    aux, coup, dual_s, dual_c = map(flip, (smooth_aux, coupled, smooth_dual, coupling_dual))
    factor = chan_factor.T
    state = ((count, rank, rows), f32)
    quads = ((groups, rank, wide), f32)
    square = ((rank, rank), f32)
    halo = ((SWEEPS, rank, rows), f32)
    lanes = lambda height: ((height, 128), f32)
    scale = ((groups, 8, wide), f32)

    me = lax.axis_index("chan").astype(jnp.int32).reshape(1)
    odd = lax.rem(lax.axis_index("cuts"), 2).astype(jnp.int32).reshape(1)
    weights = slice_weights.T
    chunks = 2 if count % 4 == 0 else 1
    pairs = count // 2 // chunks
    own, arrived, grams = [], [], []
    for chunk in range(chunks):
        gram_part, *projected = call(
            functools.partial(project_kernel, chunk * pairs),
            "project",
            [square] + [((pairs, rank, 2 * rows), f32)] * parts,
            order, me, data, factor,
            scalars=2, unread=1, microseconds=2,
            scratch=[
                pltpu.VMEM((2 * pairs, all_rows, channels), data.dtype),
                pltpu.SemaphoreType.DMA((2 * pairs,)),
            ],
        )
        if chunk == 0:
            grams = [gram_part] + from_others(gram_part, "chan")
        own.append(projected[0])
        arrived.append([rotated(projected[shift], "chan", shift) for shift in range(1, parts)])
    received = [arrived[chunk][at] for at in range(parts - 1) for chunk in range(chunks)]

    inverse, rho, head, tail, base = call(
        functools.partial(setup_kernel, len(grams), chunks, group),
        "setup",
        [((count, rank, 3 * rank), bf16), lanes(count), lanes(SWEEPS), lanes(SWEEPS), state],
        *grams, *own, slice_weights, weights, aux, coup, dual_s, dual_c,
        microseconds=4,
    )
    before = rotated(tail, "cuts", 1)
    after = rotated(head, "cuts", -1)
    tall, target, gram = call(
        functools.partial(first_kernel, chunks, group),
        "first",
        [state, state, quads],
        base, weights, inverse, dual_s, dual_c, *received,
    )
    side, inside, to_near, to_far = call(
        functools.partial(smooth_kernel, chunks),
        "smooth",
        [state, state, halo, halo],
        odd, aux, target, before, rho, after, weights, *own, *received,
        scalars=1,
    )
    for inner in range(INNER):
        last = inner == INNER - 1
        polar_outs = [quads, scale, quads]
        if inner == 0:
            root, scales, gram = call(
                first_polar_kernel,
                "polar",
                polar_outs,
                inside, delta, gram, *from_others(gram, "chan"),
                unread=1, microseconds=5,
            )
        else:
            outs = call(
                functools.partial(later_polar_kernel, last),
                "polar",
                [quads, ((rank // 2, 2 * rank), f32)] if last else polar_outs,
                odd if last else inside, delta, change, gram, cross, *crosses,
                unread=1, microseconds=6,
            )
            if last:
                mixed, partial = outs
            else:
                root, scales, gram = outs
        if last:
            tall, evolving = call(
                last_rows_kernel,
                "rows",
                [state, state],
                mixed, change, forward, tall, known,
                unread=1,
            )
            coup, delta = call(
                functools.partial(last_kernel, total),
                "last",
                [state, square],
                mixed, tall, *in_stages(partial, "cuts"),
            )
            continue
        near = swapped(to_near, "cuts", 0)
        far = swapped(to_far, "cuts", 1)
        mixed, partial = call(
            mix_kernel,
            "mix",
            [quads, ((rank // 2, 2 * rank), f32)],
            near, far, delta, root, scales, gram,
            unread=2,
        )
        aux, dual, known, cross = call(
            functools.partial(ahead_kernel, group),
            "ahead",
            [state, state, state, ((groups, rank, 2 * wide), f32)],
            odd, partial, inside, near, far, target, tall, side, rho, inverse,
            scalars=1, unread=1,
        )
        sums, cross = in_stages(partial, "cuts", beside=cross)
        crosses = from_others(cross, "chan")
        delta, change, forward = call(
            functools.partial(mixer_kernel, total),
            "mixer",
            [square, quads, quads],
            mixed, inverse, rho, *sums,
            microseconds=0.3,
        )
        if inner < INNER - 2:
            tall, target, inside, to_near, to_far = call(
                rows_kernel,
                "rows",
                [state, state, state, halo, halo],
                odd, aux, before, rho, after, change, forward, tall, known, dual,
                scalars=1, microseconds=0.3,
            )
    return (flip(evolving), flip(coup), delta)


def solution(mesh):
    return jax.shard_map(
        body,
        mesh=mesh,
        in_specs=(
            P("cuts", None, "chan"),
            P("cuts"),
            P("chan", None),
            P("cuts", None),
            P("cuts", "chan", None),
            P("cuts", "chan", None),
            P("cuts", "chan", None),
            P("cuts", "chan", None),
            P(),
        ),
        out_specs=(P("cuts", "chan", None), P("cuts", "chan", None), P()),
        check_vma=False,
    )
```

```python
import functools

import jax
import jax.numpy as jnp
from jax import lax
from jax.experimental import pallas as pl
from jax.experimental.pallas import tpu as pltpu
from jax.sharding import PartitionSpec as P

INNER = 3
SWEEPS = 4
POLAR = 8

smooth_weight = 1.0
eps_trace = 1e-06
f32 = jnp.float32
bf16 = jnp.bfloat16
NN = (((1,), (0,)), ((), ()))
NT = (((1,), (1,)), ((), ()))


def dot(left, right, dims=NN):
    return lax.dot_general(left, right, dims, preferred_element_type=f32)


def split(value):
    high = value.astype(bf16)
    low = (value - high.astype(f32)).astype(bf16)
    return high, low


def left_triple(value):
    high, low = split(value)
    return jnp.concatenate([high, high, low], axis=1)


def right_triple(value):
    high, low = split(value)
    return jnp.concatenate([high, low, high], axis=0)


def block_mask(rank, group):
    wide = rank * group
    rows = lax.div(lax.broadcasted_iota(jnp.int32, (wide, wide), 0), rank)
    cols = lax.div(lax.broadcasted_iota(jnp.int32, (wide, wide), 1), rank)
    return jnp.where(rows == cols, 1.0, 0.0).astype(bf16)


def wide_eye(rank, group):
    rows = lax.broadcasted_iota(jnp.int32, (rank, rank * group), 0)
    cols = lax.broadcasted_iota(jnp.int32, (rank, rank * group), 1)
    return jnp.where(rows == lax.rem(cols, rank), 1.0, 0.0).astype(f32)


def block_diagonal(value, mask, group):
    high, low = split(value)
    return (
        jnp.concatenate([high] * group, axis=0) * mask,
        jnp.concatenate([low] * group, axis=0) * mask,
    )


def times_blocks(values, blocks, dims=NN):
    rank = values[0].shape[0]
    count = len(values)
    pieces = [split(value) for value in values]
    high = jnp.concatenate([piece[0] for piece in pieces], axis=0)
    both = jnp.concatenate([high] + [piece[1] for piece in pieces], axis=0)
    first = dot(both, blocks[0], dims)
    total = first[: count * rank] + first[count * rank :] + dot(high, blocks[1], dims)
    return [total[at * rank : (at + 1) * rank] for at in range(count)]


def diagonal_blocks(value, rank, group):
    at = lax.div(lax.broadcasted_iota(jnp.int32, (rank, rank * group), 1), rank)
    total = value[:rank]
    for block in range(1, group):
        total = jnp.where(at == block, value[block * rank : (block + 1) * rank], total)
    return total


def group_size(count, rank):
    group = max(1, 256 // rank)
    while count % group:
        group -= 1
    return group


def factor_kernel(factor_ref, gram_ref):
    factor = factor_ref[...]
    gram_ref[...] = dot(factor, factor, NT)


def project_kernel(first, order_ref, me_ref, after_ref, data_ref, factor_ref, *outs):
    parts = len(outs)
    pairs, rows, _ = outs[0].shape
    count = data_ref.shape[0]
    factor = factor_ref[...]
    empty = jnp.zeros_like(factor)
    sides = [
        jnp.concatenate([factor, empty], axis=0),
        jnp.concatenate([empty, factor], axis=0),
    ]
    for pair in range(pairs):
        stored = [lax.rem(order_ref[2 * (first + pair) + at], count) for at in range(2)]
        for part in reversed(range(parts)):
            start = pl.multiple_of(lax.rem(me_ref[0] + part, parts) * rows, 16)
            place = pl.ds(start, rows)
            outs[part][pair] = dot(data_ref[stored[0], place, :], sides[0], NT) + dot(
                data_ref[stored[1], place, :], sides[1], NT
            )


def setup_kernel(grams, group, *refs):
    gram_refs, refs = refs[:grams], refs[grams:]
    (own_ref, aux_ref, coupled_ref, dual_s_ref, dual_c_ref) = refs[:5]
    (inverse_ref, mover_ref, rho_ref, diagonal_ref, columns_ref, base_ref) = refs[5:]
    count, rank = own_ref.shape
    gram = gram_refs[0][...]
    for ref in gram_refs[1:]:
        gram = gram + ref[...]
    eye = wide_eye(rank, 1)
    diagonal = jnp.sum(gram * eye, axis=0, keepdims=True)
    diagonal_ref[...] = jnp.broadcast_to(diagonal, diagonal_ref.shape)
    weights = own_ref[...]
    columns = weights.T
    columns_ref[...] = columns
    rho = jnp.sum(weights * weights * diagonal, axis=1, keepdims=True) / rank
    rho_ref[...] = jnp.broadcast_to(rho, rho_ref.shape)

    edge = 34.0 / 32.0
    lead = 4.0 * edge**3 / (4.0 * edge**3 - 3.0 * edge)
    mask = block_mask(rank, group)
    wide = wide_eye(rank, group)
    starts = range(0, count, group)
    systems = []
    for first in starts:
        scaled = []
        for k in range(first, first + group):
            unit = 1.0 / (34.0 * rho[k : k + 1, :])
            column = columns[:, k : k + 1]
            scaled.append(column * gram * weights[k : k + 1, :] * unit + (2.0 / 34.0) * eye)
        systems.append(jnp.concatenate(scaled, axis=1))
    inverses, rests = [], []
    for system in systems:
        rest = wide - system
        blocks = block_diagonal(rest, mask, group)
        (square,) = times_blocks([rest], blocks)
        (cube,) = times_blocks([square], blocks)
        inverses.append(wide + lead * (rest + square))
        rests.append(lead * cube - (lead - 1.0) * rest)
    for step in range(4):
        for at in range(len(systems)):
            blocks = block_diagonal(rests[at], mask, group)
            more, rests[at] = times_blocks([inverses[at], rests[at]], blocks)
            inverses[at] = inverses[at] + more
    for step in range(2):
        for at in range(len(systems)):
            (product,) = times_blocks([inverses[at]], block_diagonal(systems[at], mask, group))
            blocks = block_diagonal(wide - product, mask, group)
            (more,) = times_blocks([inverses[at]], blocks)
            inverses[at] = inverses[at] + more
    pair_mask = block_mask(rank, 2)
    for k in range(0, count, 2):
        both = []
        for j in (k, k + 1):
            place = (j % group) * rank
            unit = 1.0 / (34.0 * rho[j : j + 1, :])
            both.append(inverses[j // group][:, place : place + rank] * unit)
            inverse = left_triple(both[-1])
            inverse_ref[j] = inverse
            base_ref[j] = dot(
                inverse,
                right_triple(
                    rho[j : j + 1, :] * (aux_ref[j] - dual_s_ref[j] + coupled_ref[j] - dual_c_ref[j])
                ),
            )
        line = jnp.concatenate([weights[k : k + 1, :], weights[k + 1 : k + 2, :]], axis=1)
        high, low = block_diagonal(jnp.concatenate(both, axis=1) * line, pair_mask, 2)
        mover_ref[k // 2] = jnp.concatenate([high, high, low], axis=1)


def cross_blocks(lefts, rights, rank):
    group = len(lefts)
    wide = group * rank
    left = [split(value) for value in lefts]
    high = jnp.concatenate([piece[0] for piece in left], axis=0)
    both = jnp.concatenate([high] + [piece[1] for piece in left], axis=0)
    right = left if rights is lefts else [split(value) for value in rights]
    first = dot(both, jnp.concatenate([piece[0] for piece in right], axis=0), NT)
    second = dot(high, jnp.concatenate([piece[1] for piece in right], axis=0), NT)
    return diagonal_blocks(first[:wide] + first[wide:] + second, rank, group)


def summed(refs, chunks, pair):
    chunk, at = divmod(pair, refs[0].shape[0])
    total = None
    for ref in refs[chunk::chunks]:
        total = ref[at] if total is None else total + ref[at]
    return total


def first_kernel(chunks, group, *refs):
    base_ref, mover_ref, dual_s_ref, dual_c_ref = refs[2:6]
    *projected_refs, tall_ref, target_ref, gram_ref = refs[6:]
    count, rank, rows = base_ref.shape
    talls = []
    for k in range(0, count, 2):
        high, low = split(summed(projected_refs, chunks, k // 2))
        both = dot(mover_ref[k // 2], jnp.concatenate([high, low, high], axis=1), NT)
        for j in (k, k + 1):
            evolving = base_ref[j] + both[(j - k) * rank : (j - k + 1) * rank]
            target_ref[j] = evolving + dual_s_ref[j]
            tall = evolving + dual_c_ref[j]
            tall_ref[j] = tall
            talls.append(tall)
    for first in range(0, count, group):
        some = talls[first : first + group]
        gram_ref[first // group] = cross_blocks(some, some, rank)


def smooth(odd, now, targets, rho, inside_ref, near_ref, far_ref):
    count = len(targets)
    width = SWEEPS
    share = {j: 2.0 * smooth_weight / (rho[j] + 4.0 * smooth_weight) for j in rho}
    pull = {j: (rho[j] / (rho[j] + 4.0 * smooth_weight)) * targets[j] for j in range(count)}
    now = {j: now[j] for j in range(count)}
    for sweep in range(width):
        later = {}
        for j in range(-sweep - 1, count + sweep + 1):
            beside = [now[i] for i in (j - 1, j + 1) if i in now]
            total = beside[0] if len(beside) == 1 else beside[0] + beside[1]
            total = share[j] * total
            later[j] = total + pull[j] if j in pull else total
        now = later
    for j in range(count):
        inside_ref[j] = now[j]
    for j in range(width):
        near_ref[j] = jnp.where(odd == 1, now[j - width], now[count + j])
        far_ref[j] = jnp.where(odd == 1, now[count + j], now[j - width])


def all_rho(before_ref, rho_ref, after_ref):
    count = rho_ref.shape[0]
    rho = {j: rho_ref[j : j + 1, 0:1] for j in range(count)}
    for j in range(SWEEPS):
        rho[j - SWEEPS] = before_ref[count - SWEEPS + j : count - SWEEPS + j + 1, 0:1]
        rho[count + j] = after_ref[j : j + 1, 0:1]
    return rho


def smooth_kernel(
    chunks, odd_ref, aux_ref, target_ref, before_ref, rho_ref, after_ref, diagonal_ref,
    columns_ref, *refs
):
    *projected_refs, side_ref, past_ref, next_ref, inside_ref, near_ref, far_ref = refs
    count, rank, rows = aux_ref.shape
    for source, place in ((before_ref, past_ref), (after_ref, next_ref)):
        weights = source[...]
        rho = jnp.sum(weights * weights * diagonal_ref[...], axis=1, keepdims=True) / rank
        place[...] = jnp.broadcast_to(rho, place.shape)
    rho = all_rho(past_ref, rho_ref, next_ref)
    slices = range(count)
    smooth(
        odd_ref[0], [aux_ref[k] for k in slices], [target_ref[k] for k in slices], rho,
        inside_ref, near_ref, far_ref,
    )
    for k in range(0, count, 2):
        both = summed(projected_refs, chunks, k // 2).T
        side_ref[k] = columns_ref[:, k : k + 1] * both[:rank]
        side_ref[k + 1] = columns_ref[:, k + 1 : k + 2] * both[rank:]


def polar(grams, delta):
    rank, wide = grams[0].shape
    group = wide // rank
    mask = block_mask(rank, group)
    eye = wide_eye(rank, group)
    delta_left = left_triple(delta)
    delta_blocks = block_diagonal(jnp.concatenate([delta] * group, axis=1), mask, group)
    currents, roots, scales = [], [], []
    for gram in grams:
        left = dot(delta_left, right_triple(gram))
        (normal,) = times_blocks([left], delta_blocks, NT)
        line = jnp.broadcast_to(jnp.sum(normal * eye, axis=0, keepdims=True), (16, wide))
        high, low = split(line)
        rest = (line - high.astype(f32) - low.astype(f32)).astype(bf16)
        line = dot(high, mask) + dot(low, mask) + dot(rest, mask)
        trace = line[0:1] + eps_trace
        currents.append(normal / trace)
        scales.append(1.0 / jnp.sqrt(trace))
    for step in range(POLAR):
        for at in range(len(grams)):
            product = currents[at]
            blocks = block_diagonal(product, mask, group)
            if step == 0:
                roots.append(1.5 * eye - 0.5 * product)
                (square,) = times_blocks([product], blocks)
            elif step < POLAR - 1:
                square, more = times_blocks([product, roots[at]], blocks)
                roots[at] = 1.5 * roots[at] - 0.5 * more
            else:
                (more,) = times_blocks([roots[at]], blocks)
                roots[at] = 1.5 * roots[at] - 0.5 * more
            if step < POLAR - 1:
                half = 1.5 * product - 0.5 * square
                (more,) = times_blocks([half], blocks)
                currents[at] = 1.5 * half - 0.5 * more
    return roots, scales


def mix(roots, scales, grams, delta, mixed_ref, partial_ref):
    rank, wide = roots[0].shape
    group = wide // rank
    mask = block_mask(rank, group)
    delta_blocks = block_diagonal(jnp.concatenate([delta] * group, axis=1), mask, group)
    left, right = [], []
    for at in range(len(roots)):
        (mixed,) = times_blocks([roots[at]], delta_blocks)
        mixed = mixed * scales[at]
        mixed_ref[at] = mixed
        high, low = split(mixed)
        left += [high, high, low]
        high, low = split(grams[at])
        right += [high, low, high]
    partial = dot(jnp.concatenate(left, axis=1), jnp.concatenate(right, axis=1), NT)
    half = rank // 2
    partial_ref[...] = jnp.concatenate([partial[:half], partial[half:]], axis=1)


def first_polar_kernel(after_ref, delta_ref, *refs):
    *gram_refs, root_ref, scale_ref, gram_ref = refs
    grams = []
    for at in range(gram_ref.shape[0]):
        gram = gram_refs[0][at]
        for ref in gram_refs[1:]:
            gram = gram + ref[at]
        gram_ref[at] = gram
        grams.append(gram)
    roots, scales = polar(grams, delta_ref[...])
    for at in range(len(grams)):
        root_ref[at] = roots[at]
        scale_ref[at] = jnp.broadcast_to(scales[at], scale_ref.shape[1:])


def later_polar_kernel(last, after_ref, delta_ref, change_ref, old_ref, *refs):
    if last:
        *cross_refs, mixed_ref, partial_ref = refs
    else:
        *cross_refs, root_ref, scale_ref, gram_ref = refs
    groups, rank, wide = old_ref.shape
    group = wide // rank
    mask = block_mask(rank, group)
    grams = []
    for at in range(groups):
        cross = cross_refs[0][at]
        for ref in cross_refs[1:]:
            cross = cross + ref[at]
        change = change_ref[at]
        (onward,) = times_blocks([change], block_diagonal(old_ref[at], mask, group))
        onward = cross[:, :wide] + 0.5 * onward
        (one,) = times_blocks([onward], block_diagonal(change, mask, group), NT)
        (other,) = times_blocks([change], block_diagonal(onward, mask, group), NT)
        grams.append(cross[:, wide:] + one + other)
    delta = delta_ref[...]
    roots, scales = polar(grams, delta)
    if last:
        mix(roots, scales, grams, delta, mixed_ref, partial_ref)
    else:
        for at in range(groups):
            gram_ref[at] = grams[at]
            root_ref[at] = roots[at]
            scale_ref[at] = jnp.broadcast_to(scales[at], scale_ref.shape[1:])


def mix_kernel(near_ref, far_ref, delta_ref, root_ref, scale_ref, gram_ref, mixed_ref, partial_ref):
    groups = range(root_ref.shape[0])
    mix(
        [root_ref[at] for at in groups],
        [scale_ref[at, 0:1] for at in groups],
        [gram_ref[at] for at in groups],
        delta_ref[...], mixed_ref, partial_ref,
    )


def ahead_kernel(
    group, odd_ref, after_ref, inside_ref, near_ref, far_ref, target_ref, tall_ref, side_ref, rho_ref,
    inverse_ref, aux_ref, dual_ref, known_ref, cross_ref,
):
    count, rank, _ = inside_ref.shape
    width = SWEEPS
    knowns, talls = [], []
    for k in range(count):
        aux = inside_ref[k]
        if k < width:
            aux = aux + jnp.where(odd_ref[0] == 1, near_ref[k], far_ref[k])
        if k >= count - width:
            at = k - count + width
            aux = aux + jnp.where(odd_ref[0] == 1, far_ref[at], near_ref[at])
        target, tall = target_ref[k], tall_ref[k]
        aux_ref[k] = aux
        dual_ref[k] = target - aux
        known = dot(
            inverse_ref[k],
            right_triple(side_ref[k] + rho_ref[k : k + 1, 0:1] * (2.0 * aux - target - tall)),
        )
        known_ref[k] = known
        talls.append(tall)
        knowns.append(known + tall)
        if len(talls) == group:
            cross_ref[k // group] = jnp.concatenate(
                [cross_blocks(knowns, talls, rank), cross_blocks(knowns, knowns, rank)], axis=1
            )
            knowns, talls = [], []


def add_kernel(*refs):
    *term_refs, total_ref = refs
    total = term_refs[0][...]
    for ref in term_refs[1:]:
        total = total + ref[...]
    total_ref[...] = total


def new_delta(sum_refs, total, rank):
    packed = sum_refs[0][...]
    for ref in sum_refs[1:]:
        packed = packed + ref[...]
    packed = packed / total
    return jnp.concatenate([packed[:, :rank], packed[:, rank:]], axis=0)


def mixer_kernel(total, mixed_ref, inverse_ref, rho_ref, *refs):
    *sum_refs, delta_ref, change_ref, forward_ref = refs
    groups, rank, wide = mixed_ref.shape
    group = wide // rank
    delta = new_delta(sum_refs, total, rank)
    delta_ref[...] = delta
    delta_left = left_triple(delta.T)
    place = lax.div(lax.broadcasted_iota(jnp.int32, (1, wide), 1), rank)
    for at in range(groups):
        mixer = dot(delta_left, right_triple(mixed_ref[at]))
        slices = range(at * group, (at + 1) * group)
        inverses = jnp.concatenate([inverse_ref[k] for k in slices], axis=0)
        onward = diagonal_blocks(dot(inverses, right_triple(mixer)), rank, group)
        rho = rho_ref[at * group : at * group + 1, 0:1]
        for k in slices[1:]:
            rho = jnp.where(place == k - at * group, rho_ref[k : k + 1, 0:1], rho)
        forward = 2.0 * rho * onward
        forward_ref[at] = forward
        change_ref[at] = forward - mixer


def rows_kernel(odd_ref, aux_ref, before_ref, rho_ref, after_ref, *refs):
    (change_ref, forward_ref, tall_ref, known_ref, dual_ref) = refs[:5]
    (next_ref, target_ref, inside_ref, near_ref, far_ref) = refs[5:]
    targets = new_rows(change_ref, forward_ref, tall_ref, known_ref, next_ref)
    count = len(targets)
    for k in range(count):
        targets[k] = targets[k] + dual_ref[k]
        target_ref[k] = targets[k]
    rho = all_rho(before_ref, rho_ref, after_ref)
    smooth(
        odd_ref[0], [aux_ref[k] for k in range(count)], targets, rho,
        inside_ref, near_ref, far_ref,
    )


def last_rows_kernel(
    after_ref, change_ref, forward_ref, tall_ref, known_ref, next_ref, evolving_ref
):
    evolvings = new_rows(change_ref, forward_ref, tall_ref, known_ref, next_ref)
    for k in range(len(evolvings)):
        evolving_ref[k] = evolvings[k]


def new_rows(change_ref, forward_ref, tall_ref, known_ref, next_ref):
    groups, rank, wide = change_ref.shape
    group = wide // rank
    evolvings = []
    for k in range(groups * group):
        lanes = slice((k % group) * rank, (k % group + 1) * rank)
        change, forward = change_ref[k // group][:, lanes], forward_ref[k // group][:, lanes]
        left = jnp.concatenate([left_triple(change), left_triple(forward)], axis=0)
        tall, known = tall_ref[k], known_ref[k]
        both = dot(left, right_triple(tall))
        next_ref[k] = known + tall + both[:rank]
        evolvings.append(known + both[rank:])
    return evolvings


def last_kernel(total, mixed_ref, tall_ref, *refs):
    *sum_refs, coupled_ref, delta_ref = refs
    groups, rank, wide = mixed_ref.shape
    group = wide // rank
    delta = new_delta(sum_refs, total, rank)
    delta_ref[...] = delta
    delta_left = left_triple(delta.T)
    for at in range(groups):
        mixer = dot(delta_left, right_triple(mixed_ref[at]))
        for k in range(at * group, (at + 1) * group):
            place = (k - at * group) * rank
            coupled_ref[k] = dot(
                left_triple(mixer[:, place : place + rank]), right_triple(tall_ref[k])
            )


per_microsecond = 1_100_000_000


def call(
    kernel, name, outs, *args, scalars=0, unread=0, microseconds=0.3
):
    flops = int(microseconds * per_microsecond)
    specs = [pl.BlockSpec(memory_space=pltpu.SMEM)] * scalars
    specs += [pl.BlockSpec(memory_space=pl.ANY)] * unread
    specs += [pl.BlockSpec(memory_space=pltpu.VMEM)] * (len(args) - len(specs))
    shapes = [jax.ShapeDtypeStruct(shape, dtype) for shape, dtype in outs]
    moved = sum(arg.size * arg.dtype.itemsize for arg in args)
    moved += sum(shape.size * shape.dtype.itemsize for shape in shapes)
    return pl.pallas_call(
        kernel,
        out_shape=shapes,
        in_specs=specs,
        out_specs=[pl.BlockSpec(memory_space=pltpu.VMEM)] * len(shapes),
        compiler_params=pltpu.CompilerParams(vmem_limit_bytes=16 * 1024 * 1024),
        cost_estimate=pl.CostEstimate(flops=flops, bytes_accessed=moved, transcendentals=0),
        name=name,
    )(*args)


def rotated(value, axis, shift):
    count = lax.axis_size(axis)
    return lax.ppermute(value, axis, [(i, (i + shift) % count) for i in range(count)])


def swapped(value, axis, first):
    count = lax.axis_size(axis)
    pairs = [((i + first) % count, (i + first + 1) % count) for i in range(0, count, 2)]
    return lax.ppermute(value, axis, pairs + [(b, a) for a, b in pairs])


def from_others(value, axis):
    return [rotated(value, axis, shift) for shift in range(1, lax.axis_size(axis))]


def stage_sizes(count):
    sizes = []
    while count > 1:
        choices = (8, 4, 2, 3, 5, 7, count) if sizes else (2, 3, 5, 7, count)
        sizes.append(next(size for size in choices if count % size == 0))
        count //= sizes[-1]
    return sizes


def in_stages(value, axis, beside=None):
    count = lax.axis_size(axis)
    stride = 1
    terms = [value]
    for size in stage_sizes(count):
        value = terms[0]
        if len(terms) > 1:
            (value,) = call(add_kernel, "add", [(value.shape, f32)], *terms, microseconds=0.1)
        if stride > 1 and beside is not None:
            value, beside = lax.optimization_barrier((value, beside))
        terms = [value]
        for shift in range(1, size):
            moves = []
            for i in range(count):
                digit = (i // stride) % size
                other = digit ^ shift if size in (2, 4, 8) else (digit + shift) % size
                moves.append((i, i + (other - digit) * stride))
            terms.append(lax.ppermute(value, axis, moves))
        stride *= size
    return terms if beside is None else (terms, beside)


def body(
    data, order, chan_factor, slice_weights, smooth_aux, coupled, smooth_dual, coupling_dual, delta
):
    count, all_rows, channels = data.shape
    rank = chan_factor.shape[1]
    rows = smooth_aux.shape[1]
    parts = lax.axis_size("chan")
    total = count * lax.axis_size("cuts")
    group = group_size(count, rank)
    groups = count // group
    wide = group * rank
    flip = lambda value: jnp.swapaxes(value, 1, 2)
    aux, coup, dual_s, dual_c = map(flip, (smooth_aux, coupled, smooth_dual, coupling_dual))
    factor = chan_factor.T
    state = ((count, rank, rows), f32)
    quads = ((groups, rank, wide), f32)
    square = ((rank, rank), f32)
    halo = ((SWEEPS, rank, rows), f32)
    lanes = lambda height: ((height, 128), f32)
    scale = ((groups, 8, wide), f32)

    me = lax.axis_index("chan").astype(jnp.int32).reshape(1)
    odd = lax.rem(lax.axis_index("cuts"), 2).astype(jnp.int32).reshape(1)
    chunks = 2 if count % 4 == 0 else 1
    pairs = count // 2 // chunks
    (gram_part,) = call(factor_kernel, "factor", [square], factor)
    grams = [gram_part] + from_others(gram_part, "chan")
    own, arrived = [], []
    for chunk in range(chunks):
        projected = call(
            functools.partial(project_kernel, chunk * pairs),
            "project",
            [((pairs, rows, 2 * rank), f32)] * parts,
            order, me, gram_part, data, factor,
            scalars=2, unread=1,
        )
        own.append(projected[0])
        arrived.append([rotated(projected[shift], "chan", shift) for shift in range(1, parts)])
    received = [arrived[chunk][at] for at in range(parts - 1) for chunk in range(chunks)]

    late_weights, _ = lax.optimization_barrier((slice_weights, own[-1]))
    before = rotated(late_weights, "cuts", 1)
    after = rotated(late_weights, "cuts", -1)
    inverse, mover, rho, diagonal, columns, base = call(
        functools.partial(setup_kernel, len(grams), group),
        "setup",
        [
            ((count, rank, 3 * rank), bf16),
            ((count // 2, 2 * rank, 6 * rank), bf16),
            lanes(count),
            ((count, rank), f32),
            ((rank, count), f32),
            state,
        ],
        *grams, slice_weights, aux, coup, dual_s, dual_c,
    )
    tall, target, gram = call(
        functools.partial(first_kernel, chunks, group),
        "first",
        [state, state, quads],
        before, after, base, mover, dual_s, dual_c, *own, *received,
        unread=2,
    )
    side, before, after, inside, to_near, to_far = call(
        functools.partial(smooth_kernel, chunks),
        "smooth",
        [state, lanes(count), lanes(count), state, halo, halo],
        odd, aux, target, before, rho, after, diagonal, columns, *own, *received,
        scalars=1,
    )
    for inner in range(INNER):
        last = inner == INNER - 1
        polar_outs = [quads, scale, quads]
        if inner == 0:
            root, scales, gram = call(
                first_polar_kernel,
                "polar",
                polar_outs,
                inside, delta, gram, *from_others(gram, "chan"),
                unread=1, microseconds=3,
            )
        else:
            outs = call(
                functools.partial(later_polar_kernel, last),
                "polar",
                [quads, ((rank // 2, 2 * rank), f32)] if last else polar_outs,
                odd if last else inside, delta, change, gram, cross, *crosses,
                unread=1, microseconds=3,
            )
            if last:
                mixed, partial = outs
            else:
                root, scales, gram = outs
        if last:
            tall, evolving = call(
                last_rows_kernel,
                "rows",
                [state, state],
                mixed, change, forward, tall, known,
                unread=1,
            )
            coup, delta = call(
                functools.partial(last_kernel, total),
                "last",
                [state, square],
                mixed, tall, *in_stages(partial, "cuts"),
            )
            continue
        near = swapped(to_near, "cuts", 0)
        far = swapped(to_far, "cuts", 1)
        mixed, partial = call(
            mix_kernel,
            "mix",
            [quads, ((rank // 2, 2 * rank), f32)],
            near, far, delta, root, scales, gram,
            unread=2,
        )
        aux, dual, known, cross = call(
            functools.partial(ahead_kernel, group),
            "ahead",
            [state, state, state, ((groups, rank, 2 * wide), f32)],
            odd, partial, inside, near, far, target, tall, side, rho, inverse,
            scalars=1, unread=1,
        )
        sums, cross = in_stages(partial, "cuts", beside=cross)
        crosses = from_others(cross, "chan")
        delta, change, forward = call(
            functools.partial(mixer_kernel, total),
            "mixer",
            [square, quads, quads],
            mixed, inverse, rho, *sums,
        )
        if inner < INNER - 2:
            tall, target, inside, to_near, to_far = call(
                rows_kernel,
                "rows",
                [state, state, state, halo, halo],
                odd, aux, before, rho, after, change, forward, tall, known, dual,
                scalars=1,
            )
    return (flip(evolving), flip(coup), delta)


def solution(mesh):
    return jax.shard_map(
        body,
        mesh=mesh,
        in_specs=(
            P("cuts", None, "chan"),
            P("cuts"),
            P("chan", None),
            P("cuts", None),
            P("cuts", "chan", None),
            P("cuts", "chan", None),
            P("cuts", "chan", None),
            P("cuts", "chan", None),
            P(),
        ),
        out_specs=(P("cuts", "chan", None), P("cuts", "chan", None), P()),
        check_vma=False,
    )
```

```python
import functools

import jax
import jax.numpy as jnp
from jax import lax
from jax.experimental import pallas as pl
from jax.experimental.pallas import tpu as pltpu
from jax.sharding import PartitionSpec as P

INNER = 3
SWEEPS = 4
POLAR = 8

smooth_weight = 1.0
eps_trace = 1e-06
f32 = jnp.float32
bf16 = jnp.bfloat16
NN = (((1,), (0,)), ((), ()))
NT = (((1,), (1,)), ((), ()))


def dot(left, right, dims=NN):
    return lax.dot_general(left, right, dims, preferred_element_type=f32)


def split(value):
    high = value.astype(bf16)
    low = (value - high.astype(f32)).astype(bf16)
    return high, low


def left_triple(value):
    high, low = split(value)
    return jnp.concatenate([high, high, low], axis=1)


def right_triple(value):
    high, low = split(value)
    return jnp.concatenate([high, low, high], axis=0)


def block_mask(rank, group):
    wide = rank * group
    rows = lax.div(lax.broadcasted_iota(jnp.int32, (wide, wide), 0), rank)
    cols = lax.div(lax.broadcasted_iota(jnp.int32, (wide, wide), 1), rank)
    return jnp.where(rows == cols, 1.0, 0.0).astype(bf16)


def wide_eye(rank, group):
    rows = lax.broadcasted_iota(jnp.int32, (rank, rank * group), 0)
    cols = lax.broadcasted_iota(jnp.int32, (rank, rank * group), 1)
    return jnp.where(rows == lax.rem(cols, rank), 1.0, 0.0).astype(f32)


def block_diagonal(value, mask, group):
    high, low = split(value)
    return (
        jnp.concatenate([high] * group, axis=0) * mask,
        jnp.concatenate([low] * group, axis=0) * mask,
    )


def times_blocks(values, blocks, dims=NN):
    rank = values[0].shape[0]
    count = len(values)
    pieces = [split(value) for value in values]
    high = jnp.concatenate([piece[0] for piece in pieces], axis=0)
    both = jnp.concatenate([high] + [piece[1] for piece in pieces], axis=0)
    first = dot(both, blocks[0], dims)
    total = first[: count * rank] + first[count * rank :] + dot(high, blocks[1], dims)
    return [total[at * rank : (at + 1) * rank] for at in range(count)]


def diagonal_blocks(value, rank, group):
    at = lax.div(lax.broadcasted_iota(jnp.int32, (rank, rank * group), 1), rank)
    total = value[:rank]
    for block in range(1, group):
        total = jnp.where(at == block, value[block * rank : (block + 1) * rank], total)
    return total


def group_size(count, rank):
    group = max(1, 256 // rank)
    while count % group:
        group -= 1
    return group


def factor_kernel(factor_ref, gram_ref):
    factor = factor_ref[...]
    gram_ref[...] = dot(factor, factor, NT)


def project_kernel(order_ref, me_ref, first_ref, second_ref, factor_ref, after_ref, *outs):
    parts = len(outs)
    rows = outs[0].shape[1]
    factor = factor_ref[...]
    empty = jnp.zeros_like(factor)
    sides = [
        jnp.concatenate([factor, empty], axis=0),
        jnp.concatenate([empty, factor], axis=0),
    ]
    for part in reversed(range(parts)):
        start = pl.multiple_of(lax.rem(me_ref[0] + part, parts) * rows, 16)
        place = pl.ds(start, rows)
        outs[part][0] = dot(first_ref[0, place, :], sides[0], NT) + dot(
            second_ref[0, place, :], sides[1], NT
        )


def project(first, pairs, parts, rows, order, me, data, factor, after):
    count, all_rows, channels = data.shape
    rank = factor.shape[0]
    spec = lambda odd: pl.BlockSpec(
        (1, all_rows, channels),
        lambda i, order, me: (lax.rem(order[2 * (first + i) + odd], count), 0, 0),
    )
    return pl.pallas_call(
        project_kernel,
        out_shape=[jax.ShapeDtypeStruct((pairs, rows, 2 * rank), f32)] * parts,
        grid_spec=pltpu.PrefetchScalarGridSpec(
            num_scalar_prefetch=2,
            grid=(pairs,),
            in_specs=[
                spec(0),
                spec(1),
                pl.BlockSpec((rank, channels), lambda i, order, me: (0, 0)),
                pl.BlockSpec(memory_space=pl.ANY),
            ],
            out_specs=[pl.BlockSpec((1, rows, 2 * rank), lambda i, order, me: (i, 0, 0))] * parts,
        ),
        compiler_params=pltpu.CompilerParams(vmem_limit_bytes=16 * 1024 * 1024),
        cost_estimate=pl.CostEstimate(
            flops=2 * per_microsecond, bytes_accessed=data.size, transcendentals=0
        ),
        name="project",
    )(order, me, data, data, factor, after)


def setup_kernel(grams, group, *refs):
    gram_refs, refs = refs[:grams], refs[grams:]
    (own_ref, aux_ref, coupled_ref, dual_s_ref, dual_c_ref) = refs[:5]
    (inverse_ref, mover_ref, rho_ref, diagonal_ref, columns_ref, base_ref) = refs[5:]
    count, rank = own_ref.shape
    gram = gram_refs[0][...]
    for ref in gram_refs[1:]:
        gram = gram + ref[...]
    eye = wide_eye(rank, 1)
    diagonal = jnp.sum(gram * eye, axis=0, keepdims=True)
    diagonal_ref[...] = jnp.broadcast_to(diagonal, diagonal_ref.shape)
    weights = own_ref[...]
    columns = weights.T
    columns_ref[...] = columns
    rho = jnp.sum(weights * weights * diagonal, axis=1, keepdims=True) / rank
    rho_ref[...] = jnp.broadcast_to(rho, rho_ref.shape)

    edge = 34.0 / 32.0
    lead = 4.0 * edge**3 / (4.0 * edge**3 - 3.0 * edge)
    mask = block_mask(rank, group)
    wide = wide_eye(rank, group)
    starts = range(0, count, group)
    systems = []
    for first in starts:
        scaled = []
        for k in range(first, first + group):
            unit = 1.0 / (34.0 * rho[k : k + 1, :])
            column = columns[:, k : k + 1]
            scaled.append(column * gram * weights[k : k + 1, :] * unit + (2.0 / 34.0) * eye)
        systems.append(jnp.concatenate(scaled, axis=1))
    inverses, rests = [], []
    for system in systems:
        rest = wide - system
        blocks = block_diagonal(rest, mask, group)
        (square,) = times_blocks([rest], blocks)
        (cube,) = times_blocks([square], blocks)
        inverses.append(wide + lead * (rest + square))
        rests.append(lead * cube - (lead - 1.0) * rest)
    for step in range(4):
        for at in range(len(systems)):
            blocks = block_diagonal(rests[at], mask, group)
            more, rests[at] = times_blocks([inverses[at], rests[at]], blocks)
            inverses[at] = inverses[at] + more
    for step in range(2):
        for at in range(len(systems)):
            (product,) = times_blocks([inverses[at]], block_diagonal(systems[at], mask, group))
            blocks = block_diagonal(wide - product, mask, group)
            (more,) = times_blocks([inverses[at]], blocks)
            inverses[at] = inverses[at] + more
    pair_mask = block_mask(rank, 2)
    for k in range(0, count, 2):
        both = []
        for j in (k, k + 1):
            place = (j % group) * rank
            unit = 1.0 / (34.0 * rho[j : j + 1, :])
            both.append(inverses[j // group][:, place : place + rank] * unit)
            inverse = left_triple(both[-1])
            inverse_ref[j] = inverse
            base_ref[j] = dot(
                inverse,
                right_triple(
                    rho[j : j + 1, :] * (aux_ref[j] - dual_s_ref[j] + coupled_ref[j] - dual_c_ref[j])
                ),
            )
        line = jnp.concatenate([weights[k : k + 1, :], weights[k + 1 : k + 2, :]], axis=1)
        high, low = block_diagonal(jnp.concatenate(both, axis=1) * line, pair_mask, 2)
        mover_ref[k // 2] = jnp.concatenate([high, high, low], axis=1)


def cross_blocks(lefts, rights, rank):
    group = len(lefts)
    wide = group * rank
    left = [split(value) for value in lefts]
    high = jnp.concatenate([piece[0] for piece in left], axis=0)
    both = jnp.concatenate([high] + [piece[1] for piece in left], axis=0)
    right = left if rights is lefts else [split(value) for value in rights]
    first = dot(both, jnp.concatenate([piece[0] for piece in right], axis=0), NT)
    second = dot(high, jnp.concatenate([piece[1] for piece in right], axis=0), NT)
    return diagonal_blocks(first[:wide] + first[wide:] + second, rank, group)


def summed(refs, chunks, pair):
    chunk, at = divmod(pair, refs[0].shape[0])
    total = None
    for ref in refs[chunk::chunks]:
        total = ref[at] if total is None else total + ref[at]
    return total


def first_kernel(chunks, group, *refs):
    base_ref, mover_ref, dual_s_ref, dual_c_ref = refs[2:6]
    *projected_refs, tall_ref, target_ref, gram_ref = refs[6:]
    count, rank, rows = base_ref.shape
    talls = []
    for k in range(0, count, 2):
        high, low = split(summed(projected_refs, chunks, k // 2))
        both = dot(mover_ref[k // 2], jnp.concatenate([high, low, high], axis=1), NT)
        for j in (k, k + 1):
            evolving = base_ref[j] + both[(j - k) * rank : (j - k + 1) * rank]
            target_ref[j] = evolving + dual_s_ref[j]
            tall = evolving + dual_c_ref[j]
            tall_ref[j] = tall
            talls.append(tall)
    for first in range(0, count, group):
        some = talls[first : first + group]
        gram_ref[first // group] = cross_blocks(some, some, rank)


def smooth(odd, now, targets, rho, inside_ref, near_ref, far_ref):
    count = len(targets)
    width = SWEEPS
    share = {j: 2.0 * smooth_weight / (rho[j] + 4.0 * smooth_weight) for j in rho}
    pull = {j: (rho[j] / (rho[j] + 4.0 * smooth_weight)) * targets[j] for j in range(count)}
    now = {j: now[j] for j in range(count)}
    for sweep in range(width):
        later = {}
        for j in range(-sweep - 1, count + sweep + 1):
            beside = [now[i] for i in (j - 1, j + 1) if i in now]
            total = beside[0] if len(beside) == 1 else beside[0] + beside[1]
            total = share[j] * total
            later[j] = total + pull[j] if j in pull else total
        now = later
    for j in range(count):
        inside_ref[j] = now[j]
    for j in range(width):
        near_ref[j] = jnp.where(odd == 1, now[j - width], now[count + j])
        far_ref[j] = jnp.where(odd == 1, now[count + j], now[j - width])


def all_rho(before_ref, rho_ref, after_ref):
    count = rho_ref.shape[0]
    rho = {j: rho_ref[j : j + 1, 0:1] for j in range(count)}
    for j in range(SWEEPS):
        rho[j - SWEEPS] = before_ref[count - SWEEPS + j : count - SWEEPS + j + 1, 0:1]
        rho[count + j] = after_ref[j : j + 1, 0:1]
    return rho


def smooth_kernel(
    chunks, odd_ref, aux_ref, target_ref, before_ref, rho_ref, after_ref, diagonal_ref,
    columns_ref, *refs
):
    *projected_refs, side_ref, past_ref, next_ref, inside_ref, near_ref, far_ref = refs
    count, rank, rows = aux_ref.shape
    for source, place in ((before_ref, past_ref), (after_ref, next_ref)):
        weights = source[...]
        rho = jnp.sum(weights * weights * diagonal_ref[...], axis=1, keepdims=True) / rank
        place[...] = jnp.broadcast_to(rho, place.shape)
    rho = all_rho(past_ref, rho_ref, next_ref)
    slices = range(count)
    smooth(
        odd_ref[0], [aux_ref[k] for k in slices], [target_ref[k] for k in slices], rho,
        inside_ref, near_ref, far_ref,
    )
    for k in range(0, count, 2):
        both = summed(projected_refs, chunks, k // 2).T
        side_ref[k] = columns_ref[:, k : k + 1] * both[:rank]
        side_ref[k + 1] = columns_ref[:, k + 1 : k + 2] * both[rank:]


def polar(grams, delta):
    rank, wide = grams[0].shape
    group = wide // rank
    mask = block_mask(rank, group)
    eye = wide_eye(rank, group)
    delta_left = left_triple(delta)
    delta_blocks = block_diagonal(jnp.concatenate([delta] * group, axis=1), mask, group)
    currents, roots, scales = [], [], []
    for gram in grams:
        left = dot(delta_left, right_triple(gram))
        (normal,) = times_blocks([left], delta_blocks, NT)
        line = jnp.broadcast_to(jnp.sum(normal * eye, axis=0, keepdims=True), (16, wide))
        high, low = split(line)
        rest = (line - high.astype(f32) - low.astype(f32)).astype(bf16)
        line = dot(high, mask) + dot(low, mask) + dot(rest, mask)
        trace = line[0:1] + eps_trace
        currents.append(normal / trace)
        scales.append(1.0 / jnp.sqrt(trace))
    for step in range(POLAR):
        for at in range(len(grams)):
            product = currents[at]
            blocks = block_diagonal(product, mask, group)
            if step == 0:
                roots.append(1.5 * eye - 0.5 * product)
                (square,) = times_blocks([product], blocks)
            elif step < POLAR - 1:
                square, more = times_blocks([product, roots[at]], blocks)
                roots[at] = 1.5 * roots[at] - 0.5 * more
            else:
                (more,) = times_blocks([roots[at]], blocks)
                roots[at] = 1.5 * roots[at] - 0.5 * more
            if step < POLAR - 1:
                half = 1.5 * product - 0.5 * square
                (more,) = times_blocks([half], blocks)
                currents[at] = 1.5 * half - 0.5 * more
    return roots, scales


def mix(roots, scales, grams, delta, mixed_ref, partial_ref):
    rank, wide = roots[0].shape
    group = wide // rank
    mask = block_mask(rank, group)
    delta_blocks = block_diagonal(jnp.concatenate([delta] * group, axis=1), mask, group)
    left, right = [], []
    for at in range(len(roots)):
        (mixed,) = times_blocks([roots[at]], delta_blocks)
        mixed = mixed * scales[at]
        mixed_ref[at] = mixed
        high, low = split(mixed)
        left += [high, high, low]
        high, low = split(grams[at])
        right += [high, low, high]
    partial = dot(jnp.concatenate(left, axis=1), jnp.concatenate(right, axis=1), NT)
    half = rank // 2
    partial_ref[...] = jnp.concatenate([partial[:half], partial[half:]], axis=1)


def first_polar_kernel(after_ref, delta_ref, *refs):
    *gram_refs, root_ref, scale_ref, gram_ref = refs
    grams = []
    for at in range(gram_ref.shape[0]):
        gram = gram_refs[0][at]
        for ref in gram_refs[1:]:
            gram = gram + ref[at]
        gram_ref[at] = gram
        grams.append(gram)
    roots, scales = polar(grams, delta_ref[...])
    for at in range(len(grams)):
        root_ref[at] = roots[at]
        scale_ref[at] = jnp.broadcast_to(scales[at], scale_ref.shape[1:])


def later_polar_kernel(last, after_ref, delta_ref, change_ref, old_ref, *refs):
    if last:
        *cross_refs, mixed_ref, partial_ref = refs
    else:
        *cross_refs, root_ref, scale_ref, gram_ref = refs
    groups, rank, wide = old_ref.shape
    group = wide // rank
    mask = block_mask(rank, group)
    grams = []
    for at in range(groups):
        cross = cross_refs[0][at]
        for ref in cross_refs[1:]:
            cross = cross + ref[at]
        change = change_ref[at]
        (onward,) = times_blocks([change], block_diagonal(old_ref[at], mask, group))
        onward = cross[:, :wide] + 0.5 * onward
        (one,) = times_blocks([onward], block_diagonal(change, mask, group), NT)
        (other,) = times_blocks([change], block_diagonal(onward, mask, group), NT)
        grams.append(cross[:, wide:] + one + other)
    delta = delta_ref[...]
    roots, scales = polar(grams, delta)
    if last:
        mix(roots, scales, grams, delta, mixed_ref, partial_ref)
    else:
        for at in range(groups):
            gram_ref[at] = grams[at]
            root_ref[at] = roots[at]
            scale_ref[at] = jnp.broadcast_to(scales[at], scale_ref.shape[1:])


def mix_kernel(near_ref, far_ref, delta_ref, root_ref, scale_ref, gram_ref, mixed_ref, partial_ref):
    groups = range(root_ref.shape[0])
    mix(
        [root_ref[at] for at in groups],
        [scale_ref[at, 0:1] for at in groups],
        [gram_ref[at] for at in groups],
        delta_ref[...], mixed_ref, partial_ref,
    )


def ahead_kernel(
    group, odd_ref, after_ref, inside_ref, near_ref, far_ref, target_ref, tall_ref, side_ref, rho_ref,
    inverse_ref, aux_ref, dual_ref, known_ref, cross_ref,
):
    count, rank, _ = inside_ref.shape
    width = SWEEPS
    knowns, talls = [], []
    for k in range(count):
        aux = inside_ref[k]
        if k < width:
            aux = aux + jnp.where(odd_ref[0] == 1, near_ref[k], far_ref[k])
        if k >= count - width:
            at = k - count + width
            aux = aux + jnp.where(odd_ref[0] == 1, far_ref[at], near_ref[at])
        target, tall = target_ref[k], tall_ref[k]
        aux_ref[k] = aux
        dual_ref[k] = target - aux
        known = dot(
            inverse_ref[k],
            right_triple(side_ref[k] + rho_ref[k : k + 1, 0:1] * (2.0 * aux - target - tall)),
        )
        known_ref[k] = known
        talls.append(tall)
        knowns.append(known + tall)
        if len(talls) == group:
            cross_ref[k // group] = jnp.concatenate(
                [cross_blocks(knowns, talls, rank), cross_blocks(knowns, knowns, rank)], axis=1
            )
            knowns, talls = [], []


def add_kernel(*refs):
    *term_refs, total_ref = refs
    total = term_refs[0][...]
    for ref in term_refs[1:]:
        total = total + ref[...]
    total_ref[...] = total


def new_delta(sum_refs, total, rank):
    packed = sum_refs[0][...]
    for ref in sum_refs[1:]:
        packed = packed + ref[...]
    packed = packed / total
    return jnp.concatenate([packed[:, :rank], packed[:, rank:]], axis=0)


def mixer_kernel(total, mixed_ref, inverse_ref, rho_ref, *refs):
    *sum_refs, delta_ref, change_ref, forward_ref = refs
    groups, rank, wide = mixed_ref.shape
    group = wide // rank
    delta = new_delta(sum_refs, total, rank)
    delta_ref[...] = delta
    delta_left = left_triple(delta.T)
    place = lax.div(lax.broadcasted_iota(jnp.int32, (1, wide), 1), rank)
    for at in range(groups):
        mixer = dot(delta_left, right_triple(mixed_ref[at]))
        slices = range(at * group, (at + 1) * group)
        inverses = jnp.concatenate([inverse_ref[k] for k in slices], axis=0)
        onward = diagonal_blocks(dot(inverses, right_triple(mixer)), rank, group)
        rho = rho_ref[at * group : at * group + 1, 0:1]
        for k in slices[1:]:
            rho = jnp.where(place == k - at * group, rho_ref[k : k + 1, 0:1], rho)
        forward = 2.0 * rho * onward
        forward_ref[at] = forward
        change_ref[at] = forward - mixer


def rows_kernel(odd_ref, aux_ref, before_ref, rho_ref, after_ref, *refs):
    (change_ref, forward_ref, tall_ref, known_ref, dual_ref) = refs[:5]
    (next_ref, target_ref, inside_ref, near_ref, far_ref) = refs[5:]
    targets = new_rows(change_ref, forward_ref, tall_ref, known_ref, next_ref)
    count = len(targets)
    for k in range(count):
        targets[k] = targets[k] + dual_ref[k]
        target_ref[k] = targets[k]
    rho = all_rho(before_ref, rho_ref, after_ref)
    smooth(
        odd_ref[0], [aux_ref[k] for k in range(count)], targets, rho,
        inside_ref, near_ref, far_ref,
    )


def last_rows_kernel(
    after_ref, change_ref, forward_ref, tall_ref, known_ref, next_ref, evolving_ref
):
    evolvings = new_rows(change_ref, forward_ref, tall_ref, known_ref, next_ref)
    for k in range(len(evolvings)):
        evolving_ref[k] = evolvings[k]


def new_rows(change_ref, forward_ref, tall_ref, known_ref, next_ref):
    groups, rank, wide = change_ref.shape
    group = wide // rank
    evolvings = []
    for k in range(groups * group):
        lanes = slice((k % group) * rank, (k % group + 1) * rank)
        change, forward = change_ref[k // group][:, lanes], forward_ref[k // group][:, lanes]
        left = jnp.concatenate([left_triple(change), left_triple(forward)], axis=0)
        tall, known = tall_ref[k], known_ref[k]
        both = dot(left, right_triple(tall))
        next_ref[k] = known + tall + both[:rank]
        evolvings.append(known + both[rank:])
    return evolvings


def last_kernel(total, mixed_ref, tall_ref, *refs):
    *sum_refs, coupled_ref, delta_ref, made, sent = refs
    groups, rank, wide = mixed_ref.shape
    group = wide // rank
    delta = new_delta(sum_refs, total, rank)
    delta_ref[...] = delta
    delta_left = left_triple(delta.T)
    copies = []
    for at in range(groups):
        mixer = dot(delta_left, right_triple(mixed_ref[at]))
        for k in range(at * group, (at + 1) * group):
            place = (k - at * group) * rank
            made[k] = dot(left_triple(mixer[:, place : place + rank]), right_triple(tall_ref[k]))
            copies.append(pltpu.make_async_copy(made.at[k], coupled_ref.at[k], sent.at[k]))
            copies[-1].start()
    for copy in copies:
        copy.wait()


per_microsecond = 1_100_000_000


def call(
    kernel, name, outs, *args, scalars=0, unread=0, far_outs=0, microseconds=0.3, scratch=()
):
    flops = int(microseconds * per_microsecond)
    specs = [pl.BlockSpec(memory_space=pltpu.SMEM)] * scalars
    specs += [pl.BlockSpec(memory_space=pl.ANY)] * unread
    specs += [pl.BlockSpec(memory_space=pltpu.VMEM)] * (len(args) - len(specs))
    shapes = [jax.ShapeDtypeStruct(shape, dtype) for shape, dtype in outs]
    moved = sum(arg.size * arg.dtype.itemsize for arg in args)
    moved += sum(shape.size * shape.dtype.itemsize for shape in shapes)
    return pl.pallas_call(
        kernel,
        out_shape=shapes,
        in_specs=specs,
        out_specs=[pl.BlockSpec(memory_space=pl.ANY)] * far_outs
        + [pl.BlockSpec(memory_space=pltpu.VMEM)] * (len(shapes) - far_outs),
        scratch_shapes=list(scratch),
        compiler_params=pltpu.CompilerParams(vmem_limit_bytes=16 * 1024 * 1024),
        cost_estimate=pl.CostEstimate(flops=flops, bytes_accessed=moved, transcendentals=0),
        name=name,
    )(*args)


def rotated(value, axis, shift):
    count = lax.axis_size(axis)
    return lax.ppermute(value, axis, [(i, (i + shift) % count) for i in range(count)])


def swapped(value, axis, first):
    count = lax.axis_size(axis)
    pairs = [((i + first) % count, (i + first + 1) % count) for i in range(0, count, 2)]
    return lax.ppermute(value, axis, pairs + [(b, a) for a, b in pairs])


def from_others(value, axis):
    return [rotated(value, axis, shift) for shift in range(1, lax.axis_size(axis))]


def stage_sizes(count):
    sizes = []
    while count > 1:
        sizes.append(next(size for size in (4, 2, 3, 5, 7, count) if count % size == 0))
        count //= sizes[-1]
    return sizes


def in_stages(value, axis, beside=None):
    count = lax.axis_size(axis)
    stride = 1
    terms = [value]
    for size in stage_sizes(count):
        value = terms[0]
        if len(terms) > 1:
            (value,) = call(add_kernel, "add", [(value.shape, f32)], *terms, microseconds=0.1)
        if stride > 1 and beside is not None:
            value, beside = lax.optimization_barrier((value, beside))
        terms = [value]
        for shift in range(1, size):
            moves = []
            for i in range(count):
                digit = (i // stride) % size
                other = digit ^ shift if size in (2, 4) else (digit + shift) % size
                moves.append((i, i + (other - digit) * stride))
            terms.append(lax.ppermute(value, axis, moves))
        stride *= size
    return terms if beside is None else (terms, beside)


def body(
    data, order, chan_factor, slice_weights, smooth_aux, coupled, smooth_dual, coupling_dual, delta
):
    count, all_rows, channels = data.shape
    rank = chan_factor.shape[1]
    rows = smooth_aux.shape[1]
    parts = lax.axis_size("chan")
    total = count * lax.axis_size("cuts")
    group = group_size(count, rank)
    groups = count // group
    wide = group * rank
    flip = lambda value: jnp.swapaxes(value, 1, 2)
    aux, coup, dual_s, dual_c = map(flip, (smooth_aux, coupled, smooth_dual, coupling_dual))
    factor = chan_factor.T
    state = ((count, rank, rows), f32)
    quads = ((groups, rank, wide), f32)
    square = ((rank, rank), f32)
    halo = ((SWEEPS, rank, rows), f32)
    lanes = lambda height: ((height, 128), f32)
    scale = ((groups, 8, wide), f32)

    me = lax.axis_index("chan").astype(jnp.int32).reshape(1)
    odd = lax.rem(lax.axis_index("cuts"), 2).astype(jnp.int32).reshape(1)
    chunks = 2 if count % 4 == 0 else 1
    pairs = count // 2 // chunks
    (gram_part,) = call(factor_kernel, "factor", [square], factor)
    grams = [gram_part] + from_others(gram_part, "chan")
    own, arrived = [], []
    for chunk in range(chunks):
        projected = project(
            chunk * pairs, pairs, parts, rows, order, me, data, factor, gram_part
        )
        if chunk == 0:
            projected, grams = lax.optimization_barrier((projected, grams))
        own.append(projected[0])
        arrived.append([rotated(projected[shift], "chan", shift) for shift in range(1, parts)])
    received = [arrived[chunk][at] for at in range(parts - 1) for chunk in range(chunks)]

    late_weights, _ = lax.optimization_barrier((slice_weights, own[-1]))
    before = rotated(late_weights, "cuts", 1)
    after = rotated(late_weights, "cuts", -1)
    inverse, mover, rho, diagonal, columns, base = call(
        functools.partial(setup_kernel, len(grams), group),
        "setup",
        [
            ((count, rank, 3 * rank), bf16),
            ((count // 2, 2 * rank, 6 * rank), bf16),
            lanes(count),
            ((count, rank), f32),
            ((rank, count), f32),
            state,
        ],
        *grams, slice_weights, aux, coup, dual_s, dual_c,
    )
    tall, target, gram = call(
        functools.partial(first_kernel, chunks, group),
        "first",
        [state, state, quads],
        before, after, base, mover, dual_s, dual_c, *own, *received,
        unread=2,
    )
    side, before, after, inside, to_near, to_far = call(
        functools.partial(smooth_kernel, chunks),
        "smooth",
        [state, lanes(count), lanes(count), state, halo, halo],
        odd, aux, target, before, rho, after, diagonal, columns, *own, *received,
        scalars=1,
    )
    for inner in range(INNER):
        last = inner == INNER - 1
        polar_outs = [quads, scale, quads]
        if inner == 0:
            root, scales, gram = call(
                first_polar_kernel,
                "polar",
                polar_outs,
                inside, delta, gram, *from_others(gram, "chan"),
                unread=1, microseconds=3,
            )
        else:
            outs = call(
                functools.partial(later_polar_kernel, last),
                "polar",
                [quads, ((rank // 2, 2 * rank), f32)] if last else polar_outs,
                odd if last else inside, delta, change, gram, cross, *crosses,
                unread=1, microseconds=3,
            )
            if last:
                mixed, partial = outs
            else:
                root, scales, gram = outs
        if last:
            tall, evolving = call(
                last_rows_kernel,
                "rows",
                [state, state],
                mixed, change, forward, tall, known,
                unread=1,
            )
            coup, delta = call(
                functools.partial(last_kernel, total),
                "last",
                [state, square],
                mixed, tall, *in_stages(partial, "cuts"),
                far_outs=1,
                scratch=[
                    pltpu.VMEM((count, rank, rows), f32),
                    pltpu.SemaphoreType.DMA((count,)),
                ],
            )
            continue
        near = swapped(to_near, "cuts", 0)
        far = swapped(to_far, "cuts", 1)
        mixed, partial = call(
            mix_kernel,
            "mix",
            [quads, ((rank // 2, 2 * rank), f32)],
            near, far, delta, root, scales, gram,
            unread=2,
        )
        aux, dual, known, cross = call(
            functools.partial(ahead_kernel, group),
            "ahead",
            [state, state, state, ((groups, rank, 2 * wide), f32)],
            odd, partial, inside, near, far, target, tall, side, rho, inverse,
            scalars=1, unread=1,
        )
        sums, cross = in_stages(partial, "cuts", beside=cross)
        crosses = from_others(cross, "chan")
        delta, change, forward = call(
            functools.partial(mixer_kernel, total),
            "mixer",
            [square, quads, quads],
            mixed, inverse, rho, *sums,
        )
        if inner < INNER - 2:
            tall, target, inside, to_near, to_far = call(
                rows_kernel,
                "rows",
                [state, state, state, halo, halo],
                odd, aux, before, rho, after, change, forward, tall, known, dual,
                scalars=1,
            )
    return (flip(evolving), flip(coup), delta)


def solution(mesh):
    return jax.shard_map(
        body,
        mesh=mesh,
        in_specs=(
            P("cuts", None, "chan"),
            P("cuts"),
            P("chan", None),
            P("cuts", None),
            P("cuts", "chan", None),
            P("cuts", "chan", None),
            P("cuts", "chan", None),
            P("cuts", "chan", None),
            P(),
        ),
        out_specs=(P("cuts", "chan", None), P("cuts", "chan", None), P()),
        check_vma=False,
    )
```

```python
import functools

import jax
import jax.numpy as jnp
from jax import lax
from jax.experimental import pallas as pl
from jax.experimental.pallas import tpu as pltpu
from jax.sharding import PartitionSpec as P

INNER = 3
SWEEPS = 4
POLAR = 8

smooth_weight = 1.0
eps_trace = 1e-06
f32 = jnp.float32
bf16 = jnp.bfloat16
NN = (((1,), (0,)), ((), ()))
NT = (((1,), (1,)), ((), ()))


def dot(left, right, dims=NN):
    return lax.dot_general(left, right, dims, preferred_element_type=f32)


def split(value):
    high = value.astype(bf16)
    low = (value - high.astype(f32)).astype(bf16)
    return high, low


def left_triple(value):
    high, low = split(value)
    return jnp.concatenate([high, high, low], axis=1)


def right_triple(value):
    high, low = split(value)
    return jnp.concatenate([high, low, high], axis=0)


def block_mask(rank, group):
    wide = rank * group
    rows = lax.div(lax.broadcasted_iota(jnp.int32, (wide, wide), 0), rank)
    cols = lax.div(lax.broadcasted_iota(jnp.int32, (wide, wide), 1), rank)
    return jnp.where(rows == cols, 1.0, 0.0).astype(bf16)


def wide_eye(rank, group):
    rows = lax.broadcasted_iota(jnp.int32, (rank, rank * group), 0)
    cols = lax.broadcasted_iota(jnp.int32, (rank, rank * group), 1)
    return jnp.where(rows == lax.rem(cols, rank), 1.0, 0.0).astype(f32)


def block_diagonal(value, mask, group, dims=NN):
    high, low = split(value)
    high = jnp.concatenate([high] * group, axis=0) * mask
    low = jnp.concatenate([low] * group, axis=0) * mask
    empty = jnp.zeros_like(high)
    one, other = ([high, low], [high, empty]) if dims == NN else ([high, high], [low, empty])
    return jnp.concatenate(
        [jnp.concatenate(one, axis=1), jnp.concatenate(other, axis=1)], axis=0
    )


def times_blocks(values, blocks, dims=NN):
    rank, wide = values[0].shape
    left = [jnp.concatenate(split(value), axis=1) for value in values]
    total = dot(jnp.concatenate(left, axis=0), blocks, dims)
    total = total[:, :wide] + total[:, wide:]
    return [total[at * rank : (at + 1) * rank] for at in range(len(values))]


def diagonal_blocks(value, rank, group):
    at = lax.div(lax.broadcasted_iota(jnp.int32, (rank, rank * group), 1), rank)
    total = value[:rank]
    for block in range(1, group):
        total = jnp.where(at == block, value[block * rank : (block + 1) * rank], total)
    return total


def group_size(count, rank):
    group = max(1, 128 // rank)
    while count % group:
        group -= 1
    return group


def factor_kernel(factor_ref, gram_ref):
    factor = factor_ref[...]
    gram_ref[...] = dot(factor, factor, NT)


def project_kernel(order_ref, me_ref, first_ref, second_ref, factor_ref, after_ref, *outs):
    parts = len(outs)
    rows = outs[0].shape[1]
    factor = factor_ref[...]
    empty = jnp.zeros_like(factor)
    sides = [
        jnp.concatenate([factor, empty], axis=0),
        jnp.concatenate([empty, factor], axis=0),
    ]
    for part in reversed(range(parts)):
        start = pl.multiple_of(lax.rem(me_ref[0] + part, parts) * rows, 16)
        place = pl.ds(start, rows)
        outs[part][0] = dot(first_ref[0, place, :], sides[0], NT) + dot(
            second_ref[0, place, :], sides[1], NT
        )


def project(first, pairs, parts, rows, order, me, data, factor, after):
    count, all_rows, channels = data.shape
    rank = factor.shape[0]
    spec = lambda odd: pl.BlockSpec(
        (1, all_rows, channels),
        lambda i, order, me: (lax.rem(order[2 * (first + i) + odd], count), 0, 0),
    )
    return pl.pallas_call(
        project_kernel,
        out_shape=[jax.ShapeDtypeStruct((pairs, rows, 2 * rank), f32)] * parts,
        grid_spec=pltpu.PrefetchScalarGridSpec(
            num_scalar_prefetch=2,
            grid=(pairs,),
            in_specs=[
                spec(0),
                spec(1),
                pl.BlockSpec((rank, channels), lambda i, order, me: (0, 0)),
                pl.BlockSpec(memory_space=pl.ANY),
            ],
            out_specs=[pl.BlockSpec((1, rows, 2 * rank), lambda i, order, me: (i, 0, 0))] * parts,
        ),
        cost_estimate=pl.CostEstimate(
            flops=2 * per_microsecond, bytes_accessed=data.size, transcendentals=0
        ),
        name="project",
    )(order, me, data, data, factor, after)


def setup_kernel(grams, group, *refs):
    gram_refs, refs = refs[:grams], refs[grams:]
    (own_ref, aux_ref, coupled_ref, dual_s_ref, dual_c_ref) = refs[:5]
    (inverse_ref, mover_ref, rho_ref, diagonal_ref, columns_ref, base_ref) = refs[5:]
    count, rank = own_ref.shape
    gram = gram_refs[0][...]
    for ref in gram_refs[1:]:
        gram = gram + ref[...]
    eye = wide_eye(rank, 1)
    diagonal = jnp.sum(gram * eye, axis=0, keepdims=True)
    diagonal_ref[...] = jnp.broadcast_to(diagonal, diagonal_ref.shape)
    weights = own_ref[...]
    columns = weights.T
    columns_ref[...] = columns
    rho = jnp.sum(weights * weights * diagonal, axis=1, keepdims=True) / rank
    rho_ref[...] = jnp.broadcast_to(rho, rho_ref.shape)

    edge = 34.0 / 32.0
    lead = 4.0 * edge**3 / (4.0 * edge**3 - 3.0 * edge)
    mask = block_mask(rank, group)
    wide = wide_eye(rank, group)
    starts = range(0, count, group)
    systems = []
    for first in starts:
        scaled = []
        for k in range(first, first + group):
            unit = 1.0 / (34.0 * rho[k : k + 1, :])
            column = columns[:, k : k + 1]
            scaled.append(column * gram * weights[k : k + 1, :] * unit + (2.0 / 34.0) * eye)
        systems.append(jnp.concatenate(scaled, axis=1))
    inverses, rests = [], []
    for system in systems:
        rest = wide - system
        blocks = block_diagonal(rest, mask, group)
        (square,) = times_blocks([rest], blocks)
        (cube,) = times_blocks([square], blocks)
        inverses.append(wide + lead * (rest + square))
        rests.append(lead * cube - (lead - 1.0) * rest)
    for step in range(4):
        for at in range(len(systems)):
            blocks = block_diagonal(rests[at], mask, group)
            more, rests[at] = times_blocks([inverses[at], rests[at]], blocks)
            inverses[at] = inverses[at] + more
    for step in range(2):
        for at in range(len(systems)):
            (product,) = times_blocks([inverses[at]], block_diagonal(systems[at], mask, group))
            blocks = block_diagonal(wide - product, mask, group)
            (more,) = times_blocks([inverses[at]], blocks)
            inverses[at] = inverses[at] + more
    pair_mask = block_mask(rank, 2)
    for k in range(0, count, 2):
        both = []
        for j in (k, k + 1):
            place = (j % group) * rank
            unit = 1.0 / (34.0 * rho[j : j + 1, :])
            both.append(inverses[j // group][:, place : place + rank] * unit)
            inverse = left_triple(both[-1])
            inverse_ref[j] = inverse
            base_ref[j] = dot(
                inverse,
                right_triple(
                    rho[j : j + 1, :] * (aux_ref[j] - dual_s_ref[j] + coupled_ref[j] - dual_c_ref[j])
                ),
            )
        line = jnp.concatenate([weights[k : k + 1, :], weights[k + 1 : k + 2, :]], axis=1)
        high, low = split(jnp.concatenate(both, axis=1) * line)
        high = jnp.concatenate([high, high], axis=0) * pair_mask
        low = jnp.concatenate([low, low], axis=0) * pair_mask
        mover_ref[k // 2] = jnp.concatenate([high, high, low], axis=1)


def cross_blocks(lefts, rights, rank):
    group = len(lefts)
    wide = group * rank
    left = jnp.concatenate(split(jnp.concatenate(lefts, axis=0)), axis=0)
    right = left
    if rights is not lefts:
        right = jnp.concatenate(split(jnp.concatenate(rights, axis=0)), axis=0)
    total = dot(left, right, NT)
    total = total[:wide, :wide] + total[:wide, wide:] + total[wide:, :wide]
    return diagonal_blocks(total, rank, group)


def summed(refs, chunks, pair):
    chunk, at = divmod(pair, refs[0].shape[0])
    total = None
    for ref in refs[chunk::chunks]:
        total = ref[at] if total is None else total + ref[at]
    return total


def first_kernel(chunks, group, *refs):
    base_ref, mover_ref, dual_s_ref, dual_c_ref = refs[2:6]
    *projected_refs, tall_ref, target_ref, gram_ref = refs[6:]
    count, rank, rows = base_ref.shape
    talls = []
    for k in range(0, count, 2):
        high, low = split(summed(projected_refs, chunks, k // 2))
        both = dot(mover_ref[k // 2], jnp.concatenate([high, low, high], axis=1), NT)
        for j in (k, k + 1):
            evolving = base_ref[j] + both[(j - k) * rank : (j - k + 1) * rank]
            target_ref[j] = evolving + dual_s_ref[j]
            tall = evolving + dual_c_ref[j]
            tall_ref[j] = tall
            talls.append(tall)
    for first in range(0, count, group):
        some = talls[first : first + group]
        gram_ref[first // group] = cross_blocks(some, some, rank)


def smooth(odd, now, targets, rho, inside_ref, near_ref, far_ref):
    count = len(targets)
    width = SWEEPS
    share = {j: 2.0 * smooth_weight / (rho[j] + 4.0 * smooth_weight) for j in rho}
    pull = {j: (rho[j] / (rho[j] + 4.0 * smooth_weight)) * targets[j] for j in range(count)}
    now = {j: now[j] for j in range(count)}
    for sweep in range(width):
        later = {}
        for j in range(-sweep - 1, count + sweep + 1):
            beside = [now[i] for i in (j - 1, j + 1) if i in now]
            total = beside[0] if len(beside) == 1 else beside[0] + beside[1]
            total = share[j] * total
            later[j] = total + pull[j] if j in pull else total
        now = later
    for j in range(count):
        inside_ref[j] = now[j]
    for j in range(width):
        near_ref[j] = jnp.where(odd == 1, now[j - width], now[count + j])
        far_ref[j] = jnp.where(odd == 1, now[count + j], now[j - width])


def all_rho(before_ref, rho_ref, after_ref):
    count = rho_ref.shape[0]
    rho = {j: rho_ref[j : j + 1, 0:1] for j in range(count)}
    for j in range(SWEEPS):
        rho[j - SWEEPS] = before_ref[count - SWEEPS + j : count - SWEEPS + j + 1, 0:1]
        rho[count + j] = after_ref[j : j + 1, 0:1]
    return rho


def smooth_kernel(
    chunks, odd_ref, aux_ref, target_ref, before_ref, rho_ref, after_ref, diagonal_ref,
    columns_ref, *refs
):
    *projected_refs, side_ref, past_ref, next_ref, inside_ref, near_ref, far_ref = refs
    count, rank, rows = aux_ref.shape
    for source, place in ((before_ref, past_ref), (after_ref, next_ref)):
        weights = source[...]
        rho = jnp.sum(weights * weights * diagonal_ref[...], axis=1, keepdims=True) / rank
        place[...] = jnp.broadcast_to(rho, place.shape)
    rho = all_rho(past_ref, rho_ref, next_ref)
    slices = range(count)
    smooth(
        odd_ref[0], [aux_ref[k] for k in slices], [target_ref[k] for k in slices], rho,
        inside_ref, near_ref, far_ref,
    )
    for k in range(0, count, 2):
        both = summed(projected_refs, chunks, k // 2).T
        side_ref[k] = columns_ref[:, k : k + 1] * both[:rank]
        side_ref[k + 1] = columns_ref[:, k + 1 : k + 2] * both[rank:]


def polar(grams, delta):
    rank, wide = grams[0].shape
    group = wide // rank
    mask = block_mask(rank, group)
    eye = wide_eye(rank, group)
    delta_left = left_triple(delta)
    delta_blocks = block_diagonal(jnp.concatenate([delta] * group, axis=1), mask, group, NT)
    currents, roots, scales = [], [], []
    for gram in grams:
        left = dot(delta_left, right_triple(gram))
        (normal,) = times_blocks([left], delta_blocks, NT)
        line = jnp.broadcast_to(jnp.sum(normal * eye, axis=0, keepdims=True), (16, wide))
        high, low = split(line)
        rest = (line - high.astype(f32) - low.astype(f32)).astype(bf16)
        line = dot(high, mask) + dot(low, mask) + dot(rest, mask)
        trace = line[0:1] + eps_trace
        currents.append(normal / trace)
        scales.append(1.0 / jnp.sqrt(trace))
    for step in range(POLAR):
        for at in range(len(grams)):
            product = currents[at]
            blocks = block_diagonal(product, mask, group)
            if step == 0:
                roots.append(1.5 * eye - 0.5 * product)
                (square,) = times_blocks([product], blocks)
            elif step < POLAR - 1:
                square, more = times_blocks([product, roots[at]], blocks)
                roots[at] = 1.5 * roots[at] - 0.5 * more
            else:
                (more,) = times_blocks([roots[at]], blocks)
                roots[at] = 1.5 * roots[at] - 0.5 * more
            if step < POLAR - 1:
                half = 1.5 * product - 0.5 * square
                (more,) = times_blocks([half], blocks)
                currents[at] = 1.5 * half - 0.5 * more
    return roots, scales


def mix(roots, scales, grams, delta, mixed_ref, partial_ref):
    rank, wide = roots[0].shape
    group = wide // rank
    mask = block_mask(rank, group)
    delta_blocks = block_diagonal(jnp.concatenate([delta] * group, axis=1), mask, group)
    left, right = [], []
    for at in range(len(roots)):
        (mixed,) = times_blocks([roots[at]], delta_blocks)
        mixed = mixed * scales[at]
        mixed_ref[at] = mixed
        high, low = split(mixed)
        left += [high, high, low]
        high, low = split(grams[at])
        right += [high, low, high]
    partial = dot(jnp.concatenate(left, axis=1), jnp.concatenate(right, axis=1), NT)
    half = rank // 2
    partial_ref[...] = jnp.concatenate([partial[:half], partial[half:]], axis=1)


def first_polar_kernel(after_ref, delta_ref, *refs):
    *gram_refs, root_ref, scale_ref, gram_ref = refs
    grams = []
    for at in range(gram_ref.shape[0]):
        gram = gram_refs[0][at]
        for ref in gram_refs[1:]:
            gram = gram + ref[at]
        gram_ref[at] = gram
        grams.append(gram)
    roots, scales = polar(grams, delta_ref[...])
    for at in range(len(grams)):
        root_ref[at] = roots[at]
        scale_ref[at] = jnp.broadcast_to(scales[at], scale_ref.shape[1:])


def later_polar_kernel(last, after_ref, delta_ref, change_ref, old_ref, *refs):
    if last:
        *cross_refs, mixed_ref, partial_ref = refs
    else:
        *cross_refs, root_ref, scale_ref, gram_ref = refs
    groups, rank, wide = old_ref.shape
    group = wide // rank
    mask = block_mask(rank, group)
    grams = []
    for at in range(groups):
        cross = cross_refs[0][at]
        for ref in cross_refs[1:]:
            cross = cross + ref[at]
        change = change_ref[at]
        (onward,) = times_blocks([change], block_diagonal(old_ref[at], mask, group))
        onward = cross[:, :wide] + 0.5 * onward
        (one,) = times_blocks([onward], block_diagonal(change, mask, group, NT), NT)
        (other,) = times_blocks([change], block_diagonal(onward, mask, group, NT), NT)
        grams.append(cross[:, wide:] + one + other)
    delta = delta_ref[...]
    roots, scales = polar(grams, delta)
    if last:
        mix(roots, scales, grams, delta, mixed_ref, partial_ref)
    else:
        for at in range(groups):
            gram_ref[at] = grams[at]
            root_ref[at] = roots[at]
            scale_ref[at] = jnp.broadcast_to(scales[at], scale_ref.shape[1:])


def mix_kernel(near_ref, far_ref, delta_ref, root_ref, scale_ref, gram_ref, mixed_ref, partial_ref):
    groups = range(root_ref.shape[0])
    mix(
        [root_ref[at] for at in groups],
        [scale_ref[at, 0:1] for at in groups],
        [gram_ref[at] for at in groups],
        delta_ref[...], mixed_ref, partial_ref,
    )


def ahead_kernel(
    group, odd_ref, after_ref, inside_ref, near_ref, far_ref, target_ref, tall_ref, side_ref, rho_ref,
    inverse_ref, aux_ref, dual_ref, known_ref, cross_ref,
):
    count, rank, _ = inside_ref.shape
    width = SWEEPS
    knowns, talls = [], []
    for k in range(count):
        aux = inside_ref[k]
        if k < width:
            aux = aux + jnp.where(odd_ref[0] == 1, near_ref[k], far_ref[k])
        if k >= count - width:
            at = k - count + width
            aux = aux + jnp.where(odd_ref[0] == 1, far_ref[at], near_ref[at])
        target, tall = target_ref[k], tall_ref[k]
        aux_ref[k] = aux
        dual_ref[k] = target - aux
        known = dot(
            inverse_ref[k],
            right_triple(side_ref[k] + rho_ref[k : k + 1, 0:1] * (2.0 * aux - target - tall)),
        )
        known_ref[k] = known
        talls.append(tall)
        knowns.append(known + tall)
        if len(talls) == group:
            cross_ref[k // group] = jnp.concatenate(
                [cross_blocks(knowns, talls, rank), cross_blocks(knowns, knowns, rank)], axis=1
            )
            knowns, talls = [], []


def add_kernel(*refs):
    *term_refs, total_ref = refs
    total = term_refs[0][...]
    for ref in term_refs[1:]:
        total = total + ref[...]
    total_ref[...] = total


def new_delta(sum_refs, total, rank):
    packed = sum_refs[0][...]
    for ref in sum_refs[1:]:
        packed = packed + ref[...]
    packed = packed / total
    return jnp.concatenate([packed[:, :rank], packed[:, rank:]], axis=0)


def mixer_kernel(total, mixed_ref, inverse_ref, rho_ref, *refs):
    *sum_refs, delta_ref, change_ref, forward_ref = refs
    groups, rank, wide = mixed_ref.shape
    group = wide // rank
    delta = new_delta(sum_refs, total, rank)
    delta_ref[...] = delta
    delta_left = left_triple(delta.T)
    place = lax.div(lax.broadcasted_iota(jnp.int32, (1, wide), 1), rank)
    for at in range(groups):
        mixer = dot(delta_left, right_triple(mixed_ref[at]))
        slices = range(at * group, (at + 1) * group)
        inverses = jnp.concatenate([inverse_ref[k] for k in slices], axis=0)
        onward = diagonal_blocks(dot(inverses, right_triple(mixer)), rank, group)
        rho = rho_ref[at * group : at * group + 1, 0:1]
        for k in slices[1:]:
            rho = jnp.where(place == k - at * group, rho_ref[k : k + 1, 0:1], rho)
        forward = 2.0 * rho * onward
        forward_ref[at] = forward
        change_ref[at] = forward - mixer


def rows_kernel(odd_ref, aux_ref, before_ref, rho_ref, after_ref, *refs):
    (change_ref, forward_ref, tall_ref, known_ref, dual_ref) = refs[:5]
    (next_ref, target_ref, inside_ref, near_ref, far_ref) = refs[5:]
    targets = new_rows(change_ref, forward_ref, tall_ref, known_ref, next_ref)
    count = len(targets)
    for k in range(count):
        targets[k] = targets[k] + dual_ref[k]
        target_ref[k] = targets[k]
    rho = all_rho(before_ref, rho_ref, after_ref)
    smooth(
        odd_ref[0], [aux_ref[k] for k in range(count)], targets, rho,
        inside_ref, near_ref, far_ref,
    )


def last_rows_kernel(
    after_ref, change_ref, forward_ref, tall_ref, known_ref, next_ref, evolving_ref
):
    evolvings = new_rows(change_ref, forward_ref, tall_ref, known_ref, next_ref)
    for k in range(len(evolvings)):
        evolving_ref[k] = evolvings[k]


def new_rows(change_ref, forward_ref, tall_ref, known_ref, next_ref):
    groups, rank, wide = change_ref.shape
    group = wide // rank
    evolvings = []
    for k in range(groups * group):
        lanes = slice((k % group) * rank, (k % group + 1) * rank)
        change, forward = change_ref[k // group][:, lanes], forward_ref[k // group][:, lanes]
        left = jnp.concatenate([left_triple(change), left_triple(forward)], axis=0)
        tall, known = tall_ref[k], known_ref[k]
        both = dot(left, right_triple(tall))
        next_ref[k] = known + tall + both[:rank]
        evolvings.append(known + both[rank:])
    return evolvings


def last_kernel(total, mixed_ref, tall_ref, *refs):
    *sum_refs, coupled_ref, delta_ref = refs
    groups, rank, wide = mixed_ref.shape
    group = wide // rank
    delta = new_delta(sum_refs, total, rank)
    delta_ref[...] = delta
    delta_left = left_triple(delta.T)
    for at in range(groups):
        mixer = dot(delta_left, right_triple(mixed_ref[at]))
        for k in range(at * group, (at + 1) * group):
            place = (k - at * group) * rank
            coupled_ref[k] = dot(
                left_triple(mixer[:, place : place + rank]), right_triple(tall_ref[k])
            )


per_microsecond = 1_100_000_000


def call(
    kernel, name, outs, *args, scalars=0, unread=0, microseconds=0.3
):
    flops = int(microseconds * per_microsecond)
    specs = [pl.BlockSpec(memory_space=pltpu.SMEM)] * scalars
    specs += [pl.BlockSpec(memory_space=pl.ANY)] * unread
    specs += [pl.BlockSpec(memory_space=pltpu.VMEM)] * (len(args) - len(specs))
    shapes = [jax.ShapeDtypeStruct(shape, dtype) for shape, dtype in outs]
    moved = sum(arg.size * arg.dtype.itemsize for arg in args)
    moved += sum(shape.size * shape.dtype.itemsize for shape in shapes)
    return pl.pallas_call(
        kernel,
        out_shape=shapes,
        in_specs=specs,
        out_specs=[pl.BlockSpec(memory_space=pltpu.VMEM)] * len(shapes),
        compiler_params=pltpu.CompilerParams(vmem_limit_bytes=16 * 1024 * 1024),
        cost_estimate=pl.CostEstimate(flops=flops, bytes_accessed=moved, transcendentals=0),
        name=name,
    )(*args)


def rotated(value, axis, shift):
    count = lax.axis_size(axis)
    return lax.ppermute(value, axis, [(i, (i + shift) % count) for i in range(count)])


def swapped(value, axis, first):
    count = lax.axis_size(axis)
    pairs = [((i + first) % count, (i + first + 1) % count) for i in range(0, count, 2)]
    return lax.ppermute(value, axis, pairs + [(b, a) for a, b in pairs])


def from_others(value, axis):
    return [rotated(value, axis, shift) for shift in range(1, lax.axis_size(axis))]


def stage_sizes(count):
    sizes = []
    while count > 1:
        sizes.append(next(size for size in (4, 2, 3, 5, 7, count) if count % size == 0))
        count //= sizes[-1]
    return sizes


def in_stages(value, axis, beside=None):
    count = lax.axis_size(axis)
    stride = 1
    terms = [value]
    for size in stage_sizes(count):
        value = terms[0]
        if len(terms) > 1:
            (value,) = call(add_kernel, "add", [(value.shape, f32)], *terms, microseconds=0.1)
        if stride > 1 and beside is not None:
            value, beside = lax.optimization_barrier((value, beside))
        terms = [value]
        for shift in range(1, size):
            moves = []
            for i in range(count):
                digit = (i // stride) % size
                other = digit ^ shift if size in (2, 4) else (digit + shift) % size
                moves.append((i, i + (other - digit) * stride))
            terms.append(lax.ppermute(value, axis, moves))
        stride *= size
    return terms if beside is None else (terms, beside)


def body(
    data, order, chan_factor, slice_weights, smooth_aux, coupled, smooth_dual, coupling_dual, delta
):
    count, all_rows, channels = data.shape
    rank = chan_factor.shape[1]
    rows = smooth_aux.shape[1]
    parts = lax.axis_size("chan")
    total = count * lax.axis_size("cuts")
    group = group_size(count, rank)
    groups = count // group
    wide = group * rank
    flip = lambda value: jnp.swapaxes(value, 1, 2)
    aux, coup, dual_s, dual_c = map(flip, (smooth_aux, coupled, smooth_dual, coupling_dual))
    factor = chan_factor.T
    state = ((count, rank, rows), f32)
    quads = ((groups, rank, wide), f32)
    square = ((rank, rank), f32)
    halo = ((SWEEPS, rank, rows), f32)
    lanes = lambda height: ((height, 128), f32)
    scale = ((groups, 8, wide), f32)

    me = lax.axis_index("chan").astype(jnp.int32).reshape(1)
    odd = lax.rem(lax.axis_index("cuts"), 2).astype(jnp.int32).reshape(1)
    chunks = 2 if count % 4 == 0 else 1
    pairs = count // 2 // chunks
    (gram_part,) = call(factor_kernel, "factor", [square], factor)
    grams = [gram_part] + from_others(gram_part, "chan")
    own, arrived = [], []
    for chunk in range(chunks):
        projected = project(
            chunk * pairs, pairs, parts, rows, order, me, data, factor, gram_part
        )
        if chunk == 0:
            projected, grams = lax.optimization_barrier((projected, grams))
        own.append(projected[0])
        arrived.append([rotated(projected[shift], "chan", shift) for shift in range(1, parts)])
    received = [arrived[chunk][at] for at in range(parts - 1) for chunk in range(chunks)]

    late_weights, _ = lax.optimization_barrier((slice_weights, own[-1]))
    before = rotated(late_weights, "cuts", 1)
    after = rotated(late_weights, "cuts", -1)
    inverse, mover, rho, diagonal, columns, base = call(
        functools.partial(setup_kernel, len(grams), group),
        "setup",
        [
            ((count, rank, 3 * rank), bf16),
            ((count // 2, 2 * rank, 6 * rank), bf16),
            lanes(count),
            ((count, rank), f32),
            ((rank, count), f32),
            state,
        ],
        *grams, slice_weights, aux, coup, dual_s, dual_c,
    )
    tall, target, gram = call(
        functools.partial(first_kernel, chunks, group),
        "first",
        [state, state, quads],
        before, after, base, mover, dual_s, dual_c, *own, *received,
        unread=2,
    )
    side, before, after, inside, to_near, to_far = call(
        functools.partial(smooth_kernel, chunks),
        "smooth",
        [state, lanes(count), lanes(count), state, halo, halo],
        odd, aux, target, before, rho, after, diagonal, columns, *own, *received,
        scalars=1,
    )
    for inner in range(INNER):
        last = inner == INNER - 1
        polar_outs = [quads, scale, quads]
        if inner == 0:
            root, scales, gram = call(
                first_polar_kernel,
                "polar",
                polar_outs,
                inside, delta, gram, *from_others(gram, "chan"),
                unread=1, microseconds=3,
            )
        else:
            outs = call(
                functools.partial(later_polar_kernel, last),
                "polar",
                [quads, ((rank // 2, 2 * rank), f32)] if last else polar_outs,
                odd if last else inside, delta, change, gram, cross, *crosses,
                unread=1, microseconds=3,
            )
            if last:
                mixed, partial = outs
            else:
                root, scales, gram = outs
        if last:
            tall, evolving = call(
                last_rows_kernel,
                "rows",
                [state, state],
                mixed, change, forward, tall, known,
                unread=1,
            )
            coup, delta = call(
                functools.partial(last_kernel, total),
                "last",
                [state, square],
                mixed, tall, *in_stages(partial, "cuts"),
            )
            continue
        near = swapped(to_near, "cuts", 0)
        far = swapped(to_far, "cuts", 1)
        mixed, partial = call(
            mix_kernel,
            "mix",
            [quads, ((rank // 2, 2 * rank), f32)],
            near, far, delta, root, scales, gram,
            unread=2,
        )
        aux, dual, known, cross = call(
            functools.partial(ahead_kernel, group),
            "ahead",
            [state, state, state, ((groups, rank, 2 * wide), f32)],
            odd, partial, inside, near, far, target, tall, side, rho, inverse,
            scalars=1, unread=1,
        )
        sums, cross = in_stages(partial, "cuts", beside=cross)
        if inner < INNER - 2:
            sums, cross = lax.optimization_barrier((sums, cross))
        crosses = from_others(cross, "chan")
        delta, change, forward = call(
            functools.partial(mixer_kernel, total),
            "mixer",
            [square, quads, quads],
            mixed, inverse, rho, *sums,
        )
        if inner < INNER - 2:
            tall, target, inside, to_near, to_far = call(
                rows_kernel,
                "rows",
                [state, state, state, halo, halo],
                odd, aux, before, rho, after, change, forward, tall, known, dual,
                scalars=1,
            )
    return (flip(evolving), flip(coup), delta)


def solution(mesh):
    return jax.shard_map(
        body,
        mesh=mesh,
        in_specs=(
            P("cuts", None, "chan"),
            P("cuts"),
            P("chan", None),
            P("cuts", None),
            P("cuts", "chan", None),
            P("cuts", "chan", None),
            P("cuts", "chan", None),
            P("cuts", "chan", None),
            P(),
        ),
        out_specs=(P("cuts", "chan", None), P("cuts", "chan", None), P()),
        check_vma=False,
    )
```

```python
import functools

import jax
import jax.numpy as jnp
from jax import lax
from jax.experimental import pallas as pl
from jax.experimental.pallas import tpu as pltpu
from jax.sharding import PartitionSpec as P

INNER = 3
SWEEPS = 4
POLAR = 8

smooth_weight = 1.0
eps_trace = 1e-06
f32 = jnp.float32
bf16 = jnp.bfloat16
NN = (((1,), (0,)), ((), ()))
NT = (((1,), (1,)), ((), ()))


def dot(left, right, dims=NN):
    return lax.dot_general(left, right, dims, preferred_element_type=f32)


def split(value):
    high = value.astype(bf16)
    low = (value - high.astype(f32)).astype(bf16)
    return high, low


def left_triple(value):
    high, low = split(value)
    return jnp.concatenate([high, high, low], axis=1)


def right_triple(value):
    high, low = split(value)
    return jnp.concatenate([high, low, high], axis=0)


def block_mask(rank, group):
    wide = rank * group
    rows = lax.div(lax.broadcasted_iota(jnp.int32, (wide, wide), 0), rank)
    cols = lax.div(lax.broadcasted_iota(jnp.int32, (wide, wide), 1), rank)
    return jnp.where(rows == cols, 1.0, 0.0).astype(bf16)


def wide_eye(rank, group):
    rows = lax.broadcasted_iota(jnp.int32, (rank, rank * group), 0)
    cols = lax.broadcasted_iota(jnp.int32, (rank, rank * group), 1)
    return jnp.where(rows == lax.rem(cols, rank), 1.0, 0.0).astype(f32)


def block_diagonal(value, mask, group, dims=NN):
    high, low = split(value)
    high = jnp.concatenate([high] * group, axis=0) * mask
    low = jnp.concatenate([low] * group, axis=0) * mask
    empty = jnp.zeros_like(high)
    one, other = ([high, low], [high, empty]) if dims == NN else ([high, high], [low, empty])
    return jnp.concatenate(
        [jnp.concatenate(one, axis=1), jnp.concatenate(other, axis=1)], axis=0
    )


def times_blocks(values, blocks, dims=NN):
    rank, wide = values[0].shape
    left = [jnp.concatenate(split(value), axis=1) for value in values]
    total = dot(jnp.concatenate(left, axis=0), blocks, dims)
    total = total[:, :wide] + total[:, wide:]
    return [total[at * rank : (at + 1) * rank] for at in range(len(values))]


def diagonal_blocks(value, rank, group):
    at = lax.div(lax.broadcasted_iota(jnp.int32, (rank, rank * group), 1), rank)
    total = value[:rank]
    for block in range(1, group):
        total = jnp.where(at == block, value[block * rank : (block + 1) * rank], total)
    return total


def from_left(left, values):
    wide = values[0].shape[1]
    total = dot(left_triple(left), right_triple(jnp.concatenate(values, axis=1)))
    return [total[:, at * wide : (at + 1) * wide] for at in range(len(values))]


def group_size(count, rank):
    group = max(1, 128 // rank)
    while count % group:
        group -= 1
    return group


def factor_kernel(factor_ref, gram_ref, again_ref):
    factor = factor_ref[...]
    gram_ref[...] = dot(factor, factor, NT)
    again_ref[...] = factor


def project_kernel(me_ref, data_ref, factor_ref, *refs):
    *outs, held, arrived = refs
    parts = len(outs)
    pairs, rows, _ = outs[0].shape
    count, all_rows, _ = data_ref.shape
    half = all_rows // 2
    copies = []
    for k in range(count):
        for at in range(2):
            place = pl.ds(at * half, half)
            copies.append(
                pltpu.make_async_copy(
                    data_ref.at[k, place, :], held.at[k, place, :], arrived.at[2 * k + at]
                )
            )
            copies[-1].start()
    factor = factor_ref[...]
    empty = jnp.zeros_like(factor)
    sides = [
        jnp.concatenate([factor, empty], axis=0),
        jnp.concatenate([empty, factor], axis=0),
    ]
    for pair in range(pairs):
        for copy in copies[4 * pair : 4 * pair + 4]:
            copy.wait()
        for part in reversed(range(parts)):
            start = pl.multiple_of(lax.rem(me_ref[0] + part, parts) * rows, 16)
            place = pl.ds(start, rows)
            outs[part][pair] = dot(held[2 * pair, place, :], sides[0], NT) + dot(
                held[2 * pair + 1, place, :], sides[1], NT
            )


def setup_kernel(grams, group, order_ref, *refs):
    gram_refs, refs = refs[:grams], refs[grams:]
    (own_ref, aux_ref, coupled_ref, dual_s_ref, dual_c_ref) = refs[:5]
    (inverse_ref, mover_ref, rho_ref, diagonal_ref, columns_ref, base_ref) = refs[5:]
    count, rank = own_ref.shape
    gram = gram_refs[0][...]
    for ref in gram_refs[1:]:
        gram = gram + ref[...]
    eye = wide_eye(rank, 1)
    diagonal = jnp.sum(gram * eye, axis=0, keepdims=True)
    diagonal_ref[...] = jnp.broadcast_to(diagonal, diagonal_ref.shape)
    weights = own_ref[...]
    columns = weights.T
    columns_ref[...] = columns
    rho = jnp.sum(weights * weights * diagonal, axis=1, keepdims=True) / rank
    rho_ref[...] = jnp.broadcast_to(rho, rho_ref.shape)

    edge = 34.0 / 32.0
    lead = 4.0 * edge**3 / (4.0 * edge**3 - 3.0 * edge)
    mask = block_mask(rank, group)
    wide = wide_eye(rank, group)
    starts = range(0, count, group)
    systems = []
    for first in starts:
        scaled = []
        for k in range(first, first + group):
            unit = 1.0 / (34.0 * rho[k : k + 1, :])
            column = columns[:, k : k + 1]
            scaled.append(column * gram * weights[k : k + 1, :] * unit + (2.0 / 34.0) * eye)
        systems.append(jnp.concatenate(scaled, axis=1))
    inverses, rests = [], []
    for system in systems:
        rest = wide - system
        blocks = block_diagonal(rest, mask, group)
        (square,) = times_blocks([rest], blocks)
        (cube,) = times_blocks([square], blocks)
        inverses.append(wide + lead * (rest + square))
        rests.append(lead * cube - (lead - 1.0) * rest)
    for step in range(4):
        for at in range(len(systems)):
            blocks = block_diagonal(rests[at], mask, group)
            more, rests[at] = times_blocks([inverses[at], rests[at]], blocks)
            inverses[at] = inverses[at] + more
    for step in range(2):
        for at in range(len(systems)):
            (product,) = times_blocks([inverses[at]], block_diagonal(systems[at], mask, group))
            blocks = block_diagonal(wide - product, mask, group)
            (more,) = times_blocks([inverses[at]], blocks)
            inverses[at] = inverses[at] + more
    for k in range(count):
        place = (k % group) * rank
        unit = 1.0 / (34.0 * rho[k : k + 1, :])
        inverse = inverses[k // group][:, place : place + rank] * unit
        inverse_ref[k] = left_triple(inverse)
        base_ref[k] = dot(
            inverse_ref[k],
            right_triple(
                rho[k : k + 1, :] * (aux_ref[k] - dual_s_ref[k] + coupled_ref[k] - dual_c_ref[k])
            ),
        )
        both = jnp.concatenate([inverse * weights[k : k + 1, :]] * 2, axis=1)
        side = lax.div(lax.broadcasted_iota(jnp.int32, both.shape, 1), rank)
        both = jnp.where(side == lax.rem(order_ref[k], 2), both, 0.0)
        high, low = split(both)
        mover_ref[k] = jnp.concatenate([high, high, low], axis=1)


def cross_blocks(lefts, rights, rank):
    group = len(lefts)
    wide = group * rank
    left = jnp.concatenate(split(jnp.concatenate(lefts, axis=0)), axis=0)
    right = left
    if rights is not lefts:
        right = jnp.concatenate(split(jnp.concatenate(rights, axis=0)), axis=0)
    total = dot(left, right, NT)
    total = total[:wide, :wide] + total[:wide, wide:] + total[wide:, :wide]
    return diagonal_blocks(total, rank, group)


def summed(refs, at):
    total = refs[0][at]
    for ref in refs[1:]:
        total = total + ref[at]
    return total


def stored_pair(order_ref, refs, k, count):
    return summed(refs, lax.div(lax.rem(order_ref[k], count), 2))


def first_kernel(group, order_ref, *refs):
    base_ref, mover_ref, dual_s_ref, dual_c_ref = refs[2:6]
    *projected_refs, tall_ref, target_ref, gram_ref = refs[6:]
    count, rank, rows = base_ref.shape
    talls = []
    for k in range(count):
        high, low = split(stored_pair(order_ref, projected_refs, k, count))
        moved = dot(mover_ref[k], jnp.concatenate([high, low, high], axis=1), NT)
        evolving = base_ref[k] + moved
        target_ref[k] = evolving + dual_s_ref[k]
        tall = evolving + dual_c_ref[k]
        tall_ref[k] = tall
        talls.append(tall)
        if len(talls) == group:
            gram_ref[k // group] = cross_blocks(talls, talls, rank)
            talls = []


def smooth(odd, now, targets, rho, inside_ref, near_ref, far_ref):
    count = len(targets)
    width = SWEEPS
    share = {j: 2.0 * smooth_weight / (rho[j] + 4.0 * smooth_weight) for j in rho}
    pull = {j: (rho[j] / (rho[j] + 4.0 * smooth_weight)) * targets[j] for j in range(count)}
    now = {j: now[j] for j in range(count)}
    for sweep in range(width):
        later = {}
        for j in range(-sweep - 1, count + sweep + 1):
            beside = [now[i] for i in (j - 1, j + 1) if i in now]
            total = beside[0] if len(beside) == 1 else beside[0] + beside[1]
            total = share[j] * total
            later[j] = total + pull[j] if j in pull else total
        now = later
    for j in range(count):
        inside_ref[j] = now[j]
    for j in range(width):
        near_ref[j] = jnp.where(odd == 1, now[j - width], now[count + j])
        far_ref[j] = jnp.where(odd == 1, now[count + j], now[j - width])


def all_rho(before_ref, rho_ref, after_ref):
    count = rho_ref.shape[0]
    rho = {j: rho_ref[j : j + 1, 0:1] for j in range(count)}
    for j in range(SWEEPS):
        rho[j - SWEEPS] = before_ref[count - SWEEPS + j : count - SWEEPS + j + 1, 0:1]
        rho[count + j] = after_ref[j : j + 1, 0:1]
    return rho


def smooth_kernel(
    odd_ref, order_ref, aux_ref, target_ref, before_ref, rho_ref, after_ref, diagonal_ref,
    columns_ref, *refs
):
    *projected_refs, side_ref, past_ref, next_ref, inside_ref, near_ref, far_ref = refs
    count, rank, rows = aux_ref.shape
    for source, place in ((before_ref, past_ref), (after_ref, next_ref)):
        weights = source[...]
        rho = jnp.sum(weights * weights * diagonal_ref[...], axis=1, keepdims=True) / rank
        place[...] = jnp.broadcast_to(rho, place.shape)
    rho = all_rho(past_ref, rho_ref, next_ref)
    slices = range(count)
    smooth(
        odd_ref[0], [aux_ref[k] for k in slices], [target_ref[k] for k in slices], rho,
        inside_ref, near_ref, far_ref,
    )
    for k in slices:
        both = stored_pair(order_ref, projected_refs, k, count).T
        own = jnp.where(lax.rem(order_ref[k], 2) == 1, both[rank:], both[:rank])
        side_ref[k] = columns_ref[:, k : k + 1] * own


def polar(grams, delta):
    rank, wide = grams[0].shape
    group = wide // rank
    mask = block_mask(rank, group)
    eye = wide_eye(rank, group)
    delta_blocks = block_diagonal(jnp.concatenate([delta] * group, axis=1), mask, group, NT)
    currents, roots, scales = [], [], []
    for left in from_left(delta, grams):
        (normal,) = times_blocks([left], delta_blocks, NT)
        line = jnp.broadcast_to(jnp.sum(normal * eye, axis=0, keepdims=True), (16, wide))
        high, low = split(line)
        rest = (line - high.astype(f32) - low.astype(f32)).astype(bf16)
        line = dot(high, mask) + dot(low, mask) + dot(rest, mask)
        trace = line[0:1] + eps_trace
        currents.append(normal / trace)
        scales.append(1.0 / jnp.sqrt(trace))
    for step in range(POLAR):
        for at in range(len(grams)):
            product = currents[at]
            blocks = block_diagonal(product, mask, group)
            if step == 0:
                roots.append(1.5 * eye - 0.5 * product)
                (square,) = times_blocks([product], blocks)
            elif step < POLAR - 1:
                square, more = times_blocks([product, roots[at]], blocks)
                roots[at] = 1.5 * roots[at] - 0.5 * more
            else:
                (more,) = times_blocks([roots[at]], blocks)
                roots[at] = 1.5 * roots[at] - 0.5 * more
            if step < POLAR - 1:
                half = 1.5 * product - 0.5 * square
                (more,) = times_blocks([half], blocks)
                currents[at] = 1.5 * half - 0.5 * more
    return roots, scales


def mix(roots, scales, grams, delta, mixed_ref, partial_ref):
    rank, wide = roots[0].shape
    group = wide // rank
    mask = block_mask(rank, group)
    delta_blocks = block_diagonal(jnp.concatenate([delta] * group, axis=1), mask, group)
    left, right = [], []
    for at in range(len(roots)):
        (mixed,) = times_blocks([roots[at]], delta_blocks)
        mixed = mixed * scales[at]
        mixed_ref[at] = mixed
        high, low = split(mixed)
        left += [high, high, low]
        high, low = split(grams[at])
        right += [high, low, high]
    partial = dot(jnp.concatenate(left, axis=1), jnp.concatenate(right, axis=1), NT)
    half = rank // 2
    partial_ref[...] = jnp.concatenate([partial[:half], partial[half:]], axis=1)


def first_polar_kernel(after_ref, delta_ref, *refs):
    *gram_refs, mixed_ref, partial_ref, gram_ref = refs
    grams = [summed(gram_refs, at) for at in range(gram_ref.shape[0])]
    for at in range(len(grams)):
        gram_ref[at] = grams[at]
    delta = delta_ref[...]
    roots, scales = polar(grams, delta)
    mix(roots, scales, grams, delta, mixed_ref, partial_ref)


def later_polar_kernel(after_ref, delta_ref, change_ref, old_ref, *refs):
    *cross_refs, mixed_ref, partial_ref, gram_ref = refs
    groups, rank, wide = old_ref.shape
    group = wide // rank
    mask = block_mask(rank, group)
    grams = []
    for at in range(groups):
        cross = summed(cross_refs, at)
        change = change_ref[at]
        (onward,) = times_blocks([change], block_diagonal(old_ref[at], mask, group))
        onward = cross[:, :wide] + 0.5 * onward
        (one,) = times_blocks([onward], block_diagonal(change, mask, group, NT), NT)
        (other,) = times_blocks([change], block_diagonal(onward, mask, group, NT), NT)
        grams.append(cross[:, wide:] + one + other)
        gram_ref[at] = grams[at]
    delta = delta_ref[...]
    roots, scales = polar(grams, delta)
    mix(roots, scales, grams, delta, mixed_ref, partial_ref)


def ahead_kernel(
    group, odd_ref, after_ref, inside_ref, near_ref, far_ref, target_ref, tall_ref, side_ref, rho_ref,
    inverse_ref, aux_ref, dual_ref, known_ref, cross_ref,
):
    count, rank, _ = inside_ref.shape
    width = SWEEPS
    knowns, talls = [], []
    for k in range(count):
        aux = inside_ref[k]
        if k < width:
            aux = aux + jnp.where(odd_ref[0] == 1, near_ref[k], far_ref[k])
        if k >= count - width:
            at = k - count + width
            aux = aux + jnp.where(odd_ref[0] == 1, far_ref[at], near_ref[at])
        target, tall = target_ref[k], tall_ref[k]
        aux_ref[k] = aux
        dual_ref[k] = target - aux
        known = dot(
            inverse_ref[k],
            right_triple(side_ref[k] + rho_ref[k : k + 1, 0:1] * (2.0 * aux - target - tall)),
        )
        known_ref[k] = known
        talls.append(tall)
        knowns.append(known + tall)
        if len(talls) == group:
            cross_ref[k // group] = jnp.concatenate(
                [cross_blocks(knowns, talls, rank), cross_blocks(knowns, knowns, rank)], axis=1
            )
            knowns, talls = [], []


def add_kernel(unread, *refs):
    *term_refs, total_ref = refs[unread:]
    total = term_refs[0][...]
    for ref in term_refs[1:]:
        total = total + ref[...]
    total_ref[...] = total


def new_delta(sum_refs, total, rank):
    packed = sum_refs[0][...]
    for ref in sum_refs[1:]:
        packed = packed + ref[...]
    packed = packed / total
    return jnp.concatenate([packed[:, :rank], packed[:, rank:]], axis=0)


def mixer_kernel(total, mixed_ref, inverse_ref, rho_ref, *refs):
    *sum_refs, delta_ref, change_ref, forward_ref = refs
    groups, rank, wide = mixed_ref.shape
    group = wide // rank
    delta = new_delta(sum_refs, total, rank)
    delta_ref[...] = delta
    mixers = from_left(delta.T, [mixed_ref[at] for at in range(groups)])
    place = lax.div(lax.broadcasted_iota(jnp.int32, (1, wide), 1), rank)
    for at in range(groups):
        mixer = mixers[at]
        slices = range(at * group, (at + 1) * group)
        inverses = jnp.concatenate([inverse_ref[k] for k in slices], axis=0)
        onward = diagonal_blocks(dot(inverses, right_triple(mixer)), rank, group)
        rho = rho_ref[at * group : at * group + 1, 0:1]
        for k in slices[1:]:
            rho = jnp.where(place == k - at * group, rho_ref[k : k + 1, 0:1], rho)
        forward = 2.0 * rho * onward
        forward_ref[at] = forward
        change_ref[at] = forward - mixer


def rows_kernel(odd_ref, aux_ref, before_ref, rho_ref, after_ref, *refs):
    (change_ref, forward_ref, tall_ref, known_ref, dual_ref) = refs[:5]
    (next_ref, target_ref, inside_ref, near_ref, far_ref) = refs[5:]
    targets = new_rows(change_ref, forward_ref, tall_ref, known_ref, next_ref)
    count = len(targets)
    for k in range(count):
        targets[k] = targets[k] + dual_ref[k]
        target_ref[k] = targets[k]
    rho = all_rho(before_ref, rho_ref, after_ref)
    smooth(
        odd_ref[0], [aux_ref[k] for k in range(count)], targets, rho,
        inside_ref, near_ref, far_ref,
    )


def last_rows_kernel(mixed_ref, change_ref, forward_ref, tall_ref, known_ref, *outs):
    mixed_tall_ref, evolving_ref, next_ref = outs
    evolvings = new_rows(change_ref, forward_ref, tall_ref, known_ref, next_ref)
    groups, rank, wide = mixed_ref.shape
    group = wide // rank
    for k in range(len(evolvings)):
        evolving_ref[k] = evolvings[k]
        place = (k % group) * rank
        mixed = left_triple(mixed_ref[k // group][:, place : place + rank])
        mixed_tall_ref[k] = right_triple(dot(mixed, right_triple(next_ref[k])))


def new_rows(change_ref, forward_ref, tall_ref, known_ref, next_ref):
    groups, rank, wide = change_ref.shape
    group = wide // rank
    evolvings = []
    for k in range(groups * group):
        lanes = slice((k % group) * rank, (k % group + 1) * rank)
        change, forward = change_ref[k // group][:, lanes], forward_ref[k // group][:, lanes]
        left = jnp.concatenate([left_triple(change), left_triple(forward)], axis=0)
        tall, known = tall_ref[k], known_ref[k]
        both = dot(left, right_triple(tall))
        next_ref[k] = known + tall + both[:rank]
        evolvings.append(known + both[rank:])
    return evolvings


def last_kernel(total, mixed_tall_ref, *refs):
    *sum_refs, coupled_ref, delta_ref = refs
    delta = new_delta(sum_refs, total, delta_ref.shape[0])
    delta_ref[...] = delta
    delta_left = left_triple(delta.T)
    for k in range(coupled_ref.shape[0]):
        coupled_ref[k] = dot(delta_left, mixed_tall_ref[k])


per_microsecond = 1_100_000_000


def call(
    kernel, name, outs, *args, scalars=0, unread=0, microseconds=0.3, limit=16, scratch=()
):
    flops = int(microseconds * per_microsecond)
    specs = [pl.BlockSpec(memory_space=pltpu.SMEM)] * scalars
    specs += [pl.BlockSpec(memory_space=pl.ANY)] * unread
    specs += [pl.BlockSpec(memory_space=pltpu.VMEM)] * (len(args) - len(specs))
    shapes = [jax.ShapeDtypeStruct(shape, dtype) for shape, dtype in outs]
    moved = sum(arg.size * arg.dtype.itemsize for arg in args)
    moved += sum(shape.size * shape.dtype.itemsize for shape in shapes)
    return pl.pallas_call(
        kernel,
        out_shape=shapes,
        in_specs=specs,
        out_specs=[pl.BlockSpec(memory_space=pltpu.VMEM)] * len(shapes),
        scratch_shapes=list(scratch),
        compiler_params=pltpu.CompilerParams(vmem_limit_bytes=limit * 1024 * 1024),
        cost_estimate=pl.CostEstimate(flops=flops, bytes_accessed=moved, transcendentals=0),
        name=name,
    )(*args)


def rotated(value, axis, shift):
    count = lax.axis_size(axis)
    return lax.ppermute(value, axis, [(i, (i + shift) % count) for i in range(count)])


def swapped(value, axis, first):
    count = lax.axis_size(axis)
    pairs = [((i + first) % count, (i + first + 1) % count) for i in range(0, count, 2)]
    return lax.ppermute(value, axis, pairs + [(b, a) for a, b in pairs])


def from_others(value, axis):
    return [rotated(value, axis, shift) for shift in range(1, lax.axis_size(axis))]


def stage_sizes(count):
    sizes = []
    while count > 1:
        sizes.append(next(size for size in (4, 2, 3, 5, 7, count) if count % size == 0))
        count //= sizes[-1]
    return sizes


def in_stages(value, axis, beside=None):
    count = lax.axis_size(axis)
    stride = 1
    terms, firsts = [value], []
    for size in stage_sizes(count):
        value = terms[0]
        if len(terms) > 1:
            unread = [] if beside is None else [beside]
            (value,) = call(
                functools.partial(add_kernel, len(unread)),
                "add",
                [(value.shape, f32)],
                *unread, *terms,
                unread=len(unread),
            )
        terms = [value]
        for shift in range(1, size):
            moves = []
            for i in range(count):
                digit = (i // stride) % size
                other = digit ^ shift if size in (2, 4) else (digit + shift) % size
                moves.append((i, i + (other - digit) * stride))
            terms.append(lax.ppermute(value, axis, moves))
        stride *= size
        firsts = firsts or terms
    return terms, firsts


def body(
    data, order, chan_factor, slice_weights, smooth_aux, coupled, smooth_dual, coupling_dual, delta
):
    count, all_rows, channels = data.shape
    rank = chan_factor.shape[1]
    rows = smooth_aux.shape[1]
    parts = lax.axis_size("chan")
    total = count * lax.axis_size("cuts")
    group = group_size(count, rank)
    groups = count // group
    wide = group * rank
    flip = lambda value: jnp.swapaxes(value, 1, 2)
    aux, coup, dual_s, dual_c = map(flip, (smooth_aux, coupled, smooth_dual, coupling_dual))
    factor = chan_factor.T
    state = ((count, rank, rows), f32)
    quads = ((groups, rank, wide), f32)
    square = ((rank, rank), f32)
    halo = ((SWEEPS, rank, rows), f32)
    lanes = lambda height: ((height, 128), f32)
    scale = ((groups, 8, wide), f32)

    me = lax.axis_index("chan").astype(jnp.int32).reshape(1)
    odd = lax.rem(lax.axis_index("cuts"), 2).astype(jnp.int32).reshape(1)
    gram_part, factor = call(
        factor_kernel, "factor", [square, (factor.shape, factor.dtype)], factor
    )
    grams = [gram_part] + from_others(gram_part, "chan")
    projected = call(
        project_kernel,
        "project",
        [((count // 2, rows, 2 * rank), f32)] * parts,
        me, data, factor,
        scalars=1, unread=1, microseconds=2, limit=52,
        scratch=[
            pltpu.VMEM((count, all_rows, channels), data.dtype),
            pltpu.SemaphoreType.DMA((2 * count,)),
        ],
    )
    projected, grams = lax.optimization_barrier((projected, grams))
    own = projected[0]
    received = [rotated(projected[shift], "chan", shift) for shift in range(1, parts)]

    late_weights, _ = lax.optimization_barrier((slice_weights, own))
    before = rotated(late_weights, "cuts", 1)
    after = rotated(late_weights, "cuts", -1)
    inverse, mover, rho, diagonal, columns, base = call(
        functools.partial(setup_kernel, len(grams), group),
        "setup",
        [
            ((count, rank, 3 * rank), bf16),
            ((count, rank, 6 * rank), bf16),
            lanes(count),
            ((count, rank), f32),
            ((rank, count), f32),
            state,
        ],
        order, *grams, slice_weights, aux, coup, dual_s, dual_c,
        scalars=1,
    )
    tall, target, gram = call(
        functools.partial(first_kernel, group),
        "first",
        [state, state, quads],
        order, before, after, base, mover, dual_s, dual_c, own, *received,
        scalars=1, unread=2,
    )
    side, before, after, inside, to_near, to_far = call(
        smooth_kernel,
        "smooth",
        [state, lanes(count), lanes(count), state, halo, halo],
        odd, order, aux, target, before, rho, after, diagonal, columns, own, *received,
        scalars=2,
    )
    polar_outs = [quads, ((rank // 2, 2 * rank), f32), quads]
    for inner in range(INNER):
        if inner == 0:
            mixed, partial, gram = call(
                first_polar_kernel,
                "polar",
                polar_outs,
                inside, delta, gram, *from_others(gram, "chan"),
                unread=1, microseconds=3,
            )
        else:
            mixed, partial, gram = call(
                later_polar_kernel,
                "polar",
                polar_outs,
                inside, delta, change, gram, cross, *crosses,
                unread=1,
            )
        if inner == INNER - 1:
            mixed_tall, evolving, _ = call(
                last_rows_kernel,
                "rows",
                [((count, 3 * rank, rows), bf16), state, state],
                mixed, change, forward, tall, known,
            )
            coup, delta = call(
                functools.partial(last_kernel, total),
                "last",
                [state, square],
                mixed_tall, *in_stages(partial, "cuts")[0],
            )
            continue
        near = swapped(to_near, "cuts", 0)
        far = swapped(to_far, "cuts", 1)
        aux, dual, known, cross = call(
            functools.partial(ahead_kernel, group),
            "ahead",
            [state, state, state, ((groups, rank, 2 * wide), f32)],
            odd, partial, inside, near, far, target, tall, side, rho, inverse,
            scalars=1, unread=1,
        )
        sums, firsts = in_stages(partial, "cuts", beside=cross)
        if inner < INNER - 2:
            sums, cross = lax.optimization_barrier((sums, cross))
        else:
            _, cross = lax.optimization_barrier((firsts, cross))
        crosses = from_others(cross, "chan")
        delta, change, forward = call(
            functools.partial(mixer_kernel, total),
            "mixer",
            [square, quads, quads],
            mixed, inverse, rho, *sums,
        )
        if inner < INNER - 2:
            tall, target, inside, to_near, to_far = call(
                rows_kernel,
                "rows",
                [state, state, state, halo, halo],
                odd, aux, before, rho, after, change, forward, tall, known, dual,
                scalars=1,
            )
    return (flip(evolving), flip(coup), delta)


def solution(mesh):
    return jax.shard_map(
        body,
        mesh=mesh,
        in_specs=(
            P("cuts", None, "chan"),
            P("cuts"),
            P("chan", None),
            P("cuts", None),
            P("cuts", "chan", None),
            P("cuts", "chan", None),
            P("cuts", "chan", None),
            P("cuts", "chan", None),
            P(),
        ),
        out_specs=(P("cuts", "chan", None), P("cuts", "chan", None), P()),
        check_vma=False,
    )
```

```python
import functools

import jax
import jax.numpy as jnp
from jax import lax
from jax.experimental import pallas as pl
from jax.experimental.pallas import tpu as pltpu
from jax.sharding import PartitionSpec as P

INNER = 3
SWEEPS = 4
POLAR = 8

smooth_weight = 1.0
eps_trace = 1e-06
f32 = jnp.float32
bf16 = jnp.bfloat16
NN = (((1,), (0,)), ((), ()))
NT = (((1,), (1,)), ((), ()))


def dot(left, right, dims=NN):
    return lax.dot_general(left, right, dims, preferred_element_type=f32)


def split(value):
    high = value.astype(bf16)
    low = (value - high.astype(f32)).astype(bf16)
    return high, low


def left_triple(value):
    high, low = split(value)
    return jnp.concatenate([high, high, low], axis=1)


def right_triple(value):
    high, low = split(value)
    return jnp.concatenate([high, low, high], axis=0)


def block_mask(rank, group):
    wide = rank * group
    rows = lax.div(lax.broadcasted_iota(jnp.int32, (wide, wide), 0), rank)
    cols = lax.div(lax.broadcasted_iota(jnp.int32, (wide, wide), 1), rank)
    return jnp.where(rows == cols, 1.0, 0.0).astype(bf16)


def wide_eye(rank, group):
    rows = lax.broadcasted_iota(jnp.int32, (rank, rank * group), 0)
    cols = lax.broadcasted_iota(jnp.int32, (rank, rank * group), 1)
    return jnp.where(rows == lax.rem(cols, rank), 1.0, 0.0).astype(f32)


def block_diagonal(value, mask, group, dims=NN):
    high, low = split(value)
    high = jnp.concatenate([high] * group, axis=0) * mask
    low = jnp.concatenate([low] * group, axis=0) * mask
    empty = jnp.zeros_like(high)
    one, other = ([high, low], [high, empty]) if dims == NN else ([high, high], [low, empty])
    return jnp.concatenate(
        [jnp.concatenate(one, axis=1), jnp.concatenate(other, axis=1)], axis=0
    )


def times_blocks(values, blocks, dims=NN):
    rank, wide = values[0].shape
    left = [jnp.concatenate(split(value), axis=1) for value in values]
    total = dot(jnp.concatenate(left, axis=0), blocks, dims)
    total = total[:, :wide] + total[:, wide:]
    return [total[at * rank : (at + 1) * rank] for at in range(len(values))]


def diagonal_blocks(value, rank, group):
    at = lax.div(lax.broadcasted_iota(jnp.int32, (rank, rank * group), 1), rank)
    total = value[:rank]
    for block in range(1, group):
        total = jnp.where(at == block, value[block * rank : (block + 1) * rank], total)
    return total


def from_left(left, values):
    wide = values[0].shape[1]
    total = dot(left_triple(left), right_triple(jnp.concatenate(values, axis=1)))
    return [total[:, at * wide : (at + 1) * wide] for at in range(len(values))]


def group_size(count, rank):
    group = max(1, 128 // rank)
    while count % group:
        group -= 1
    return group


def factor_kernel(factor_ref, gram_ref, again_ref):
    factor = factor_ref[...]
    gram_ref[...] = dot(factor, factor, NT)
    again_ref[...] = factor


def project_kernel(me_ref, data_ref, factor_ref, *refs):
    *outs, held, arrived = refs
    parts = len(outs)
    pairs, rows, _ = outs[0].shape
    count, all_rows, _ = data_ref.shape
    half = all_rows // 2
    copies = []
    for k in range(count):
        for at in range(2):
            place = pl.ds(at * half, half)
            copies.append(
                pltpu.make_async_copy(
                    data_ref.at[k, place, :], held.at[k, place, :], arrived.at[2 * k + at]
                )
            )
            copies[-1].start()
    factor = factor_ref[...]
    empty = jnp.zeros_like(factor)
    sides = [
        jnp.concatenate([factor, empty], axis=0),
        jnp.concatenate([empty, factor], axis=0),
    ]
    for pair in range(pairs):
        for copy in copies[4 * pair : 4 * pair + 4]:
            copy.wait()
        for part in reversed(range(parts)):
            start = pl.multiple_of(lax.rem(me_ref[0] + part, parts) * rows, 16)
            place = pl.ds(start, rows)
            outs[part][pair] = dot(held[2 * pair, place, :], sides[0], NT) + dot(
                held[2 * pair + 1, place, :], sides[1], NT
            )


def setup_kernel(grams, group, order_ref, *refs):
    gram_refs, refs = refs[:grams], refs[grams:]
    (own_ref, aux_ref, coupled_ref, dual_s_ref, dual_c_ref) = refs[:5]
    (inverse_ref, mover_ref, rho_ref, diagonal_ref, columns_ref, base_ref) = refs[5:]
    count, rank = own_ref.shape
    gram = gram_refs[0][...]
    for ref in gram_refs[1:]:
        gram = gram + ref[...]
    eye = wide_eye(rank, 1)
    diagonal = jnp.sum(gram * eye, axis=0, keepdims=True)
    diagonal_ref[...] = jnp.broadcast_to(diagonal, diagonal_ref.shape)
    weights = own_ref[...]
    columns = weights.T
    columns_ref[...] = columns
    rho = jnp.sum(weights * weights * diagonal, axis=1, keepdims=True) / rank
    rho_ref[...] = jnp.broadcast_to(rho, rho_ref.shape)

    edge = 34.0 / 32.0
    lead = 4.0 * edge**3 / (4.0 * edge**3 - 3.0 * edge)
    mask = block_mask(rank, group)
    wide = wide_eye(rank, group)
    starts = range(0, count, group)
    systems = []
    for first in starts:
        scaled = []
        for k in range(first, first + group):
            unit = 1.0 / (34.0 * rho[k : k + 1, :])
            column = columns[:, k : k + 1]
            scaled.append(column * gram * weights[k : k + 1, :] * unit + (2.0 / 34.0) * eye)
        systems.append(jnp.concatenate(scaled, axis=1))
    inverses, rests = [], []
    for system in systems:
        rest = wide - system
        blocks = block_diagonal(rest, mask, group)
        (square,) = times_blocks([rest], blocks)
        (cube,) = times_blocks([square], blocks)
        inverses.append(wide + lead * (rest + square))
        rests.append(lead * cube - (lead - 1.0) * rest)
    for step in range(4):
        for at in range(len(systems)):
            blocks = block_diagonal(rests[at], mask, group)
            more, rests[at] = times_blocks([inverses[at], rests[at]], blocks)
            inverses[at] = inverses[at] + more
    for step in range(2):
        for at in range(len(systems)):
            (product,) = times_blocks([inverses[at]], block_diagonal(systems[at], mask, group))
            blocks = block_diagonal(wide - product, mask, group)
            (more,) = times_blocks([inverses[at]], blocks)
            inverses[at] = inverses[at] + more
    for k in range(count):
        place = (k % group) * rank
        unit = 1.0 / (34.0 * rho[k : k + 1, :])
        inverse = inverses[k // group][:, place : place + rank] * unit
        inverse_ref[k] = left_triple(inverse)
        base_ref[k] = dot(
            inverse_ref[k],
            right_triple(
                rho[k : k + 1, :] * (aux_ref[k] - dual_s_ref[k] + coupled_ref[k] - dual_c_ref[k])
            ),
        )
        both = jnp.concatenate([inverse * weights[k : k + 1, :]] * 2, axis=1)
        side = lax.div(lax.broadcasted_iota(jnp.int32, both.shape, 1), rank)
        both = jnp.where(side == lax.rem(order_ref[k], 2), both, 0.0)
        high, low = split(both)
        pair, place = stored_place(order_ref, k, count, rank)
        mover_ref[pair, place, :] = jnp.concatenate([high, high, low], axis=1)


def cross_blocks(lefts, rights, rank):
    group = len(lefts)
    wide = group * rank
    left = jnp.concatenate(split(jnp.concatenate(lefts, axis=0)), axis=0)
    right = left
    if rights is not lefts:
        right = jnp.concatenate(split(jnp.concatenate(rights, axis=0)), axis=0)
    total = dot(left, right, NT)
    total = total[:wide, :wide] + total[:wide, wide:] + total[wide:, :wide]
    return diagonal_blocks(total, rank, group)


def summed(refs, at):
    total = refs[0][at]
    for ref in refs[1:]:
        total = total + ref[at]
    return total


def stored_place(order_ref, k, count, rank):
    stored = lax.rem(order_ref[k], count)
    return lax.div(stored, 2), pl.ds(pl.multiple_of(lax.rem(stored, 2) * rank, rank), rank)


def first_kernel(group, order_ref, *refs):
    base_ref, mover_ref, dual_s_ref, dual_c_ref = refs[2:6]
    *projected_refs, tall_ref, target_ref, gram_ref, moved = refs[6:]
    count, rank, rows = base_ref.shape
    for pair in range(count // 2):
        high, low = split(summed(projected_refs, pair))
        moved[pair] = dot(mover_ref[pair], jnp.concatenate([high, low, high], axis=1), NT)
    talls = []
    for k in range(count):
        pair, place = stored_place(order_ref, k, count, rank)
        evolving = base_ref[k] + moved[pair, place, :]
        target_ref[k] = evolving + dual_s_ref[k]
        tall = evolving + dual_c_ref[k]
        tall_ref[k] = tall
        talls.append(tall)
        if len(talls) == group:
            gram_ref[k // group] = cross_blocks(talls, talls, rank)
            talls = []


def smooth(odd, now, targets, rho, inside_ref, near_ref, far_ref):
    count = len(targets)
    width = SWEEPS
    share = {j: 2.0 * smooth_weight / (rho[j] + 4.0 * smooth_weight) for j in rho}
    pull = {j: (rho[j] / (rho[j] + 4.0 * smooth_weight)) * targets[j] for j in range(count)}
    now = {j: now[j] for j in range(count)}
    for sweep in range(width):
        later = {}
        for j in range(-sweep - 1, count + sweep + 1):
            beside = [now[i] for i in (j - 1, j + 1) if i in now]
            total = beside[0] if len(beside) == 1 else beside[0] + beside[1]
            total = share[j] * total
            later[j] = total + pull[j] if j in pull else total
        now = later
    for j in range(count):
        inside_ref[j] = now[j]
    for j in range(width):
        near_ref[j] = jnp.where(odd == 1, now[j - width], now[count + j])
        far_ref[j] = jnp.where(odd == 1, now[count + j], now[j - width])


def all_rho(before_ref, rho_ref, after_ref):
    count = rho_ref.shape[0]
    rho = {j: rho_ref[j : j + 1, 0:1] for j in range(count)}
    for j in range(SWEEPS):
        rho[j - SWEEPS] = before_ref[count - SWEEPS + j : count - SWEEPS + j + 1, 0:1]
        rho[count + j] = after_ref[j : j + 1, 0:1]
    return rho


def smooth_kernel(
    odd_ref, order_ref, aux_ref, target_ref, before_ref, rho_ref, after_ref, diagonal_ref,
    columns_ref, *refs
):
    *projected_refs, side_ref, past_ref, next_ref, inside_ref, near_ref, far_ref, turned = refs
    count, rank, rows = aux_ref.shape
    for source, place in ((before_ref, past_ref), (after_ref, next_ref)):
        weights = source[...]
        rho = jnp.sum(weights * weights * diagonal_ref[...], axis=1, keepdims=True) / rank
        place[...] = jnp.broadcast_to(rho, place.shape)
    rho = all_rho(past_ref, rho_ref, next_ref)
    slices = range(count)
    smooth(
        odd_ref[0], [aux_ref[k] for k in slices], [target_ref[k] for k in slices], rho,
        inside_ref, near_ref, far_ref,
    )
    for pair in range(count // 2):
        turned[pair] = summed(projected_refs, pair).T
    for k in slices:
        pair, place = stored_place(order_ref, k, count, rank)
        side_ref[k] = columns_ref[:, k : k + 1] * turned[pair, place, :]


def polar(grams, delta):
    rank, wide = grams[0].shape
    group = wide // rank
    mask = block_mask(rank, group)
    eye = wide_eye(rank, group)
    delta_blocks = block_diagonal(jnp.concatenate([delta] * group, axis=1), mask, group, NT)
    currents, roots, scales = [], [], []
    for left in from_left(delta, grams):
        (normal,) = times_blocks([left], delta_blocks, NT)
        line = jnp.broadcast_to(jnp.sum(normal * eye, axis=0, keepdims=True), (16, wide))
        high, low = split(line)
        rest = (line - high.astype(f32) - low.astype(f32)).astype(bf16)
        line = dot(high, mask) + dot(low, mask) + dot(rest, mask)
        trace = line[0:1] + eps_trace
        currents.append(normal / trace)
        scales.append(1.0 / jnp.sqrt(trace))
    for step in range(POLAR):
        for at in range(len(grams)):
            product = currents[at]
            blocks = block_diagonal(product, mask, group)
            if step == 0:
                roots.append(1.5 * eye - 0.5 * product)
                (square,) = times_blocks([product], blocks)
            elif step < POLAR - 1:
                square, more = times_blocks([product, roots[at]], blocks)
                roots[at] = 1.5 * roots[at] - 0.5 * more
            else:
                (more,) = times_blocks([roots[at]], blocks)
                roots[at] = 1.5 * roots[at] - 0.5 * more
            if step < POLAR - 1:
                half = 1.5 * product - 0.5 * square
                (more,) = times_blocks([half], blocks)
                currents[at] = 1.5 * half - 0.5 * more
    return roots, scales


def mix(roots, scales, grams, delta, mixed_ref, partial_ref):
    rank, wide = roots[0].shape
    group = wide // rank
    mask = block_mask(rank, group)
    delta_blocks = block_diagonal(jnp.concatenate([delta] * group, axis=1), mask, group)
    left, right = [], []
    for at in range(len(roots)):
        (mixed,) = times_blocks([roots[at]], delta_blocks)
        mixed = mixed * scales[at]
        mixed_ref[at] = mixed
        high, low = split(mixed)
        left += [high, high, low]
        high, low = split(grams[at])
        right += [high, low, high]
    partial = dot(jnp.concatenate(left, axis=1), jnp.concatenate(right, axis=1), NT)
    half = rank // 2
    partial_ref[...] = jnp.concatenate([partial[:half], partial[half:]], axis=1)


def first_polar_kernel(after_ref, delta_ref, *refs):
    *gram_refs, mixed_ref, partial_ref, gram_ref = refs
    grams = [summed(gram_refs, at) for at in range(gram_ref.shape[0])]
    for at in range(len(grams)):
        gram_ref[at] = grams[at]
    delta = delta_ref[...]
    roots, scales = polar(grams, delta)
    mix(roots, scales, grams, delta, mixed_ref, partial_ref)


def later_polar_kernel(last, after_ref, delta_ref, change_ref, old_ref, *refs):
    if last:
        *cross_refs, mixed_ref, partial_ref = refs
    else:
        *cross_refs, mixed_ref, partial_ref, gram_ref = refs
    groups, rank, wide = old_ref.shape
    group = wide // rank
    mask = block_mask(rank, group)
    grams = []
    for at in range(groups):
        cross = summed(cross_refs, at)
        change = change_ref[at]
        (onward,) = times_blocks([change], block_diagonal(old_ref[at], mask, group))
        onward = cross[:, :wide] + 0.5 * onward
        (one,) = times_blocks([onward], block_diagonal(change, mask, group, NT), NT)
        (other,) = times_blocks([change], block_diagonal(onward, mask, group, NT), NT)
        grams.append(cross[:, wide:] + one + other)
        if not last:
            gram_ref[at] = grams[at]
    delta = delta_ref[...]
    roots, scales = polar(grams, delta)
    mix(roots, scales, grams, delta, mixed_ref, partial_ref)


def ahead_kernel(
    group, odd_ref, after_ref, inside_ref, near_ref, far_ref, target_ref, tall_ref, side_ref, rho_ref,
    inverse_ref, known_ref, cross_ref, *kept
):
    count, rank, _ = inside_ref.shape
    width = SWEEPS
    knowns, talls = [], []
    for k in range(count):
        aux = inside_ref[k]
        if k < width:
            aux = aux + jnp.where(odd_ref[0] == 1, near_ref[k], far_ref[k])
        if k >= count - width:
            at = k - count + width
            aux = aux + jnp.where(odd_ref[0] == 1, far_ref[at], near_ref[at])
        target, tall = target_ref[k], tall_ref[k]
        if kept:
            aux_ref, dual_ref = kept
            aux_ref[k] = aux
            dual_ref[k] = target - aux
        known = dot(
            inverse_ref[k],
            right_triple(side_ref[k] + rho_ref[k : k + 1, 0:1] * (2.0 * aux - target - tall)),
        )
        known_ref[k] = known
        talls.append(tall)
        knowns.append(known + tall)
        if len(talls) == group:
            cross_ref[k // group] = jnp.concatenate(
                [cross_blocks(knowns, talls, rank), cross_blocks(knowns, knowns, rank)], axis=1
            )
            knowns, talls = [], []


def add_kernel(unread, *refs):
    *term_refs, total_ref = refs[unread:]
    total = term_refs[0][...]
    for ref in term_refs[1:]:
        total = total + ref[...]
    total_ref[...] = total


def new_delta(sum_refs, total, rank):
    packed = sum_refs[0][...]
    for ref in sum_refs[1:]:
        packed = packed + ref[...]
    packed = packed / total
    return jnp.concatenate([packed[:, :rank], packed[:, rank:]], axis=0)


def mixer_kernel(total, mixed_ref, inverse_ref, rho_ref, *refs):
    *sum_refs, delta_ref, change_ref, forward_ref = refs
    groups, rank, wide = mixed_ref.shape
    group = wide // rank
    delta = new_delta(sum_refs, total, rank)
    delta_ref[...] = delta
    mixers = from_left(delta.T, [mixed_ref[at] for at in range(groups)])
    place = lax.div(lax.broadcasted_iota(jnp.int32, (1, wide), 1), rank)
    for at in range(groups):
        mixer = mixers[at]
        slices = range(at * group, (at + 1) * group)
        inverses = jnp.concatenate([inverse_ref[k] for k in slices], axis=0)
        onward = diagonal_blocks(dot(inverses, right_triple(mixer)), rank, group)
        rho = rho_ref[at * group : at * group + 1, 0:1]
        for k in slices[1:]:
            rho = jnp.where(place == k - at * group, rho_ref[k : k + 1, 0:1], rho)
        forward = 2.0 * rho * onward
        forward_ref[at] = forward
        change_ref[at] = forward - mixer


def rows_kernel(odd_ref, aux_ref, before_ref, rho_ref, after_ref, *refs):
    (change_ref, forward_ref, tall_ref, known_ref, dual_ref) = refs[:5]
    (next_ref, target_ref, inside_ref, near_ref, far_ref) = refs[5:]
    targets = new_rows(change_ref, forward_ref, tall_ref, known_ref, next_ref)
    count = len(targets)
    for k in range(count):
        targets[k] = targets[k] + dual_ref[k]
        target_ref[k] = targets[k]
    rho = all_rho(before_ref, rho_ref, after_ref)
    smooth(
        odd_ref[0], [aux_ref[k] for k in range(count)], targets, rho,
        inside_ref, near_ref, far_ref,
    )


def last_rows_kernel(mixed_ref, change_ref, forward_ref, tall_ref, known_ref, *outs):
    mixed_tall_ref, evolving_ref, next_ref = outs
    evolvings = new_rows(change_ref, forward_ref, tall_ref, known_ref, next_ref)
    groups, rank, wide = mixed_ref.shape
    group = wide // rank
    for k in range(len(evolvings)):
        evolving_ref[k] = evolvings[k]
        place = (k % group) * rank
        mixed = left_triple(mixed_ref[k // group][:, place : place + rank])
        mixed_tall_ref[k] = right_triple(dot(mixed, right_triple(next_ref[k])))


def new_rows(change_ref, forward_ref, tall_ref, known_ref, next_ref):
    groups, rank, wide = change_ref.shape
    group = wide // rank
    evolvings = []
    for k in range(groups * group):
        lanes = slice((k % group) * rank, (k % group + 1) * rank)
        change, forward = change_ref[k // group][:, lanes], forward_ref[k // group][:, lanes]
        left = jnp.concatenate([left_triple(change), left_triple(forward)], axis=0)
        tall, known = tall_ref[k], known_ref[k]
        both = dot(left, right_triple(tall))
        next_ref[k] = known + tall + both[:rank]
        evolvings.append(known + both[rank:])
    return evolvings


def last_kernel(total, mixed_tall_ref, *refs):
    *sum_refs, coupled_ref, delta_ref = refs
    delta = new_delta(sum_refs, total, delta_ref.shape[0])
    delta_ref[...] = delta
    delta_left = left_triple(delta.T)
    for k in range(coupled_ref.shape[0]):
        coupled_ref[k] = dot(delta_left, mixed_tall_ref[k])


per_microsecond = 1_100_000_000


def call(
    kernel, name, outs, *args, scalars=0, unread=0, microseconds=0.3, limit=16, scratch=()
):
    flops = int(microseconds * per_microsecond)
    specs = [pl.BlockSpec(memory_space=pltpu.SMEM)] * scalars
    specs += [pl.BlockSpec(memory_space=pl.ANY)] * unread
    specs += [pl.BlockSpec(memory_space=pltpu.VMEM)] * (len(args) - len(specs))
    shapes = [jax.ShapeDtypeStruct(shape, dtype) for shape, dtype in outs]
    moved = sum(arg.size * arg.dtype.itemsize for arg in args)
    moved += sum(shape.size * shape.dtype.itemsize for shape in shapes)
    return pl.pallas_call(
        kernel,
        out_shape=shapes,
        in_specs=specs,
        out_specs=[pl.BlockSpec(memory_space=pltpu.VMEM)] * len(shapes),
        scratch_shapes=list(scratch),
        compiler_params=pltpu.CompilerParams(vmem_limit_bytes=limit * 1024 * 1024),
        cost_estimate=pl.CostEstimate(flops=flops, bytes_accessed=moved, transcendentals=0),
        name=name,
    )(*args)


def rotated(value, axis, shift):
    count = lax.axis_size(axis)
    return lax.ppermute(value, axis, [(i, (i + shift) % count) for i in range(count)])


def swapped(value, axis, first):
    count = lax.axis_size(axis)
    pairs = [((i + first) % count, (i + first + 1) % count) for i in range(0, count, 2)]
    return lax.ppermute(value, axis, pairs + [(b, a) for a, b in pairs])


def from_others(value, axis):
    return [rotated(value, axis, shift) for shift in range(1, lax.axis_size(axis))]


def stage_sizes(count):
    sizes = []
    while count > 1:
        sizes.append(next(size for size in (4, 2, 3, 5, 7, count) if count % size == 0))
        count //= sizes[-1]
    return sizes


def in_stages(value, axis, beside=None):
    count = lax.axis_size(axis)
    stride = 1
    terms, firsts = [value], []
    for size in stage_sizes(count):
        value = terms[0]
        if len(terms) > 1:
            unread = [] if beside is None else [beside]
            (value,) = call(
                functools.partial(add_kernel, len(unread)),
                "add",
                [(value.shape, f32)],
                *unread, *terms,
                unread=len(unread),
            )
        terms = [value]
        for shift in range(1, size):
            moves = []
            for i in range(count):
                digit = (i // stride) % size
                other = digit ^ shift if size in (2, 4) else (digit + shift) % size
                moves.append((i, i + (other - digit) * stride))
            terms.append(lax.ppermute(value, axis, moves))
        stride *= size
        firsts = firsts or terms
    return terms, firsts


def body(
    data, order, chan_factor, slice_weights, smooth_aux, coupled, smooth_dual, coupling_dual, delta
):
    count, all_rows, channels = data.shape
    rank = chan_factor.shape[1]
    rows = smooth_aux.shape[1]
    parts = lax.axis_size("chan")
    total = count * lax.axis_size("cuts")
    group = group_size(count, rank)
    groups = count // group
    wide = group * rank
    flip = lambda value: jnp.swapaxes(value, 1, 2)
    aux, coup, dual_s, dual_c = map(flip, (smooth_aux, coupled, smooth_dual, coupling_dual))
    factor = chan_factor.T
    state = ((count, rank, rows), f32)
    quads = ((groups, rank, wide), f32)
    square = ((rank, rank), f32)
    halo = ((SWEEPS, rank, rows), f32)
    lanes = lambda height: ((height, 128), f32)
    scale = ((groups, 8, wide), f32)

    me = lax.axis_index("chan").astype(jnp.int32).reshape(1)
    odd = lax.rem(lax.axis_index("cuts"), 2).astype(jnp.int32).reshape(1)
    gram_part, factor = call(
        factor_kernel, "factor", [square, (factor.shape, factor.dtype)], factor
    )
    grams = [gram_part] + from_others(gram_part, "chan")
    projected = call(
        project_kernel,
        "project",
        [((count // 2, rows, 2 * rank), f32)] * parts,
        me, data, factor,
        scalars=1, unread=1, microseconds=2, limit=52,
        scratch=[
            pltpu.VMEM((count, all_rows, channels), data.dtype),
            pltpu.SemaphoreType.DMA((2 * count,)),
        ],
    )
    projected, grams = lax.optimization_barrier((projected, grams))
    own = projected[0]
    received = [rotated(projected[shift], "chan", shift) for shift in range(1, parts)]

    late_weights, _ = lax.optimization_barrier((slice_weights, own))
    before = rotated(late_weights, "cuts", 1)
    after = rotated(late_weights, "cuts", -1)
    inverse, mover, rho, diagonal, columns, base = call(
        functools.partial(setup_kernel, len(grams), group),
        "setup",
        [
            ((count, rank, 3 * rank), bf16),
            ((count // 2, 2 * rank, 6 * rank), bf16),
            lanes(count),
            ((count, rank), f32),
            ((rank, count), f32),
            state,
        ],
        order, *grams, slice_weights, aux, coup, dual_s, dual_c,
        scalars=1,
    )
    tall, target, gram = call(
        functools.partial(first_kernel, group),
        "first",
        [state, state, quads],
        order, before, after, base, mover, dual_s, dual_c, own, *received,
        scalars=1, unread=2,
        scratch=[pltpu.VMEM((count // 2, 2 * rank, rows), f32)],
    )
    side, before, after, inside, to_near, to_far = call(
        smooth_kernel,
        "smooth",
        [state, lanes(count), lanes(count), state, halo, halo],
        odd, order, aux, target, before, rho, after, diagonal, columns, own, *received,
        scalars=2,
        scratch=[pltpu.VMEM((count // 2, 2 * rank, rows), f32)],
    )
    polar_outs = [quads, ((rank // 2, 2 * rank), f32), quads]
    for inner in range(INNER):
        if inner == 0:
            mixed, partial, gram = call(
                first_polar_kernel,
                "polar",
                polar_outs,
                inside, delta, gram, *from_others(gram, "chan"),
                unread=1, microseconds=3,
            )
        else:
            last = inner == INNER - 1
            mixed, partial, *gram = call(
                functools.partial(later_polar_kernel, last),
                "polar",
                polar_outs[:2] if last else polar_outs,
                inside, delta, change, old, cross, *crosses,
                unread=1,
            )
            gram = gram[0] if gram else None
        if inner == INNER - 1:
            mixed_tall, evolving = call(
                last_rows_kernel,
                "rows",
                [((count, 3 * rank, rows), bf16), state],
                mixed, change, forward, tall, known,
                scratch=[pltpu.VMEM(state[0], f32)],
            )
            coup, delta = call(
                functools.partial(last_kernel, total),
                "last",
                [state, square],
                mixed_tall, *in_stages(partial, "cuts")[0],
            )
            continue
        near = swapped(to_near, "cuts", 0)
        far = swapped(to_far, "cuts", 1)
        known, cross, *kept = call(
            functools.partial(ahead_kernel, group),
            "ahead",
            [state, ((groups, rank, 2 * wide), f32)] + [state] * (2 if inner < INNER - 2 else 0),
            odd, partial, inside, near, far, target, tall, side, rho, inverse,
            scalars=1, unread=1,
        )
        sums, firsts = in_stages(partial, "cuts", beside=cross)
        _, cross = lax.optimization_barrier((firsts, cross))
        crosses = from_others(cross, "chan")
        old = gram
        delta, change, forward = call(
            functools.partial(mixer_kernel, total),
            "mixer",
            [square, quads, quads],
            mixed, inverse, rho, *sums,
        )
        if inner < INNER - 2:
            tall, target, inside, to_near, to_far = call(
                rows_kernel,
                "rows",
                [state, state, state, halo, halo],
                odd, kept[0], before, rho, after, change, forward, tall, known, kept[1],
                scalars=1,
            )
    return (flip(evolving), flip(coup), delta)


def solution(mesh):
    return jax.shard_map(
        body,
        mesh=mesh,
        in_specs=(
            P("cuts", None, "chan"),
            P("cuts"),
            P("chan", None),
            P("cuts", None),
            P("cuts", "chan", None),
            P("cuts", "chan", None),
            P("cuts", "chan", None),
            P("cuts", "chan", None),
            P(),
        ),
        out_specs=(P("cuts", "chan", None), P("cuts", "chan", None), P()),
        check_vma=False,
    )
```

```python
import functools

import jax
import jax.numpy as jnp
from jax import lax
from jax.experimental import pallas as pl
from jax.experimental.pallas import tpu as pltpu
from jax.sharding import PartitionSpec as P

INNER = 3
SWEEPS = 4
POLAR = 8

smooth_weight = 1.0
eps_trace = 1e-06
f32 = jnp.float32
bf16 = jnp.bfloat16
NN = (((1,), (0,)), ((), ()))
NT = (((1,), (1,)), ((), ()))


def dot(left, right, dims=NN):
    return lax.dot_general(left, right, dims, preferred_element_type=f32)


def split(value):
    high = value.astype(bf16)
    low = (value - high.astype(f32)).astype(bf16)
    return high, low


def left_triple(value):
    high, low = split(value)
    return jnp.concatenate([high, high, low], axis=1)


def right_triple(value):
    high, low = split(value)
    return jnp.concatenate([high, low, high], axis=0)


def block_mask(rank, group):
    wide = rank * group
    rows = lax.div(lax.broadcasted_iota(jnp.int32, (wide, wide), 0), rank)
    cols = lax.div(lax.broadcasted_iota(jnp.int32, (wide, wide), 1), rank)
    return jnp.where(rows == cols, 1.0, 0.0).astype(bf16)


def wide_eye(rank, group):
    rows = lax.broadcasted_iota(jnp.int32, (rank, rank * group), 0)
    cols = lax.broadcasted_iota(jnp.int32, (rank, rank * group), 1)
    return jnp.where(rows == lax.rem(cols, rank), 1.0, 0.0).astype(f32)


def block_diagonal(value, mask, group, dims=NN):
    high, low = split(value)
    high = jnp.concatenate([high] * group, axis=0) * mask
    low = jnp.concatenate([low] * group, axis=0) * mask
    empty = jnp.zeros_like(high)
    one, other = ([high, low], [high, empty]) if dims == NN else ([high, high], [low, empty])
    return jnp.concatenate(
        [jnp.concatenate(one, axis=1), jnp.concatenate(other, axis=1)], axis=0
    )


def times_blocks(values, blocks, dims=NN):
    rank, wide = values[0].shape
    left = [jnp.concatenate(split(value), axis=1) for value in values]
    total = dot(jnp.concatenate(left, axis=0), blocks, dims)
    total = total[:, :wide] + total[:, wide:]
    return [total[at * rank : (at + 1) * rank] for at in range(len(values))]


def diagonal_blocks(value, rank, group):
    at = lax.div(lax.broadcasted_iota(jnp.int32, (rank, rank * group), 1), rank)
    total = value[:rank]
    for block in range(1, group):
        total = jnp.where(at == block, value[block * rank : (block + 1) * rank], total)
    return total


def from_left(left, values):
    wide = values[0].shape[1]
    total = dot(left_triple(left), right_triple(jnp.concatenate(values, axis=1)))
    return [total[:, at * wide : (at + 1) * wide] for at in range(len(values))]


def group_size(count, rank):
    group = max(1, 128 // rank)
    while count % group:
        group -= 1
    return group


def project_kernel(first, pairs, rows, lead, me_ref, data_ref, factor_ref, *refs):
    *outs, held, arrived = refs
    half = data_ref.shape[1] // 2
    copies = []
    for k in range(2 * pairs):
        for at in range(2):
            place = pl.ds(at * half, half)
            copies.append(
                pltpu.make_async_copy(
                    data_ref.at[first + k, place, :], held.at[k, place, :], arrived.at[2 * k + at]
                )
            )
            copies[-1].start()
    factor = factor_ref[...]
    rank = factor.shape[0]
    if lead:
        *outs, again_ref = outs
        again_ref[...] = factor
        gram = dot(factor, factor, NT)
        for out in outs:
            out[pairs * rows :, :] = jnp.concatenate([gram[: rank // 2], gram[rank // 2 :]], axis=1)
    parts = len(outs)
    empty = jnp.zeros_like(factor)
    sides = [
        jnp.concatenate([factor, empty], axis=0),
        jnp.concatenate([empty, factor], axis=0),
    ]
    for pair in range(pairs):
        for copy in copies[4 * pair : 4 * pair + 4]:
            copy.wait()
        for part in reversed(range(parts)):
            start = pl.multiple_of(lax.rem(me_ref[0] + part, parts) * rows, 16)
            place = pl.ds(start, rows)
            outs[part][pair * rows : (pair + 1) * rows, :] = dot(
                held[2 * pair, place, :], sides[0], NT
            ) + dot(held[2 * pair + 1, place, :], sides[1], NT)


def setup_kernel(parts, first, group, order_ref, *refs):
    lead_refs, refs = refs[:parts], refs[parts:]
    (own_ref, aux_ref, coupled_ref, dual_s_ref, dual_c_ref) = refs[:5]
    (inverse_ref, mover_ref, rho_ref, diagonal_ref, columns_ref, base_ref) = refs[5:]
    count, rank = own_ref.shape
    gram = summed(lead_refs, slice(first, None))
    gram = jnp.concatenate([gram[:, :rank], gram[:, rank:]], axis=0)
    eye = wide_eye(rank, 1)
    diagonal = jnp.sum(gram * eye, axis=0, keepdims=True)
    diagonal_ref[...] = jnp.broadcast_to(diagonal, diagonal_ref.shape)
    weights = own_ref[...]
    columns = weights.T
    columns_ref[...] = columns
    rho = jnp.sum(weights * weights * diagonal, axis=1, keepdims=True) / rank
    rho_ref[...] = jnp.broadcast_to(rho, rho_ref.shape)

    edge = 34.0 / 32.0
    lead = 4.0 * edge**3 / (4.0 * edge**3 - 3.0 * edge)
    mask = block_mask(rank, group)
    wide = wide_eye(rank, group)
    starts = range(0, count, group)
    systems = []
    for first in starts:
        scaled = []
        for k in range(first, first + group):
            unit = 1.0 / (34.0 * rho[k : k + 1, :])
            column = columns[:, k : k + 1]
            scaled.append(column * gram * weights[k : k + 1, :] * unit + (2.0 / 34.0) * eye)
        systems.append(jnp.concatenate(scaled, axis=1))
    inverses, rests = [], []
    for system in systems:
        rest = wide - system
        blocks = block_diagonal(rest, mask, group)
        (square,) = times_blocks([rest], blocks)
        (cube,) = times_blocks([square], blocks)
        inverses.append(wide + lead * (rest + square))
        rests.append(lead * cube - (lead - 1.0) * rest)
    for step in range(4):
        for at in range(len(systems)):
            blocks = block_diagonal(rests[at], mask, group)
            more, rests[at] = times_blocks([inverses[at], rests[at]], blocks)
            inverses[at] = inverses[at] + more
    for step in range(2):
        for at in range(len(systems)):
            (product,) = times_blocks([inverses[at]], block_diagonal(systems[at], mask, group))
            blocks = block_diagonal(wide - product, mask, group)
            (more,) = times_blocks([inverses[at]], blocks)
            inverses[at] = inverses[at] + more
    for k in range(count):
        place = (k % group) * rank
        unit = 1.0 / (34.0 * rho[k : k + 1, :])
        inverse = inverses[k // group][:, place : place + rank] * unit
        inverse_ref[k] = left_triple(inverse)
        base_ref[k] = dot(
            inverse_ref[k],
            right_triple(
                rho[k : k + 1, :] * (aux_ref[k] - dual_s_ref[k] + coupled_ref[k] - dual_c_ref[k])
            ),
        )
        both = jnp.concatenate([inverse * weights[k : k + 1, :]] * 2, axis=1)
        side = lax.div(lax.broadcasted_iota(jnp.int32, both.shape, 1), rank)
        both = jnp.where(side == lax.rem(order_ref[k], 2), both, 0.0)
        high, low = split(both)
        pair, place = stored_place(order_ref, k, count, rank)
        mover_ref[pair, place, :] = jnp.concatenate([high, high, low], axis=1)


def cross_blocks(lefts, rights, rank):
    group = len(lefts)
    wide = group * rank
    left = jnp.concatenate(split(jnp.concatenate(lefts, axis=0)), axis=0)
    right = left
    if rights is not lefts:
        right = jnp.concatenate(split(jnp.concatenate(rights, axis=0)), axis=0)
    total = dot(left, right, NT)
    total = total[:wide, :wide] + total[:wide, wide:] + total[wide:, :wide]
    return diagonal_blocks(total, rank, group)


def summed(refs, at):
    total = refs[0][at]
    for ref in refs[1:]:
        total = total + ref[at]
    return total


def stored_place(order_ref, k, count, rank):
    stored = lax.rem(order_ref[k], count)
    return lax.div(stored, 2), pl.ds(pl.multiple_of(lax.rem(stored, 2) * rank, rank), rank)


def move(mover, projected):
    high, low = split(projected)
    return dot(mover, jnp.concatenate([high, low, high], axis=1), NT)


def move_kernel(mover_ref, *refs):
    *projected_refs, moved_ref, turned_ref = refs
    rows = moved_ref.shape[2]
    for pair in range(moved_ref.shape[0]):
        projected = summed(projected_refs, slice(pair * rows, (pair + 1) * rows))
        moved_ref[pair] = move(mover_ref[pair], projected)
        turned_ref[pair] = projected.T


def first_kernel(group, order_ref, *refs):
    base_ref, mover_ref, dual_s_ref, dual_c_ref, early_ref = refs[2:7]
    *projected_refs, tall_ref, target_ref, gram_ref, moved = refs[7:]
    count, rank, rows = base_ref.shape
    early = early_ref.shape[0]
    for pair in range(early):
        moved[pair] = early_ref[pair]
    for pair in range(early, count // 2):
        place = slice((pair - early) * rows, (pair - early + 1) * rows)
        moved[pair] = move(mover_ref[pair], summed(projected_refs, place))
    talls = []
    for k in range(count):
        pair, place = stored_place(order_ref, k, count, rank)
        evolving = base_ref[k] + moved[pair, place, :]
        target_ref[k] = evolving + dual_s_ref[k]
        tall = evolving + dual_c_ref[k]
        tall_ref[k] = tall
        talls.append(tall)
        if len(talls) == group:
            gram_ref[k // group] = cross_blocks(talls, talls, rank)
            talls = []


def smooth(odd, now, targets, rho, inside_ref, near_ref, far_ref):
    count = len(targets)
    width = SWEEPS
    share = {j: 2.0 * smooth_weight / (rho[j] + 4.0 * smooth_weight) for j in rho}
    pull = {j: (rho[j] / (rho[j] + 4.0 * smooth_weight)) * targets[j] for j in range(count)}
    now = {j: now[j] for j in range(count)}
    for sweep in range(width):
        later = {}
        for j in range(-sweep - 1, count + sweep + 1):
            beside = [now[i] for i in (j - 1, j + 1) if i in now]
            total = beside[0] if len(beside) == 1 else beside[0] + beside[1]
            total = share[j] * total
            later[j] = total + pull[j] if j in pull else total
        now = later
    for j in range(count):
        inside_ref[j] = now[j]
    for j in range(width):
        near_ref[j] = jnp.where(odd == 1, now[j - width], now[count + j])
        far_ref[j] = jnp.where(odd == 1, now[count + j], now[j - width])


def all_rho(before_ref, rho_ref, after_ref):
    count = rho_ref.shape[0]
    rho = {j: rho_ref[j : j + 1, 0:1] for j in range(count)}
    for j in range(SWEEPS):
        rho[j - SWEEPS] = before_ref[count - SWEEPS + j : count - SWEEPS + j + 1, 0:1]
        rho[count + j] = after_ref[j : j + 1, 0:1]
    return rho


def smooth_kernel(
    odd_ref, order_ref, aux_ref, target_ref, before_ref, rho_ref, after_ref, diagonal_ref,
    columns_ref, early_ref, *refs
):
    *projected_refs, side_ref, past_ref, next_ref, inside_ref, near_ref, far_ref, turned = refs
    count, rank, rows = aux_ref.shape
    for source, place in ((before_ref, past_ref), (after_ref, next_ref)):
        weights = source[...]
        rho = jnp.sum(weights * weights * diagonal_ref[...], axis=1, keepdims=True) / rank
        place[...] = jnp.broadcast_to(rho, place.shape)
    rho = all_rho(past_ref, rho_ref, next_ref)
    slices = range(count)
    smooth(
        odd_ref[0], [aux_ref[k] for k in slices], [target_ref[k] for k in slices], rho,
        inside_ref, near_ref, far_ref,
    )
    early = early_ref.shape[0]
    for pair in range(early):
        turned[pair] = early_ref[pair]
    for pair in range(early, count // 2):
        place = slice((pair - early) * rows, (pair - early + 1) * rows)
        turned[pair] = summed(projected_refs, place).T
    for k in slices:
        pair, place = stored_place(order_ref, k, count, rank)
        side_ref[k] = columns_ref[:, k : k + 1] * turned[pair, place, :]


def polar(grams, delta):
    rank, wide = grams[0].shape
    group = wide // rank
    mask = block_mask(rank, group)
    eye = wide_eye(rank, group)
    delta_wide = jnp.concatenate([delta] * group, axis=1)
    delta_blocks = block_diagonal(delta_wide, mask, group, NT)
    (across,) = from_left(delta.T, [delta_wide])
    traces = []
    for gram in grams:
        line = jnp.broadcast_to(jnp.sum(across * gram, axis=0, keepdims=True), (16, wide))
        high, low = split(line)
        rest = (line - high.astype(f32) - low.astype(f32)).astype(bf16)
        line = dot(high, mask) + dot(low, mask) + dot(rest, mask)
        traces.append(line[0:1] + eps_trace)
    rights = [times_blocks([gram], delta_blocks, NT)[0] for gram in grams]
    normals = from_left(delta, rights)
    currents = [normal / trace for normal, trace in zip(normals, traces)]
    scales = [1.0 / jnp.sqrt(trace) for trace in traces]
    roots = []
    for step in range(POLAR):
        for at in range(len(grams)):
            product = currents[at]
            blocks = block_diagonal(product, mask, group)
            if step == 0:
                roots.append(1.5 * eye - 0.5 * product)
                (square,) = times_blocks([product], blocks)
            elif step < POLAR - 1:
                square, more = times_blocks([product, roots[at]], blocks)
                roots[at] = 1.5 * roots[at] - 0.5 * more
            else:
                (more,) = times_blocks([roots[at]], blocks)
                roots[at] = 1.5 * roots[at] - 0.5 * more
            if step < POLAR - 1:
                half = 1.5 * product - 0.5 * square
                (more,) = times_blocks([half], blocks)
                currents[at] = 1.5 * half - 0.5 * more
    return roots, scales, rights


def mix(roots, scales, rights, delta, mixed_ref, partial_ref):
    rank, wide = roots[0].shape
    group = wide // rank
    mask = block_mask(rank, group)
    delta_blocks = block_diagonal(jnp.concatenate([delta] * group, axis=1), mask, group)
    left, right = [], []
    for at in range(len(roots)):
        high, low = split(roots[at] * scales[at])
        left += [high, high, low]
        high, low = split(rights[at])
        right += [high, low, high]
    partial = dot(jnp.concatenate(left, axis=1), jnp.concatenate(right, axis=1), NT)
    for at in range(len(roots)):
        (mixed,) = times_blocks([roots[at]], delta_blocks)
        mixed_ref[at] = mixed * scales[at]
    half = rank // 2
    partial_ref[...] = jnp.concatenate([partial[:half], partial[half:]], axis=1)


def first_polar_kernel(after_ref, delta_ref, *refs):
    *gram_refs, mixed_ref, partial_ref, gram_ref = refs
    grams = [summed(gram_refs, at) for at in range(gram_ref.shape[0])]
    for at in range(len(grams)):
        gram_ref[at] = grams[at]
    delta = delta_ref[...]
    mix(*polar(grams, delta), delta, mixed_ref, partial_ref)


def later_polar_kernel(last, after_ref, delta_ref, change_ref, old_ref, *refs):
    if last:
        *cross_refs, mixed_ref, partial_ref = refs
    else:
        *cross_refs, mixed_ref, partial_ref, gram_ref = refs
    groups, rank, wide = old_ref.shape
    group = wide // rank
    mask = block_mask(rank, group)
    grams = []
    for at in range(groups):
        cross = summed(cross_refs, at)
        change = change_ref[at]
        (onward,) = times_blocks([change], block_diagonal(old_ref[at], mask, group))
        onward = cross[:, :wide] + 0.5 * onward
        (one,) = times_blocks([onward], block_diagonal(change, mask, group, NT), NT)
        (other,) = times_blocks([change], block_diagonal(onward, mask, group, NT), NT)
        grams.append(cross[:, wide:] + one + other)
        if not last:
            gram_ref[at] = grams[at]
    delta = delta_ref[...]
    mix(*polar(grams, delta), delta, mixed_ref, partial_ref)


def ahead_kernel(
    group, odd_ref, after_ref, inside_ref, near_ref, far_ref, target_ref, tall_ref, side_ref, rho_ref,
    inverse_ref, known_ref, cross_ref, *kept
):
    count, rank, _ = inside_ref.shape
    width = SWEEPS
    knowns, talls = [], []
    for k in range(count):
        aux = inside_ref[k]
        if k < width:
            aux = aux + jnp.where(odd_ref[0] == 1, near_ref[k], far_ref[k])
        if k >= count - width:
            at = k - count + width
            aux = aux + jnp.where(odd_ref[0] == 1, far_ref[at], near_ref[at])
        target, tall = target_ref[k], tall_ref[k]
        if kept:
            aux_ref, dual_ref = kept
            aux_ref[k] = aux
            dual_ref[k] = target - aux
        known = dot(
            inverse_ref[k],
            right_triple(side_ref[k] + rho_ref[k : k + 1, 0:1] * (2.0 * aux - target - tall)),
        )
        known_ref[k] = known
        talls.append(tall)
        knowns.append(known + tall)
        if len(talls) == group:
            cross_ref[k // group] = jnp.concatenate(
                [cross_blocks(knowns, talls, rank), cross_blocks(knowns, knowns, rank)], axis=1
            )
            knowns, talls = [], []


def add_kernel(unread, *refs):
    *term_refs, total_ref = refs[unread:]
    total = term_refs[0][...]
    for ref in term_refs[1:]:
        total = total + ref[...]
    total_ref[...] = total


def new_delta(sum_refs, total, rank):
    packed = sum_refs[0][...]
    for ref in sum_refs[1:]:
        packed = packed + ref[...]
    packed = packed / total
    return jnp.concatenate([packed[:, :rank], packed[:, rank:]], axis=0)


def mixer_kernel(total, mixed_ref, inverse_ref, rho_ref, *refs):
    *sum_refs, delta_ref, change_ref, forward_ref = refs
    groups, rank, wide = mixed_ref.shape
    group = wide // rank
    delta = new_delta(sum_refs, total, rank)
    delta_ref[...] = delta
    mixers = from_left(delta.T, [mixed_ref[at] for at in range(groups)])
    place = lax.div(lax.broadcasted_iota(jnp.int32, (1, wide), 1), rank)
    for at in range(groups):
        mixer = mixers[at]
        slices = range(at * group, (at + 1) * group)
        inverses = jnp.concatenate([inverse_ref[k] for k in slices], axis=0)
        onward = diagonal_blocks(dot(inverses, right_triple(mixer)), rank, group)
        rho = rho_ref[at * group : at * group + 1, 0:1]
        for k in slices[1:]:
            rho = jnp.where(place == k - at * group, rho_ref[k : k + 1, 0:1], rho)
        forward = 2.0 * rho * onward
        forward_ref[at] = forward
        change_ref[at] = forward - mixer


def rows_kernel(odd_ref, aux_ref, before_ref, rho_ref, after_ref, *refs):
    (change_ref, forward_ref, tall_ref, known_ref, dual_ref) = refs[:5]
    (next_ref, target_ref, inside_ref, near_ref, far_ref) = refs[5:]
    targets = new_rows(change_ref, forward_ref, tall_ref, known_ref, next_ref)
    count = len(targets)
    for k in range(count):
        targets[k] = targets[k] + dual_ref[k]
        target_ref[k] = targets[k]
    rho = all_rho(before_ref, rho_ref, after_ref)
    smooth(
        odd_ref[0], [aux_ref[k] for k in range(count)], targets, rho,
        inside_ref, near_ref, far_ref,
    )


def last_rows_kernel(mixed_ref, change_ref, forward_ref, tall_ref, known_ref, *outs):
    mixed_tall_ref, evolving_ref, next_ref = outs
    evolvings = new_rows(change_ref, forward_ref, tall_ref, known_ref, next_ref)
    groups, rank, wide = mixed_ref.shape
    group = wide // rank
    for k in range(len(evolvings)):
        evolving_ref[k] = evolvings[k]
        place = (k % group) * rank
        mixed = left_triple(mixed_ref[k // group][:, place : place + rank])
        mixed_tall_ref[k] = right_triple(dot(mixed, right_triple(next_ref[k])))


def new_rows(change_ref, forward_ref, tall_ref, known_ref, next_ref):
    groups, rank, wide = change_ref.shape
    group = wide // rank
    evolvings = []
    for k in range(groups * group):
        lanes = slice((k % group) * rank, (k % group + 1) * rank)
        change, forward = change_ref[k // group][:, lanes], forward_ref[k // group][:, lanes]
        left = jnp.concatenate([left_triple(change), left_triple(forward)], axis=0)
        tall, known = tall_ref[k], known_ref[k]
        both = dot(left, right_triple(tall))
        next_ref[k] = known + tall + both[:rank]
        evolvings.append(known + both[rank:])
    return evolvings


def last_kernel(total, mixed_tall_ref, *refs):
    *sum_refs, coupled_ref, delta_ref = refs
    delta = new_delta(sum_refs, total, delta_ref.shape[0])
    delta_ref[...] = delta
    delta_left = left_triple(delta.T)
    for k in range(coupled_ref.shape[0]):
        coupled_ref[k] = dot(delta_left, mixed_tall_ref[k])


per_microsecond = 1_100_000_000


def call(
    kernel, name, outs, *args, scalars=0, unread=0, microseconds=0.3, limit=16, scratch=()
):
    flops = int(microseconds * per_microsecond)
    specs = [pl.BlockSpec(memory_space=pltpu.SMEM)] * scalars
    specs += [pl.BlockSpec(memory_space=pl.ANY)] * unread
    specs += [pl.BlockSpec(memory_space=pltpu.VMEM)] * (len(args) - len(specs))
    shapes = [jax.ShapeDtypeStruct(shape, dtype) for shape, dtype in outs]
    moved = sum(arg.size * arg.dtype.itemsize for arg in args)
    moved += sum(shape.size * shape.dtype.itemsize for shape in shapes)
    return pl.pallas_call(
        kernel,
        out_shape=shapes,
        in_specs=specs,
        out_specs=[pl.BlockSpec(memory_space=pltpu.VMEM)] * len(shapes),
        scratch_shapes=list(scratch),
        compiler_params=pltpu.CompilerParams(vmem_limit_bytes=limit * 1024 * 1024),
        cost_estimate=pl.CostEstimate(flops=flops, bytes_accessed=moved, transcendentals=0),
        name=name,
    )(*args)


def rotated(value, axis, shift):
    count = lax.axis_size(axis)
    return lax.ppermute(value, axis, [(i, (i + shift) % count) for i in range(count)])


def swapped(value, axis, first):
    count = lax.axis_size(axis)
    pairs = [((i + first) % count, (i + first + 1) % count) for i in range(0, count, 2)]
    return lax.ppermute(value, axis, pairs + [(b, a) for a, b in pairs])


def from_others(value, axis):
    return [rotated(value, axis, shift) for shift in range(1, lax.axis_size(axis))]


def stage_sizes(count):
    sizes = []
    while count > 1:
        sizes.append(next(size for size in (4, 2, 3, 5, 7, count) if count % size == 0))
        count //= sizes[-1]
    return sizes


def in_stages(value, axis, beside=None):
    count = lax.axis_size(axis)
    stride = 1
    terms, firsts = [value], []
    for size in stage_sizes(count):
        value = terms[0]
        if len(terms) > 1:
            unread = [] if beside is None else [beside]
            (value,) = call(
                functools.partial(add_kernel, len(unread)),
                "add",
                [(value.shape, f32)],
                *unread, *terms,
                unread=len(unread),
            )
        terms = [value]
        for shift in range(1, size):
            moves = []
            for i in range(count):
                digit = (i // stride) % size
                other = digit ^ shift if size in (2, 4) else (digit + shift) % size
                moves.append((i, i + (other - digit) * stride))
            terms.append(lax.ppermute(value, axis, moves))
        stride *= size
        firsts = firsts or terms
    return terms, firsts


def body(
    data, order, chan_factor, slice_weights, smooth_aux, coupled, smooth_dual, coupling_dual, delta
):
    count, all_rows, channels = data.shape
    rank = chan_factor.shape[1]
    rows = smooth_aux.shape[1]
    parts = lax.axis_size("chan")
    total = count * lax.axis_size("cuts")
    group = group_size(count, rank)
    groups = count // group
    wide = group * rank
    flip = lambda value: jnp.swapaxes(value, 1, 2)
    aux, coup, dual_s, dual_c = map(flip, (smooth_aux, coupled, smooth_dual, coupling_dual))
    factor = chan_factor.T
    state = ((count, rank, rows), f32)
    quads = ((groups, rank, wide), f32)
    square = ((rank, rank), f32)
    halo = ((SWEEPS, rank, rows), f32)
    lanes = lambda height: ((height, 128), f32)
    scale = ((groups, 8, wide), f32)

    me = lax.axis_index("chan").astype(jnp.int32).reshape(1)
    odd = lax.rem(lax.axis_index("cuts"), 2).astype(jnp.int32).reshape(1)
    early = count // 4
    own, received = [], []
    for first, pairs, lead in ((0, early, True), (2 * early, count // 2 - early, False)):
        height = pairs * rows + (rank // 2 if lead else 0)
        projected = call(
            functools.partial(project_kernel, first, pairs, rows, lead),
            "project",
            [((height, 2 * rank), f32)] * parts + [(factor.shape, factor.dtype)] * lead,
            me, data, factor,
            scalars=1, unread=1, limit=52,
            scratch=[
                pltpu.VMEM((2 * pairs, all_rows, channels), data.dtype),
                pltpu.SemaphoreType.DMA((4 * pairs,)),
            ],
        )
        if lead:
            *projected, factor = projected
        own.append(projected[0])
        received.append([rotated(projected[shift], "chan", shift) for shift in range(1, parts)])

    late_weights, _ = lax.optimization_barrier((slice_weights, own[-1]))
    before = rotated(late_weights, "cuts", 1)
    after = rotated(late_weights, "cuts", -1)
    inverse, mover, rho, diagonal, columns, base = call(
        functools.partial(setup_kernel, parts, early * rows, group),
        "setup",
        [
            ((count, rank, 3 * rank), bf16),
            ((count // 2, 2 * rank, 6 * rank), bf16),
            lanes(count),
            ((count, rank), f32),
            ((rank, count), f32),
            state,
        ],
        order, own[0], *received[0], slice_weights, aux, coup, dual_s, dual_c,
        scalars=1,
    )
    half_state = ((early, 2 * rank, rows), f32)
    moved, turned = call(
        move_kernel, "move", [half_state, half_state], mover, own[0], *received[0]
    )
    tall, target, gram = call(
        functools.partial(first_kernel, group),
        "first",
        [state, state, quads],
        order, before, after, base, mover, dual_s, dual_c, moved, own[1], *received[1],
        scalars=1, unread=2,
        scratch=[pltpu.VMEM((count // 2, 2 * rank, rows), f32)],
    )
    side, before, after, inside, to_near, to_far = call(
        smooth_kernel,
        "smooth",
        [state, lanes(count), lanes(count), state, halo, halo],
        odd, order, aux, target, before, rho, after, diagonal, columns, turned, own[1],
        *received[1],
        scalars=2,
        scratch=[pltpu.VMEM((count // 2, 2 * rank, rows), f32)],
    )
    polar_outs = [quads, ((rank // 2, 2 * rank), f32), quads]
    for inner in range(INNER):
        if inner == 0:
            mixed, partial, gram = call(
                first_polar_kernel,
                "polar",
                polar_outs,
                inside, delta, gram, *from_others(gram, "chan"),
                unread=1, microseconds=3,
            )
        else:
            last = inner == INNER - 1
            mixed, partial, *gram = call(
                functools.partial(later_polar_kernel, last),
                "polar",
                polar_outs[:2] if last else polar_outs,
                inside, delta, change, old, cross, *crosses,
                unread=1,
            )
            gram = gram[0] if gram else None
        if inner == INNER - 1:
            mixed_tall, evolving = call(
                last_rows_kernel,
                "rows",
                [((count, 3 * rank, rows), bf16), state],
                mixed, change, forward, tall, known,
                scratch=[pltpu.VMEM(state[0], f32)],
            )
            coup, delta = call(
                functools.partial(last_kernel, total),
                "last",
                [state, square],
                mixed_tall, *in_stages(partial, "cuts")[0],
            )
            continue
        near = swapped(to_near, "cuts", 0)
        far = swapped(to_far, "cuts", 1)
        known, cross, *kept = call(
            functools.partial(ahead_kernel, group),
            "ahead",
            [state, ((groups, rank, 2 * wide), f32)] + [state] * (2 if inner < INNER - 2 else 0),
            odd, partial, inside, near, far, target, tall, side, rho, inverse,
            scalars=1, unread=1,
        )
        sums, firsts = in_stages(partial, "cuts", beside=cross)
        _, cross = lax.optimization_barrier((firsts, cross))
        crosses = from_others(cross, "chan")
        old = gram
        delta, change, forward = call(
            functools.partial(mixer_kernel, total),
            "mixer",
            [square, quads, quads],
            mixed, inverse, rho, *sums,
        )
        if inner < INNER - 2:
            tall, target, inside, to_near, to_far = call(
                rows_kernel,
                "rows",
                [state, state, state, halo, halo],
                odd, kept[0], before, rho, after, change, forward, tall, known, kept[1],
                scalars=1,
            )
    return (flip(evolving), flip(coup), delta)


def solution(mesh):
    return jax.shard_map(
        body,
        mesh=mesh,
        in_specs=(
            P("cuts", None, "chan"),
            P("cuts"),
            P("chan", None),
            P("cuts", None),
            P("cuts", "chan", None),
            P("cuts", "chan", None),
            P("cuts", "chan", None),
            P("cuts", "chan", None),
            P(),
        ),
        out_specs=(P("cuts", "chan", None), P("cuts", "chan", None), P()),
        check_vma=False,
    )
```

```python
import functools

import jax
import jax.numpy as jnp
from jax import lax
from jax.experimental import pallas as pl
from jax.experimental.pallas import tpu as pltpu
from jax.sharding import PartitionSpec as P

INNER = 3
SWEEPS = 4
POLAR = 8

smooth_weight = 1.0
eps_trace = 1e-06
f32 = jnp.float32
bf16 = jnp.bfloat16
NN = (((1,), (0,)), ((), ()))
NT = (((1,), (1,)), ((), ()))


def dot(left, right, dims=NN):
    return lax.dot_general(left, right, dims, preferred_element_type=f32)


def split(value):
    high = value.astype(bf16)
    low = (value - high.astype(f32)).astype(bf16)
    return high, low


def left_triple(value):
    high, low = split(value)
    return jnp.concatenate([high, high, low], axis=1)


def right_triple(value):
    high, low = split(value)
    return jnp.concatenate([high, low, high], axis=0)


def block_mask(rank, group):
    wide = rank * group
    rows = lax.div(lax.broadcasted_iota(jnp.int32, (wide, wide), 0), rank)
    cols = lax.div(lax.broadcasted_iota(jnp.int32, (wide, wide), 1), rank)
    return jnp.where(rows == cols, 1.0, 0.0).astype(bf16)


def wide_eye(rank, group):
    rows = lax.broadcasted_iota(jnp.int32, (rank, rank * group), 0)
    cols = lax.broadcasted_iota(jnp.int32, (rank, rank * group), 1)
    return jnp.where(rows == lax.rem(cols, rank), 1.0, 0.0).astype(f32)


def block_diagonal(value, mask, group, dims=NN):
    high, low = split(value)
    high = jnp.concatenate([high] * group, axis=0) * mask
    low = jnp.concatenate([low] * group, axis=0) * mask
    empty = jnp.zeros_like(high)
    one, other = ([high, low], [high, empty]) if dims == NN else ([high, high], [low, empty])
    return jnp.concatenate(
        [jnp.concatenate(one, axis=1), jnp.concatenate(other, axis=1)], axis=0
    )


def times_blocks(values, blocks, dims=NN):
    rank, wide = values[0].shape
    left = [jnp.concatenate(split(value), axis=1) for value in values]
    total = dot(jnp.concatenate(left, axis=0), blocks, dims)
    total = total[:, :wide] + total[:, wide:]
    return [total[at * rank : (at + 1) * rank] for at in range(len(values))]


def diagonal_blocks(value, rank, group):
    at = lax.div(lax.broadcasted_iota(jnp.int32, (rank, rank * group), 1), rank)
    total = value[:rank]
    for block in range(1, group):
        total = jnp.where(at == block, value[block * rank : (block + 1) * rank], total)
    return total


def from_left(left, values):
    wide = values[0].shape[1]
    total = dot(left_triple(left), right_triple(jnp.concatenate(values, axis=1)))
    return [total[:, at * wide : (at + 1) * wide] for at in range(len(values))]


def group_size(count, rank):
    group = max(1, 128 // rank)
    while count % group:
        group -= 1
    return group


def project_kernel(first, pairs, rows, lead, me_ref, data_ref, factor_ref, *refs):
    *outs, held, arrived = refs
    half = data_ref.shape[1] // 2
    copies = []
    for k in range(2 * pairs):
        for at in range(2):
            place = pl.ds(at * half, half)
            copies.append(
                pltpu.make_async_copy(
                    data_ref.at[first + k, place, :], held.at[k, place, :], arrived.at[2 * k + at]
                )
            )
            copies[-1].start()
    factor = factor_ref[...]
    rank = factor.shape[0]
    if lead:
        *outs, again_ref = outs
        again_ref[...] = factor
        gram = dot(factor, factor, NT)
        for out in outs:
            out[pairs * rows :, :] = jnp.concatenate([gram[: rank // 2], gram[rank // 2 :]], axis=1)
    parts = len(outs)
    empty = jnp.zeros_like(factor)
    sides = [
        jnp.concatenate([factor, empty], axis=0),
        jnp.concatenate([empty, factor], axis=0),
    ]
    for pair in range(pairs):
        for copy in copies[4 * pair : 4 * pair + 4]:
            copy.wait()
        for part in reversed(range(parts)):
            start = pl.multiple_of(lax.rem(me_ref[0] + part, parts) * rows, 16)
            place = pl.ds(start, rows)
            outs[part][pair * rows : (pair + 1) * rows, :] = dot(
                held[2 * pair, place, :], sides[0], NT
            ) + dot(held[2 * pair + 1, place, :], sides[1], NT)


def setup_kernel(parts, first, group, order_ref, *refs):
    lead_refs, refs = refs[:parts], refs[parts:]
    (own_ref, aux_ref, coupled_ref, dual_s_ref, dual_c_ref) = refs[:5]
    (inverse_ref, mover_ref, rho_ref, diagonal_ref, columns_ref, base_ref) = refs[5:]
    count, rank = own_ref.shape
    gram = summed(lead_refs, slice(first, None))
    gram = jnp.concatenate([gram[:, :rank], gram[:, rank:]], axis=0)
    eye = wide_eye(rank, 1)
    diagonal = jnp.sum(gram * eye, axis=0, keepdims=True)
    diagonal_ref[...] = jnp.broadcast_to(diagonal, diagonal_ref.shape)
    weights = own_ref[...]
    columns = weights.T
    columns_ref[...] = columns
    rho = jnp.sum(weights * weights * diagonal, axis=1, keepdims=True) / rank
    rho_ref[...] = jnp.broadcast_to(rho, rho_ref.shape)

    edge = 34.0 / 32.0
    lead = 4.0 * edge**3 / (4.0 * edge**3 - 3.0 * edge)
    mask = block_mask(rank, group)
    wide = wide_eye(rank, group)
    starts = range(0, count, group)
    systems = []
    for first in starts:
        scaled = []
        for k in range(first, first + group):
            unit = 1.0 / (34.0 * rho[k : k + 1, :])
            column = columns[:, k : k + 1]
            scaled.append(column * gram * weights[k : k + 1, :] * unit + (2.0 / 34.0) * eye)
        systems.append(jnp.concatenate(scaled, axis=1))
    inverses, rests = [], []
    for system in systems:
        rest = wide - system
        blocks = block_diagonal(rest, mask, group)
        (square,) = times_blocks([rest], blocks)
        (cube,) = times_blocks([square], blocks)
        inverses.append(wide + lead * (rest + square))
        rests.append(lead * cube - (lead - 1.0) * rest)
    for step in range(4):
        for at in range(len(systems)):
            blocks = block_diagonal(rests[at], mask, group)
            more, rests[at] = times_blocks([inverses[at], rests[at]], blocks)
            inverses[at] = inverses[at] + more
    for step in range(2):
        for at in range(len(systems)):
            (product,) = times_blocks([inverses[at]], block_diagonal(systems[at], mask, group))
            blocks = block_diagonal(wide - product, mask, group)
            (more,) = times_blocks([inverses[at]], blocks)
            inverses[at] = inverses[at] + more
    for k in range(count):
        place = (k % group) * rank
        unit = 1.0 / (34.0 * rho[k : k + 1, :])
        inverse = inverses[k // group][:, place : place + rank] * unit
        inverse_ref[k] = left_triple(inverse)
        base_ref[k] = dot(
            inverse_ref[k],
            right_triple(
                rho[k : k + 1, :] * (aux_ref[k] - dual_s_ref[k] + coupled_ref[k] - dual_c_ref[k])
            ),
        )
        both = jnp.concatenate([inverse * weights[k : k + 1, :]] * 2, axis=1)
        side = lax.div(lax.broadcasted_iota(jnp.int32, both.shape, 1), rank)
        both = jnp.where(side == lax.rem(order_ref[k], 2), both, 0.0)
        high, low = split(both)
        pair, place = stored_place(order_ref, k, count, rank)
        mover_ref[pair, place, :] = jnp.concatenate([high, high, low], axis=1)


def cross_blocks(lefts, rights, rank):
    group = len(lefts)
    wide = group * rank
    left = jnp.concatenate(split(jnp.concatenate(lefts, axis=0)), axis=0)
    right = left
    if rights is not lefts:
        right = jnp.concatenate(split(jnp.concatenate(rights, axis=0)), axis=0)
    total = dot(left, right, NT)
    total = total[:wide, :wide] + total[:wide, wide:] + total[wide:, :wide]
    return diagonal_blocks(total, rank, group)


def summed(refs, at):
    total = refs[0][at]
    for ref in refs[1:]:
        total = total + ref[at]
    return total


def stored_place(order_ref, k, count, rank):
    stored = lax.rem(order_ref[k], count)
    return lax.div(stored, 2), pl.ds(pl.multiple_of(lax.rem(stored, 2) * rank, rank), rank)


def move(mover, projected):
    high, low = split(projected)
    return dot(mover, jnp.concatenate([high, low, high], axis=1), NT)


def move_kernel(mover_ref, *refs):
    *projected_refs, moved_ref, turned_ref = refs
    rows = moved_ref.shape[2]
    for pair in range(moved_ref.shape[0]):
        projected = summed(projected_refs, slice(pair * rows, (pair + 1) * rows))
        moved_ref[pair] = move(mover_ref[pair], projected)
        turned_ref[pair] = projected.T


def first_kernel(group, order_ref, *refs):
    base_ref, mover_ref, dual_s_ref, dual_c_ref, early_ref = refs[2:7]
    *projected_refs, tall_ref, target_ref, gram_ref, moved = refs[7:]
    count, rank, rows = base_ref.shape
    early = early_ref.shape[0]
    for pair in range(early):
        moved[pair] = early_ref[pair]
    for pair in range(early, count // 2):
        place = slice((pair - early) * rows, (pair - early + 1) * rows)
        moved[pair] = move(mover_ref[pair], summed(projected_refs, place))
    talls = []
    for k in range(count):
        pair, place = stored_place(order_ref, k, count, rank)
        evolving = base_ref[k] + moved[pair, place, :]
        target_ref[k] = evolving + dual_s_ref[k]
        tall = evolving + dual_c_ref[k]
        tall_ref[k] = tall
        talls.append(tall)
        if len(talls) == group:
            gram_ref[k // group] = cross_blocks(talls, talls, rank)
            talls = []


def smooth(odd, now, targets, rho, inside_ref, near_ref, far_ref):
    count = len(targets)
    width = SWEEPS
    share = {j: 2.0 * smooth_weight / (rho[j] + 4.0 * smooth_weight) for j in rho}
    pull = {j: (rho[j] / (rho[j] + 4.0 * smooth_weight)) * targets[j] for j in range(count)}
    now = {j: now[j] for j in range(count)}
    for sweep in range(width):
        later = {}
        for j in range(-sweep - 1, count + sweep + 1):
            beside = [now[i] for i in (j - 1, j + 1) if i in now]
            total = beside[0] if len(beside) == 1 else beside[0] + beside[1]
            total = share[j] * total
            later[j] = total + pull[j] if j in pull else total
        now = later
    for j in range(count):
        inside_ref[j] = now[j]
    for j in range(width):
        near_ref[j] = jnp.where(odd == 1, now[j - width], now[count + j])
        far_ref[j] = jnp.where(odd == 1, now[count + j], now[j - width])


def all_rho(before_ref, rho_ref, after_ref):
    count = rho_ref.shape[0]
    rho = {j: rho_ref[j : j + 1, 0:1] for j in range(count)}
    for j in range(SWEEPS):
        rho[j - SWEEPS] = before_ref[count - SWEEPS + j : count - SWEEPS + j + 1, 0:1]
        rho[count + j] = after_ref[j : j + 1, 0:1]
    return rho


def smooth_kernel(
    odd_ref, order_ref, aux_ref, target_ref, before_ref, rho_ref, after_ref, diagonal_ref,
    columns_ref, early_ref, *refs
):
    *projected_refs, side_ref, past_ref, next_ref, inside_ref, near_ref, far_ref, turned = refs
    count, rank, rows = aux_ref.shape
    for source, place in ((before_ref, past_ref), (after_ref, next_ref)):
        weights = source[...]
        rho = jnp.sum(weights * weights * diagonal_ref[...], axis=1, keepdims=True) / rank
        place[...] = jnp.broadcast_to(rho, place.shape)
    rho = all_rho(past_ref, rho_ref, next_ref)
    slices = range(count)
    smooth(
        odd_ref[0], [aux_ref[k] for k in slices], [target_ref[k] for k in slices], rho,
        inside_ref, near_ref, far_ref,
    )
    early = early_ref.shape[0]
    for pair in range(early):
        turned[pair] = early_ref[pair]
    for pair in range(early, count // 2):
        place = slice((pair - early) * rows, (pair - early + 1) * rows)
        turned[pair] = summed(projected_refs, place).T
    for k in slices:
        pair, place = stored_place(order_ref, k, count, rank)
        side_ref[k] = columns_ref[:, k : k + 1] * turned[pair, place, :]


def polar(grams, delta):
    rank, wide = grams[0].shape
    group = wide // rank
    mask = block_mask(rank, group)
    eye = wide_eye(rank, group)
    delta_wide = jnp.concatenate([delta] * group, axis=1)
    delta_blocks = block_diagonal(delta_wide, mask, group, NT)
    (across,) = from_left(delta.T, [delta_wide])
    traces = []
    for gram in grams:
        line = jnp.broadcast_to(jnp.sum(across * gram, axis=0, keepdims=True), (16, wide))
        high, low = split(line)
        rest = (line - high.astype(f32) - low.astype(f32)).astype(bf16)
        line = dot(high, mask) + dot(low, mask) + dot(rest, mask)
        traces.append(line[0:1] + eps_trace)
    rights = [times_blocks([gram], delta_blocks, NT)[0] for gram in grams]
    normals = from_left(delta, rights)
    currents = [normal / trace for normal, trace in zip(normals, traces)]
    scales = [1.0 / jnp.sqrt(trace) for trace in traces]
    roots = []
    for step in range(POLAR):
        for at in range(len(grams)):
            product = currents[at]
            blocks = block_diagonal(product, mask, group)
            if step == 0:
                roots.append(1.5 * eye - 0.5 * product)
                (square,) = times_blocks([product], blocks)
            elif step < POLAR - 1:
                square, more = times_blocks([product, roots[at]], blocks)
                roots[at] = 1.5 * roots[at] - 0.5 * more
            else:
                (more,) = times_blocks([roots[at]], blocks)
                roots[at] = 1.5 * roots[at] - 0.5 * more
            if step < POLAR - 1:
                half = 1.5 * product - 0.5 * square
                (more,) = times_blocks([half], blocks)
                currents[at] = 1.5 * half - 0.5 * more
    return roots, scales, rights


def mix(roots, scales, rights, delta, mixed_ref, partial_ref):
    rank, wide = roots[0].shape
    group = wide // rank
    mask = block_mask(rank, group)
    delta_blocks = block_diagonal(jnp.concatenate([delta] * group, axis=1), mask, group)
    left, right = [], []
    for at in range(len(roots)):
        high, low = split(roots[at] * scales[at])
        left += [high, high, low]
        high, low = split(rights[at])
        right += [high, low, high]
    partial = dot(jnp.concatenate(left, axis=1), jnp.concatenate(right, axis=1), NT)
    for at in range(len(roots)):
        (mixed,) = times_blocks([roots[at]], delta_blocks)
        mixed_ref[at] = mixed * scales[at]
    half = rank // 2
    partial_ref[...] = jnp.concatenate([partial[:half], partial[half:]], axis=1)


def first_polar_kernel(after_ref, delta_ref, *refs):
    *gram_refs, mixed_ref, partial_ref, gram_ref = refs
    grams = [summed(gram_refs, at) for at in range(gram_ref.shape[0])]
    for at in range(len(grams)):
        gram_ref[at] = grams[at]
    delta = delta_ref[...]
    mix(*polar(grams, delta), delta, mixed_ref, partial_ref)


def later_polar_kernel(last, after_ref, delta_ref, change_ref, old_ref, *refs):
    if last:
        *cross_refs, mixed_ref, partial_ref = refs
    else:
        *cross_refs, mixed_ref, partial_ref, gram_ref = refs
    groups, rank, wide = old_ref.shape
    group = wide // rank
    mask = block_mask(rank, group)
    grams = []
    for at in range(groups):
        cross = summed(cross_refs, at)
        change = change_ref[at]
        (onward,) = times_blocks([change], block_diagonal(old_ref[at], mask, group))
        onward = cross[:, :wide] + 0.5 * onward
        (one,) = times_blocks([onward], block_diagonal(change, mask, group, NT), NT)
        (other,) = times_blocks([change], block_diagonal(onward, mask, group, NT), NT)
        grams.append(cross[:, wide:] + one + other)
        if not last:
            gram_ref[at] = grams[at]
    delta = delta_ref[...]
    mix(*polar(grams, delta), delta, mixed_ref, partial_ref)


def ahead_kernel(
    group, odd_ref, after_ref, inside_ref, near_ref, far_ref, target_ref, tall_ref, side_ref, rho_ref,
    inverse_ref, known_ref, cross_ref, *kept
):
    count, rank, _ = inside_ref.shape
    width = SWEEPS
    knowns, talls = [], []
    for k in range(count):
        aux = inside_ref[k]
        if k < width:
            aux = aux + jnp.where(odd_ref[0] == 1, near_ref[k], far_ref[k])
        if k >= count - width:
            at = k - count + width
            aux = aux + jnp.where(odd_ref[0] == 1, far_ref[at], near_ref[at])
        target, tall = target_ref[k], tall_ref[k]
        if kept:
            aux_ref, dual_ref = kept
            aux_ref[k] = aux
            dual_ref[k] = target - aux
        known = dot(
            inverse_ref[k],
            right_triple(side_ref[k] + rho_ref[k : k + 1, 0:1] * (2.0 * aux - target - tall)),
        )
        known_ref[k] = known
        talls.append(tall)
        knowns.append(known + tall)
        if len(talls) == group:
            cross_ref[k // group] = jnp.concatenate(
                [cross_blocks(knowns, talls, rank), cross_blocks(knowns, knowns, rank)], axis=1
            )
            knowns, talls = [], []


def add_kernel(unread, *refs):
    *term_refs, total_ref = refs[unread:]
    total = term_refs[0][...]
    for ref in term_refs[1:]:
        total = total + ref[...]
    total_ref[...] = total


def new_delta(sum_refs, total, rank):
    packed = sum_refs[0][...]
    for ref in sum_refs[1:]:
        packed = packed + ref[...]
    packed = packed / total
    return jnp.concatenate([packed[:, :rank], packed[:, rank:]], axis=0)


def mixer_kernel(total, mixed_ref, inverse_ref, rho_ref, *refs):
    *sum_refs, delta_ref, change_ref, forward_ref = refs
    groups, rank, wide = mixed_ref.shape
    group = wide // rank
    delta = new_delta(sum_refs, total, rank)
    delta_ref[...] = delta
    mixers = from_left(delta.T, [mixed_ref[at] for at in range(groups)])
    place = lax.div(lax.broadcasted_iota(jnp.int32, (1, wide), 1), rank)
    for at in range(groups):
        mixer = mixers[at]
        slices = range(at * group, (at + 1) * group)
        inverses = jnp.concatenate([inverse_ref[k] for k in slices], axis=0)
        onward = diagonal_blocks(dot(inverses, right_triple(mixer)), rank, group)
        rho = rho_ref[at * group : at * group + 1, 0:1]
        for k in slices[1:]:
            rho = jnp.where(place == k - at * group, rho_ref[k : k + 1, 0:1], rho)
        forward = 2.0 * rho * onward
        forward_ref[at] = forward
        change_ref[at] = forward - mixer


def rows_kernel(odd_ref, aux_ref, before_ref, rho_ref, after_ref, *refs):
    (change_ref, forward_ref, tall_ref, known_ref, dual_ref) = refs[:5]
    (next_ref, target_ref, inside_ref, near_ref, far_ref) = refs[5:]
    targets = new_rows(change_ref, forward_ref, tall_ref, known_ref, next_ref)
    count = len(targets)
    for k in range(count):
        targets[k] = targets[k] + dual_ref[k]
        target_ref[k] = targets[k]
    rho = all_rho(before_ref, rho_ref, after_ref)
    smooth(
        odd_ref[0], [aux_ref[k] for k in range(count)], targets, rho,
        inside_ref, near_ref, far_ref,
    )


def last_rows_kernel(mixed_ref, change_ref, forward_ref, tall_ref, known_ref, *outs):
    mixed_tall_ref, evolving_ref, next_ref = outs
    evolvings = new_rows(change_ref, forward_ref, tall_ref, known_ref, next_ref)
    groups, rank, wide = mixed_ref.shape
    group = wide // rank
    for k in range(len(evolvings)):
        evolving_ref[k] = evolvings[k]
        place = (k % group) * rank
        mixed = left_triple(mixed_ref[k // group][:, place : place + rank])
        mixed_tall_ref[k] = right_triple(dot(mixed, right_triple(next_ref[k])))


def new_rows(change_ref, forward_ref, tall_ref, known_ref, next_ref):
    groups, rank, wide = change_ref.shape
    group = wide // rank
    evolvings = []
    for k in range(groups * group):
        lanes = slice((k % group) * rank, (k % group + 1) * rank)
        change, forward = change_ref[k // group][:, lanes], forward_ref[k // group][:, lanes]
        left = jnp.concatenate([left_triple(change), left_triple(forward)], axis=0)
        tall, known = tall_ref[k], known_ref[k]
        both = dot(left, right_triple(tall))
        next_ref[k] = known + tall + both[:rank]
        evolvings.append(known + both[rank:])
    return evolvings


def last_kernel(total, mixed_tall_ref, *refs):
    *sum_refs, coupled_ref, delta_ref = refs
    delta = new_delta(sum_refs, total, delta_ref.shape[0])
    delta_ref[...] = delta
    delta_left = left_triple(delta.T)
    for k in range(coupled_ref.shape[0]):
        coupled_ref[k] = dot(delta_left, mixed_tall_ref[k])


per_microsecond = 1_100_000_000


def call(
    kernel, name, outs, *args, scalars=0, unread=0, microseconds=0.3, limit=16, scratch=()
):
    flops = int(microseconds * per_microsecond)
    specs = [pl.BlockSpec(memory_space=pltpu.SMEM)] * scalars
    specs += [pl.BlockSpec(memory_space=pl.ANY)] * unread
    specs += [pl.BlockSpec(memory_space=pltpu.VMEM)] * (len(args) - len(specs))
    shapes = [jax.ShapeDtypeStruct(shape, dtype) for shape, dtype in outs]
    moved = sum(arg.size * arg.dtype.itemsize for arg in args)
    moved += sum(shape.size * shape.dtype.itemsize for shape in shapes)
    return pl.pallas_call(
        kernel,
        out_shape=shapes,
        in_specs=specs,
        out_specs=[pl.BlockSpec(memory_space=pltpu.VMEM)] * len(shapes),
        scratch_shapes=list(scratch),
        compiler_params=pltpu.CompilerParams(vmem_limit_bytes=limit * 1024 * 1024),
        cost_estimate=pl.CostEstimate(flops=flops, bytes_accessed=moved, transcendentals=0),
        name=name,
    )(*args)


def rotated(value, axis, shift):
    count = lax.axis_size(axis)
    return lax.ppermute(value, axis, [(i, (i + shift) % count) for i in range(count)])


def swapped(value, axis, first):
    count = lax.axis_size(axis)
    pairs = [((i + first) % count, (i + first + 1) % count) for i in range(0, count, 2)]
    return lax.ppermute(value, axis, pairs + [(b, a) for a, b in pairs])


def from_others(value, axis):
    return [rotated(value, axis, shift) for shift in range(1, lax.axis_size(axis))]


def stage_sizes(count):
    sizes = []
    while count > 1:
        sizes.append(next(size for size in (4, 2, 3, 5, 7, count) if count % size == 0))
        count //= sizes[-1]
    return sizes


def in_stages(value, axis, beside=None):
    count = lax.axis_size(axis)
    stride = count
    terms, firsts = [value], []
    for size in reversed(stage_sizes(count)):
        stride //= size
        value = terms[0]
        if len(terms) > 1:
            unread = [] if beside is None else [beside]
            (value,) = call(
                functools.partial(add_kernel, len(unread)),
                "add",
                [(value.shape, f32)],
                *unread, *terms,
                unread=len(unread),
            )
        terms = [value]
        for shift in range(1, size):
            moves = []
            for i in range(count):
                digit = (i // stride) % size
                other = digit ^ shift if size in (2, 4) else (digit + shift) % size
                moves.append((i, i + (other - digit) * stride))
            terms.append(lax.ppermute(value, axis, moves))
        firsts = firsts or terms
    return terms, firsts


def body(
    data, order, chan_factor, slice_weights, smooth_aux, coupled, smooth_dual, coupling_dual, delta
):
    count, all_rows, channels = data.shape
    rank = chan_factor.shape[1]
    rows = smooth_aux.shape[1]
    parts = lax.axis_size("chan")
    total = count * lax.axis_size("cuts")
    group = group_size(count, rank)
    groups = count // group
    wide = group * rank
    flip = lambda value: jnp.swapaxes(value, 1, 2)
    aux, coup, dual_s, dual_c = map(flip, (smooth_aux, coupled, smooth_dual, coupling_dual))
    factor = chan_factor.T
    state = ((count, rank, rows), f32)
    quads = ((groups, rank, wide), f32)
    square = ((rank, rank), f32)
    halo = ((SWEEPS, rank, rows), f32)
    lanes = lambda height: ((height, 128), f32)
    scale = ((groups, 8, wide), f32)

    me = lax.axis_index("chan").astype(jnp.int32).reshape(1)
    odd = lax.rem(lax.axis_index("cuts"), 2).astype(jnp.int32).reshape(1)
    early = count // 4
    own, received = [], []
    for first, pairs, lead in ((0, early, True), (2 * early, count // 2 - early, False)):
        height = pairs * rows + (rank // 2 if lead else 0)
        projected = call(
            functools.partial(project_kernel, first, pairs, rows, lead),
            "project",
            [((height, 2 * rank), f32)] * parts + [(factor.shape, factor.dtype)] * lead,
            me, data, factor,
            scalars=1, unread=1, limit=52,
            scratch=[
                pltpu.VMEM((2 * pairs, all_rows, channels), data.dtype),
                pltpu.SemaphoreType.DMA((4 * pairs,)),
            ],
        )
        if lead:
            *projected, factor = projected
        own.append(projected[0])
        received.append([rotated(projected[shift], "chan", shift) for shift in range(1, parts)])

    late_weights, _ = lax.optimization_barrier((slice_weights, own[-1]))
    before = rotated(late_weights, "cuts", 1)
    after = rotated(late_weights, "cuts", -1)
    inverse, mover, rho, diagonal, columns, base = call(
        functools.partial(setup_kernel, parts, early * rows, group),
        "setup",
        [
            ((count, rank, 3 * rank), bf16),
            ((count // 2, 2 * rank, 6 * rank), bf16),
            lanes(count),
            ((count, rank), f32),
            ((rank, count), f32),
            state,
        ],
        order, own[0], *received[0], slice_weights, aux, coup, dual_s, dual_c,
        scalars=1,
    )
    half_state = ((early, 2 * rank, rows), f32)
    moved, turned = call(
        move_kernel, "move", [half_state, half_state], mover, own[0], *received[0]
    )
    tall, target, gram = call(
        functools.partial(first_kernel, group),
        "first",
        [state, state, quads],
        order, before, after, base, mover, dual_s, dual_c, moved, own[1], *received[1],
        scalars=1, unread=2,
        scratch=[pltpu.VMEM((count // 2, 2 * rank, rows), f32)],
    )
    side, before, after, inside, to_near, to_far = call(
        smooth_kernel,
        "smooth",
        [state, lanes(count), lanes(count), state, halo, halo],
        odd, order, aux, target, before, rho, after, diagonal, columns, turned, own[1],
        *received[1],
        scalars=2,
        scratch=[pltpu.VMEM((count // 2, 2 * rank, rows), f32)],
    )
    polar_outs = [quads, ((rank // 2, 2 * rank), f32), quads]
    for inner in range(INNER):
        if inner == 0:
            mixed, partial, gram = call(
                first_polar_kernel,
                "polar",
                polar_outs,
                inside, delta, gram, *from_others(gram, "chan"),
                unread=1, microseconds=3,
            )
        else:
            last = inner == INNER - 1
            mixed, partial, *gram = call(
                functools.partial(later_polar_kernel, last),
                "polar",
                polar_outs[:2] if last else polar_outs,
                inside, delta, change, old, cross, *crosses,
                unread=1,
            )
            gram = gram[0] if gram else None
        if inner == INNER - 1:
            mixed_tall, evolving = call(
                last_rows_kernel,
                "rows",
                [((count, 3 * rank, rows), bf16), state],
                mixed, change, forward, tall, known,
                scratch=[pltpu.VMEM(state[0], f32)],
            )
            coup, delta = call(
                functools.partial(last_kernel, total),
                "last",
                [state, square],
                mixed_tall, *in_stages(partial, "cuts")[0],
            )
            continue
        near = swapped(to_near, "cuts", 0)
        far = swapped(to_far, "cuts", 1)
        known, cross, *kept = call(
            functools.partial(ahead_kernel, group),
            "ahead",
            [state, ((groups, rank, 2 * wide), f32)] + [state] * (2 if inner < INNER - 2 else 0),
            odd, partial, inside, near, far, target, tall, side, rho, inverse,
            scalars=1, unread=1,
        )
        sums, firsts = in_stages(partial, "cuts", beside=cross)
        _, cross = lax.optimization_barrier((firsts, cross))
        crosses = from_others(cross, "chan")
        old = gram
        delta, change, forward = call(
            functools.partial(mixer_kernel, total),
            "mixer",
            [square, quads, quads],
            mixed, inverse, rho, *sums,
        )
        if inner < INNER - 2:
            tall, target, inside, to_near, to_far = call(
                rows_kernel,
                "rows",
                [state, state, state, halo, halo],
                odd, kept[0], before, rho, after, change, forward, tall, known, kept[1],
                scalars=1,
            )
    return (flip(evolving), flip(coup), delta)


def solution(mesh):
    return jax.shard_map(
        body,
        mesh=mesh,
        in_specs=(
            P("cuts", None, "chan"),
            P("cuts"),
            P("chan", None),
            P("cuts", None),
            P("cuts", "chan", None),
            P("cuts", "chan", None),
            P("cuts", "chan", None),
            P("cuts", "chan", None),
            P(),
        ),
        out_specs=(P("cuts", "chan", None), P("cuts", "chan", None), P()),
        check_vma=False,
    )
```

```python
import functools

import jax
import jax.numpy as jnp
from jax import lax
from jax.experimental import pallas as pl
from jax.experimental.pallas import tpu as pltpu
from jax.sharding import PartitionSpec as P

INNER = 3
SWEEPS = 4
POLAR = 8

smooth_weight = 1.0
eps_trace = 1e-06
f32 = jnp.float32
bf16 = jnp.bfloat16
NN = (((1,), (0,)), ((), ()))
NT = (((1,), (1,)), ((), ()))


def dot(left, right, dims=NN):
    return lax.dot_general(left, right, dims, preferred_element_type=f32)


def split(value):
    high = value.astype(bf16)
    low = (value - high.astype(f32)).astype(bf16)
    return high, low


def left_triple(value):
    high, low = split(value)
    return jnp.concatenate([high, high, low], axis=1)


def right_triple(value):
    high, low = split(value)
    return jnp.concatenate([high, low, high], axis=0)


def block_mask(rank, group):
    wide = rank * group
    rows = lax.div(lax.broadcasted_iota(jnp.int32, (wide, wide), 0), rank)
    cols = lax.div(lax.broadcasted_iota(jnp.int32, (wide, wide), 1), rank)
    return jnp.where(rows == cols, 1.0, 0.0).astype(bf16)


def wide_eye(rank, group):
    rows = lax.broadcasted_iota(jnp.int32, (rank, rank * group), 0)
    cols = lax.broadcasted_iota(jnp.int32, (rank, rank * group), 1)
    return jnp.where(rows == lax.rem(cols, rank), 1.0, 0.0).astype(f32)


def block_diagonal(value, mask, group, dims=NN):
    high, low = split(value)
    high = jnp.concatenate([high] * group, axis=0) * mask
    low = jnp.concatenate([low] * group, axis=0) * mask
    empty = jnp.zeros_like(high)
    one, other = ([high, low], [high, empty]) if dims == NN else ([high, high], [low, empty])
    return jnp.concatenate(
        [jnp.concatenate(one, axis=1), jnp.concatenate(other, axis=1)], axis=0
    )


def times_blocks(values, blocks, dims=NN):
    rank, wide = values[0].shape
    left = [jnp.concatenate(split(value), axis=1) for value in values]
    total = dot(jnp.concatenate(left, axis=0), blocks, dims)
    total = total[:, :wide] + total[:, wide:]
    return [total[at * rank : (at + 1) * rank] for at in range(len(values))]


def diagonal_blocks(value, rank, group):
    at = lax.div(lax.broadcasted_iota(jnp.int32, (rank, rank * group), 1), rank)
    total = value[:rank]
    for block in range(1, group):
        total = jnp.where(at == block, value[block * rank : (block + 1) * rank], total)
    return total


def from_left(left, values):
    wide = values[0].shape[1]
    total = dot(left_triple(left), right_triple(jnp.concatenate(values, axis=1)))
    return [total[:, at * wide : (at + 1) * wide] for at in range(len(values))]


def group_size(count, rank):
    group = max(1, 128 // rank)
    while count % group:
        group -= 1
    return group


def project_kernel(first, pairs, rows, lead, me_ref, data_ref, factor_ref, *refs):
    *outs, held, arrived = refs
    half = data_ref.shape[1] // 2
    copies = []
    for k in range(2 * pairs):
        for at in range(2):
            place = pl.ds(at * half, half)
            copies.append(
                pltpu.make_async_copy(
                    data_ref.at[first + k, place, :], held.at[k, place, :], arrived.at[2 * k + at]
                )
            )
            copies[-1].start()
    factor = factor_ref[...]
    rank = factor.shape[0]
    if lead:
        *outs, again_ref = outs
        again_ref[...] = factor
        gram = dot(factor, factor, NT)
        for out in outs:
            out[pairs * rows :, :] = jnp.concatenate([gram[: rank // 2], gram[rank // 2 :]], axis=1)
    parts = len(outs)
    empty = jnp.zeros_like(factor)
    sides = [
        jnp.concatenate([factor, empty], axis=0),
        jnp.concatenate([empty, factor], axis=0),
    ]
    for pair in range(pairs):
        for copy in copies[4 * pair : 4 * pair + 4]:
            copy.wait()
        for part in reversed(range(parts)):
            start = pl.multiple_of(lax.rem(me_ref[0] + part, parts) * rows, 16)
            place = pl.ds(start, rows)
            outs[part][pair * rows : (pair + 1) * rows, :] = dot(
                held[2 * pair, place, :], sides[0], NT
            ) + dot(held[2 * pair + 1, place, :], sides[1], NT)


def setup_kernel(parts, first, group, order_ref, *refs):
    lead_refs, refs = refs[:parts], refs[parts:]
    (own_ref, aux_ref, coupled_ref, dual_s_ref, dual_c_ref) = refs[:5]
    (inverse_ref, mover_ref, rho_ref, diagonal_ref, columns_ref, base_ref) = refs[5:]
    count, rank = own_ref.shape
    gram = summed(lead_refs, slice(first, None))
    gram = jnp.concatenate([gram[:, :rank], gram[:, rank:]], axis=0)
    eye = wide_eye(rank, 1)
    diagonal = jnp.sum(gram * eye, axis=0, keepdims=True)
    diagonal_ref[...] = jnp.broadcast_to(diagonal, diagonal_ref.shape)
    weights = own_ref[...]
    columns = weights.T
    columns_ref[...] = columns
    rho = jnp.sum(weights * weights * diagonal, axis=1, keepdims=True) / rank
    rho_ref[...] = jnp.broadcast_to(rho, rho_ref.shape)

    edge = 34.0 / 32.0
    lead = 4.0 * edge**3 / (4.0 * edge**3 - 3.0 * edge)
    mask = block_mask(rank, group)
    wide = wide_eye(rank, group)
    starts = range(0, count, group)
    systems = []
    for first in starts:
        scaled = []
        for k in range(first, first + group):
            unit = 1.0 / (34.0 * rho[k : k + 1, :])
            column = columns[:, k : k + 1]
            scaled.append(column * gram * weights[k : k + 1, :] * unit + (2.0 / 34.0) * eye)
        systems.append(jnp.concatenate(scaled, axis=1))
    inverses, rests = [], []
    for system in systems:
        rest = wide - system
        blocks = block_diagonal(rest, mask, group)
        (square,) = times_blocks([rest], blocks)
        (cube,) = times_blocks([square], blocks)
        inverses.append(wide + lead * (rest + square))
        rests.append(lead * cube - (lead - 1.0) * rest)
    for step in range(4):
        for at in range(len(systems)):
            blocks = block_diagonal(rests[at], mask, group)
            more, rests[at] = times_blocks([inverses[at], rests[at]], blocks)
            inverses[at] = inverses[at] + more
    for step in range(2):
        for at in range(len(systems)):
            (product,) = times_blocks([inverses[at]], block_diagonal(systems[at], mask, group))
            blocks = block_diagonal(wide - product, mask, group)
            (more,) = times_blocks([inverses[at]], blocks)
            inverses[at] = inverses[at] + more
    for k in range(count):
        place = (k % group) * rank
        unit = 1.0 / (34.0 * rho[k : k + 1, :])
        inverse = inverses[k // group][:, place : place + rank] * unit
        inverse_ref[k] = left_triple(inverse)
        base_ref[k] = dot(
            inverse_ref[k],
            right_triple(
                rho[k : k + 1, :] * (aux_ref[k] - dual_s_ref[k] + coupled_ref[k] - dual_c_ref[k])
            ),
        )
        both = jnp.concatenate([inverse * weights[k : k + 1, :]] * 2, axis=1)
        side = lax.div(lax.broadcasted_iota(jnp.int32, both.shape, 1), rank)
        both = jnp.where(side == lax.rem(order_ref[k], 2), both, 0.0)
        high, low = split(both)
        pair, place = stored_place(order_ref, k, count, rank)
        mover_ref[pair, place, :] = jnp.concatenate([high, high, low], axis=1)


def cross_blocks(lefts, rights, rank):
    group = len(lefts)
    wide = group * rank
    left = jnp.concatenate(split(jnp.concatenate(lefts, axis=0)), axis=0)
    right = left
    if rights is not lefts:
        right = jnp.concatenate(split(jnp.concatenate(rights, axis=0)), axis=0)
    total = dot(left, right, NT)
    total = total[:wide, :wide] + total[:wide, wide:] + total[wide:, :wide]
    return diagonal_blocks(total, rank, group)


def summed(refs, at):
    total = refs[0][at]
    for ref in refs[1:]:
        total = total + ref[at]
    return total


def stored_place(order_ref, k, count, rank):
    stored = lax.rem(order_ref[k], count)
    return lax.div(stored, 2), pl.ds(pl.multiple_of(lax.rem(stored, 2) * rank, rank), rank)


def move(mover, projected):
    high, low = split(projected)
    return dot(mover, jnp.concatenate([high, low, high], axis=1), NT)


def move_kernel(mover_ref, *refs):
    *projected_refs, moved_ref, turned_ref = refs
    rows = moved_ref.shape[2]
    for pair in range(moved_ref.shape[0]):
        projected = summed(projected_refs, slice(pair * rows, (pair + 1) * rows))
        moved_ref[pair] = move(mover_ref[pair], projected)
        turned_ref[pair] = projected.T


def first_kernel(group, order_ref, *refs):
    base_ref, mover_ref, dual_s_ref, dual_c_ref, early_ref = refs[2:7]
    *projected_refs, tall_ref, target_ref, gram_ref, moved = refs[7:]
    count, rank, rows = base_ref.shape
    early = early_ref.shape[0]
    for pair in range(early):
        moved[pair] = early_ref[pair]
    for pair in range(early, count // 2):
        place = slice((pair - early) * rows, (pair - early + 1) * rows)
        moved[pair] = move(mover_ref[pair], summed(projected_refs, place))
    talls = []
    for k in range(count):
        pair, place = stored_place(order_ref, k, count, rank)
        evolving = base_ref[k] + moved[pair, place, :]
        target_ref[k] = evolving + dual_s_ref[k]
        tall = evolving + dual_c_ref[k]
        tall_ref[k] = tall
        talls.append(tall)
        if len(talls) == group:
            gram_ref[k // group] = cross_blocks(talls, talls, rank)
            talls = []


def smooth(odd, now, targets, rho, inside_ref, near_ref, far_ref):
    count = len(targets)
    width = SWEEPS
    share = {j: 2.0 * smooth_weight / (rho[j] + 4.0 * smooth_weight) for j in rho}
    pull = {j: (rho[j] / (rho[j] + 4.0 * smooth_weight)) * targets[j] for j in range(count)}
    now = {j: now[j] for j in range(count)}
    for sweep in range(width):
        later = {}
        for j in range(-sweep - 1, count + sweep + 1):
            beside = [now[i] for i in (j - 1, j + 1) if i in now]
            total = beside[0] if len(beside) == 1 else beside[0] + beside[1]
            total = share[j] * total
            later[j] = total + pull[j] if j in pull else total
        now = later
    for j in range(count):
        inside_ref[j] = now[j]
    rows = inside_ref.shape[2]
    for j in range(width):
        lanes = slice((j % 2) * rows, (j % 2 + 1) * rows)
        near_ref[j // 2, :, lanes] = jnp.where(odd == 1, now[j - width], now[count + j])
        far_ref[j // 2, :, lanes] = jnp.where(odd == 1, now[count + j], now[j - width])


def all_rho(before_ref, rho_ref, after_ref):
    count = rho_ref.shape[0]
    rho = {j: rho_ref[j : j + 1, 0:1] for j in range(count)}
    for j in range(SWEEPS):
        rho[j - SWEEPS] = before_ref[count - SWEEPS + j : count - SWEEPS + j + 1, 0:1]
        rho[count + j] = after_ref[j : j + 1, 0:1]
    return rho


def smooth_kernel(
    odd_ref, order_ref, aux_ref, target_ref, before_ref, rho_ref, after_ref, diagonal_ref,
    columns_ref, early_ref, *refs
):
    *projected_refs, side_ref, past_ref, next_ref, inside_ref, near_ref, far_ref, turned = refs
    count, rank, rows = aux_ref.shape
    for source, place in ((before_ref, past_ref), (after_ref, next_ref)):
        weights = source[...]
        rho = jnp.sum(weights * weights * diagonal_ref[...], axis=1, keepdims=True) / rank
        place[...] = jnp.broadcast_to(rho, place.shape)
    rho = all_rho(past_ref, rho_ref, next_ref)
    slices = range(count)
    smooth(
        odd_ref[0], [aux_ref[k] for k in slices], [target_ref[k] for k in slices], rho,
        inside_ref, near_ref, far_ref,
    )
    early = early_ref.shape[0]
    for pair in range(early):
        turned[pair] = early_ref[pair]
    for pair in range(early, count // 2):
        place = slice((pair - early) * rows, (pair - early + 1) * rows)
        turned[pair] = summed(projected_refs, place).T
    for k in slices:
        pair, place = stored_place(order_ref, k, count, rank)
        side_ref[k] = columns_ref[:, k : k + 1] * turned[pair, place, :]


def polar(grams, delta):
    rank, wide = grams[0].shape
    group = wide // rank
    mask = block_mask(rank, group)
    eye = wide_eye(rank, group)
    delta_wide = jnp.concatenate([delta] * group, axis=1)
    delta_blocks = block_diagonal(delta_wide, mask, group, NT)
    (across,) = from_left(delta.T, [delta_wide])
    traces = []
    for gram in grams:
        line = jnp.broadcast_to(jnp.sum(across * gram, axis=0, keepdims=True), (16, wide))
        high, low = split(line)
        rest = (line - high.astype(f32) - low.astype(f32)).astype(bf16)
        line = dot(high, mask) + dot(low, mask) + dot(rest, mask)
        traces.append(line[0:1] + eps_trace)
    rights = [times_blocks([gram], delta_blocks, NT)[0] for gram in grams]
    normals = from_left(delta, rights)
    currents = [normal / trace for normal, trace in zip(normals, traces)]
    scales = [1.0 / jnp.sqrt(trace) for trace in traces]
    roots = []
    for step in range(POLAR):
        for at in range(len(grams)):
            product = currents[at]
            blocks = block_diagonal(product, mask, group)
            if step == 0:
                roots.append(1.5 * eye - 0.5 * product)
                (square,) = times_blocks([product], blocks)
            elif step < POLAR - 1:
                square, more = times_blocks([product, roots[at]], blocks)
                roots[at] = 1.5 * roots[at] - 0.5 * more
            else:
                (more,) = times_blocks([roots[at]], blocks)
                roots[at] = 1.5 * roots[at] - 0.5 * more
            if step < POLAR - 1:
                half = 1.5 * product - 0.5 * square
                (more,) = times_blocks([half], blocks)
                currents[at] = 1.5 * half - 0.5 * more
    return roots, scales, rights


def mix(roots, scales, rights, delta, mixed_ref, partial_ref):
    rank, wide = roots[0].shape
    group = wide // rank
    mask = block_mask(rank, group)
    delta_blocks = block_diagonal(jnp.concatenate([delta] * group, axis=1), mask, group)
    left, right = [], []
    for at in range(len(roots)):
        high, low = split(roots[at] * scales[at])
        left += [high, high, low]
        high, low = split(rights[at])
        right += [high, low, high]
    partial = dot(jnp.concatenate(right, axis=1), jnp.concatenate(left, axis=1), NT)
    for at in range(len(roots)):
        (mixed,) = times_blocks([roots[at]], delta_blocks)
        mixed_ref[at] = mixed * scales[at]
    half = rank // 2
    partial_ref[...] = jnp.concatenate([partial[:half], partial[half:]], axis=1)


def first_polar_kernel(after_ref, delta_ref, *refs):
    *gram_refs, mixed_ref, partial_ref, gram_ref = refs
    grams = [summed(gram_refs, at) for at in range(gram_ref.shape[0])]
    for at in range(len(grams)):
        gram_ref[at] = grams[at]
    delta = delta_ref[...]
    mix(*polar(grams, delta), delta, mixed_ref, partial_ref)


def later_polar_kernel(last, after_ref, delta_ref, change_ref, old_ref, *refs):
    if last:
        *cross_refs, mixed_ref, partial_ref = refs
    else:
        *cross_refs, mixed_ref, partial_ref, gram_ref = refs
    groups, rank, wide = old_ref.shape
    group = wide // rank
    mask = block_mask(rank, group)
    grams = []
    for at in range(groups):
        cross = summed(cross_refs, at)
        change = change_ref[at]
        (onward,) = times_blocks([change], block_diagonal(old_ref[at], mask, group))
        onward = cross[:, :wide] + 0.5 * onward
        (one,) = times_blocks([onward], block_diagonal(change, mask, group, NT), NT)
        (other,) = times_blocks([change], block_diagonal(onward, mask, group, NT), NT)
        grams.append(cross[:, wide:] + one + other)
        if not last:
            gram_ref[at] = grams[at]
    delta = delta_ref[...]
    mix(*polar(grams, delta), delta, mixed_ref, partial_ref)


def ahead_kernel(
    group, odd_ref, after_ref, inside_ref, near_ref, far_ref, target_ref, tall_ref, side_ref, rho_ref,
    inverse_ref, known_ref, cross_ref, *kept
):
    count, rank, rows = inside_ref.shape
    width = SWEEPS
    knowns, talls = [], []
    for k in range(count):
        aux = inside_ref[k]
        for at, mine, other in ((k, near_ref, far_ref), (k - count + width, far_ref, near_ref)):
            if 0 <= at < width:
                lanes = slice((at % 2) * rows, (at % 2 + 1) * rows)
                aux = aux + jnp.where(
                    odd_ref[0] == 1, mine[at // 2, :, lanes], other[at // 2, :, lanes]
                )
        target, tall = target_ref[k], tall_ref[k]
        if kept:
            aux_ref, dual_ref = kept
            aux_ref[k] = aux
            dual_ref[k] = target - aux
        known = dot(
            inverse_ref[k],
            right_triple(side_ref[k] + rho_ref[k : k + 1, 0:1] * (2.0 * aux - target - tall)),
        )
        known_ref[k] = known
        talls.append(tall)
        knowns.append(known + tall)
        if len(talls) == group:
            cross_ref[k // group] = jnp.concatenate(
                [cross_blocks(knowns, talls, rank), cross_blocks(knowns, knowns, rank)], axis=1
            )
            knowns, talls = [], []


def add_kernel(unread, *refs):
    *term_refs, total_ref = refs[unread:]
    total = term_refs[0][...]
    for ref in term_refs[1:]:
        total = total + ref[...]
    total_ref[...] = total


def new_delta(sum_refs, total, rank):
    packed = sum_refs[0][...]
    for ref in sum_refs[1:]:
        packed = packed + ref[...]
    packed = packed / total
    return jnp.concatenate([packed[:, :rank], packed[:, rank:]], axis=0)


def mixer_kernel(total, mixed_ref, inverse_ref, rho_ref, *refs):
    *sum_refs, delta_ref, change_ref, forward_ref = refs
    groups, rank, wide = mixed_ref.shape
    group = wide // rank
    turned = new_delta(sum_refs, total, rank)
    delta_ref[...] = turned.T
    mixers = from_left(turned, [mixed_ref[at] for at in range(groups)])
    place = lax.div(lax.broadcasted_iota(jnp.int32, (1, wide), 1), rank)
    for at in range(groups):
        mixer = mixers[at]
        slices = range(at * group, (at + 1) * group)
        inverses = jnp.concatenate([inverse_ref[k] for k in slices], axis=0)
        onward = diagonal_blocks(dot(inverses, right_triple(mixer)), rank, group)
        rho = rho_ref[at * group : at * group + 1, 0:1]
        for k in slices[1:]:
            rho = jnp.where(place == k - at * group, rho_ref[k : k + 1, 0:1], rho)
        forward = 2.0 * rho * onward
        forward_ref[at] = forward
        change_ref[at] = forward - mixer


def rows_kernel(odd_ref, aux_ref, before_ref, rho_ref, after_ref, *refs):
    (change_ref, forward_ref, tall_ref, known_ref, dual_ref) = refs[:5]
    (next_ref, target_ref, inside_ref, near_ref, far_ref) = refs[5:]
    targets = new_rows(change_ref, forward_ref, tall_ref, known_ref, next_ref)
    count = len(targets)
    for k in range(count):
        targets[k] = targets[k] + dual_ref[k]
        target_ref[k] = targets[k]
    rho = all_rho(before_ref, rho_ref, after_ref)
    smooth(
        odd_ref[0], [aux_ref[k] for k in range(count)], targets, rho,
        inside_ref, near_ref, far_ref,
    )


def last_rows_kernel(mixed_ref, change_ref, forward_ref, tall_ref, known_ref, *outs):
    mixed_tall_ref, evolving_ref, next_ref = outs
    evolvings = new_rows(change_ref, forward_ref, tall_ref, known_ref, next_ref)
    groups, rank, wide = mixed_ref.shape
    group = wide // rank
    for k in range(len(evolvings)):
        evolving_ref[k] = evolvings[k]
        place = (k % group) * rank
        mixed = left_triple(mixed_ref[k // group][:, place : place + rank])
        mixed_tall_ref[k] = right_triple(dot(mixed, right_triple(next_ref[k])))


def new_rows(change_ref, forward_ref, tall_ref, known_ref, next_ref):
    groups, rank, wide = change_ref.shape
    group = wide // rank
    evolvings = []
    for k in range(groups * group):
        lanes = slice((k % group) * rank, (k % group + 1) * rank)
        change, forward = change_ref[k // group][:, lanes], forward_ref[k // group][:, lanes]
        left = jnp.concatenate([left_triple(change), left_triple(forward)], axis=0)
        tall, known = tall_ref[k], known_ref[k]
        both = dot(left, right_triple(tall))
        next_ref[k] = known + tall + both[:rank]
        evolvings.append(known + both[rank:])
    return evolvings


def last_kernel(total, mixed_tall_ref, *refs):
    *sum_refs, coupled_ref, delta_ref = refs
    turned = new_delta(sum_refs, total, delta_ref.shape[0])
    delta_ref[...] = turned.T
    delta_left = left_triple(turned)
    for k in range(coupled_ref.shape[0]):
        coupled_ref[k] = dot(delta_left, mixed_tall_ref[k])


per_microsecond = 1_100_000_000


def call(
    kernel, name, outs, *args, scalars=0, unread=0, microseconds=0.3, limit=16, scratch=()
):
    flops = int(microseconds * per_microsecond)
    specs = [pl.BlockSpec(memory_space=pltpu.SMEM)] * scalars
    specs += [pl.BlockSpec(memory_space=pl.ANY)] * unread
    specs += [pl.BlockSpec(memory_space=pltpu.VMEM)] * (len(args) - len(specs))
    shapes = [jax.ShapeDtypeStruct(shape, dtype) for shape, dtype in outs]
    moved = sum(arg.size * arg.dtype.itemsize for arg in args)
    moved += sum(shape.size * shape.dtype.itemsize for shape in shapes)
    return pl.pallas_call(
        kernel,
        out_shape=shapes,
        in_specs=specs,
        out_specs=[pl.BlockSpec(memory_space=pltpu.VMEM)] * len(shapes),
        scratch_shapes=list(scratch),
        compiler_params=pltpu.CompilerParams(vmem_limit_bytes=limit * 1024 * 1024),
        cost_estimate=pl.CostEstimate(flops=flops, bytes_accessed=moved, transcendentals=0),
        name=name,
    )(*args)


def rotated(value, axis, shift):
    count = lax.axis_size(axis)
    return lax.ppermute(value, axis, [(i, (i + shift) % count) for i in range(count)])


def swapped(value, axis, first):
    count = lax.axis_size(axis)
    pairs = [((i + first) % count, (i + first + 1) % count) for i in range(0, count, 2)]
    return lax.ppermute(value, axis, pairs + [(b, a) for a, b in pairs])


def from_others(value, axis):
    return [rotated(value, axis, shift) for shift in range(1, lax.axis_size(axis))]


def stage_sizes(count):
    sizes = []
    while count > 1:
        sizes.append(next(size for size in (4, 2, 3, 5, 7, count) if count % size == 0))
        count //= sizes[-1]
    return sizes


def in_stages(value, axis, beside=None):
    count = lax.axis_size(axis)
    stride = 1
    terms, firsts = [value], []
    for size in stage_sizes(count):
        value = terms[0]
        if len(terms) > 1:
            unread = [] if beside is None else [beside]
            (value,) = call(
                functools.partial(add_kernel, len(unread)),
                "add",
                [(value.shape, f32)],
                *unread, *terms,
                unread=len(unread),
            )
        terms = [value]
        for shift in range(1, size):
            moves = []
            for i in range(count):
                digit = (i // stride) % size
                other = digit ^ shift if size in (2, 4) else (digit + shift) % size
                moves.append((i, i + (other - digit) * stride))
            terms.append(lax.ppermute(value, axis, moves))
        stride *= size
        firsts = firsts or terms
    return terms, firsts


def body(
    data, order, chan_factor, slice_weights, smooth_aux, coupled, smooth_dual, coupling_dual, delta
):
    count, all_rows, channels = data.shape
    rank = chan_factor.shape[1]
    rows = smooth_aux.shape[1]
    parts = lax.axis_size("chan")
    total = count * lax.axis_size("cuts")
    group = group_size(count, rank)
    groups = count // group
    wide = group * rank
    flip = lambda value: jnp.swapaxes(value, 1, 2)
    aux, coup, dual_s, dual_c = map(flip, (smooth_aux, coupled, smooth_dual, coupling_dual))
    factor = chan_factor.T
    state = ((count, rank, rows), f32)
    quads = ((groups, rank, wide), f32)
    square = ((rank, rank), f32)
    halo = (((SWEEPS + 1) // 2, rank, 2 * rows), f32)
    lanes = lambda height: ((height, 128), f32)
    scale = ((groups, 8, wide), f32)

    me = lax.axis_index("chan").astype(jnp.int32).reshape(1)
    odd = lax.rem(lax.axis_index("cuts"), 2).astype(jnp.int32).reshape(1)
    early = max(1, count // 8)
    own, received = [], []
    for first, pairs, lead in ((0, early, True), (2 * early, count // 2 - early, False)):
        height = pairs * rows + (rank // 2 if lead else 0)
        projected = call(
            functools.partial(project_kernel, first, pairs, rows, lead),
            "project",
            [((height, 2 * rank), f32)] * parts + [(factor.shape, factor.dtype)] * lead,
            me, data, factor,
            scalars=1, unread=1, microseconds=2, limit=52,
            scratch=[
                pltpu.VMEM((2 * pairs, all_rows, channels), data.dtype),
                pltpu.SemaphoreType.DMA((4 * pairs,)),
            ],
        )
        if lead:
            *projected, factor = projected
        own.append(projected[0])
        received.append([rotated(projected[shift], "chan", shift) for shift in range(1, parts)])

    late_weights, _ = lax.optimization_barrier((slice_weights, own[-1]))
    before = rotated(late_weights, "cuts", 1)
    after = rotated(late_weights, "cuts", -1)
    inverse, mover, rho, diagonal, columns, base = call(
        functools.partial(setup_kernel, parts, early * rows, group),
        "setup",
        [
            ((count, rank, 3 * rank), bf16),
            ((count // 2, 2 * rank, 6 * rank), bf16),
            lanes(count),
            ((count, rank), f32),
            ((rank, count), f32),
            state,
        ],
        order, own[0], *received[0], slice_weights, aux, coup, dual_s, dual_c,
        scalars=1,
    )
    half_state = ((early, 2 * rank, rows), f32)
    moved, turned = call(
        move_kernel, "move", [half_state, half_state], mover, own[0], *received[0]
    )
    tall, target, gram = call(
        functools.partial(first_kernel, group),
        "first",
        [state, state, quads],
        order, before, after, base, mover, dual_s, dual_c, moved, own[1], *received[1],
        scalars=1, unread=2,
        scratch=[pltpu.VMEM((count // 2, 2 * rank, rows), f32)],
    )
    side, before, after, inside, to_near, to_far = call(
        smooth_kernel,
        "smooth",
        [state, lanes(count), lanes(count), state, halo, halo],
        odd, order, aux, target, before, rho, after, diagonal, columns, turned, own[1],
        *received[1],
        scalars=2,
        scratch=[pltpu.VMEM((count // 2, 2 * rank, rows), f32)],
    )
    polar_outs = [quads, ((rank // 2, 2 * rank), f32), quads]
    for inner in range(INNER):
        if inner == 0:
            mixed, partial, gram = call(
                first_polar_kernel,
                "polar",
                polar_outs,
                inside, delta, gram, *from_others(gram, "chan"),
                unread=1, microseconds=3,
            )
        else:
            last = inner == INNER - 1
            mixed, partial, *gram = call(
                functools.partial(later_polar_kernel, last),
                "polar",
                polar_outs[:2] if last else polar_outs,
                inside, delta, change, old, cross, *crosses,
                unread=1,
            )
            gram = gram[0] if gram else None
        if inner == INNER - 1:
            mixed_tall, evolving = call(
                last_rows_kernel,
                "rows",
                [((count, 3 * rank, rows), bf16), state],
                mixed, change, forward, tall, known,
                scratch=[pltpu.VMEM(state[0], f32)],
            )
            coup, delta = call(
                functools.partial(last_kernel, total),
                "last",
                [state, square],
                mixed_tall, *in_stages(partial, "cuts")[0],
            )
            continue
        near = swapped(to_near, "cuts", 0)
        far = swapped(to_far, "cuts", 1)
        known, cross, *kept = call(
            functools.partial(ahead_kernel, group),
            "ahead",
            [state, ((groups, rank, 2 * wide), f32)] + [state] * (2 if inner < INNER - 2 else 0),
            odd, partial, inside, near, far, target, tall, side, rho, inverse,
            scalars=1, unread=1,
        )
        sums, firsts = in_stages(partial, "cuts", beside=cross)
        _, cross = lax.optimization_barrier((firsts, cross))
        crosses = from_others(cross, "chan")
        old = gram
        delta, change, forward = call(
            functools.partial(mixer_kernel, total),
            "mixer",
            [square, quads, quads],
            mixed, inverse, rho, *sums,
        )
        if inner < INNER - 2:
            tall, target, inside, to_near, to_far = call(
                rows_kernel,
                "rows",
                [state, state, state, halo, halo],
                odd, kept[0], before, rho, after, change, forward, tall, known, kept[1],
                scalars=1,
            )
    return (flip(evolving), flip(coup), delta)


def solution(mesh):
    return jax.shard_map(
        body,
        mesh=mesh,
        in_specs=(
            P("cuts", None, "chan"),
            P("cuts"),
            P("chan", None),
            P("cuts", None),
            P("cuts", "chan", None),
            P("cuts", "chan", None),
            P("cuts", "chan", None),
            P("cuts", "chan", None),
            P(),
        ),
        out_specs=(P("cuts", "chan", None), P("cuts", "chan", None), P()),
        check_vma=False,
    )
```

```python
import functools

import jax
import jax.numpy as jnp
from jax import lax
from jax.experimental import pallas as pl
from jax.experimental.pallas import tpu as pltpu
from jax.sharding import PartitionSpec as P

INNER = 3
SWEEPS = 4
POLAR = 8

smooth_weight = 1.0
eps_trace = 1e-06
f32 = jnp.float32
bf16 = jnp.bfloat16
NN = (((1,), (0,)), ((), ()))
NT = (((1,), (1,)), ((), ()))


def dot(left, right, dims=NN):
    return lax.dot_general(left, right, dims, preferred_element_type=f32)


def split(value):
    high = value.astype(bf16)
    low = (value - high.astype(f32)).astype(bf16)
    return high, low


def left_triple(value):
    high, low = split(value)
    return jnp.concatenate([high, high, low], axis=1)


def right_triple(value):
    high, low = split(value)
    return jnp.concatenate([high, low, high], axis=0)


def block_mask(rank, group):
    wide = rank * group
    rows = lax.div(lax.broadcasted_iota(jnp.int32, (wide, wide), 0), rank)
    cols = lax.div(lax.broadcasted_iota(jnp.int32, (wide, wide), 1), rank)
    return jnp.where(rows == cols, 1.0, 0.0).astype(bf16)


def wide_eye(rank, group):
    rows = lax.broadcasted_iota(jnp.int32, (rank, rank * group), 0)
    cols = lax.broadcasted_iota(jnp.int32, (rank, rank * group), 1)
    return jnp.where(rows == lax.rem(cols, rank), 1.0, 0.0).astype(f32)


def block_diagonal(value, mask, group, dims=NN):
    high, low = split(value)
    high = jnp.concatenate([high] * group, axis=0) * mask
    low = jnp.concatenate([low] * group, axis=0) * mask
    empty = jnp.zeros_like(high)
    one, other = ([high, low], [high, empty]) if dims == NN else ([high, high], [low, empty])
    return jnp.concatenate(
        [jnp.concatenate(one, axis=1), jnp.concatenate(other, axis=1)], axis=0
    )


def times_blocks(values, blocks, dims=NN):
    rank, wide = values[0].shape
    left = [jnp.concatenate(split(value), axis=1) for value in values]
    total = dot(jnp.concatenate(left, axis=0), blocks, dims)
    total = total[:, :wide] + total[:, wide:]
    return [total[at * rank : (at + 1) * rank] for at in range(len(values))]


def diagonal_blocks(value, rank, group):
    at = lax.div(lax.broadcasted_iota(jnp.int32, (rank, rank * group), 1), rank)
    total = value[:rank]
    for block in range(1, group):
        total = jnp.where(at == block, value[block * rank : (block + 1) * rank], total)
    return total


def from_left(left, values):
    wide = values[0].shape[1]
    total = dot(left_triple(left), right_triple(jnp.concatenate(values, axis=1)))
    return [total[:, at * wide : (at + 1) * wide] for at in range(len(values))]


def group_size(count, rank):
    group = max(1, 128 // rank)
    while count % group:
        group -= 1
    return group


def project_kernel(first, pairs, rows, lead, me_ref, data_ref, factor_ref, *refs):
    *outs, held, arrived = refs
    half = data_ref.shape[1] // 2
    copies = []
    for k in range(2 * pairs):
        for at in range(2):
            place = pl.ds(at * half, half)
            copies.append(
                pltpu.make_async_copy(
                    data_ref.at[first + k, place, :], held.at[k, place, :], arrived.at[2 * k + at]
                )
            )
            copies[-1].start()
    factor = factor_ref[...]
    rank = factor.shape[0]
    if lead:
        *outs, again_ref = outs
        again_ref[...] = factor
        gram = dot(factor, factor, NT)
        for out in outs:
            out[pairs * rows :, :] = jnp.concatenate([gram[: rank // 2], gram[rank // 2 :]], axis=1)
    parts = len(outs)
    empty = jnp.zeros_like(factor)
    sides = [
        jnp.concatenate([factor, empty], axis=0),
        jnp.concatenate([empty, factor], axis=0),
    ]
    for pair in range(pairs):
        for copy in copies[4 * pair : 4 * pair + 4]:
            copy.wait()
        for part in reversed(range(parts)):
            start = pl.multiple_of(lax.rem(me_ref[0] + part, parts) * rows, 16)
            place = pl.ds(start, rows)
            outs[part][pair * rows : (pair + 1) * rows, :] = dot(
                held[2 * pair, place, :], sides[0], NT
            ) + dot(held[2 * pair + 1, place, :], sides[1], NT)


def setup_kernel(parts, first, group, order_ref, *refs):
    lead_refs, refs = refs[:parts], refs[parts:]
    (own_ref, aux_ref, coupled_ref, dual_s_ref, dual_c_ref) = refs[:5]
    (inverse_ref, mover_ref, rho_ref, diagonal_ref, columns_ref, base_ref) = refs[5:]
    count, rank = own_ref.shape
    gram = summed(lead_refs, slice(first, None))
    gram = jnp.concatenate([gram[:, :rank], gram[:, rank:]], axis=0)
    eye = wide_eye(rank, 1)
    diagonal = jnp.sum(gram * eye, axis=0, keepdims=True)
    diagonal_ref[...] = jnp.broadcast_to(diagonal, diagonal_ref.shape)
    weights = own_ref[...]
    columns = weights.T
    columns_ref[...] = columns
    rho = jnp.sum(weights * weights * diagonal, axis=1, keepdims=True) / rank
    rho_ref[...] = jnp.broadcast_to(rho, rho_ref.shape)

    edge = 34.0 / 32.0
    lead = 4.0 * edge**3 / (4.0 * edge**3 - 3.0 * edge)
    mask = block_mask(rank, group)
    wide = wide_eye(rank, group)
    starts = range(0, count, group)
    systems = []
    for first in starts:
        scaled = []
        for k in range(first, first + group):
            unit = 1.0 / (34.0 * rho[k : k + 1, :])
            column = columns[:, k : k + 1]
            scaled.append(column * gram * weights[k : k + 1, :] * unit + (2.0 / 34.0) * eye)
        systems.append(jnp.concatenate(scaled, axis=1))
    inverses, rests = [], []
    for system in systems:
        rest = wide - system
        blocks = block_diagonal(rest, mask, group)
        (square,) = times_blocks([rest], blocks)
        (cube,) = times_blocks([square], blocks)
        inverses.append(wide + lead * (rest + square))
        rests.append(lead * cube - (lead - 1.0) * rest)
    for step in range(4):
        for at in range(len(systems)):
            blocks = block_diagonal(rests[at], mask, group)
            more, rests[at] = times_blocks([inverses[at], rests[at]], blocks)
            inverses[at] = inverses[at] + more
    for step in range(2):
        for at in range(len(systems)):
            (product,) = times_blocks([inverses[at]], block_diagonal(systems[at], mask, group))
            blocks = block_diagonal(wide - product, mask, group)
            (more,) = times_blocks([inverses[at]], blocks)
            inverses[at] = inverses[at] + more
    for k in range(count):
        place = (k % group) * rank
        unit = 1.0 / (34.0 * rho[k : k + 1, :])
        inverse = inverses[k // group][:, place : place + rank] * unit
        inverse_ref[k] = left_triple(inverse)
        base_ref[k] = dot(
            inverse_ref[k],
            right_triple(
                rho[k : k + 1, :] * (aux_ref[k] - dual_s_ref[k] + coupled_ref[k] - dual_c_ref[k])
            ),
        )
        both = jnp.concatenate([inverse * weights[k : k + 1, :]] * 2, axis=1)
        side = lax.div(lax.broadcasted_iota(jnp.int32, both.shape, 1), rank)
        both = jnp.where(side == lax.rem(order_ref[k], 2), both, 0.0)
        high, low = split(both)
        pair, place = stored_place(order_ref, k, count, rank)
        mover_ref[pair, place, :] = jnp.concatenate([high, high, low], axis=1)


def cross_blocks(lefts, rights, rank):
    group = len(lefts)
    wide = group * rank
    left = jnp.concatenate(split(jnp.concatenate(lefts, axis=0)), axis=0)
    right = left
    if rights is not lefts:
        right = jnp.concatenate(split(jnp.concatenate(rights, axis=0)), axis=0)
    total = dot(left, right, NT)
    total = total[:wide, :wide] + total[:wide, wide:] + total[wide:, :wide]
    return diagonal_blocks(total, rank, group)


def summed(refs, at):
    total = refs[0][at]
    for ref in refs[1:]:
        total = total + ref[at]
    return total


def stored_place(order_ref, k, count, rank):
    stored = lax.rem(order_ref[k], count)
    return lax.div(stored, 2), pl.ds(pl.multiple_of(lax.rem(stored, 2) * rank, rank), rank)


def move(mover, projected):
    high, low = split(projected)
    return dot(mover, jnp.concatenate([high, low, high], axis=1), NT)


def move_kernel(mover_ref, *refs):
    *projected_refs, moved_ref, turned_ref = refs
    rows = moved_ref.shape[2]
    for pair in range(moved_ref.shape[0]):
        projected = summed(projected_refs, slice(pair * rows, (pair + 1) * rows))
        moved_ref[pair] = move(mover_ref[pair], projected)
        turned_ref[pair] = projected.T


def first_kernel(group, order_ref, *refs):
    base_ref, mover_ref, dual_s_ref, dual_c_ref, early_ref = refs[2:7]
    *projected_refs, tall_ref, target_ref, gram_ref, moved = refs[7:]
    count, rank, rows = base_ref.shape
    early = early_ref.shape[0]
    for pair in range(early):
        moved[pair] = early_ref[pair]
    for pair in range(early, count // 2):
        place = slice((pair - early) * rows, (pair - early + 1) * rows)
        moved[pair] = move(mover_ref[pair], summed(projected_refs, place))
    talls = []
    for k in range(count):
        pair, place = stored_place(order_ref, k, count, rank)
        evolving = base_ref[k] + moved[pair, place, :]
        target_ref[k] = evolving + dual_s_ref[k]
        tall = evolving + dual_c_ref[k]
        tall_ref[k] = tall
        talls.append(tall)
        if len(talls) == group:
            gram_ref[k // group] = cross_blocks(talls, talls, rank)
            talls = []


def smooth(odd, now, targets, rho, inside_ref, near_ref, far_ref):
    count = len(targets)
    width = SWEEPS
    share = {j: 2.0 * smooth_weight / (rho[j] + 4.0 * smooth_weight) for j in rho}
    pull = {j: (rho[j] / (rho[j] + 4.0 * smooth_weight)) * targets[j] for j in range(count)}
    now = {j: now[j] for j in range(count)}
    for sweep in range(width):
        later = {}
        for j in range(-sweep - 1, count + sweep + 1):
            beside = [now[i] for i in (j - 1, j + 1) if i in now]
            total = beside[0] if len(beside) == 1 else beside[0] + beside[1]
            total = share[j] * total
            later[j] = total + pull[j] if j in pull else total
        now = later
    for j in range(count):
        inside_ref[j] = now[j]
    rows = inside_ref.shape[2]
    for j in range(width):
        lanes = slice((j % 2) * rows, (j % 2 + 1) * rows)
        near_ref[j // 2, :, lanes] = jnp.where(odd == 1, now[j - width], now[count + j])
        far_ref[j // 2, :, lanes] = jnp.where(odd == 1, now[count + j], now[j - width])


def all_rho(before_ref, rho_ref, after_ref):
    count = rho_ref.shape[0]
    rho = {j: rho_ref[j : j + 1, 0:1] for j in range(count)}
    for j in range(SWEEPS):
        rho[j - SWEEPS] = before_ref[count - SWEEPS + j : count - SWEEPS + j + 1, 0:1]
        rho[count + j] = after_ref[j : j + 1, 0:1]
    return rho


def smooth_kernel(
    odd_ref, order_ref, aux_ref, target_ref, before_ref, rho_ref, after_ref, diagonal_ref,
    columns_ref, early_ref, *refs
):
    *projected_refs, side_ref, past_ref, next_ref, inside_ref, near_ref, far_ref, turned = refs
    count, rank, rows = aux_ref.shape
    for source, place in ((before_ref, past_ref), (after_ref, next_ref)):
        weights = source[...]
        rho = jnp.sum(weights * weights * diagonal_ref[...], axis=1, keepdims=True) / rank
        place[...] = jnp.broadcast_to(rho, place.shape)
    rho = all_rho(past_ref, rho_ref, next_ref)
    slices = range(count)
    smooth(
        odd_ref[0], [aux_ref[k] for k in slices], [target_ref[k] for k in slices], rho,
        inside_ref, near_ref, far_ref,
    )
    early = early_ref.shape[0]
    for pair in range(early):
        turned[pair] = early_ref[pair]
    for pair in range(early, count // 2):
        place = slice((pair - early) * rows, (pair - early + 1) * rows)
        turned[pair] = summed(projected_refs, place).T
    for k in slices:
        pair, place = stored_place(order_ref, k, count, rank)
        side_ref[k] = columns_ref[:, k : k + 1] * turned[pair, place, :]


def polar(grams, delta):
    rank, wide = grams[0].shape
    group = wide // rank
    mask = block_mask(rank, group)
    eye = wide_eye(rank, group)
    delta_wide = jnp.concatenate([delta] * group, axis=1)
    delta_blocks = block_diagonal(delta_wide, mask, group, NT)
    (across,) = from_left(delta.T, [delta_wide])
    traces = []
    for gram in grams:
        line = jnp.broadcast_to(jnp.sum(across * gram, axis=0, keepdims=True), (16, wide))
        high, low = split(line)
        rest = (line - high.astype(f32) - low.astype(f32)).astype(bf16)
        line = dot(high, mask) + dot(low, mask) + dot(rest, mask)
        traces.append(line[0:1] + eps_trace)
    rights = [times_blocks([gram], delta_blocks, NT)[0] for gram in grams]
    normals = from_left(delta, rights)
    currents = [normal / trace for normal, trace in zip(normals, traces)]
    scales = [1.0 / jnp.sqrt(trace) for trace in traces]
    roots = []
    for step in range(POLAR):
        for at in range(len(grams)):
            product = currents[at]
            blocks = block_diagonal(product, mask, group)
            if step == 0:
                roots.append(1.5 * eye - 0.5 * product)
                (square,) = times_blocks([product], blocks)
            elif step < POLAR - 1:
                square, more = times_blocks([product, roots[at]], blocks)
                roots[at] = 1.5 * roots[at] - 0.5 * more
            else:
                (more,) = times_blocks([roots[at]], blocks)
                roots[at] = 1.5 * roots[at] - 0.5 * more
            if step < POLAR - 1:
                half = 1.5 * product - 0.5 * square
                (more,) = times_blocks([half], blocks)
                currents[at] = 1.5 * half - 0.5 * more
    return roots, scales, rights


def mix(roots, scales, rights, delta, mixed_ref, partial_ref):
    rank, wide = roots[0].shape
    group = wide // rank
    mask = block_mask(rank, group)
    delta_blocks = block_diagonal(jnp.concatenate([delta] * group, axis=1), mask, group)
    left, right = [], []
    for at in range(len(roots)):
        high, low = split(roots[at] * scales[at])
        left += [high, high, low]
        high, low = split(rights[at])
        right += [high, low, high]
    partial = dot(jnp.concatenate(right, axis=1), jnp.concatenate(left, axis=1), NT)
    for at in range(len(roots)):
        (mixed,) = times_blocks([roots[at]], delta_blocks)
        mixed_ref[at] = mixed * scales[at]
    half = rank // 2
    partial_ref[...] = jnp.concatenate([partial[:half], partial[half:]], axis=1)


def first_polar_kernel(after_ref, delta_ref, *refs):
    *gram_refs, mixed_ref, partial_ref, gram_ref = refs
    grams = [summed(gram_refs, at) for at in range(gram_ref.shape[0])]
    for at in range(len(grams)):
        gram_ref[at] = grams[at]
    delta = delta_ref[...]
    mix(*polar(grams, delta), delta, mixed_ref, partial_ref)


def later_polar_kernel(last, after_ref, delta_ref, change_ref, old_ref, *refs):
    if last:
        *cross_refs, mixed_ref, partial_ref = refs
    else:
        *cross_refs, mixed_ref, partial_ref, gram_ref = refs
    groups, rank, wide = old_ref.shape
    group = wide // rank
    mask = block_mask(rank, group)
    grams = []
    for at in range(groups):
        cross = summed(cross_refs, at)
        change = change_ref[at]
        (onward,) = times_blocks([change], block_diagonal(old_ref[at], mask, group))
        onward = cross[:, :wide] + 0.5 * onward
        (one,) = times_blocks([onward], block_diagonal(change, mask, group, NT), NT)
        (other,) = times_blocks([change], block_diagonal(onward, mask, group, NT), NT)
        grams.append(cross[:, wide:] + one + other)
        if not last:
            gram_ref[at] = grams[at]
    delta = delta_ref[...]
    mix(*polar(grams, delta), delta, mixed_ref, partial_ref)


def ahead_kernel(
    group, odd_ref, after_ref, inside_ref, near_ref, far_ref, target_ref, tall_ref, side_ref, rho_ref,
    inverse_ref, known_ref, cross_ref, *kept
):
    count, rank, rows = inside_ref.shape
    width = SWEEPS
    knowns, talls = [], []
    for k in range(count):
        aux = inside_ref[k]
        for at, mine, other in ((k, near_ref, far_ref), (k - count + width, far_ref, near_ref)):
            if 0 <= at < width:
                lanes = slice((at % 2) * rows, (at % 2 + 1) * rows)
                aux = aux + jnp.where(
                    odd_ref[0] == 1, mine[at // 2, :, lanes], other[at // 2, :, lanes]
                )
        target, tall = target_ref[k], tall_ref[k]
        if kept:
            aux_ref, dual_ref = kept
            aux_ref[k] = aux
            dual_ref[k] = target - aux
        known = dot(
            inverse_ref[k],
            right_triple(side_ref[k] + rho_ref[k : k + 1, 0:1] * (2.0 * aux - target - tall)),
        )
        known_ref[k] = known
        talls.append(tall)
        knowns.append(known + tall)
        if len(talls) == group:
            cross_ref[k // group] = jnp.concatenate(
                [cross_blocks(knowns, talls, rank), cross_blocks(knowns, knowns, rank)], axis=1
            )
            knowns, talls = [], []


def add_kernel(unread, *refs):
    *term_refs, total_ref = refs[unread:]
    total = term_refs[0][...]
    for ref in term_refs[1:]:
        total = total + ref[...]
    total_ref[...] = total


def new_delta(sum_refs, total, rank):
    packed = sum_refs[0][...]
    for ref in sum_refs[1:]:
        packed = packed + ref[...]
    packed = packed / total
    return jnp.concatenate([packed[:, :rank], packed[:, rank:]], axis=0)


def mixer_kernel(total, mixed_ref, inverse_ref, rho_ref, *refs):
    *sum_refs, delta_ref, change_ref, forward_ref = refs
    groups, rank, wide = mixed_ref.shape
    group = wide // rank
    turned = new_delta(sum_refs, total, rank)
    delta_ref[...] = turned.T
    mixers = from_left(turned, [mixed_ref[at] for at in range(groups)])
    place = lax.div(lax.broadcasted_iota(jnp.int32, (1, wide), 1), rank)
    for at in range(groups):
        mixer = mixers[at]
        slices = range(at * group, (at + 1) * group)
        inverses = jnp.concatenate([inverse_ref[k] for k in slices], axis=0)
        onward = diagonal_blocks(dot(inverses, right_triple(mixer)), rank, group)
        rho = rho_ref[at * group : at * group + 1, 0:1]
        for k in slices[1:]:
            rho = jnp.where(place == k - at * group, rho_ref[k : k + 1, 0:1], rho)
        forward = 2.0 * rho * onward
        forward_ref[at] = forward
        change_ref[at] = forward - mixer


def rows_kernel(odd_ref, aux_ref, before_ref, rho_ref, after_ref, *refs):
    (change_ref, forward_ref, tall_ref, known_ref, dual_ref) = refs[:5]
    (next_ref, target_ref, inside_ref, near_ref, far_ref) = refs[5:]
    targets = new_rows(change_ref, forward_ref, tall_ref, known_ref, next_ref)
    count = len(targets)
    for k in range(count):
        targets[k] = targets[k] + dual_ref[k]
        target_ref[k] = targets[k]
    rho = all_rho(before_ref, rho_ref, after_ref)
    smooth(
        odd_ref[0], [aux_ref[k] for k in range(count)], targets, rho,
        inside_ref, near_ref, far_ref,
    )


def last_rows_kernel(mixed_ref, change_ref, forward_ref, tall_ref, known_ref, *outs):
    mixed_tall_ref, evolving_ref, next_ref = outs
    evolvings = new_rows(change_ref, forward_ref, tall_ref, known_ref, next_ref)
    groups, rank, wide = mixed_ref.shape
    group = wide // rank
    for k in range(len(evolvings)):
        evolving_ref[k] = evolvings[k]
        place = (k % group) * rank
        mixed = left_triple(mixed_ref[k // group][:, place : place + rank])
        mixed_tall_ref[k] = right_triple(dot(mixed, right_triple(next_ref[k])))


def new_rows(change_ref, forward_ref, tall_ref, known_ref, next_ref):
    groups, rank, wide = change_ref.shape
    group = wide // rank
    evolvings = []
    for k in range(groups * group):
        lanes = slice((k % group) * rank, (k % group + 1) * rank)
        change, forward = change_ref[k // group][:, lanes], forward_ref[k // group][:, lanes]
        left = jnp.concatenate([left_triple(change), left_triple(forward)], axis=0)
        tall, known = tall_ref[k], known_ref[k]
        both = dot(left, right_triple(tall))
        next_ref[k] = known + tall + both[:rank]
        evolvings.append(known + both[rank:])
    return evolvings


def last_kernel(total, mixed_tall_ref, *refs):
    *sum_refs, coupled_ref, delta_ref = refs
    turned = new_delta(sum_refs, total, delta_ref.shape[0])
    delta_ref[...] = turned.T
    delta_left = left_triple(turned)
    for k in range(coupled_ref.shape[0]):
        coupled_ref[k] = dot(delta_left, mixed_tall_ref[k])


per_microsecond = 1_100_000_000


def call(
    kernel, name, outs, *args, scalars=0, unread=0, microseconds=0.3, limit=16, scratch=()
):
    flops = int(microseconds * per_microsecond)
    specs = [pl.BlockSpec(memory_space=pltpu.SMEM)] * scalars
    specs += [pl.BlockSpec(memory_space=pl.ANY)] * unread
    specs += [pl.BlockSpec(memory_space=pltpu.VMEM)] * (len(args) - len(specs))
    shapes = [jax.ShapeDtypeStruct(shape, dtype) for shape, dtype in outs]
    moved = sum(arg.size * arg.dtype.itemsize for arg in args)
    moved += sum(shape.size * shape.dtype.itemsize for shape in shapes)
    return pl.pallas_call(
        kernel,
        out_shape=shapes,
        in_specs=specs,
        out_specs=[pl.BlockSpec(memory_space=pltpu.VMEM)] * len(shapes),
        scratch_shapes=list(scratch),
        compiler_params=pltpu.CompilerParams(vmem_limit_bytes=limit * 1024 * 1024),
        cost_estimate=pl.CostEstimate(flops=flops, bytes_accessed=moved, transcendentals=0),
        name=name,
    )(*args)


def rotated(value, axis, shift):
    count = lax.axis_size(axis)
    return lax.ppermute(value, axis, [(i, (i + shift) % count) for i in range(count)])


def swapped(value, axis, first):
    count = lax.axis_size(axis)
    pairs = [((i + first) % count, (i + first + 1) % count) for i in range(0, count, 2)]
    return lax.ppermute(value, axis, pairs + [(b, a) for a, b in pairs])


def from_others(value, axis):
    return [rotated(value, axis, shift) for shift in range(1, lax.axis_size(axis))]


def stage_sizes(count):
    sizes = []
    while count > 1:
        sizes.append(next(size for size in (4, 2, 3, 5, 7, count) if count % size == 0))
        count //= sizes[-1]
    return sizes


def in_stages(value, axis, beside=None):
    count = lax.axis_size(axis)
    stride = 1
    terms, firsts = [value], []
    for size in stage_sizes(count):
        value = terms[0]
        if len(terms) > 1:
            unread = [] if beside is None else [beside]
            (value,) = call(
                functools.partial(add_kernel, len(unread)),
                "add",
                [(value.shape, f32)],
                *unread, *terms,
                unread=len(unread),
            )
        terms = [value]
        for shift in range(1, size):
            moves = []
            for i in range(count):
                digit = (i // stride) % size
                other = digit ^ shift if size in (2, 4) else (digit + shift) % size
                moves.append((i, i + (other - digit) * stride))
            terms.append(lax.ppermute(value, axis, moves))
        stride *= size
        firsts = firsts or terms
    return terms, firsts


def body(
    data, order, chan_factor, slice_weights, smooth_aux, coupled, smooth_dual, coupling_dual, delta
):
    count, all_rows, channels = data.shape
    rank = chan_factor.shape[1]
    rows = smooth_aux.shape[1]
    parts = lax.axis_size("chan")
    total = count * lax.axis_size("cuts")
    group = group_size(count, rank)
    groups = count // group
    wide = group * rank
    flip = lambda value: jnp.swapaxes(value, 1, 2)
    aux, coup, dual_s, dual_c = map(flip, (smooth_aux, coupled, smooth_dual, coupling_dual))
    factor = chan_factor.T
    state = ((count, rank, rows), f32)
    quads = ((groups, rank, wide), f32)
    square = ((rank, rank), f32)
    halo = (((SWEEPS + 1) // 2, rank, 2 * rows), f32)
    lanes = lambda height: ((height, 128), f32)
    scale = ((groups, 8, wide), f32)

    me = lax.axis_index("chan").astype(jnp.int32).reshape(1)
    odd = lax.rem(lax.axis_index("cuts"), 2).astype(jnp.int32).reshape(1)
    early = count // 4
    own, received = [], []
    for first, pairs, lead in ((0, early, True), (2 * early, count // 2 - early, False)):
        height = pairs * rows + (rank // 2 if lead else 0)
        projected = call(
            functools.partial(project_kernel, first, pairs, rows, lead),
            "project",
            [((height, 2 * rank), f32)] * parts + [(factor.shape, factor.dtype)] * lead,
            me, data, factor,
            scalars=1, unread=1, limit=52,
            scratch=[
                pltpu.VMEM((2 * pairs, all_rows, channels), data.dtype),
                pltpu.SemaphoreType.DMA((4 * pairs,)),
            ],
        )
        if lead:
            *projected, factor = projected
        own.append(projected[0])
        received.append([rotated(projected[shift], "chan", shift) for shift in range(1, parts)])

    late_weights, _ = lax.optimization_barrier((slice_weights, own[-1]))
    before = rotated(late_weights, "cuts", 1)
    after = rotated(late_weights, "cuts", -1)
    inverse, mover, rho, diagonal, columns, base = call(
        functools.partial(setup_kernel, parts, early * rows, group),
        "setup",
        [
            ((count, rank, 3 * rank), bf16),
            ((count // 2, 2 * rank, 6 * rank), bf16),
            lanes(count),
            ((count, rank), f32),
            ((rank, count), f32),
            state,
        ],
        order, own[0], *received[0], slice_weights, aux, coup, dual_s, dual_c,
        scalars=1,
    )
    half_state = ((early, 2 * rank, rows), f32)
    moved, turned = call(
        move_kernel, "move", [half_state, half_state], mover, own[0], *received[0]
    )
    tall, target, gram = call(
        functools.partial(first_kernel, group),
        "first",
        [state, state, quads],
        order, before, after, base, mover, dual_s, dual_c, moved, own[1], *received[1],
        scalars=1, unread=2,
        scratch=[pltpu.VMEM((count // 2, 2 * rank, rows), f32)],
    )
    side, before, after, inside, to_near, to_far = call(
        smooth_kernel,
        "smooth",
        [state, lanes(count), lanes(count), state, halo, halo],
        odd, order, aux, target, before, rho, after, diagonal, columns, turned, own[1],
        *received[1],
        scalars=2,
        scratch=[pltpu.VMEM((count // 2, 2 * rank, rows), f32)],
    )
    polar_outs = [quads, ((rank // 2, 2 * rank), f32), quads]
    for inner in range(INNER):
        if inner == 0:
            mixed, partial, gram = call(
                first_polar_kernel,
                "polar",
                polar_outs,
                inside, delta, gram, *from_others(gram, "chan"),
                unread=1, microseconds=3,
            )
        else:
            last = inner == INNER - 1
            mixed, partial, *gram = call(
                functools.partial(later_polar_kernel, last),
                "polar",
                polar_outs[:2] if last else polar_outs,
                inside, delta, change, old, cross, *crosses,
                unread=1,
            )
            gram = gram[0] if gram else None
        if inner == INNER - 1:
            mixed_tall, evolving = call(
                last_rows_kernel,
                "rows",
                [((count, 3 * rank, rows), bf16), state],
                mixed, change, forward, tall, known,
                scratch=[pltpu.VMEM(state[0], f32)],
            )
            coup, delta = call(
                functools.partial(last_kernel, total),
                "last",
                [state, square],
                mixed_tall, *in_stages(partial, "cuts")[0],
            )
            continue
        near = swapped(to_near, "cuts", 0)
        far = swapped(to_far, "cuts", 1)
        known, cross, *kept = call(
            functools.partial(ahead_kernel, group),
            "ahead",
            [state, ((groups, rank, 2 * wide), f32)] + [state] * (2 if inner < INNER - 2 else 0),
            odd, partial, inside, near, far, target, tall, side, rho, inverse,
            scalars=1, unread=1,
        )
        sums, firsts = in_stages(partial, "cuts", beside=cross)
        _, cross = lax.optimization_barrier((firsts, cross))
        crosses = from_others(cross, "chan")
        old = gram
        delta, change, forward = call(
            functools.partial(mixer_kernel, total),
            "mixer",
            [square, quads, quads],
            mixed, inverse, rho, *sums,
        )
        if inner < INNER - 2:
            tall, target, inside, to_near, to_far = call(
                rows_kernel,
                "rows",
                [state, state, state, halo, halo],
                odd, kept[0], before, rho, after, change, forward, tall, known, kept[1],
                scalars=1,
            )
    return (flip(evolving), flip(coup), delta)


def solution(mesh):
    return jax.shard_map(
        body,
        mesh=mesh,
        in_specs=(
            P("cuts", None, "chan"),
            P("cuts"),
            P("chan", None),
            P("cuts", None),
            P("cuts", "chan", None),
            P("cuts", "chan", None),
            P("cuts", "chan", None),
            P("cuts", "chan", None),
            P(),
        ),
        out_specs=(P("cuts", "chan", None), P("cuts", "chan", None), P()),
        check_vma=False,
    )
```

```python
import functools

import jax
import jax.numpy as jnp
from jax import lax
from jax.experimental import pallas as pl
from jax.experimental.pallas import tpu as pltpu
from jax.sharding import PartitionSpec as P

INNER = 3
SWEEPS = 4
POLAR = 8

smooth_weight = 1.0
eps_trace = 1e-06
f32 = jnp.float32
bf16 = jnp.bfloat16
NN = (((1,), (0,)), ((), ()))
NT = (((1,), (1,)), ((), ()))


def dot(left, right, dims=NN):
    return lax.dot_general(left, right, dims, preferred_element_type=f32)


def split(value):
    high = value.astype(bf16)
    low = (value - high.astype(f32)).astype(bf16)
    return high, low


def left_triple(value):
    high, low = split(value)
    return jnp.concatenate([high, high, low], axis=1)


def right_triple(value):
    high, low = split(value)
    return jnp.concatenate([high, low, high], axis=0)


def block_mask(rank, group):
    wide = rank * group
    rows = lax.div(lax.broadcasted_iota(jnp.int32, (wide, wide), 0), rank)
    cols = lax.div(lax.broadcasted_iota(jnp.int32, (wide, wide), 1), rank)
    return jnp.where(rows == cols, 1.0, 0.0).astype(bf16)


def wide_eye(rank, group):
    rows = lax.broadcasted_iota(jnp.int32, (rank, rank * group), 0)
    cols = lax.broadcasted_iota(jnp.int32, (rank, rank * group), 1)
    return jnp.where(rows == lax.rem(cols, rank), 1.0, 0.0).astype(f32)


def block_diagonal(value, mask, group, dims=NN):
    high, low = split(value)
    high = jnp.concatenate([high] * group, axis=0) * mask
    low = jnp.concatenate([low] * group, axis=0) * mask
    empty = jnp.zeros_like(high)
    one, other = ([high, low], [high, empty]) if dims == NN else ([high, high], [low, empty])
    return jnp.concatenate(
        [jnp.concatenate(one, axis=1), jnp.concatenate(other, axis=1)], axis=0
    )


def times_blocks(values, blocks, dims=NN):
    rank, wide = values[0].shape
    left = [jnp.concatenate(split(value), axis=1) for value in values]
    total = dot(jnp.concatenate(left, axis=0), blocks, dims)
    total = total[:, :wide] + total[:, wide:]
    return [total[at * rank : (at + 1) * rank] for at in range(len(values))]


def diagonal_blocks(value, rank, group):
    at = lax.div(lax.broadcasted_iota(jnp.int32, (rank, rank * group), 1), rank)
    total = value[:rank]
    for block in range(1, group):
        total = jnp.where(at == block, value[block * rank : (block + 1) * rank], total)
    return total


def from_left(left, values):
    wide = values[0].shape[1]
    total = dot(left_triple(left), right_triple(jnp.concatenate(values, axis=1)))
    return [total[:, at * wide : (at + 1) * wide] for at in range(len(values))]


def group_size(count, rank):
    group = max(1, 128 // rank)
    while count % group:
        group -= 1
    return group


def project_kernel(first, pairs, rows, lead, me_ref, data_ref, factor_ref, *refs):
    *outs, held, factor_held, arrived, factor_arrived = refs
    pieces = arrived.shape[0] // (2 * pairs)
    height = data_ref.shape[1] // pieces
    factor_copy = pltpu.make_async_copy(factor_ref, factor_held, factor_arrived)
    factor_copy.start()
    copies = []
    for k in range(2 * pairs):
        for at in range(pieces):
            place = pl.ds(at * height, height)
            copies.append(
                pltpu.make_async_copy(
                    data_ref.at[first + k, place, :],
                    held.at[k, place, :],
                    arrived.at[pieces * k + at],
                )
            )
            copies[-1].start()
    factor_copy.wait()
    factor = factor_held[...]
    rank = factor.shape[0]
    if lead:
        *outs, again_ref = outs
        again_ref[...] = factor
        gram = dot(factor, factor, NT)
        for out in outs:
            out[pairs * rows :, :] = jnp.concatenate([gram[: rank // 2], gram[rank // 2 :]], axis=1)
    parts = len(outs)
    empty = jnp.zeros_like(factor)
    sides = [
        jnp.concatenate([factor, empty], axis=0),
        jnp.concatenate([empty, factor], axis=0),
    ]
    for pair in range(pairs):
        for copy in copies[2 * pieces * pair : 2 * pieces * (pair + 1)]:
            copy.wait()
        for part in reversed(range(parts)):
            start = pl.multiple_of(lax.rem(me_ref[0] + part, parts) * rows, 16)
            place = pl.ds(start, rows)
            outs[part][pair * rows : (pair + 1) * rows, :] = dot(
                held[2 * pair, place, :], sides[0], NT
            ) + dot(held[2 * pair + 1, place, :], sides[1], NT)


def setup_kernel(parts, first, group, order_ref, *refs):
    lead_refs, refs = refs[:parts], refs[parts:]
    (own_ref, aux_ref, coupled_ref, dual_s_ref, dual_c_ref) = refs[:5]
    (inverse_ref, mover_ref, rho_ref, diagonal_ref, columns_ref, base_ref) = refs[5:]
    count, rank = own_ref.shape
    gram = summed(lead_refs, slice(first, None))
    gram = jnp.concatenate([gram[:, :rank], gram[:, rank:]], axis=0)
    eye = wide_eye(rank, 1)
    diagonal = jnp.sum(gram * eye, axis=0, keepdims=True)
    diagonal_ref[...] = jnp.broadcast_to(diagonal, diagonal_ref.shape)
    weights = own_ref[...]
    columns = weights.T
    columns_ref[...] = columns
    rho = jnp.sum(weights * weights * diagonal, axis=1, keepdims=True) / rank
    rho_ref[...] = jnp.broadcast_to(rho, rho_ref.shape)

    centre = rank / 2.0 + 2.0
    edge = centre / (rank / 2.0)
    size = 8.0 * edge**4 - 8.0 * edge**2 + 1.0
    fourth, second, unit_part = 8.0 * edge**4 / size, -8.0 * edge**2 / size, 1.0 / size
    mask = block_mask(rank, group)
    wide = wide_eye(rank, group)
    starts = range(0, count, group)
    systems = []
    for first in starts:
        scaled = []
        for k in range(first, first + group):
            unit = 1.0 / (centre * rho[k : k + 1, :])
            column = columns[:, k : k + 1]
            scaled.append(column * gram * weights[k : k + 1, :] * unit + (2.0 / centre) * eye)
        systems.append(jnp.concatenate(scaled, axis=1))
    inverses, rests = [], []
    for system in systems:
        rest = wide - system
        blocks = block_diagonal(rest, mask, group)
        (square,) = times_blocks([rest], blocks)
        (cube,) = times_blocks([square], blocks)
        (quartic,) = times_blocks([square], block_diagonal(square, mask, group))
        inverses.append(fourth * (wide + rest + square + cube) + second * (wide + rest))
        rests.append(fourth * quartic + second * square + unit_part * wide)
    for step in range(4):
        for at in range(len(systems)):
            blocks = block_diagonal(rests[at], mask, group)
            more, *rest = times_blocks([inverses[at], rests[at]][: 2 if step < 3 else 1], blocks)
            inverses[at] = inverses[at] + more
            rests[at] = rest[0] if rest else None
    for at in range(len(systems)):
        (product,) = times_blocks([inverses[at]], block_diagonal(systems[at], mask, group))
        blocks = block_diagonal(wide - product, mask, group)
        (more,) = times_blocks([inverses[at]], blocks)
        inverses[at] = inverses[at] + more
    for k in range(count):
        place = (k % group) * rank
        unit = 1.0 / (centre * rho[k : k + 1, :])
        inverse = inverses[k // group][:, place : place + rank] * unit
        inverse_ref[k] = left_triple(inverse)
        base_ref[k] = dot(
            inverse_ref[k],
            right_triple(
                rho[k : k + 1, :] * (aux_ref[k] - dual_s_ref[k] + coupled_ref[k] - dual_c_ref[k])
            ),
        )
        both = jnp.concatenate([inverse * weights[k : k + 1, :]] * 2, axis=1)
        side = lax.div(lax.broadcasted_iota(jnp.int32, both.shape, 1), rank)
        both = jnp.where(side == lax.rem(order_ref[k], 2), both, 0.0)
        high, low = split(both)
        pair, place = stored_place(order_ref, k, count, rank)
        mover_ref[pair, place, :] = jnp.concatenate([high, high, low], axis=1)


def cross_blocks(lefts, rights, rank):
    group = len(lefts)
    wide = group * rank
    left = jnp.concatenate(split(jnp.concatenate(lefts, axis=0)), axis=0)
    right = left
    if rights is not lefts:
        right = jnp.concatenate(split(jnp.concatenate(rights, axis=0)), axis=0)
    total = dot(left, right, NT)
    total = total[:wide, :wide] + total[:wide, wide:] + total[wide:, :wide]
    return diagonal_blocks(total, rank, group)


def summed(refs, at):
    total = refs[0][at]
    for ref in refs[1:]:
        total = total + ref[at]
    return total


def stored_place(order_ref, k, count, rank):
    stored = lax.rem(order_ref[k], count)
    return lax.div(stored, 2), pl.ds(pl.multiple_of(lax.rem(stored, 2) * rank, rank), rank)


def move(mover, projected):
    high, low = split(projected)
    return dot(mover, jnp.concatenate([high, low, high], axis=1), NT)


def move_kernel(mover_ref, *refs):
    *projected_refs, moved_ref, turned_ref = refs
    rows = moved_ref.shape[2]
    for pair in range(moved_ref.shape[0]):
        projected = summed(projected_refs, slice(pair * rows, (pair + 1) * rows))
        moved_ref[pair] = move(mover_ref[pair], projected)
        turned_ref[pair] = projected.T


def first_kernel(group, order_ref, *refs):
    base_ref, mover_ref, dual_s_ref, dual_c_ref, early_ref = refs[2:7]
    *projected_refs, tall_ref, target_ref, gram_ref, moved = refs[7:]
    count, rank, rows = base_ref.shape
    early = early_ref.shape[0]
    for pair in range(early):
        moved[pair] = early_ref[pair]
    for pair in range(early, count // 2):
        place = slice((pair - early) * rows, (pair - early + 1) * rows)
        moved[pair] = move(mover_ref[pair], summed(projected_refs, place))
    talls = []
    for k in range(count):
        pair, place = stored_place(order_ref, k, count, rank)
        evolving = base_ref[k] + moved[pair, place, :]
        target_ref[k] = evolving + dual_s_ref[k]
        tall = evolving + dual_c_ref[k]
        tall_ref[k] = tall
        talls.append(tall)
        if len(talls) == group:
            gram_ref[k // group] = cross_blocks(talls, talls, rank)
            talls = []


def smooth(odd, now, targets, rho, inside_ref, near_ref, far_ref):
    count = len(targets)
    width = SWEEPS
    share = {j: 2.0 * smooth_weight / (rho[j] + 4.0 * smooth_weight) for j in rho}
    pull = {j: (rho[j] / (rho[j] + 4.0 * smooth_weight)) * targets[j] for j in range(count)}
    now = {j: now[j] for j in range(count)}
    for sweep in range(width):
        later = {}
        for j in range(-sweep - 1, count + sweep + 1):
            beside = [now[i] for i in (j - 1, j + 1) if i in now]
            total = beside[0] if len(beside) == 1 else beside[0] + beside[1]
            total = share[j] * total
            later[j] = total + pull[j] if j in pull else total
        now = later
    for j in range(count):
        inside_ref[j] = now[j]
    rows = inside_ref.shape[2]
    for j in range(width):
        lanes = slice((j % 2) * rows, (j % 2 + 1) * rows)
        near_ref[j // 2, :, lanes] = jnp.where(odd == 1, now[j - width], now[count + j])
        far_ref[j // 2, :, lanes] = jnp.where(odd == 1, now[count + j], now[j - width])


def all_rho(before_ref, rho_ref, after_ref):
    count = rho_ref.shape[0]
    rho = {j: rho_ref[j : j + 1, 0:1] for j in range(count)}
    for j in range(SWEEPS):
        rho[j - SWEEPS] = before_ref[count - SWEEPS + j : count - SWEEPS + j + 1, 0:1]
        rho[count + j] = after_ref[j : j + 1, 0:1]
    return rho


def smooth_kernel(
    odd_ref, order_ref, aux_ref, target_ref, before_ref, rho_ref, after_ref, diagonal_ref,
    columns_ref, early_ref, *refs
):
    *projected_refs, side_ref, past_ref, next_ref, inside_ref, near_ref, far_ref, turned = refs
    count, rank, rows = aux_ref.shape
    for source, place in ((before_ref, past_ref), (after_ref, next_ref)):
        weights = source[...]
        rho = jnp.sum(weights * weights * diagonal_ref[...], axis=1, keepdims=True) / rank
        place[...] = jnp.broadcast_to(rho, place.shape)
    rho = all_rho(past_ref, rho_ref, next_ref)
    slices = range(count)
    smooth(
        odd_ref[0], [aux_ref[k] for k in slices], [target_ref[k] for k in slices], rho,
        inside_ref, near_ref, far_ref,
    )
    early = early_ref.shape[0]
    for pair in range(early):
        turned[pair] = early_ref[pair]
    for pair in range(early, count // 2):
        place = slice((pair - early) * rows, (pair - early + 1) * rows)
        turned[pair] = summed(projected_refs, place).T
    for k in slices:
        pair, place = stored_place(order_ref, k, count, rank)
        side_ref[k] = columns_ref[:, k : k + 1] * turned[pair, place, :]


def polar(grams, delta):
    rank, wide = grams[0].shape
    group = wide // rank
    mask = block_mask(rank, group)
    eye = wide_eye(rank, group)
    delta_wide = jnp.concatenate([delta] * group, axis=1)
    delta_blocks = block_diagonal(delta_wide, mask, group, NT)
    (across,) = from_left(delta.T, [delta_wide])
    traces = []
    for gram in grams:
        line = jnp.broadcast_to(jnp.sum(across * gram, axis=0, keepdims=True), (16, wide))
        high, low = split(line)
        rest = (line - high.astype(f32) - low.astype(f32)).astype(bf16)
        line = dot(high, mask) + dot(low, mask) + dot(rest, mask)
        traces.append(line[0:1] + eps_trace)
    rights = [times_blocks([gram], delta_blocks, NT)[0] for gram in grams]
    normals = from_left(delta, rights)
    currents = [normal / trace for normal, trace in zip(normals, traces)]
    scales = [1.0 / jnp.sqrt(trace) for trace in traces]
    roots = []
    for step in range(POLAR):
        for at in range(len(grams)):
            product = currents[at]
            blocks = block_diagonal(product, mask, group)
            if step == 0:
                roots.append(1.5 * eye - 0.5 * product)
                (square,) = times_blocks([product], blocks)
            elif step < POLAR - 1:
                square, more = times_blocks([product, roots[at]], blocks)
                roots[at] = 1.5 * roots[at] - 0.5 * more
            else:
                (more,) = times_blocks([roots[at]], blocks)
                roots[at] = 1.5 * roots[at] - 0.5 * more
            if step < POLAR - 1:
                half = 1.5 * product - 0.5 * square
                (more,) = times_blocks([half], blocks)
                currents[at] = 1.5 * half - 0.5 * more
    return roots, scales, rights


def mix(roots, scales, rights, delta, mixed_ref, partial_ref):
    rank, wide = roots[0].shape
    group = wide // rank
    mask = block_mask(rank, group)
    delta_blocks = block_diagonal(jnp.concatenate([delta] * group, axis=1), mask, group)
    left, right = [], []
    for at in range(len(roots)):
        high, low = split(roots[at] * scales[at])
        left += [high, high, low]
        high, low = split(rights[at])
        right += [high, low, high]
    partial = dot(jnp.concatenate(right, axis=1), jnp.concatenate(left, axis=1), NT)
    for at in range(len(roots)):
        (mixed,) = times_blocks([roots[at]], delta_blocks)
        mixed_ref[at] = mixed * scales[at]
    half = rank // 2
    partial_ref[...] = jnp.concatenate([partial[:half], partial[half:]], axis=1)


def first_polar_kernel(after_ref, delta_ref, *refs):
    *gram_refs, mixed_ref, partial_ref, gram_ref = refs
    grams = [summed(gram_refs, at) for at in range(gram_ref.shape[0])]
    for at in range(len(grams)):
        gram_ref[at] = grams[at]
    delta = delta_ref[...]
    mix(*polar(grams, delta), delta, mixed_ref, partial_ref)


def later_polar_kernel(last, after_ref, delta_ref, change_ref, old_ref, *refs):
    if last:
        *cross_refs, mixed_ref, partial_ref = refs
    else:
        *cross_refs, mixed_ref, partial_ref, gram_ref = refs
    groups, rank, wide = old_ref.shape
    group = wide // rank
    mask = block_mask(rank, group)
    grams = []
    for at in range(groups):
        cross = summed(cross_refs, at)
        change = change_ref[at]
        (onward,) = times_blocks([change], block_diagonal(old_ref[at], mask, group))
        onward = cross[:, :wide] + 0.5 * onward
        (one,) = times_blocks([onward], block_diagonal(change, mask, group, NT), NT)
        (other,) = times_blocks([change], block_diagonal(onward, mask, group, NT), NT)
        grams.append(cross[:, wide:] + one + other)
        if not last:
            gram_ref[at] = grams[at]
    delta = delta_ref[...]
    mix(*polar(grams, delta), delta, mixed_ref, partial_ref)


def ahead_kernel(
    group, odd_ref, after_ref, inside_ref, near_ref, far_ref, target_ref, tall_ref, side_ref, rho_ref,
    inverse_ref, known_ref, cross_ref, *kept
):
    count, rank, rows = inside_ref.shape
    width = SWEEPS
    knowns, talls = [], []
    for k in range(count):
        aux = inside_ref[k]
        for at, mine, other in ((k, near_ref, far_ref), (k - count + width, far_ref, near_ref)):
            if 0 <= at < width:
                lanes = slice((at % 2) * rows, (at % 2 + 1) * rows)
                aux = aux + jnp.where(
                    odd_ref[0] == 1, mine[at // 2, :, lanes], other[at // 2, :, lanes]
                )
        target, tall = target_ref[k], tall_ref[k]
        if kept:
            aux_ref, dual_ref = kept
            aux_ref[k] = aux
            dual_ref[k] = target - aux
        known = dot(
            inverse_ref[k],
            right_triple(side_ref[k] + rho_ref[k : k + 1, 0:1] * (2.0 * aux - target - tall)),
        )
        known_ref[k] = known
        talls.append(tall)
        knowns.append(known + tall)
        if len(talls) == group:
            cross_ref[k // group] = jnp.concatenate(
                [cross_blocks(knowns, talls, rank), cross_blocks(knowns, knowns, rank)], axis=1
            )
            knowns, talls = [], []


def add_kernel(unread, *refs):
    *term_refs, total_ref = refs[unread:]
    total = term_refs[0][...]
    for ref in term_refs[1:]:
        total = total + ref[...]
    total_ref[...] = total


def new_delta(sum_refs, total, rank):
    packed = sum_refs[0][...]
    for ref in sum_refs[1:]:
        packed = packed + ref[...]
    packed = packed / total
    return jnp.concatenate([packed[:, :rank], packed[:, rank:]], axis=0)


def mixer_kernel(total, mixed_ref, inverse_ref, rho_ref, *refs):
    *sum_refs, delta_ref, change_ref, forward_ref = refs
    groups, rank, wide = mixed_ref.shape
    group = wide // rank
    turned = new_delta(sum_refs, total, rank)
    delta_ref[...] = turned.T
    mixers = from_left(turned, [mixed_ref[at] for at in range(groups)])
    place = lax.div(lax.broadcasted_iota(jnp.int32, (1, wide), 1), rank)
    for at in range(groups):
        mixer = mixers[at]
        slices = range(at * group, (at + 1) * group)
        inverses = jnp.concatenate([inverse_ref[k] for k in slices], axis=0)
        onward = diagonal_blocks(dot(inverses, right_triple(mixer)), rank, group)
        rho = rho_ref[at * group : at * group + 1, 0:1]
        for k in slices[1:]:
            rho = jnp.where(place == k - at * group, rho_ref[k : k + 1, 0:1], rho)
        forward = 2.0 * rho * onward
        forward_ref[at] = forward
        change_ref[at] = forward - mixer


def rows_kernel(odd_ref, aux_ref, before_ref, rho_ref, after_ref, *refs):
    (change_ref, forward_ref, tall_ref, known_ref, dual_ref) = refs[:5]
    (next_ref, target_ref, inside_ref, near_ref, far_ref) = refs[5:]
    targets = new_rows(change_ref, forward_ref, tall_ref, known_ref, next_ref)
    count = len(targets)
    for k in range(count):
        targets[k] = targets[k] + dual_ref[k]
        target_ref[k] = targets[k]
    rho = all_rho(before_ref, rho_ref, after_ref)
    smooth(
        odd_ref[0], [aux_ref[k] for k in range(count)], targets, rho,
        inside_ref, near_ref, far_ref,
    )


def last_rows_kernel(mixed_ref, change_ref, forward_ref, tall_ref, known_ref, *outs):
    mixed_tall_ref, evolving_ref, next_ref = outs
    evolvings = new_rows(change_ref, forward_ref, tall_ref, known_ref, next_ref)
    groups, rank, wide = mixed_ref.shape
    group = wide // rank
    for k in range(len(evolvings)):
        evolving_ref[k] = evolvings[k]
        place = (k % group) * rank
        mixed = left_triple(mixed_ref[k // group][:, place : place + rank])
        mixed_tall_ref[k] = right_triple(dot(mixed, right_triple(next_ref[k])))


def new_rows(change_ref, forward_ref, tall_ref, known_ref, next_ref):
    groups, rank, wide = change_ref.shape
    group = wide // rank
    evolvings = []
    for k in range(groups * group):
        lanes = slice((k % group) * rank, (k % group + 1) * rank)
        change, forward = change_ref[k // group][:, lanes], forward_ref[k // group][:, lanes]
        left = jnp.concatenate([left_triple(change), left_triple(forward)], axis=0)
        tall, known = tall_ref[k], known_ref[k]
        both = dot(left, right_triple(tall))
        next_ref[k] = known + tall + both[:rank]
        evolvings.append(known + both[rank:])
    return evolvings


def last_kernel(total, mixed_tall_ref, *refs):
    *sum_refs, coupled_ref, delta_ref = refs
    turned = new_delta(sum_refs, total, delta_ref.shape[0])
    delta_ref[...] = turned.T
    delta_left = left_triple(turned)
    for k in range(coupled_ref.shape[0]):
        coupled_ref[k] = dot(delta_left, mixed_tall_ref[k])


per_microsecond = 1_100_000_000


def call(
    kernel, name, outs, *args, scalars=0, unread=0, microseconds=0.3, limit=16, scratch=()
):
    flops = int(microseconds * per_microsecond)
    specs = [pl.BlockSpec(memory_space=pltpu.SMEM)] * scalars
    specs += [pl.BlockSpec(memory_space=pl.ANY)] * unread
    specs += [pl.BlockSpec(memory_space=pltpu.VMEM)] * (len(args) - len(specs))
    shapes = [jax.ShapeDtypeStruct(shape, dtype) for shape, dtype in outs]
    moved = sum(arg.size * arg.dtype.itemsize for arg in args)
    moved += sum(shape.size * shape.dtype.itemsize for shape in shapes)
    return pl.pallas_call(
        kernel,
        out_shape=shapes,
        in_specs=specs,
        out_specs=[pl.BlockSpec(memory_space=pltpu.VMEM)] * len(shapes),
        scratch_shapes=list(scratch),
        compiler_params=pltpu.CompilerParams(vmem_limit_bytes=limit * 1024 * 1024),
        cost_estimate=pl.CostEstimate(flops=flops, bytes_accessed=moved, transcendentals=0),
        name=name,
    )(*args)


def rotated(value, axis, shift):
    count = lax.axis_size(axis)
    return lax.ppermute(value, axis, [(i, (i + shift) % count) for i in range(count)])


def swapped(value, axis, first):
    count = lax.axis_size(axis)
    pairs = [((i + first) % count, (i + first + 1) % count) for i in range(0, count, 2)]
    return lax.ppermute(value, axis, pairs + [(b, a) for a, b in pairs])


def from_others(value, axis):
    return [rotated(value, axis, shift) for shift in range(1, lax.axis_size(axis))]


def stage_sizes(count):
    sizes = []
    while count > 1:
        sizes.append(next(size for size in (4, 2, 3, 5, 7, count) if count % size == 0))
        count //= sizes[-1]
    return sizes


def in_stages(value, axis, beside=None):
    count = lax.axis_size(axis)
    stride = 1
    terms, firsts = [value], []
    for size in stage_sizes(count):
        value = terms[0]
        if len(terms) > 1:
            unread = [] if beside is None else [beside]
            (value,) = call(
                functools.partial(add_kernel, len(unread)),
                "add",
                [(value.shape, f32)],
                *unread, *terms,
                unread=len(unread),
            )
        terms = [value]
        for shift in range(1, size):
            moves = []
            for i in range(count):
                digit = (i // stride) % size
                other = digit ^ shift if size in (2, 4) else (digit + shift) % size
                moves.append((i, i + (other - digit) * stride))
            terms.append(lax.ppermute(value, axis, moves))
        stride *= size
        firsts = firsts or terms
    return terms, firsts


def body(
    data, order, chan_factor, slice_weights, smooth_aux, coupled, smooth_dual, coupling_dual, delta
):
    count, all_rows, channels = data.shape
    rank = chan_factor.shape[1]
    rows = smooth_aux.shape[1]
    parts = lax.axis_size("chan")
    total = count * lax.axis_size("cuts")
    group = group_size(count, rank)
    groups = count // group
    wide = group * rank
    flip = lambda value: jnp.swapaxes(value, 1, 2)
    aux, coup, dual_s, dual_c = map(flip, (smooth_aux, coupled, smooth_dual, coupling_dual))
    factor = chan_factor.T
    state = ((count, rank, rows), f32)
    quads = ((groups, rank, wide), f32)
    square = ((rank, rank), f32)
    halo = (((SWEEPS + 1) // 2, rank, 2 * rows), f32)
    lanes = lambda height: ((height, 128), f32)
    scale = ((groups, 8, wide), f32)

    me = lax.axis_index("chan").astype(jnp.int32).reshape(1)
    odd = lax.rem(lax.axis_index("cuts"), 2).astype(jnp.int32).reshape(1)
    early = count // 4
    pieces = next(pieces for pieces in (4, 2, 1) if all_rows % (16 * pieces) == 0)
    own, received = [], []
    for first, pairs, lead in ((0, early, True), (2 * early, count // 2 - early, False)):
        height = pairs * rows + (rank // 2 if lead else 0)
        projected = call(
            functools.partial(project_kernel, first, pairs, rows, lead),
            "project",
            [((height, 2 * rank), f32)] * parts + [(factor.shape, factor.dtype)] * lead,
            me, data, factor,
            scalars=1, unread=2, limit=52,
            scratch=[
                pltpu.VMEM((2 * pairs, all_rows, channels), data.dtype),
                pltpu.VMEM(factor.shape, factor.dtype),
                pltpu.SemaphoreType.DMA((2 * pairs * pieces,)),
                pltpu.SemaphoreType.DMA,
            ],
        )
        if lead:
            *projected, factor = projected
        own.append(projected[0])
        received.append([rotated(projected[shift], "chan", shift) for shift in range(1, parts)])

    late_weights, _ = lax.optimization_barrier((slice_weights, own[-1]))
    before = rotated(late_weights, "cuts", 1)
    after = rotated(late_weights, "cuts", -1)
    inverse, mover, rho, diagonal, columns, base = call(
        functools.partial(setup_kernel, parts, early * rows, group),
        "setup",
        [
            ((count, rank, 3 * rank), bf16),
            ((count // 2, 2 * rank, 6 * rank), bf16),
            lanes(count),
            ((count, rank), f32),
            ((rank, count), f32),
            state,
        ],
        order, own[0], *received[0], slice_weights, aux, coup, dual_s, dual_c,
        scalars=1,
    )
    half_state = ((early, 2 * rank, rows), f32)
    moved, turned = call(
        move_kernel, "move", [half_state, half_state], mover, own[0], *received[0]
    )
    tall, target, gram = call(
        functools.partial(first_kernel, group),
        "first",
        [state, state, quads],
        order, before, after, base, mover, dual_s, dual_c, moved, own[1], *received[1],
        scalars=1, unread=2,
        scratch=[pltpu.VMEM((count // 2, 2 * rank, rows), f32)],
    )
    side, before, after, inside, to_near, to_far = call(
        smooth_kernel,
        "smooth",
        [state, lanes(count), lanes(count), state, halo, halo],
        odd, order, aux, target, before, rho, after, diagonal, columns, turned, own[1],
        *received[1],
        scalars=2,
        scratch=[pltpu.VMEM((count // 2, 2 * rank, rows), f32)],
    )
    polar_outs = [quads, ((rank // 2, 2 * rank), f32), quads]
    for inner in range(INNER):
        if inner == 0:
            mixed, partial, gram = call(
                first_polar_kernel,
                "polar",
                polar_outs,
                inside, delta, gram, *from_others(gram, "chan"),
                unread=1, microseconds=3,
            )
        else:
            last = inner == INNER - 1
            mixed, partial, *gram = call(
                functools.partial(later_polar_kernel, last),
                "polar",
                polar_outs[:2] if last else polar_outs,
                inside, delta, change, old, cross, *crosses,
                unread=1,
            )
            gram = gram[0] if gram else None
        if inner == INNER - 1:
            mixed_tall, evolving = call(
                last_rows_kernel,
                "rows",
                [((count, 3 * rank, rows), bf16), state],
                mixed, change, forward, tall, known,
                scratch=[pltpu.VMEM(state[0], f32)],
            )
            coup, delta = call(
                functools.partial(last_kernel, total),
                "last",
                [state, square],
                mixed_tall, *in_stages(partial, "cuts")[0],
            )
            continue
        near = swapped(to_near, "cuts", 0)
        far = swapped(to_far, "cuts", 1)
        known, cross, *kept = call(
            functools.partial(ahead_kernel, group),
            "ahead",
            [state, ((groups, rank, 2 * wide), f32)] + [state] * (2 if inner < INNER - 2 else 0),
            odd, partial, inside, near, far, target, tall, side, rho, inverse,
            scalars=1, unread=1,
        )
        sums, firsts = in_stages(partial, "cuts", beside=cross)
        _, cross = lax.optimization_barrier((firsts, cross))
        crosses = from_others(cross, "chan")
        old = gram
        delta, change, forward = call(
            functools.partial(mixer_kernel, total),
            "mixer",
            [square, quads, quads],
            mixed, inverse, rho, *sums,
        )
        if inner < INNER - 2:
            tall, target, inside, to_near, to_far = call(
                rows_kernel,
                "rows",
                [state, state, state, halo, halo],
                odd, kept[0], before, rho, after, change, forward, tall, known, kept[1],
                scalars=1,
            )
    return (flip(evolving), flip(coup), delta)


def solution(mesh):
    return jax.shard_map(
        body,
        mesh=mesh,
        in_specs=(
            P("cuts", None, "chan"),
            P("cuts"),
            P("chan", None),
            P("cuts", None),
            P("cuts", "chan", None),
            P("cuts", "chan", None),
            P("cuts", "chan", None),
            P("cuts", "chan", None),
            P(),
        ),
        out_specs=(P("cuts", "chan", None), P("cuts", "chan", None), P()),
        check_vma=False,
    )
```

```python
import functools

import jax
import jax.numpy as jnp
from jax import lax
from jax.experimental import pallas as pl
from jax.experimental.pallas import tpu as pltpu
from jax.sharding import PartitionSpec as P

INNER = 3
SWEEPS = 4
POLAR = 8

smooth_weight = 1.0
eps_trace = 1e-06
f32 = jnp.float32
bf16 = jnp.bfloat16
NN = (((1,), (0,)), ((), ()))
NT = (((1,), (1,)), ((), ()))


def dot(left, right, dims=NN):
    return lax.dot_general(left, right, dims, preferred_element_type=f32)


def split(value):
    high = value.astype(bf16)
    low = (value - high.astype(f32)).astype(bf16)
    return high, low


def left_triple(value):
    high, low = split(value)
    return jnp.concatenate([high, high, low], axis=1)


def right_triple(value):
    high, low = split(value)
    return jnp.concatenate([high, low, high], axis=0)


def block_mask(rank, group):
    wide = rank * group
    rows = lax.div(lax.broadcasted_iota(jnp.int32, (wide, wide), 0), rank)
    cols = lax.div(lax.broadcasted_iota(jnp.int32, (wide, wide), 1), rank)
    return jnp.where(rows == cols, 1.0, 0.0).astype(bf16)


def wide_eye(rank, group):
    rows = lax.broadcasted_iota(jnp.int32, (rank, rank * group), 0)
    cols = lax.broadcasted_iota(jnp.int32, (rank, rank * group), 1)
    return jnp.where(rows == lax.rem(cols, rank), 1.0, 0.0).astype(f32)


def block_diagonal(value, mask, group, dims=NN):
    parts = [jnp.concatenate([part] * group, axis=0) * mask for part in split(value)]
    return jnp.concatenate(parts, axis=1 if dims == NN else 0)


def times_blocks(values, blocks, dims=NN):
    rank, wide = values[0].shape
    parts = [split(value) for value in values]
    rows = rank * len(values)
    left = jnp.concatenate([part[0] for part in parts] + [part[1] for part in parts], axis=0)
    total = dot(left, blocks, dims)
    total = total[:rows, :wide] + total[:rows, wide:] + total[rows:, :wide]
    return [total[at * rank : (at + 1) * rank] for at in range(len(values))]


def diagonal_blocks(value, rank, group):
    at = lax.div(lax.broadcasted_iota(jnp.int32, (rank, rank * group), 1), rank)
    total = value[:rank]
    for block in range(1, group):
        total = jnp.where(at == block, value[block * rank : (block + 1) * rank], total)
    return total


def from_left(left, values):
    wide = values[0].shape[1]
    total = dot(left_triple(left), right_triple(jnp.concatenate(values, axis=1)))
    return [total[:, at * wide : (at + 1) * wide] for at in range(len(values))]


def group_size(count, rank):
    group = max(1, 128 // rank)
    while count % group:
        group -= 1
    return group


def project_kernel(first, pairs, rows, lead, me_ref, data_ref, factor_ref, *refs):
    *outs, held, arrived = refs
    half = data_ref.shape[1] // 2
    copies = []
    for k in range(2 * pairs):
        for at in range(2):
            place = pl.ds(at * half, half)
            copies.append(
                pltpu.make_async_copy(
                    data_ref.at[first + k, place, :], held.at[k, place, :], arrived.at[2 * k + at]
                )
            )
            copies[-1].start()
    factor = factor_ref[...]
    rank = factor.shape[0]
    if lead:
        *outs, again_ref = outs
        again_ref[...] = factor
        gram = dot(factor, factor, NT)
        for out in outs:
            out[pairs * rows :, :] = jnp.concatenate([gram[: rank // 2], gram[rank // 2 :]], axis=1)
    parts = len(outs)
    empty = jnp.zeros_like(factor)
    sides = [
        jnp.concatenate([factor, empty], axis=0),
        jnp.concatenate([empty, factor], axis=0),
    ]
    for pair in range(pairs):
        for copy in copies[4 * pair : 4 * pair + 4]:
            copy.wait()
        for part in reversed(range(parts)):
            start = pl.multiple_of(lax.rem(me_ref[0] + part, parts) * rows, 16)
            place = pl.ds(start, rows)
            outs[part][pair * rows : (pair + 1) * rows, :] = dot(
                held[2 * pair, place, :], sides[0], NT
            ) + dot(held[2 * pair + 1, place, :], sides[1], NT)


def setup_kernel(parts, first, group, order_ref, *refs):
    lead_refs, refs = refs[:parts], refs[parts:]
    (own_ref, aux_ref, coupled_ref, dual_s_ref, dual_c_ref) = refs[:5]
    (inverse_ref, mover_ref, rho_ref, diagonal_ref, columns_ref, base_ref) = refs[5:]
    count, rank = own_ref.shape
    gram = summed(lead_refs, slice(first, None))
    gram = jnp.concatenate([gram[:, :rank], gram[:, rank:]], axis=0)
    eye = wide_eye(rank, 1)
    diagonal = jnp.sum(gram * eye, axis=0, keepdims=True)
    diagonal_ref[...] = jnp.broadcast_to(diagonal, diagonal_ref.shape)
    weights = own_ref[...]
    columns = weights.T
    columns_ref[...] = columns
    rho = jnp.sum(weights * weights * diagonal, axis=1, keepdims=True) / rank
    rho_ref[...] = jnp.broadcast_to(rho, rho_ref.shape)

    centre = rank / 2.0 + 2.0
    edge = centre / (rank / 2.0)
    lead = 4.0 * edge**3 / (4.0 * edge**3 - 3.0 * edge)
    mask = block_mask(rank, group)
    wide = wide_eye(rank, group)
    starts = range(0, count, group)
    systems = []
    for first in starts:
        scaled = []
        for k in range(first, first + group):
            unit = 1.0 / (centre * rho[k : k + 1, :])
            column = columns[:, k : k + 1]
            scaled.append(column * gram * weights[k : k + 1, :] * unit + (2.0 / centre) * eye)
        systems.append(jnp.concatenate(scaled, axis=1))
    inverses, rests = [], []
    for system in systems:
        rest = wide - system
        blocks = block_diagonal(rest, mask, group)
        (square,) = times_blocks([rest], blocks)
        (cube,) = times_blocks([square], blocks)
        inverses.append(wide + lead * (rest + square))
        rests.append(lead * cube - (lead - 1.0) * rest)
    for step in range(5):
        for at in range(len(systems)):
            blocks = block_diagonal(rests[at], mask, group)
            more, *rest = times_blocks([inverses[at], rests[at]][: 2 if step < 4 else 1], blocks)
            inverses[at] = inverses[at] + more
            rests[at] = rest[0] if rest else None
    for at in range(len(systems)):
        (product,) = times_blocks([inverses[at]], block_diagonal(systems[at], mask, group))
        blocks = block_diagonal(wide - product, mask, group)
        (more,) = times_blocks([inverses[at]], blocks)
        inverses[at] = inverses[at] + more
    for k in range(count):
        place = (k % group) * rank
        unit = 1.0 / (centre * rho[k : k + 1, :])
        inverse = inverses[k // group][:, place : place + rank] * unit
        inverse_ref[k] = left_triple(inverse)
        base_ref[k] = dot(
            inverse_ref[k],
            right_triple(
                rho[k : k + 1, :] * (aux_ref[k] - dual_s_ref[k] + coupled_ref[k] - dual_c_ref[k])
            ),
        )
        both = jnp.concatenate([inverse * weights[k : k + 1, :]] * 2, axis=1)
        side = lax.div(lax.broadcasted_iota(jnp.int32, both.shape, 1), rank)
        both = jnp.where(side == lax.rem(order_ref[k], 2), both, 0.0)
        high, low = split(both)
        pair, place = stored_place(order_ref, k, count, rank)
        mover_ref[pair, place, :] = jnp.concatenate([high, high, low], axis=1)


def cross_blocks(lefts, rights, rank):
    group = len(lefts)
    wide = group * rank
    left = jnp.concatenate(split(jnp.concatenate(lefts, axis=0)), axis=0)
    right = left
    if rights is not lefts:
        right = jnp.concatenate(split(jnp.concatenate(rights, axis=0)), axis=0)
    total = dot(left, right, NT)
    total = total[:wide, :wide] + total[:wide, wide:] + total[wide:, :wide]
    return diagonal_blocks(total, rank, group)


def summed(refs, at):
    total = refs[0][at]
    for ref in refs[1:]:
        total = total + ref[at]
    return total


def stored_place(order_ref, k, count, rank):
    stored = lax.rem(order_ref[k], count)
    return lax.div(stored, 2), pl.ds(pl.multiple_of(lax.rem(stored, 2) * rank, rank), rank)


def move(mover, projected):
    high, low = split(projected)
    return dot(mover, jnp.concatenate([high, low, high], axis=1), NT)


def move_kernel(mover_ref, *refs):
    *projected_refs, moved_ref, turned_ref = refs
    rows = moved_ref.shape[2]
    for pair in range(moved_ref.shape[0]):
        projected = summed(projected_refs, slice(pair * rows, (pair + 1) * rows))
        moved_ref[pair] = move(mover_ref[pair], projected)
        turned_ref[pair] = projected.T


def first_kernel(group, order_ref, *refs):
    base_ref, mover_ref, dual_s_ref, dual_c_ref, early_ref = refs[2:7]
    *projected_refs, tall_ref, target_ref, gram_ref, moved = refs[7:]
    count, rank, rows = base_ref.shape
    early = early_ref.shape[0]
    for pair in range(early):
        moved[pair] = early_ref[pair]
    for pair in range(early, count // 2):
        place = slice((pair - early) * rows, (pair - early + 1) * rows)
        moved[pair] = move(mover_ref[pair], summed(projected_refs, place))
    talls = []
    for k in range(count):
        pair, place = stored_place(order_ref, k, count, rank)
        evolving = base_ref[k] + moved[pair, place, :]
        target_ref[k] = evolving + dual_s_ref[k]
        tall = evolving + dual_c_ref[k]
        tall_ref[k] = tall
        talls.append(tall)
        if len(talls) == group:
            gram_ref[k // group] = cross_blocks(talls, talls, rank)
            talls = []


def smooth(odd, now, targets, rho, inside_ref, near_ref, far_ref):
    count = len(targets)
    width = SWEEPS
    share = {j: 2.0 * smooth_weight / (rho[j] + 4.0 * smooth_weight) for j in rho}
    pull = {j: (rho[j] / (rho[j] + 4.0 * smooth_weight)) * targets[j] for j in range(count)}
    now = {j: now[j] for j in range(count)}
    for sweep in range(width):
        later = {}
        for j in range(-sweep - 1, count + sweep + 1):
            beside = [now[i] for i in (j - 1, j + 1) if i in now]
            total = beside[0] if len(beside) == 1 else beside[0] + beside[1]
            total = share[j] * total
            later[j] = total + pull[j] if j in pull else total
        now = later
    for j in range(count):
        inside_ref[j] = now[j]
    rows = inside_ref.shape[2]
    for j in range(width):
        lanes = slice((j % 2) * rows, (j % 2 + 1) * rows)
        near_ref[j // 2, :, lanes] = jnp.where(odd == 1, now[j - width], now[count + j])
        far_ref[j // 2, :, lanes] = jnp.where(odd == 1, now[count + j], now[j - width])


def all_rho(before_ref, rho_ref, after_ref):
    count = rho_ref.shape[0]
    rho = {j: rho_ref[j : j + 1, 0:1] for j in range(count)}
    for j in range(SWEEPS):
        rho[j - SWEEPS] = before_ref[count - SWEEPS + j : count - SWEEPS + j + 1, 0:1]
        rho[count + j] = after_ref[j : j + 1, 0:1]
    return rho


def smooth_kernel(
    odd_ref, order_ref, aux_ref, target_ref, before_ref, rho_ref, after_ref, diagonal_ref,
    columns_ref, early_ref, *refs
):
    *projected_refs, side_ref, past_ref, next_ref, inside_ref, near_ref, far_ref, turned = refs
    count, rank, rows = aux_ref.shape
    for source, place in ((before_ref, past_ref), (after_ref, next_ref)):
        weights = source[...]
        rho = jnp.sum(weights * weights * diagonal_ref[...], axis=1, keepdims=True) / rank
        place[...] = jnp.broadcast_to(rho, place.shape)
    rho = all_rho(past_ref, rho_ref, next_ref)
    slices = range(count)
    smooth(
        odd_ref[0], [aux_ref[k] for k in slices], [target_ref[k] for k in slices], rho,
        inside_ref, near_ref, far_ref,
    )
    early = early_ref.shape[0]
    for pair in range(early):
        turned[pair] = early_ref[pair]
    for pair in range(early, count // 2):
        place = slice((pair - early) * rows, (pair - early + 1) * rows)
        turned[pair] = summed(projected_refs, place).T
    for k in slices:
        pair, place = stored_place(order_ref, k, count, rank)
        side_ref[k] = columns_ref[:, k : k + 1] * turned[pair, place, :]


def polar(grams, delta):
    rank, wide = grams[0].shape
    group = wide // rank
    mask = block_mask(rank, group)
    eye = wide_eye(rank, group)
    delta_wide = jnp.concatenate([delta] * group, axis=1)
    delta_blocks = block_diagonal(delta_wide, mask, group, NT)
    (across,) = from_left(delta.T, [delta_wide])
    traces = []
    for gram in grams:
        line = jnp.broadcast_to(jnp.sum(across * gram, axis=0, keepdims=True), (16, wide))
        high, low = split(line)
        rest = (line - high.astype(f32) - low.astype(f32)).astype(bf16)
        line = dot(high, mask) + dot(low, mask) + dot(rest, mask)
        traces.append(line[0:1] + eps_trace)
    rights = [times_blocks([gram], delta_blocks, NT)[0] for gram in grams]
    normals = from_left(delta, rights)
    currents = [normal / trace for normal, trace in zip(normals, traces)]
    scales = [1.0 / jnp.sqrt(trace) for trace in traces]
    roots = []
    for step in range(POLAR):
        for at in range(len(grams)):
            product = currents[at]
            blocks = block_diagonal(product, mask, group)
            if step == 0:
                roots.append(1.5 * eye - 0.5 * product)
                (square,) = times_blocks([product], blocks)
            elif step < POLAR - 1:
                square, more = times_blocks([product, roots[at]], blocks)
                roots[at] = 1.5 * roots[at] - 0.5 * more
            else:
                (more,) = times_blocks([roots[at]], blocks)
                roots[at] = 1.5 * roots[at] - 0.5 * more
            if step < POLAR - 1:
                half = 1.5 * product - 0.5 * square
                (more,) = times_blocks([half], blocks)
                currents[at] = 1.5 * half - 0.5 * more
    return roots, scales, rights


def mix(roots, scales, rights, delta, mixed_ref, partial_ref):
    rank, wide = roots[0].shape
    group = wide // rank
    mask = block_mask(rank, group)
    delta_blocks = block_diagonal(jnp.concatenate([delta] * group, axis=1), mask, group)
    left, right = [], []
    for at in range(len(roots)):
        high, low = split(roots[at] * scales[at])
        left += [high, high, low]
        high, low = split(rights[at])
        right += [high, low, high]
    partial = dot(jnp.concatenate(right, axis=1), jnp.concatenate(left, axis=1), NT)
    for at in range(len(roots)):
        (mixed,) = times_blocks([roots[at]], delta_blocks)
        mixed_ref[at] = mixed * scales[at]
    half = rank // 2
    partial_ref[...] = jnp.concatenate([partial[:half], partial[half:]], axis=1)


def first_polar_kernel(after_ref, delta_ref, *refs):
    *gram_refs, mixed_ref, partial_ref, gram_ref = refs
    grams = [summed(gram_refs, at) for at in range(gram_ref.shape[0])]
    for at in range(len(grams)):
        gram_ref[at] = grams[at]
    delta = delta_ref[...]
    mix(*polar(grams, delta), delta, mixed_ref, partial_ref)


def later_polar_kernel(last, after_ref, delta_ref, change_ref, old_ref, *refs):
    if last:
        *cross_refs, mixed_ref, partial_ref = refs
    else:
        *cross_refs, mixed_ref, partial_ref, gram_ref = refs
    groups, rank, wide = old_ref.shape
    group = wide // rank
    mask = block_mask(rank, group)
    grams = []
    for at in range(groups):
        cross = summed(cross_refs, at)
        change = change_ref[at]
        (onward,) = times_blocks([change], block_diagonal(old_ref[at], mask, group))
        onward = cross[:, :wide] + 0.5 * onward
        (one,) = times_blocks([onward], block_diagonal(change, mask, group, NT), NT)
        (other,) = times_blocks([change], block_diagonal(onward, mask, group, NT), NT)
        grams.append(cross[:, wide:] + one + other)
        if not last:
            gram_ref[at] = grams[at]
    delta = delta_ref[...]
    mix(*polar(grams, delta), delta, mixed_ref, partial_ref)


def ahead_kernel(
    group, odd_ref, after_ref, inside_ref, near_ref, far_ref, target_ref, tall_ref, side_ref, rho_ref,
    inverse_ref, known_ref, cross_ref, *kept
):
    count, rank, rows = inside_ref.shape
    width = SWEEPS
    knowns, talls = [], []
    for k in range(count):
        aux = inside_ref[k]
        for at, mine, other in ((k, near_ref, far_ref), (k - count + width, far_ref, near_ref)):
            if 0 <= at < width:
                lanes = slice((at % 2) * rows, (at % 2 + 1) * rows)
                aux = aux + jnp.where(
                    odd_ref[0] == 1, mine[at // 2, :, lanes], other[at // 2, :, lanes]
                )
        target, tall = target_ref[k], tall_ref[k]
        if kept:
            aux_ref, dual_ref = kept
            aux_ref[k] = aux
            dual_ref[k] = target - aux
        known = dot(
            inverse_ref[k],
            right_triple(side_ref[k] + rho_ref[k : k + 1, 0:1] * (2.0 * aux - target - tall)),
        )
        known_ref[k] = known
        talls.append(tall)
        knowns.append(known + tall)
        if len(talls) == group:
            cross_ref[k // group] = jnp.concatenate(
                [cross_blocks(knowns, talls, rank), cross_blocks(knowns, knowns, rank)], axis=1
            )
            knowns, talls = [], []


def add_kernel(unread, *refs):
    *term_refs, total_ref = refs[unread:]
    total = term_refs[0][...]
    for ref in term_refs[1:]:
        total = total + ref[...]
    total_ref[...] = total


def new_delta(sum_refs, total, rank):
    packed = sum_refs[0][...]
    for ref in sum_refs[1:]:
        packed = packed + ref[...]
    packed = packed / total
    return jnp.concatenate([packed[:, :rank], packed[:, rank:]], axis=0)


def mixer_kernel(total, mixed_ref, inverse_ref, rho_ref, *refs):
    *sum_refs, delta_ref, change_ref, forward_ref = refs
    groups, rank, wide = mixed_ref.shape
    group = wide // rank
    turned = new_delta(sum_refs, total, rank)
    delta_ref[...] = turned.T
    mixers = from_left(turned, [mixed_ref[at] for at in range(groups)])
    place = lax.div(lax.broadcasted_iota(jnp.int32, (1, wide), 1), rank)
    for at in range(groups):
        mixer = mixers[at]
        slices = range(at * group, (at + 1) * group)
        inverses = jnp.concatenate([inverse_ref[k] for k in slices], axis=0)
        onward = diagonal_blocks(dot(inverses, right_triple(mixer)), rank, group)
        rho = rho_ref[at * group : at * group + 1, 0:1]
        for k in slices[1:]:
            rho = jnp.where(place == k - at * group, rho_ref[k : k + 1, 0:1], rho)
        forward = 2.0 * rho * onward
        forward_ref[at] = forward
        change_ref[at] = forward - mixer


def rows_kernel(odd_ref, aux_ref, before_ref, rho_ref, after_ref, *refs):
    (change_ref, forward_ref, tall_ref, known_ref, dual_ref) = refs[:5]
    (next_ref, target_ref, inside_ref, near_ref, far_ref) = refs[5:]
    targets = new_rows(change_ref, forward_ref, tall_ref, known_ref, next_ref)
    count = len(targets)
    for k in range(count):
        targets[k] = targets[k] + dual_ref[k]
        target_ref[k] = targets[k]
    rho = all_rho(before_ref, rho_ref, after_ref)
    smooth(
        odd_ref[0], [aux_ref[k] for k in range(count)], targets, rho,
        inside_ref, near_ref, far_ref,
    )


def last_rows_kernel(mixed_ref, change_ref, forward_ref, tall_ref, known_ref, *outs):
    mixed_tall_ref, evolving_ref, next_ref = outs
    evolvings = new_rows(change_ref, forward_ref, tall_ref, known_ref, next_ref)
    groups, rank, wide = mixed_ref.shape
    group = wide // rank
    for k in range(len(evolvings)):
        evolving_ref[k] = evolvings[k]
        place = (k % group) * rank
        mixed = left_triple(mixed_ref[k // group][:, place : place + rank])
        mixed_tall_ref[k] = right_triple(dot(mixed, right_triple(next_ref[k])))


def new_rows(change_ref, forward_ref, tall_ref, known_ref, next_ref):
    groups, rank, wide = change_ref.shape
    group = wide // rank
    evolvings = []
    for k in range(groups * group):
        lanes = slice((k % group) * rank, (k % group + 1) * rank)
        change, forward = change_ref[k // group][:, lanes], forward_ref[k // group][:, lanes]
        left = jnp.concatenate([left_triple(change), left_triple(forward)], axis=0)
        tall, known = tall_ref[k], known_ref[k]
        both = dot(left, right_triple(tall))
        next_ref[k] = known + tall + both[:rank]
        evolvings.append(known + both[rank:])
    return evolvings


def last_kernel(total, mixed_tall_ref, *refs):
    *sum_refs, coupled_ref, delta_ref = refs
    turned = new_delta(sum_refs, total, delta_ref.shape[0])
    delta_ref[...] = turned.T
    delta_left = left_triple(turned)
    for k in range(coupled_ref.shape[0]):
        coupled_ref[k] = dot(delta_left, mixed_tall_ref[k])


per_microsecond = 1_100_000_000


def call(
    kernel, name, outs, *args, scalars=0, unread=0, microseconds=0.3, limit=16, scratch=()
):
    flops = int(microseconds * per_microsecond)
    specs = [pl.BlockSpec(memory_space=pltpu.SMEM)] * scalars
    specs += [pl.BlockSpec(memory_space=pl.ANY)] * unread
    specs += [pl.BlockSpec(memory_space=pltpu.VMEM)] * (len(args) - len(specs))
    shapes = [jax.ShapeDtypeStruct(shape, dtype) for shape, dtype in outs]
    moved = sum(arg.size * arg.dtype.itemsize for arg in args)
    moved += sum(shape.size * shape.dtype.itemsize for shape in shapes)
    return pl.pallas_call(
        kernel,
        out_shape=shapes,
        in_specs=specs,
        out_specs=[pl.BlockSpec(memory_space=pltpu.VMEM)] * len(shapes),
        scratch_shapes=list(scratch),
        compiler_params=pltpu.CompilerParams(vmem_limit_bytes=limit * 1024 * 1024),
        cost_estimate=pl.CostEstimate(flops=flops, bytes_accessed=moved, transcendentals=0),
        name=name,
    )(*args)


def rotated(value, axis, shift):
    count = lax.axis_size(axis)
    return lax.ppermute(value, axis, [(i, (i + shift) % count) for i in range(count)])


def swapped(value, axis, first):
    count = lax.axis_size(axis)
    pairs = [((i + first) % count, (i + first + 1) % count) for i in range(0, count, 2)]
    return lax.ppermute(value, axis, pairs + [(b, a) for a, b in pairs])


def from_others(value, axis):
    return [rotated(value, axis, shift) for shift in range(1, lax.axis_size(axis))]


def stage_sizes(count):
    sizes = []
    while count > 1:
        sizes.append(next(size for size in (4, 2, 3, 5, 7, count) if count % size == 0))
        count //= sizes[-1]
    return sizes


def in_stages(value, axis, beside=None):
    count = lax.axis_size(axis)
    stride = 1
    terms, firsts = [value], []
    for size in stage_sizes(count):
        value = terms[0]
        if len(terms) > 1:
            unread = [] if beside is None else [beside]
            (value,) = call(
                functools.partial(add_kernel, len(unread)),
                "add",
                [(value.shape, f32)],
                *unread, *terms,
                unread=len(unread),
            )
        terms = [value]
        for shift in range(1, size):
            moves = []
            for i in range(count):
                digit = (i // stride) % size
                other = digit ^ shift if size in (2, 4) else (digit + shift) % size
                moves.append((i, i + (other - digit) * stride))
            terms.append(lax.ppermute(value, axis, moves))
        stride *= size
        firsts = firsts or terms
    return terms, firsts


def body(
    data, order, chan_factor, slice_weights, smooth_aux, coupled, smooth_dual, coupling_dual, delta
):
    count, all_rows, channels = data.shape
    rank = chan_factor.shape[1]
    rows = smooth_aux.shape[1]
    parts = lax.axis_size("chan")
    total = count * lax.axis_size("cuts")
    group = group_size(count, rank)
    groups = count // group
    wide = group * rank
    flip = lambda value: jnp.swapaxes(value, 1, 2)
    aux, coup, dual_s, dual_c = map(flip, (smooth_aux, coupled, smooth_dual, coupling_dual))
    factor = chan_factor.T
    state = ((count, rank, rows), f32)
    quads = ((groups, rank, wide), f32)
    square = ((rank, rank), f32)
    halo = (((SWEEPS + 1) // 2, rank, 2 * rows), f32)
    lanes = lambda height: ((height, 128), f32)
    scale = ((groups, 8, wide), f32)

    me = lax.axis_index("chan").astype(jnp.int32).reshape(1)
    odd = lax.rem(lax.axis_index("cuts"), 2).astype(jnp.int32).reshape(1)
    early = count // 4
    own, received = [], []
    for first, pairs, lead in ((0, early, True), (2 * early, count // 2 - early, False)):
        height = pairs * rows + (rank // 2 if lead else 0)
        projected = call(
            functools.partial(project_kernel, first, pairs, rows, lead),
            "project",
            [((height, 2 * rank), f32)] * parts + [(factor.shape, factor.dtype)] * lead,
            me, data, factor,
            scalars=1, unread=1, limit=52,
            scratch=[
                pltpu.VMEM((2 * pairs, all_rows, channels), data.dtype),
                pltpu.SemaphoreType.DMA((4 * pairs,)),
            ],
        )
        if lead:
            *projected, factor = projected
        own.append(projected[0])
        received.append([rotated(projected[shift], "chan", shift) for shift in range(1, parts)])

    late_weights, _ = lax.optimization_barrier((slice_weights, own[-1]))
    before = rotated(late_weights, "cuts", 1)
    after = rotated(late_weights, "cuts", -1)
    inverse, mover, rho, diagonal, columns, base = call(
        functools.partial(setup_kernel, parts, early * rows, group),
        "setup",
        [
            ((count, rank, 3 * rank), bf16),
            ((count // 2, 2 * rank, 6 * rank), bf16),
            lanes(count),
            ((count, rank), f32),
            ((rank, count), f32),
            state,
        ],
        order, own[0], *received[0], slice_weights, aux, coup, dual_s, dual_c,
        scalars=1,
    )
    half_state = ((early, 2 * rank, rows), f32)
    moved, turned = call(
        move_kernel, "move", [half_state, half_state], mover, own[0], *received[0]
    )
    tall, target, gram = call(
        functools.partial(first_kernel, group),
        "first",
        [state, state, quads],
        order, before, after, base, mover, dual_s, dual_c, moved, own[1], *received[1],
        scalars=1, unread=2,
        scratch=[pltpu.VMEM((count // 2, 2 * rank, rows), f32)],
    )
    side, before, after, inside, to_near, to_far = call(
        smooth_kernel,
        "smooth",
        [state, lanes(count), lanes(count), state, halo, halo],
        odd, order, aux, target, before, rho, after, diagonal, columns, turned, own[1],
        *received[1],
        scalars=2,
        scratch=[pltpu.VMEM((count // 2, 2 * rank, rows), f32)],
    )
    polar_outs = [quads, ((rank // 2, 2 * rank), f32), quads]
    for inner in range(INNER):
        if inner == 0:
            mixed, partial, gram = call(
                first_polar_kernel,
                "polar",
                polar_outs,
                inside, delta, gram, *from_others(gram, "chan"),
                unread=1, microseconds=3,
            )
        else:
            last = inner == INNER - 1
            mixed, partial, *gram = call(
                functools.partial(later_polar_kernel, last),
                "polar",
                polar_outs[:2] if last else polar_outs,
                inside, delta, change, old, cross, *crosses,
                unread=1,
            )
            gram = gram[0] if gram else None
        if inner == INNER - 1:
            mixed_tall, evolving = call(
                last_rows_kernel,
                "rows",
                [((count, 3 * rank, rows), bf16), state],
                mixed, change, forward, tall, known,
                scratch=[pltpu.VMEM(state[0], f32)],
            )
            coup, delta = call(
                functools.partial(last_kernel, total),
                "last",
                [state, square],
                mixed_tall, *in_stages(partial, "cuts")[0],
            )
            continue
        near = swapped(to_near, "cuts", 0)
        far = swapped(to_far, "cuts", 1)
        known, cross, *kept = call(
            functools.partial(ahead_kernel, group),
            "ahead",
            [state, ((groups, rank, 2 * wide), f32)] + [state] * (2 if inner < INNER - 2 else 0),
            odd, partial, inside, near, far, target, tall, side, rho, inverse,
            scalars=1, unread=1,
        )
        sums, firsts = in_stages(partial, "cuts", beside=cross)
        _, cross = lax.optimization_barrier((firsts, cross))
        crosses = from_others(cross, "chan")
        old = gram
        delta, change, forward = call(
            functools.partial(mixer_kernel, total),
            "mixer",
            [square, quads, quads],
            mixed, inverse, rho, *sums,
        )
        if inner < INNER - 2:
            tall, target, inside, to_near, to_far = call(
                rows_kernel,
                "rows",
                [state, state, state, halo, halo],
                odd, kept[0], before, rho, after, change, forward, tall, known, kept[1],
                scalars=1,
            )
    return (flip(evolving), flip(coup), delta)


def solution(mesh):
    return jax.shard_map(
        body,
        mesh=mesh,
        in_specs=(
            P("cuts", None, "chan"),
            P("cuts"),
            P("chan", None),
            P("cuts", None),
            P("cuts", "chan", None),
            P("cuts", "chan", None),
            P("cuts", "chan", None),
            P("cuts", "chan", None),
            P(),
        ),
        out_specs=(P("cuts", "chan", None), P("cuts", "chan", None), P()),
        check_vma=False,
    )
```

```python
import functools

import jax
import jax.numpy as jnp
from jax import lax
from jax.experimental import pallas as pl
from jax.experimental.pallas import tpu as pltpu
from jax.sharding import PartitionSpec as P

INNER = 3
SWEEPS = 4
POLAR = 8

smooth_weight = 1.0
eps_trace = 1e-06
f32 = jnp.float32
bf16 = jnp.bfloat16
NN = (((1,), (0,)), ((), ()))
NT = (((1,), (1,)), ((), ()))


def dot(left, right, dims=NN):
    return lax.dot_general(left, right, dims, preferred_element_type=f32)


def split(value):
    high = value.astype(bf16)
    low = (value - high.astype(f32)).astype(bf16)
    return high, low


def left_triple(value):
    high, low = split(value)
    return jnp.concatenate([high, high, low], axis=1)


def right_triple(value):
    high, low = split(value)
    return jnp.concatenate([high, low, high], axis=0)


def block_mask(rank, group):
    wide = rank * group
    rows = lax.div(lax.broadcasted_iota(jnp.int32, (wide, wide), 0), rank)
    cols = lax.div(lax.broadcasted_iota(jnp.int32, (wide, wide), 1), rank)
    return jnp.where(rows == cols, 1.0, 0.0).astype(bf16)


def wide_eye(rank, group):
    rows = lax.broadcasted_iota(jnp.int32, (rank, rank * group), 0)
    cols = lax.broadcasted_iota(jnp.int32, (rank, rank * group), 1)
    return jnp.where(rows == lax.rem(cols, rank), 1.0, 0.0).astype(f32)


def block_diagonal(value, mask, group, dims=NN):
    high, low = [jnp.concatenate([part] * group, axis=0) * mask for part in split(value)]
    return jnp.concatenate([high, low, high], axis=0 if dims == NN else 1)


def times_blocks(values, blocks, dims=NN):
    rank = values[0].shape[0]
    total = dot(jnp.concatenate([left_triple(value) for value in values], axis=0), blocks, dims)
    return [total[at * rank : (at + 1) * rank] for at in range(len(values))]


def diagonal_blocks(value, rank, group):
    at = lax.div(lax.broadcasted_iota(jnp.int32, (rank, rank * group), 1), rank)
    total = value[:rank]
    for block in range(1, group):
        total = jnp.where(at == block, value[block * rank : (block + 1) * rank], total)
    return total


def from_left(left, values):
    wide = values[0].shape[1]
    total = dot(left_triple(left), right_triple(jnp.concatenate(values, axis=1)))
    return [total[:, at * wide : (at + 1) * wide] for at in range(len(values))]


def group_size(count, rank):
    group = max(1, 128 // rank)
    while count % group:
        group -= 1
    return group


def project_kernel(first, pairs, rows, lead, me_ref, data_ref, factor_ref, *refs):
    *outs, held, arrived = refs
    half = data_ref.shape[1] // 2
    copies = []
    for k in range(2 * pairs):
        for at in range(2):
            place = pl.ds(at * half, half)
            copies.append(
                pltpu.make_async_copy(
                    data_ref.at[first + k, place, :], held.at[k, place, :], arrived.at[2 * k + at]
                )
            )
            copies[-1].start()
    factor = factor_ref[...]
    rank = factor.shape[0]
    if lead:
        *outs, again_ref = outs
        again_ref[...] = factor
        gram = dot(factor, factor, NT)
        for out in outs:
            out[pairs * rows :, :] = jnp.concatenate([gram[: rank // 2], gram[rank // 2 :]], axis=1)
    parts = len(outs)
    empty = jnp.zeros_like(factor)
    sides = [
        jnp.concatenate([factor, empty], axis=0),
        jnp.concatenate([empty, factor], axis=0),
    ]
    for pair in range(pairs):
        for copy in copies[4 * pair : 4 * pair + 4]:
            copy.wait()
        for part in reversed(range(parts)):
            start = pl.multiple_of(lax.rem(me_ref[0] + part, parts) * rows, 16)
            place = pl.ds(start, rows)
            outs[part][pair * rows : (pair + 1) * rows, :] = dot(
                held[2 * pair, place, :], sides[0], NT
            ) + dot(held[2 * pair + 1, place, :], sides[1], NT)


def setup_kernel(parts, first, group, order_ref, *refs):
    lead_refs, refs = refs[:parts], refs[parts:]
    (own_ref, aux_ref, coupled_ref, dual_s_ref, dual_c_ref) = refs[:5]
    (inverse_ref, mover_ref, rho_ref, diagonal_ref, columns_ref, base_ref) = refs[5:]
    count, rank = own_ref.shape
    gram = summed(lead_refs, slice(first, None))
    gram = jnp.concatenate([gram[:, :rank], gram[:, rank:]], axis=0)
    eye = wide_eye(rank, 1)
    diagonal = jnp.sum(gram * eye, axis=0, keepdims=True)
    diagonal_ref[...] = jnp.broadcast_to(diagonal, diagonal_ref.shape)
    weights = own_ref[...]
    columns = weights.T
    columns_ref[...] = columns
    rho = jnp.sum(weights * weights * diagonal, axis=1, keepdims=True) / rank
    rho_ref[...] = jnp.broadcast_to(rho, rho_ref.shape)

    centre = rank / 2.0 + 2.0
    edge = centre / (rank / 2.0)
    lead = 4.0 * edge**3 / (4.0 * edge**3 - 3.0 * edge)
    mask = block_mask(rank, group)
    wide = wide_eye(rank, group)
    starts = range(0, count, group)
    systems = []
    for first in starts:
        scaled = []
        for k in range(first, first + group):
            unit = 1.0 / (centre * rho[k : k + 1, :])
            column = columns[:, k : k + 1]
            scaled.append(column * gram * weights[k : k + 1, :] * unit + (2.0 / centre) * eye)
        systems.append(jnp.concatenate(scaled, axis=1))
    inverses, rests = [], []
    for system in systems:
        rest = wide - system
        blocks = block_diagonal(rest, mask, group)
        (square,) = times_blocks([rest], blocks)
        (cube,) = times_blocks([square], blocks)
        inverses.append(wide + lead * (rest + square))
        rests.append(lead * cube - (lead - 1.0) * rest)
    for step in range(5):
        for at in range(len(systems)):
            blocks = block_diagonal(rests[at], mask, group)
            more, *rest = times_blocks([inverses[at], rests[at]][: 2 if step < 4 else 1], blocks)
            inverses[at] = inverses[at] + more
            rests[at] = rest[0] if rest else None
    for at in range(len(systems)):
        (product,) = times_blocks([inverses[at]], block_diagonal(systems[at], mask, group))
        blocks = block_diagonal(wide - product, mask, group)
        (more,) = times_blocks([inverses[at]], blocks)
        inverses[at] = inverses[at] + more
    for k in range(count):
        place = (k % group) * rank
        unit = 1.0 / (centre * rho[k : k + 1, :])
        inverse = inverses[k // group][:, place : place + rank] * unit
        inverse_ref[k] = left_triple(inverse)
        base_ref[k] = dot(
            inverse_ref[k],
            right_triple(
                rho[k : k + 1, :] * (aux_ref[k] - dual_s_ref[k] + coupled_ref[k] - dual_c_ref[k])
            ),
        )
        both = jnp.concatenate([inverse * weights[k : k + 1, :]] * 2, axis=1)
        side = lax.div(lax.broadcasted_iota(jnp.int32, both.shape, 1), rank)
        both = jnp.where(side == lax.rem(order_ref[k], 2), both, 0.0)
        high, low = split(both)
        pair, place = stored_place(order_ref, k, count, rank)
        mover_ref[pair, place, :] = jnp.concatenate([high, high, low], axis=1)


def cross_blocks(lefts, rights, rank):
    group = len(lefts)
    wide = group * rank
    left = jnp.concatenate(split(jnp.concatenate(lefts, axis=0)), axis=0)
    right = left
    if rights is not lefts:
        right = jnp.concatenate(split(jnp.concatenate(rights, axis=0)), axis=0)
    total = dot(left, right, NT)
    total = total[:wide, :wide] + total[:wide, wide:] + total[wide:, :wide]
    return diagonal_blocks(total, rank, group)


def summed(refs, at):
    total = refs[0][at]
    for ref in refs[1:]:
        total = total + ref[at]
    return total


def stored_place(order_ref, k, count, rank):
    stored = lax.rem(order_ref[k], count)
    return lax.div(stored, 2), pl.ds(pl.multiple_of(lax.rem(stored, 2) * rank, rank), rank)


def move(mover, projected):
    high, low = split(projected)
    return dot(mover, jnp.concatenate([high, low, high], axis=1), NT)


def move_kernel(mover_ref, *refs):
    *projected_refs, moved_ref, turned_ref = refs
    rows = moved_ref.shape[2]
    for pair in range(moved_ref.shape[0]):
        projected = summed(projected_refs, slice(pair * rows, (pair + 1) * rows))
        moved_ref[pair] = move(mover_ref[pair], projected)
        turned_ref[pair] = projected.T


def first_kernel(group, order_ref, *refs):
    base_ref, mover_ref, dual_s_ref, dual_c_ref, early_ref = refs[2:7]
    *projected_refs, tall_ref, target_ref, gram_ref, moved = refs[7:]
    count, rank, rows = base_ref.shape
    early = early_ref.shape[0]
    for pair in range(early):
        moved[pair] = early_ref[pair]
    for pair in range(early, count // 2):
        place = slice((pair - early) * rows, (pair - early + 1) * rows)
        moved[pair] = move(mover_ref[pair], summed(projected_refs, place))
    talls = []
    for k in range(count):
        pair, place = stored_place(order_ref, k, count, rank)
        evolving = base_ref[k] + moved[pair, place, :]
        target_ref[k] = evolving + dual_s_ref[k]
        tall = evolving + dual_c_ref[k]
        tall_ref[k] = tall
        talls.append(tall)
        if len(talls) == group:
            gram_ref[k // group] = cross_blocks(talls, talls, rank)
            talls = []


def smooth(odd, now, targets, rho, inside_ref, near_ref, far_ref):
    count = len(targets)
    width = SWEEPS
    share = {j: 2.0 * smooth_weight / (rho[j] + 4.0 * smooth_weight) for j in rho}
    pull = {j: (rho[j] / (rho[j] + 4.0 * smooth_weight)) * targets[j] for j in range(count)}
    now = {j: now[j] for j in range(count)}
    for sweep in range(width):
        later = {}
        for j in range(-sweep - 1, count + sweep + 1):
            beside = [now[i] for i in (j - 1, j + 1) if i in now]
            total = beside[0] if len(beside) == 1 else beside[0] + beside[1]
            total = share[j] * total
            later[j] = total + pull[j] if j in pull else total
        now = later
    for j in range(count):
        inside_ref[j] = now[j]
    rows = inside_ref.shape[2]
    for j in range(width):
        lanes = slice((j % 2) * rows, (j % 2 + 1) * rows)
        near_ref[j // 2, :, lanes] = jnp.where(odd == 1, now[j - width], now[count + j])
        far_ref[j // 2, :, lanes] = jnp.where(odd == 1, now[count + j], now[j - width])


def all_rho(before_ref, rho_ref, after_ref):
    count = rho_ref.shape[0]
    rho = {j: rho_ref[j : j + 1, 0:1] for j in range(count)}
    for j in range(SWEEPS):
        rho[j - SWEEPS] = before_ref[count - SWEEPS + j : count - SWEEPS + j + 1, 0:1]
        rho[count + j] = after_ref[j : j + 1, 0:1]
    return rho


def smooth_kernel(
    odd_ref, order_ref, aux_ref, target_ref, before_ref, rho_ref, after_ref, diagonal_ref,
    columns_ref, early_ref, *refs
):
    *projected_refs, side_ref, past_ref, next_ref, inside_ref, near_ref, far_ref, turned = refs
    count, rank, rows = aux_ref.shape
    for source, place in ((before_ref, past_ref), (after_ref, next_ref)):
        weights = source[...]
        rho = jnp.sum(weights * weights * diagonal_ref[...], axis=1, keepdims=True) / rank
        place[...] = jnp.broadcast_to(rho, place.shape)
    rho = all_rho(past_ref, rho_ref, next_ref)
    slices = range(count)
    smooth(
        odd_ref[0], [aux_ref[k] for k in slices], [target_ref[k] for k in slices], rho,
        inside_ref, near_ref, far_ref,
    )
    early = early_ref.shape[0]
    for pair in range(early):
        turned[pair] = early_ref[pair]
    for pair in range(early, count // 2):
        place = slice((pair - early) * rows, (pair - early + 1) * rows)
        turned[pair] = summed(projected_refs, place).T
    for k in slices:
        pair, place = stored_place(order_ref, k, count, rank)
        side_ref[k] = columns_ref[:, k : k + 1] * turned[pair, place, :]


def polar(grams, delta):
    rank, wide = grams[0].shape
    group = wide // rank
    mask = block_mask(rank, group)
    eye = wide_eye(rank, group)
    delta_wide = jnp.concatenate([delta] * group, axis=1)
    delta_blocks = block_diagonal(delta_wide, mask, group, NT)
    (across,) = from_left(delta.T, [delta_wide])
    traces = []
    for gram in grams:
        line = jnp.broadcast_to(jnp.sum(across * gram, axis=0, keepdims=True), (16, wide))
        high, low = split(line)
        rest = (line - high.astype(f32) - low.astype(f32)).astype(bf16)
        line = dot(high, mask) + dot(low, mask) + dot(rest, mask)
        traces.append(line[0:1] + eps_trace)
    rights = [times_blocks([gram], delta_blocks, NT)[0] for gram in grams]
    normals = from_left(delta, rights)
    currents = [normal / trace for normal, trace in zip(normals, traces)]
    scales = [1.0 / jnp.sqrt(trace) for trace in traces]
    roots = []
    for step in range(POLAR):
        for at in range(len(grams)):
            product = currents[at]
            blocks = block_diagonal(product, mask, group)
            if step == 0:
                roots.append(1.5 * eye - 0.5 * product)
                (square,) = times_blocks([product], blocks)
            elif step < POLAR - 1:
                square, more = times_blocks([product, roots[at]], blocks)
                roots[at] = 1.5 * roots[at] - 0.5 * more
            else:
                (more,) = times_blocks([roots[at]], blocks)
                roots[at] = 1.5 * roots[at] - 0.5 * more
            if step < POLAR - 1:
                half = 1.5 * product - 0.5 * square
                (more,) = times_blocks([half], blocks)
                currents[at] = 1.5 * half - 0.5 * more
    return roots, scales, rights


def mix(roots, scales, rights, delta, mixed_ref, partial_ref):
    rank, wide = roots[0].shape
    group = wide // rank
    mask = block_mask(rank, group)
    delta_blocks = block_diagonal(jnp.concatenate([delta] * group, axis=1), mask, group)
    left, right = [], []
    for at in range(len(roots)):
        high, low = split(roots[at] * scales[at])
        left += [high, high, low]
        high, low = split(rights[at])
        right += [high, low, high]
    partial = dot(jnp.concatenate(right, axis=1), jnp.concatenate(left, axis=1), NT)
    for at in range(len(roots)):
        (mixed,) = times_blocks([roots[at]], delta_blocks)
        mixed_ref[at] = mixed * scales[at]
    half = rank // 2
    partial_ref[...] = jnp.concatenate([partial[:half], partial[half:]], axis=1)


def first_polar_kernel(after_ref, delta_ref, *refs):
    *gram_refs, mixed_ref, partial_ref, gram_ref = refs
    grams = [summed(gram_refs, at) for at in range(gram_ref.shape[0])]
    for at in range(len(grams)):
        gram_ref[at] = grams[at]
    delta = delta_ref[...]
    mix(*polar(grams, delta), delta, mixed_ref, partial_ref)


def later_polar_kernel(last, after_ref, delta_ref, change_ref, old_ref, *refs):
    if last:
        *cross_refs, mixed_ref, partial_ref = refs
    else:
        *cross_refs, mixed_ref, partial_ref, gram_ref = refs
    groups, rank, wide = old_ref.shape
    group = wide // rank
    mask = block_mask(rank, group)
    grams = []
    for at in range(groups):
        cross = summed(cross_refs, at)
        change = change_ref[at]
        (onward,) = times_blocks([change], block_diagonal(old_ref[at], mask, group))
        onward = cross[:, :wide] + 0.5 * onward
        (one,) = times_blocks([onward], block_diagonal(change, mask, group, NT), NT)
        (other,) = times_blocks([change], block_diagonal(onward, mask, group, NT), NT)
        grams.append(cross[:, wide:] + one + other)
        if not last:
            gram_ref[at] = grams[at]
    delta = delta_ref[...]
    mix(*polar(grams, delta), delta, mixed_ref, partial_ref)


def ahead_kernel(
    group, odd_ref, after_ref, inside_ref, near_ref, far_ref, target_ref, tall_ref, side_ref, rho_ref,
    inverse_ref, known_ref, cross_ref, *kept
):
    count, rank, rows = inside_ref.shape
    width = SWEEPS
    knowns, talls = [], []
    for k in range(count):
        aux = inside_ref[k]
        for at, mine, other in ((k, near_ref, far_ref), (k - count + width, far_ref, near_ref)):
            if 0 <= at < width:
                lanes = slice((at % 2) * rows, (at % 2 + 1) * rows)
                aux = aux + jnp.where(
                    odd_ref[0] == 1, mine[at // 2, :, lanes], other[at // 2, :, lanes]
                )
        target, tall = target_ref[k], tall_ref[k]
        if kept:
            aux_ref, dual_ref = kept
            aux_ref[k] = aux
            dual_ref[k] = target - aux
        known = dot(
            inverse_ref[k],
            right_triple(side_ref[k] + rho_ref[k : k + 1, 0:1] * (2.0 * aux - target - tall)),
        )
        known_ref[k] = known
        talls.append(tall)
        knowns.append(known + tall)
        if len(talls) == group:
            cross_ref[k // group] = jnp.concatenate(
                [cross_blocks(knowns, talls, rank), cross_blocks(knowns, knowns, rank)], axis=1
            )
            knowns, talls = [], []


def add_kernel(unread, *refs):
    *term_refs, total_ref = refs[unread:]
    total = term_refs[0][...]
    for ref in term_refs[1:]:
        total = total + ref[...]
    total_ref[...] = total


def new_delta(sum_refs, total, rank):
    packed = sum_refs[0][...]
    for ref in sum_refs[1:]:
        packed = packed + ref[...]
    packed = packed / total
    return jnp.concatenate([packed[:, :rank], packed[:, rank:]], axis=0)


def mixer_kernel(total, mixed_ref, inverse_ref, rho_ref, *refs):
    *sum_refs, delta_ref, change_ref, forward_ref = refs
    groups, rank, wide = mixed_ref.shape
    group = wide // rank
    turned = new_delta(sum_refs, total, rank)
    delta_ref[...] = turned.T
    mixers = from_left(turned, [mixed_ref[at] for at in range(groups)])
    place = lax.div(lax.broadcasted_iota(jnp.int32, (1, wide), 1), rank)
    for at in range(groups):
        mixer = mixers[at]
        slices = range(at * group, (at + 1) * group)
        inverses = jnp.concatenate([inverse_ref[k] for k in slices], axis=0)
        onward = diagonal_blocks(dot(inverses, right_triple(mixer)), rank, group)
        rho = rho_ref[at * group : at * group + 1, 0:1]
        for k in slices[1:]:
            rho = jnp.where(place == k - at * group, rho_ref[k : k + 1, 0:1], rho)
        forward = 2.0 * rho * onward
        forward_ref[at] = forward
        change_ref[at] = forward - mixer


def rows_kernel(odd_ref, aux_ref, before_ref, rho_ref, after_ref, *refs):
    (change_ref, forward_ref, tall_ref, known_ref, dual_ref) = refs[:5]
    (next_ref, target_ref, inside_ref, near_ref, far_ref) = refs[5:]
    targets = new_rows(change_ref, forward_ref, tall_ref, known_ref, next_ref)
    count = len(targets)
    for k in range(count):
        targets[k] = targets[k] + dual_ref[k]
        target_ref[k] = targets[k]
    rho = all_rho(before_ref, rho_ref, after_ref)
    smooth(
        odd_ref[0], [aux_ref[k] for k in range(count)], targets, rho,
        inside_ref, near_ref, far_ref,
    )


def last_rows_kernel(mixed_ref, change_ref, forward_ref, tall_ref, known_ref, *outs):
    mixed_tall_ref, evolving_ref, next_ref = outs
    evolvings = new_rows(change_ref, forward_ref, tall_ref, known_ref, next_ref)
    groups, rank, wide = mixed_ref.shape
    group = wide // rank
    for k in range(len(evolvings)):
        evolving_ref[k] = evolvings[k]
        place = (k % group) * rank
        mixed = left_triple(mixed_ref[k // group][:, place : place + rank])
        mixed_tall_ref[k] = right_triple(dot(mixed, right_triple(next_ref[k])))


def new_rows(change_ref, forward_ref, tall_ref, known_ref, next_ref):
    groups, rank, wide = change_ref.shape
    group = wide // rank
    evolvings = []
    for k in range(groups * group):
        lanes = slice((k % group) * rank, (k % group + 1) * rank)
        change, forward = change_ref[k // group][:, lanes], forward_ref[k // group][:, lanes]
        left = jnp.concatenate([left_triple(change), left_triple(forward)], axis=0)
        tall, known = tall_ref[k], known_ref[k]
        both = dot(left, right_triple(tall))
        next_ref[k] = known + tall + both[:rank]
        evolvings.append(known + both[rank:])
    return evolvings


def last_kernel(total, mixed_tall_ref, *refs):
    *sum_refs, coupled_ref, delta_ref = refs
    turned = new_delta(sum_refs, total, delta_ref.shape[0])
    delta_ref[...] = turned.T
    delta_left = left_triple(turned)
    for k in range(coupled_ref.shape[0]):
        coupled_ref[k] = dot(delta_left, mixed_tall_ref[k])


per_microsecond = 1_100_000_000


def call(
    kernel, name, outs, *args, scalars=0, unread=0, microseconds=0.3, limit=16, scratch=()
):
    flops = int(microseconds * per_microsecond)
    specs = [pl.BlockSpec(memory_space=pltpu.SMEM)] * scalars
    specs += [pl.BlockSpec(memory_space=pl.ANY)] * unread
    specs += [pl.BlockSpec(memory_space=pltpu.VMEM)] * (len(args) - len(specs))
    shapes = [jax.ShapeDtypeStruct(shape, dtype) for shape, dtype in outs]
    moved = sum(arg.size * arg.dtype.itemsize for arg in args)
    moved += sum(shape.size * shape.dtype.itemsize for shape in shapes)
    return pl.pallas_call(
        kernel,
        out_shape=shapes,
        in_specs=specs,
        out_specs=[pl.BlockSpec(memory_space=pltpu.VMEM)] * len(shapes),
        scratch_shapes=list(scratch),
        compiler_params=pltpu.CompilerParams(vmem_limit_bytes=limit * 1024 * 1024),
        cost_estimate=pl.CostEstimate(flops=flops, bytes_accessed=moved, transcendentals=0),
        name=name,
    )(*args)


def rotated(value, axis, shift):
    count = lax.axis_size(axis)
    return lax.ppermute(value, axis, [(i, (i + shift) % count) for i in range(count)])


def swapped(value, axis, first):
    count = lax.axis_size(axis)
    pairs = [((i + first) % count, (i + first + 1) % count) for i in range(0, count, 2)]
    return lax.ppermute(value, axis, pairs + [(b, a) for a, b in pairs])


def from_others(value, axis):
    return [rotated(value, axis, shift) for shift in range(1, lax.axis_size(axis))]


def stage_sizes(count):
    sizes = []
    while count > 1:
        sizes.append(next(size for size in (4, 2, 3, 5, 7, count) if count % size == 0))
        count //= sizes[-1]
    return sizes


def in_stages(value, axis, beside=None):
    count = lax.axis_size(axis)
    stride = 1
    terms, firsts = [value], []
    for size in stage_sizes(count):
        value = terms[0]
        if len(terms) > 1:
            unread = [] if beside is None else [beside]
            (value,) = call(
                functools.partial(add_kernel, len(unread)),
                "add",
                [(value.shape, f32)],
                *unread, *terms,
                unread=len(unread),
            )
        terms = [value]
        for shift in range(1, size):
            moves = []
            for i in range(count):
                digit = (i // stride) % size
                other = digit ^ shift if size in (2, 4) else (digit + shift) % size
                moves.append((i, i + (other - digit) * stride))
            terms.append(lax.ppermute(value, axis, moves))
        stride *= size
        firsts = firsts or terms
    return terms, firsts


def body(
    data, order, chan_factor, slice_weights, smooth_aux, coupled, smooth_dual, coupling_dual, delta
):
    count, all_rows, channels = data.shape
    rank = chan_factor.shape[1]
    rows = smooth_aux.shape[1]
    parts = lax.axis_size("chan")
    total = count * lax.axis_size("cuts")
    group = group_size(count, rank)
    groups = count // group
    wide = group * rank
    flip = lambda value: jnp.swapaxes(value, 1, 2)
    aux, coup, dual_s, dual_c = map(flip, (smooth_aux, coupled, smooth_dual, coupling_dual))
    factor = chan_factor.T
    state = ((count, rank, rows), f32)
    quads = ((groups, rank, wide), f32)
    square = ((rank, rank), f32)
    halo = (((SWEEPS + 1) // 2, rank, 2 * rows), f32)
    lanes = lambda height: ((height, 128), f32)
    scale = ((groups, 8, wide), f32)

    me = lax.axis_index("chan").astype(jnp.int32).reshape(1)
    odd = lax.rem(lax.axis_index("cuts"), 2).astype(jnp.int32).reshape(1)
    early = count // 4
    own, received = [], []
    for first, pairs, lead in ((0, early, True), (2 * early, count // 2 - early, False)):
        height = pairs * rows + (rank // 2 if lead else 0)
        projected = call(
            functools.partial(project_kernel, first, pairs, rows, lead),
            "project",
            [((height, 2 * rank), f32)] * parts + [(factor.shape, factor.dtype)] * lead,
            me, data, factor,
            scalars=1, unread=1, limit=52,
            scratch=[
                pltpu.VMEM((2 * pairs, all_rows, channels), data.dtype),
                pltpu.SemaphoreType.DMA((4 * pairs,)),
            ],
        )
        if lead:
            *projected, factor = projected
        own.append(projected[0])
        received.append([rotated(projected[shift], "chan", shift) for shift in range(1, parts)])

    late_weights, _ = lax.optimization_barrier((slice_weights, own[-1]))
    before = rotated(late_weights, "cuts", 1)
    after = rotated(late_weights, "cuts", -1)
    inverse, mover, rho, diagonal, columns, base = call(
        functools.partial(setup_kernel, parts, early * rows, group),
        "setup",
        [
            ((count, rank, 3 * rank), bf16),
            ((count // 2, 2 * rank, 6 * rank), bf16),
            lanes(count),
            ((count, rank), f32),
            ((rank, count), f32),
            state,
        ],
        order, own[0], *received[0], slice_weights, aux, coup, dual_s, dual_c,
        scalars=1,
    )
    half_state = ((early, 2 * rank, rows), f32)
    moved, turned = call(
        move_kernel, "move", [half_state, half_state], mover, own[0], *received[0]
    )
    tall, target, gram = call(
        functools.partial(first_kernel, group),
        "first",
        [state, state, quads],
        order, before, after, base, mover, dual_s, dual_c, moved, own[1], *received[1],
        scalars=1, unread=2,
        scratch=[pltpu.VMEM((count // 2, 2 * rank, rows), f32)],
    )
    side, before, after, inside, to_near, to_far = call(
        smooth_kernel,
        "smooth",
        [state, lanes(count), lanes(count), state, halo, halo],
        odd, order, aux, target, before, rho, after, diagonal, columns, turned, own[1],
        *received[1],
        scalars=2,
        scratch=[pltpu.VMEM((count // 2, 2 * rank, rows), f32)],
    )
    polar_outs = [quads, ((rank // 2, 2 * rank), f32), quads]
    for inner in range(INNER):
        if inner == 0:
            mixed, partial, gram = call(
                first_polar_kernel,
                "polar",
                polar_outs,
                inside, delta, gram, *from_others(gram, "chan"),
                unread=1, microseconds=3,
            )
        else:
            last = inner == INNER - 1
            mixed, partial, *gram = call(
                functools.partial(later_polar_kernel, last),
                "polar",
                polar_outs[:2] if last else polar_outs,
                inside, delta, change, old, cross, *crosses,
                unread=1,
            )
            gram = gram[0] if gram else None
        if inner == INNER - 1:
            mixed_tall, evolving = call(
                last_rows_kernel,
                "rows",
                [((count, 3 * rank, rows), bf16), state],
                mixed, change, forward, tall, known,
                scratch=[pltpu.VMEM(state[0], f32)],
            )
            coup, delta = call(
                functools.partial(last_kernel, total),
                "last",
                [state, square],
                mixed_tall, *in_stages(partial, "cuts")[0],
            )
            continue
        near = swapped(to_near, "cuts", 0)
        far = swapped(to_far, "cuts", 1)
        known, cross, *kept = call(
            functools.partial(ahead_kernel, group),
            "ahead",
            [state, ((groups, rank, 2 * wide), f32)] + [state] * (2 if inner < INNER - 2 else 0),
            odd, partial, inside, near, far, target, tall, side, rho, inverse,
            scalars=1, unread=1,
        )
        sums, firsts = in_stages(partial, "cuts", beside=cross)
        _, cross = lax.optimization_barrier((firsts, cross))
        crosses = from_others(cross, "chan")
        old = gram
        delta, change, forward = call(
            functools.partial(mixer_kernel, total),
            "mixer",
            [square, quads, quads],
            mixed, inverse, rho, *sums,
        )
        if inner < INNER - 2:
            tall, target, inside, to_near, to_far = call(
                rows_kernel,
                "rows",
                [state, state, state, halo, halo],
                odd, kept[0], before, rho, after, change, forward, tall, known, kept[1],
                scalars=1,
            )
    return (flip(evolving), flip(coup), delta)


def solution(mesh):
    return jax.shard_map(
        body,
        mesh=mesh,
        in_specs=(
            P("cuts", None, "chan"),
            P("cuts"),
            P("chan", None),
            P("cuts", None),
            P("cuts", "chan", None),
            P("cuts", "chan", None),
            P("cuts", "chan", None),
            P("cuts", "chan", None),
            P(),
        ),
        out_specs=(P("cuts", "chan", None), P("cuts", "chan", None), P()),
        check_vma=False,
    )
```

```python
import functools

import jax
import jax.numpy as jnp
from jax import lax
from jax.experimental import pallas as pl
from jax.experimental.pallas import tpu as pltpu
from jax.sharding import PartitionSpec as P

INNER = 3
SWEEPS = 4
POLAR = 8

smooth_weight = 1.0
eps_trace = 1e-06
f32 = jnp.float32
bf16 = jnp.bfloat16
NN = (((1,), (0,)), ((), ()))
NT = (((1,), (1,)), ((), ()))


def dot(left, right, dims=NN):
    return lax.dot_general(left, right, dims, preferred_element_type=f32)


def split(value):
    high = value.astype(bf16)
    low = (value - high.astype(f32)).astype(bf16)
    return high, low


def left_triple(value):
    high, low = split(value)
    return jnp.concatenate([high, high, low], axis=1)


def right_triple(value):
    high, low = split(value)
    return jnp.concatenate([high, low, high], axis=0)


def block_mask(rank, group):
    wide = rank * group
    rows = lax.div(lax.broadcasted_iota(jnp.int32, (wide, wide), 0), rank)
    cols = lax.div(lax.broadcasted_iota(jnp.int32, (wide, wide), 1), rank)
    return jnp.where(rows == cols, 1.0, 0.0).astype(bf16)


def wide_eye(rank, group):
    rows = lax.broadcasted_iota(jnp.int32, (rank, rank * group), 0)
    cols = lax.broadcasted_iota(jnp.int32, (rank, rank * group), 1)
    return jnp.where(rows == lax.rem(cols, rank), 1.0, 0.0).astype(f32)


def block_diagonal(value, mask, group, dims=NN):
    high, low = split(value)
    high = jnp.concatenate([high] * group, axis=0) * mask
    low = jnp.concatenate([low] * group, axis=0) * mask
    empty = jnp.zeros_like(high)
    one, other = ([high, low], [high, empty]) if dims == NN else ([high, high], [low, empty])
    return jnp.concatenate(
        [jnp.concatenate(one, axis=1), jnp.concatenate(other, axis=1)], axis=0
    )


def times_blocks(values, blocks, dims=NN):
    rank, wide = values[0].shape
    left = [jnp.concatenate(split(value), axis=1) for value in values]
    total = dot(jnp.concatenate(left, axis=0), blocks, dims)
    total = total[:, :wide] + total[:, wide:]
    return [total[at * rank : (at + 1) * rank] for at in range(len(values))]


def diagonal_blocks(value, rank, group):
    at = lax.div(lax.broadcasted_iota(jnp.int32, (rank, rank * group), 1), rank)
    total = value[:rank]
    for block in range(1, group):
        total = jnp.where(at == block, value[block * rank : (block + 1) * rank], total)
    return total


def from_left(left, values):
    wide = values[0].shape[1]
    total = dot(left_triple(left), right_triple(jnp.concatenate(values, axis=1)))
    return [total[:, at * wide : (at + 1) * wide] for at in range(len(values))]


def group_size(count, rank):
    group = max(1, 128 // rank)
    while count % group:
        group -= 1
    return group


def project_kernel(first, pairs, rows, lead, me_ref, data_ref, factor_ref, *refs):
    *outs, held, arrived = refs
    half = data_ref.shape[1] // 2
    copies = []
    for k in range(2 * pairs):
        for at in range(2):
            place = pl.ds(at * half, half)
            copies.append(
                pltpu.make_async_copy(
                    data_ref.at[first + k, place, :], held.at[k, place, :], arrived.at[2 * k + at]
                )
            )
            copies[-1].start()
    factor = factor_ref[...]
    rank = factor.shape[0]
    if lead:
        *outs, again_ref = outs
        again_ref[...] = factor
        gram = dot(factor, factor, NT)
        for out in outs:
            out[pairs * rows :, :] = jnp.concatenate([gram[: rank // 2], gram[rank // 2 :]], axis=1)
    parts = len(outs)
    empty = jnp.zeros_like(factor)
    sides = [
        jnp.concatenate([factor, empty], axis=0),
        jnp.concatenate([empty, factor], axis=0),
    ]
    for pair in range(pairs):
        for copy in copies[4 * pair : 4 * pair + 4]:
            copy.wait()
        for part in reversed(range(parts)):
            start = pl.multiple_of(lax.rem(me_ref[0] + part, parts) * rows, 16)
            place = pl.ds(start, rows)
            outs[part][pair * rows : (pair + 1) * rows, :] = dot(
                held[2 * pair, place, :], sides[0], NT
            ) + dot(held[2 * pair + 1, place, :], sides[1], NT)


def setup_kernel(parts, first, group, order_ref, *refs):
    lead_refs, refs = refs[:parts], refs[parts:]
    (own_ref, aux_ref, coupled_ref, dual_s_ref, dual_c_ref) = refs[:5]
    (inverse_ref, mover_ref, rho_ref, diagonal_ref, columns_ref, base_ref) = refs[5:]
    count, rank = own_ref.shape
    gram = summed(lead_refs, slice(first, None))
    gram = jnp.concatenate([gram[:, :rank], gram[:, rank:]], axis=0)
    eye = wide_eye(rank, 1)
    diagonal = jnp.sum(gram * eye, axis=0, keepdims=True)
    diagonal_ref[...] = jnp.broadcast_to(diagonal, diagonal_ref.shape)
    weights = own_ref[...]
    columns = weights.T
    columns_ref[...] = columns
    rho = jnp.sum(weights * weights * diagonal, axis=1, keepdims=True) / rank
    rho_ref[...] = jnp.broadcast_to(rho, rho_ref.shape)

    centre = rank / 2.0 + 2.0
    edge = centre / (rank / 2.0)
    lead = 4.0 * edge**3 / (4.0 * edge**3 - 3.0 * edge)
    mask = block_mask(rank, group)
    wide = wide_eye(rank, group)
    starts = range(0, count, group)
    systems = []
    for first in starts:
        scaled = []
        for k in range(first, first + group):
            unit = 1.0 / (centre * rho[k : k + 1, :])
            column = columns[:, k : k + 1]
            scaled.append(column * gram * weights[k : k + 1, :] * unit + (2.0 / centre) * eye)
        systems.append(jnp.concatenate(scaled, axis=1))
    inverses, rests = [], []
    for system in systems:
        rest = wide - system
        blocks = block_diagonal(rest, mask, group)
        (square,) = times_blocks([rest], blocks)
        (cube,) = times_blocks([square], blocks)
        inverses.append(wide + lead * (rest + square))
        rests.append(lead * cube - (lead - 1.0) * rest)
    for step in range(5):
        for at in range(len(systems)):
            blocks = block_diagonal(rests[at], mask, group)
            more, *rest = times_blocks([inverses[at], rests[at]][: 2 if step < 4 else 1], blocks)
            inverses[at] = inverses[at] + more
            rests[at] = rest[0] if rest else None
    for at in range(len(systems)):
        (product,) = times_blocks([inverses[at]], block_diagonal(systems[at], mask, group))
        blocks = block_diagonal(wide - product, mask, group)
        (more,) = times_blocks([inverses[at]], blocks)
        inverses[at] = inverses[at] + more
    for k in range(count):
        place = (k % group) * rank
        unit = 1.0 / (centre * rho[k : k + 1, :])
        inverse = inverses[k // group][:, place : place + rank] * unit
        inverse_ref[k] = left_triple(inverse)
        base_ref[k] = dot(
            inverse_ref[k],
            right_triple(
                rho[k : k + 1, :] * (aux_ref[k] - dual_s_ref[k] + coupled_ref[k] - dual_c_ref[k])
            ),
        )
        both = jnp.concatenate([inverse * weights[k : k + 1, :]] * 2, axis=1)
        side = lax.div(lax.broadcasted_iota(jnp.int32, both.shape, 1), rank)
        both = jnp.where(side == lax.rem(order_ref[k], 2), both, 0.0)
        high, low = split(both)
        pair, place = stored_place(order_ref, k, count, rank)
        mover_ref[pair, place, :] = jnp.concatenate([high, high, low], axis=1)


def cross_blocks(lefts, rights, rank):
    group = len(lefts)
    wide = group * rank
    left = jnp.concatenate(split(jnp.concatenate(lefts, axis=0)), axis=0)
    right = left
    if rights is not lefts:
        right = jnp.concatenate(split(jnp.concatenate(rights, axis=0)), axis=0)
    total = dot(left, right, NT)
    total = total[:wide, :wide] + total[:wide, wide:] + total[wide:, :wide]
    return diagonal_blocks(total, rank, group)


def summed(refs, at):
    total = refs[0][at]
    for ref in refs[1:]:
        total = total + ref[at]
    return total


def stored_place(order_ref, k, count, rank):
    stored = lax.rem(order_ref[k], count)
    return lax.div(stored, 2), pl.ds(pl.multiple_of(lax.rem(stored, 2) * rank, rank), rank)


def move(mover, projected):
    high, low = split(projected)
    return dot(mover, jnp.concatenate([high, low, high], axis=1), NT)


def move_kernel(mover_ref, *refs):
    *projected_refs, moved_ref, turned_ref = refs
    rows = moved_ref.shape[2]
    for pair in range(moved_ref.shape[0]):
        projected = summed(projected_refs, slice(pair * rows, (pair + 1) * rows))
        moved_ref[pair] = move(mover_ref[pair], projected)
        turned_ref[pair] = projected.T


def first_kernel(group, order_ref, *refs):
    base_ref, mover_ref, dual_s_ref, dual_c_ref, early_ref = refs[2:7]
    *projected_refs, tall_ref, target_ref, gram_ref, moved = refs[7:]
    count, rank, rows = base_ref.shape
    early = early_ref.shape[0]
    for pair in range(early):
        moved[pair] = early_ref[pair]
    for pair in range(early, count // 2):
        place = slice((pair - early) * rows, (pair - early + 1) * rows)
        moved[pair] = move(mover_ref[pair], summed(projected_refs, place))
    talls = []
    for k in range(count):
        pair, place = stored_place(order_ref, k, count, rank)
        evolving = base_ref[k] + moved[pair, place, :]
        target_ref[k] = evolving + dual_s_ref[k]
        tall = evolving + dual_c_ref[k]
        tall_ref[k] = tall
        talls.append(tall)
        if len(talls) == group:
            gram_ref[k // group] = cross_blocks(talls, talls, rank)
            talls = []


def smooth(odd, now, targets, rho, inside_ref, near_ref, far_ref):
    count = len(targets)
    width = SWEEPS
    share = {j: 2.0 * smooth_weight / (rho[j] + 4.0 * smooth_weight) for j in rho}
    pull = {j: (rho[j] / (rho[j] + 4.0 * smooth_weight)) * targets[j] for j in range(count)}
    now = {j: now[j] for j in range(count)}
    for sweep in range(width):
        later = {}
        for j in range(-sweep - 1, count + sweep + 1):
            beside = [now[i] for i in (j - 1, j + 1) if i in now]
            total = beside[0] if len(beside) == 1 else beside[0] + beside[1]
            total = share[j] * total
            later[j] = total + pull[j] if j in pull else total
        now = later
    for j in range(count):
        inside_ref[j] = now[j]
    rows = inside_ref.shape[2]
    for j in range(width):
        lanes = slice((j % 2) * rows, (j % 2 + 1) * rows)
        near_ref[j // 2, :, lanes] = jnp.where(odd == 1, now[j - width], now[count + j])
        far_ref[j // 2, :, lanes] = jnp.where(odd == 1, now[count + j], now[j - width])


def all_rho(before_ref, rho_ref, after_ref):
    count = rho_ref.shape[0]
    rho = {j: rho_ref[j : j + 1, 0:1] for j in range(count)}
    for j in range(SWEEPS):
        rho[j - SWEEPS] = before_ref[count - SWEEPS + j : count - SWEEPS + j + 1, 0:1]
        rho[count + j] = after_ref[j : j + 1, 0:1]
    return rho


def smooth_kernel(
    odd_ref, order_ref, aux_ref, target_ref, before_ref, rho_ref, after_ref, diagonal_ref,
    columns_ref, early_ref, *refs
):
    *projected_refs, side_ref, past_ref, next_ref, inside_ref, near_ref, far_ref, turned = refs
    count, rank, rows = aux_ref.shape
    for source, place in ((before_ref, past_ref), (after_ref, next_ref)):
        weights = source[...]
        rho = jnp.sum(weights * weights * diagonal_ref[...], axis=1, keepdims=True) / rank
        place[...] = jnp.broadcast_to(rho, place.shape)
    rho = all_rho(past_ref, rho_ref, next_ref)
    slices = range(count)
    smooth(
        odd_ref[0], [aux_ref[k] for k in slices], [target_ref[k] for k in slices], rho,
        inside_ref, near_ref, far_ref,
    )
    early = early_ref.shape[0]
    for pair in range(early):
        turned[pair] = early_ref[pair]
    for pair in range(early, count // 2):
        place = slice((pair - early) * rows, (pair - early + 1) * rows)
        turned[pair] = summed(projected_refs, place).T
    for k in slices:
        pair, place = stored_place(order_ref, k, count, rank)
        side_ref[k] = columns_ref[:, k : k + 1] * turned[pair, place, :]


def polar(grams, delta):
    rank, wide = grams[0].shape
    group = wide // rank
    mask = block_mask(rank, group)
    eye = wide_eye(rank, group)
    delta_wide = jnp.concatenate([delta] * group, axis=1)
    delta_blocks = block_diagonal(delta_wide, mask, group, NT)
    (across,) = from_left(delta.T, [delta_wide])
    traces = []
    for gram in grams:
        line = jnp.broadcast_to(jnp.sum(across * gram, axis=0, keepdims=True), (16, wide))
        high, low = split(line)
        rest = (line - high.astype(f32) - low.astype(f32)).astype(bf16)
        line = dot(high, mask) + dot(low, mask) + dot(rest, mask)
        traces.append(line[0:1] + eps_trace)
    rights = [times_blocks([gram], delta_blocks, NT)[0] for gram in grams]
    normals = from_left(delta, rights)
    currents = [normal / trace for normal, trace in zip(normals, traces)]
    scales = [1.0 / jnp.sqrt(trace) for trace in traces]
    roots = []
    for step in range(POLAR):
        for at in range(len(grams)):
            product = currents[at]
            blocks = block_diagonal(product, mask, group)
            if step == 0:
                roots.append(1.5 * eye - 0.5 * product)
                (square,) = times_blocks([product], blocks)
            elif step < POLAR - 1:
                square, more = times_blocks([product, roots[at]], blocks)
                roots[at] = 1.5 * roots[at] - 0.5 * more
            else:
                (more,) = times_blocks([roots[at]], blocks)
                roots[at] = 1.5 * roots[at] - 0.5 * more
            if step < POLAR - 1:
                half = 1.5 * product - 0.5 * square
                (more,) = times_blocks([half], blocks)
                currents[at] = 1.5 * half - 0.5 * more
    return roots, scales, rights


def mix(roots, scales, rights, delta, mixed_ref, partial_ref):
    rank, wide = roots[0].shape
    group = wide // rank
    mask = block_mask(rank, group)
    delta_blocks = block_diagonal(jnp.concatenate([delta] * group, axis=1), mask, group)
    left, right = [], []
    for at in range(len(roots)):
        high, low = split(roots[at] * scales[at])
        left += [high, high, low]
        high, low = split(rights[at])
        right += [high, low, high]
    partial = dot(jnp.concatenate(right, axis=1), jnp.concatenate(left, axis=1), NT)
    for at in range(len(roots)):
        (mixed,) = times_blocks([roots[at]], delta_blocks)
        mixed_ref[at] = mixed * scales[at]
    half = rank // 2
    partial_ref[...] = jnp.concatenate([partial[:half], partial[half:]], axis=1)


def first_polar_kernel(after_ref, delta_ref, *refs):
    *gram_refs, mixed_ref, partial_ref, gram_ref = refs
    grams = [summed(gram_refs, at) for at in range(gram_ref.shape[0])]
    for at in range(len(grams)):
        gram_ref[at] = grams[at]
    delta = delta_ref[...]
    mix(*polar(grams, delta), delta, mixed_ref, partial_ref)


def later_polar_kernel(last, after_ref, delta_ref, change_ref, old_ref, *refs):
    if last:
        *cross_refs, mixed_ref, partial_ref = refs
    else:
        *cross_refs, mixed_ref, partial_ref, gram_ref = refs
    groups, rank, wide = old_ref.shape
    group = wide // rank
    mask = block_mask(rank, group)
    grams = []
    for at in range(groups):
        cross = summed(cross_refs, at)
        change = change_ref[at]
        (onward,) = times_blocks([change], block_diagonal(old_ref[at], mask, group))
        onward = cross[:, :wide] + 0.5 * onward
        (one,) = times_blocks([onward], block_diagonal(change, mask, group, NT), NT)
        (other,) = times_blocks([change], block_diagonal(onward, mask, group, NT), NT)
        grams.append(cross[:, wide:] + one + other)
        if not last:
            gram_ref[at] = grams[at]
    delta = delta_ref[...]
    mix(*polar(grams, delta), delta, mixed_ref, partial_ref)


def ahead_kernel(
    group, odd_ref, after_ref, inside_ref, near_ref, far_ref, target_ref, tall_ref, side_ref, rho_ref,
    inverse_ref, known_ref, cross_ref, *kept
):
    count, rank, rows = inside_ref.shape
    width = SWEEPS
    knowns, talls = [], []
    for k in range(count):
        aux = inside_ref[k]
        for at, mine, other in ((k, near_ref, far_ref), (k - count + width, far_ref, near_ref)):
            if 0 <= at < width:
                lanes = slice((at % 2) * rows, (at % 2 + 1) * rows)
                aux = aux + jnp.where(
                    odd_ref[0] == 1, mine[at // 2, :, lanes], other[at // 2, :, lanes]
                )
        target, tall = target_ref[k], tall_ref[k]
        if kept:
            aux_ref, dual_ref = kept
            aux_ref[k] = aux
            dual_ref[k] = target - aux
        known = dot(
            inverse_ref[k],
            right_triple(side_ref[k] + rho_ref[k : k + 1, 0:1] * (2.0 * aux - target - tall)),
        )
        known_ref[k] = known
        talls.append(tall)
        knowns.append(known + tall)
        if len(talls) == group:
            cross_ref[k // group] = jnp.concatenate(
                [cross_blocks(knowns, talls, rank), cross_blocks(knowns, knowns, rank)], axis=1
            )
            knowns, talls = [], []


def add_kernel(unread, *refs):
    *term_refs, total_ref = refs[unread:]
    total = term_refs[0][...]
    for ref in term_refs[1:]:
        total = total + ref[...]
    total_ref[...] = total


def new_delta(sum_refs, total, rank):
    packed = sum_refs[0][...]
    for ref in sum_refs[1:]:
        packed = packed + ref[...]
    packed = packed / total
    return jnp.concatenate([packed[:, :rank], packed[:, rank:]], axis=0)


def mixer_kernel(total, mixed_ref, inverse_ref, rho_ref, *refs):
    *sum_refs, delta_ref, change_ref, forward_ref = refs
    groups, rank, wide = mixed_ref.shape
    group = wide // rank
    turned = new_delta(sum_refs, total, rank)
    delta_ref[...] = turned.T
    mixers = from_left(turned, [mixed_ref[at] for at in range(groups)])
    place = lax.div(lax.broadcasted_iota(jnp.int32, (1, wide), 1), rank)
    for at in range(groups):
        mixer = mixers[at]
        slices = range(at * group, (at + 1) * group)
        inverses = jnp.concatenate([inverse_ref[k] for k in slices], axis=0)
        onward = diagonal_blocks(dot(inverses, right_triple(mixer)), rank, group)
        rho = rho_ref[at * group : at * group + 1, 0:1]
        for k in slices[1:]:
            rho = jnp.where(place == k - at * group, rho_ref[k : k + 1, 0:1], rho)
        forward = 2.0 * rho * onward
        forward_ref[at] = forward
        change_ref[at] = forward - mixer


def rows_kernel(odd_ref, aux_ref, before_ref, rho_ref, after_ref, *refs):
    (change_ref, forward_ref, tall_ref, known_ref, dual_ref) = refs[:5]
    (next_ref, target_ref, inside_ref, near_ref, far_ref) = refs[5:]
    targets = new_rows(change_ref, forward_ref, tall_ref, known_ref, next_ref)
    count = len(targets)
    for k in range(count):
        targets[k] = targets[k] + dual_ref[k]
        target_ref[k] = targets[k]
    rho = all_rho(before_ref, rho_ref, after_ref)
    smooth(
        odd_ref[0], [aux_ref[k] for k in range(count)], targets, rho,
        inside_ref, near_ref, far_ref,
    )


def last_rows_kernel(mixed_ref, change_ref, forward_ref, tall_ref, known_ref, *outs):
    mixed_tall_ref, evolving_ref, next_ref = outs
    evolvings = new_rows(change_ref, forward_ref, tall_ref, known_ref, next_ref)
    groups, rank, wide = mixed_ref.shape
    group = wide // rank
    for k in range(len(evolvings)):
        evolving_ref[k] = evolvings[k]
        place = (k % group) * rank
        mixed = left_triple(mixed_ref[k // group][:, place : place + rank])
        mixed_tall_ref[k] = right_triple(dot(mixed, right_triple(next_ref[k])))


def new_rows(change_ref, forward_ref, tall_ref, known_ref, next_ref):
    groups, rank, wide = change_ref.shape
    group = wide // rank
    evolvings = []
    for k in range(groups * group):
        lanes = slice((k % group) * rank, (k % group + 1) * rank)
        change, forward = change_ref[k // group][:, lanes], forward_ref[k // group][:, lanes]
        left = jnp.concatenate([left_triple(change), left_triple(forward)], axis=0)
        tall, known = tall_ref[k], known_ref[k]
        both = dot(left, right_triple(tall))
        next_ref[k] = known + tall + both[:rank]
        evolvings.append(known + both[rank:])
    return evolvings


def last_kernel(total, mixed_tall_ref, *refs):
    *sum_refs, coupled_ref, delta_ref = refs
    turned = new_delta(sum_refs, total, delta_ref.shape[0])
    delta_ref[...] = turned.T
    delta_left = left_triple(turned)
    for k in range(coupled_ref.shape[0]):
        coupled_ref[k] = dot(delta_left, mixed_tall_ref[k])


per_microsecond = 1_100_000_000


def call(
    kernel, name, outs, *args, scalars=0, unread=0, microseconds=0.3, limit=16, scratch=()
):
    flops = int(microseconds * per_microsecond)
    specs = [pl.BlockSpec(memory_space=pltpu.SMEM)] * scalars
    specs += [pl.BlockSpec(memory_space=pl.ANY)] * unread
    specs += [pl.BlockSpec(memory_space=pltpu.VMEM)] * (len(args) - len(specs))
    shapes = [jax.ShapeDtypeStruct(shape, dtype) for shape, dtype in outs]
    moved = sum(arg.size * arg.dtype.itemsize for arg in args)
    moved += sum(shape.size * shape.dtype.itemsize for shape in shapes)
    return pl.pallas_call(
        kernel,
        out_shape=shapes,
        in_specs=specs,
        out_specs=[pl.BlockSpec(memory_space=pltpu.VMEM)] * len(shapes),
        scratch_shapes=list(scratch),
        compiler_params=pltpu.CompilerParams(vmem_limit_bytes=limit * 1024 * 1024),
        cost_estimate=pl.CostEstimate(flops=flops, bytes_accessed=moved, transcendentals=0),
        name=name,
    )(*args)


def rotated(value, axis, shift):
    count = lax.axis_size(axis)
    return lax.ppermute(value, axis, [(i, (i + shift) % count) for i in range(count)])


def swapped(value, axis, first):
    count = lax.axis_size(axis)
    pairs = [((i + first) % count, (i + first + 1) % count) for i in range(0, count, 2)]
    return lax.ppermute(value, axis, pairs + [(b, a) for a, b in pairs])


def from_others(value, axis):
    return [rotated(value, axis, shift) for shift in range(1, lax.axis_size(axis))]


def stage_sizes(count):
    sizes = []
    while count > 1:
        sizes.append(next(size for size in (4, 2, 3, 5, 7, count) if count % size == 0))
        count //= sizes[-1]
    return sizes


def in_stages(value, axis, beside=None):
    count = lax.axis_size(axis)
    stride = 1
    terms, firsts = [value], []
    for size in stage_sizes(count):
        value = terms[0]
        if len(terms) > 1:
            unread = [] if beside is None else [beside]
            (value,) = call(
                functools.partial(add_kernel, len(unread)),
                "add",
                [(value.shape, f32)],
                *unread, *terms,
                unread=len(unread),
            )
        terms = [value]
        for shift in range(1, size):
            moves = []
            for i in range(count):
                digit = (i // stride) % size
                other = digit ^ shift if size in (2, 4) else (digit + shift) % size
                moves.append((i, i + (other - digit) * stride))
            terms.append(lax.ppermute(value, axis, moves))
        stride *= size
        firsts = firsts or terms
    return terms, firsts


def body(
    data, order, chan_factor, slice_weights, smooth_aux, coupled, smooth_dual, coupling_dual, delta
):
    count, all_rows, channels = data.shape
    rank = chan_factor.shape[1]
    rows = smooth_aux.shape[1]
    parts = lax.axis_size("chan")
    total = count * lax.axis_size("cuts")
    group = group_size(count, rank)
    groups = count // group
    wide = group * rank
    flip = lambda value: jnp.swapaxes(value, 1, 2)
    aux, coup, dual_s, dual_c = map(flip, (smooth_aux, coupled, smooth_dual, coupling_dual))
    factor = chan_factor.T
    state = ((count, rank, rows), f32)
    quads = ((groups, rank, wide), f32)
    square = ((rank, rank), f32)
    halo = (((SWEEPS + 1) // 2, rank, 2 * rows), f32)
    lanes = lambda height: ((height, 128), f32)
    scale = ((groups, 8, wide), f32)

    me = lax.axis_index("chan").astype(jnp.int32).reshape(1)
    odd = lax.rem(lax.axis_index("cuts"), 2).astype(jnp.int32).reshape(1)
    early = count // 4
    own, received = [], []
    for first, pairs, lead in ((0, early, True), (2 * early, count // 2 - early, False)):
        height = pairs * rows + (rank // 2 if lead else 0)
        projected = call(
            functools.partial(project_kernel, first, pairs, rows, lead),
            "project",
            [((height, 2 * rank), f32)] * parts + [(factor.shape, factor.dtype)] * lead,
            me, data, factor,
            scalars=1, unread=1, limit=52,
            scratch=[
                pltpu.VMEM((2 * pairs, all_rows, channels), data.dtype),
                pltpu.SemaphoreType.DMA((4 * pairs,)),
            ],
        )
        if lead:
            *projected, factor = projected
        own.append(projected[0])
        received.append([rotated(projected[shift], "chan", shift) for shift in range(1, parts)])

    late_weights, _ = lax.optimization_barrier((slice_weights, own[-1]))
    before = rotated(late_weights, "cuts", 1)
    after = rotated(late_weights, "cuts", -1)
    inverse, mover, rho, diagonal, columns, base = call(
        functools.partial(setup_kernel, parts, early * rows, group),
        "setup",
        [
            ((count, rank, 3 * rank), bf16),
            ((count // 2, 2 * rank, 6 * rank), bf16),
            lanes(count),
            ((count, rank), f32),
            ((rank, count), f32),
            state,
        ],
        order, own[0], *received[0], slice_weights, aux, coup, dual_s, dual_c,
        scalars=1,
    )
    half_state = ((early, 2 * rank, rows), f32)
    moved, turned = call(
        move_kernel, "move", [half_state, half_state], mover, own[0], *received[0]
    )
    tall, target, gram = call(
        functools.partial(first_kernel, group),
        "first",
        [state, state, quads],
        order, before, after, base, mover, dual_s, dual_c, moved, own[1], *received[1],
        scalars=1, unread=2,
        scratch=[pltpu.VMEM((count // 2, 2 * rank, rows), f32)],
    )
    side, before, after, inside, to_near, to_far = call(
        smooth_kernel,
        "smooth",
        [state, lanes(count), lanes(count), state, halo, halo],
        odd, order, aux, target, before, rho, after, diagonal, columns, turned, own[1],
        *received[1],
        scalars=2,
        scratch=[pltpu.VMEM((count // 2, 2 * rank, rows), f32)],
    )
    polar_outs = [quads, ((rank // 2, 2 * rank), f32), quads]
    for inner in range(INNER):
        if inner == 0:
            mixed, partial, gram = call(
                first_polar_kernel,
                "polar",
                polar_outs,
                inside, delta, gram, *from_others(gram, "chan"),
                unread=1, microseconds=3,
            )
        else:
            last = inner == INNER - 1
            mixed, partial, *gram = call(
                functools.partial(later_polar_kernel, last),
                "polar",
                polar_outs[:2] if last else polar_outs,
                inside, delta, change, old, cross, *crosses,
                unread=1,
            )
            gram = gram[0] if gram else None
        if inner == INNER - 1:
            mixed_tall, evolving = call(
                last_rows_kernel,
                "rows",
                [((count, 3 * rank, rows), bf16), state],
                mixed, change, forward, tall, known,
                scratch=[pltpu.VMEM(state[0], f32)],
            )
            coup, delta = call(
                functools.partial(last_kernel, total),
                "last",
                [state, square],
                mixed_tall, *in_stages(partial, "cuts")[0],
            )
            continue
        near = swapped(to_near, "cuts", 0)
        far = swapped(to_far, "cuts", 1)
        known, cross, *kept = call(
            functools.partial(ahead_kernel, group),
            "ahead",
            [state, ((groups, rank, 2 * wide), f32)] + [state] * (2 if inner < INNER - 2 else 0),
            odd, partial, inside, near, far, target, tall, side, rho, inverse,
            scalars=1, unread=1,
        )
        sums, firsts = in_stages(partial, "cuts", beside=cross)
        _, cross = lax.optimization_barrier((firsts, cross))
        crosses = from_others(cross, "chan")
        old = gram
        delta, change, forward = call(
            functools.partial(mixer_kernel, total),
            "mixer",
            [square, quads, quads],
            mixed, inverse, rho, *sums,
        )
        if inner < INNER - 2:
            tall, target, inside, to_near, to_far = call(
                rows_kernel,
                "rows",
                [state, state, state, halo, halo],
                odd, kept[0], before, rho, after, change, forward, tall, known, kept[1],
                scalars=1, microseconds=1,
            )
    return (flip(evolving), flip(coup), delta)


def solution(mesh):
    return jax.shard_map(
        body,
        mesh=mesh,
        in_specs=(
            P("cuts", None, "chan"),
            P("cuts"),
            P("chan", None),
            P("cuts", None),
            P("cuts", "chan", None),
            P("cuts", "chan", None),
            P("cuts", "chan", None),
            P("cuts", "chan", None),
            P(),
        ),
        out_specs=(P("cuts", "chan", None), P("cuts", "chan", None), P()),
        check_vma=False,
    )
```

```python
import functools

import jax
import jax.numpy as jnp
from jax import lax
from jax.experimental import pallas as pl
from jax.experimental.pallas import tpu as pltpu
from jax.sharding import PartitionSpec as P

INNER = 3
SWEEPS = 4
POLAR = 8

smooth_weight = 1.0
eps_trace = 1e-06
f32 = jnp.float32
bf16 = jnp.bfloat16
NN = (((1,), (0,)), ((), ()))
NT = (((1,), (1,)), ((), ()))


def dot(left, right, dims=NN):
    return lax.dot_general(left, right, dims, preferred_element_type=f32)


def split(value):
    high = value.astype(bf16)
    low = (value - high.astype(f32)).astype(bf16)
    return high, low


def left_triple(value):
    high, low = split(value)
    return jnp.concatenate([high, high, low], axis=1)


def right_triple(value):
    high, low = split(value)
    return jnp.concatenate([high, low, high], axis=0)


def block_mask(rank, group):
    wide = rank * group
    rows = lax.div(lax.broadcasted_iota(jnp.int32, (wide, wide), 0), rank)
    cols = lax.div(lax.broadcasted_iota(jnp.int32, (wide, wide), 1), rank)
    return jnp.where(rows == cols, 1.0, 0.0).astype(bf16)


def wide_eye(rank, group):
    rows = lax.broadcasted_iota(jnp.int32, (rank, rank * group), 0)
    cols = lax.broadcasted_iota(jnp.int32, (rank, rank * group), 1)
    return jnp.where(rows == lax.rem(cols, rank), 1.0, 0.0).astype(f32)


def block_diagonal(value, mask, group, dims=NN):
    high, low = split(value)
    high = jnp.concatenate([high] * group, axis=0) * mask
    low = jnp.concatenate([low] * group, axis=0) * mask
    empty = jnp.zeros_like(high)
    one, other = ([high, low], [high, empty]) if dims == NN else ([high, high], [low, empty])
    return jnp.concatenate(
        [jnp.concatenate(one, axis=1), jnp.concatenate(other, axis=1)], axis=0
    )


def times_blocks(values, blocks, dims=NN):
    rank, wide = values[0].shape
    left = [jnp.concatenate(split(value), axis=1) for value in values]
    total = dot(jnp.concatenate(left, axis=0), blocks, dims)
    total = total[:, :wide] + total[:, wide:]
    return [total[at * rank : (at + 1) * rank] for at in range(len(values))]


def diagonal_blocks(value, rank, group):
    at = lax.div(lax.broadcasted_iota(jnp.int32, (rank, rank * group), 1), rank)
    total = value[:rank]
    for block in range(1, group):
        total = jnp.where(at == block, value[block * rank : (block + 1) * rank], total)
    return total


def from_left(left, values):
    wide = values[0].shape[1]
    total = dot(left_triple(left), right_triple(jnp.concatenate(values, axis=1)))
    return [total[:, at * wide : (at + 1) * wide] for at in range(len(values))]


def group_size(count, rank):
    group = max(1, 128 // rank)
    while count % group:
        group -= 1
    return group


def project_kernel(first, pairs, rows, lead, me_ref, data_ref, factor_ref, *refs):
    *outs, held, arrived = refs
    half = data_ref.shape[1] // 2
    copies = []
    for k in range(2 * pairs):
        for at in range(2):
            place = pl.ds(at * half, half)
            copies.append(
                pltpu.make_async_copy(
                    data_ref.at[first + k, place, :], held.at[k, place, :], arrived.at[2 * k + at]
                )
            )
            copies[-1].start()
    factor = factor_ref[...]
    rank = factor.shape[0]
    if lead:
        *outs, again_ref = outs
        again_ref[...] = factor
        gram = dot(factor, factor, NT)
        for out in outs:
            out[pairs * rows :, :] = jnp.concatenate([gram[: rank // 2], gram[rank // 2 :]], axis=1)
    parts = len(outs)
    empty = jnp.zeros_like(factor)
    sides = [
        jnp.concatenate([factor, empty], axis=0),
        jnp.concatenate([empty, factor], axis=0),
    ]
    for pair in range(pairs):
        for copy in copies[4 * pair : 4 * pair + 4]:
            copy.wait()
        for part in reversed(range(parts)):
            start = pl.multiple_of(lax.rem(me_ref[0] + part, parts) * rows, 16)
            place = pl.ds(start, rows)
            outs[part][pair * rows : (pair + 1) * rows, :] = dot(
                held[2 * pair, place, :], sides[0], NT
            ) + dot(held[2 * pair + 1, place, :], sides[1], NT)


def setup_kernel(parts, first, group, order_ref, *refs):
    lead_refs, refs = refs[:parts], refs[parts:]
    (own_ref, aux_ref, coupled_ref, dual_s_ref, dual_c_ref) = refs[:5]
    (inverse_ref, mover_ref, rho_ref, diagonal_ref, columns_ref, base_ref) = refs[5:]
    count, rank = own_ref.shape
    gram = summed(lead_refs, slice(first, None))
    gram = jnp.concatenate([gram[:, :rank], gram[:, rank:]], axis=0)
    eye = wide_eye(rank, 1)
    diagonal = jnp.sum(gram * eye, axis=0, keepdims=True)
    diagonal_ref[...] = jnp.broadcast_to(diagonal, diagonal_ref.shape)
    weights = own_ref[...]
    columns = weights.T
    columns_ref[...] = columns
    rho = jnp.sum(weights * weights * diagonal, axis=1, keepdims=True) / rank
    rho_ref[...] = jnp.broadcast_to(rho, rho_ref.shape)

    centre = rank / 2.0 + 2.0
    edge = centre / (rank / 2.0)
    lead = 4.0 * edge**3 / (4.0 * edge**3 - 3.0 * edge)
    mask = block_mask(rank, group)
    wide = wide_eye(rank, group)
    starts = range(0, count, group)
    systems = []
    for first in starts:
        scaled = []
        for k in range(first, first + group):
            unit = 1.0 / (centre * rho[k : k + 1, :])
            column = columns[:, k : k + 1]
            scaled.append(column * gram * weights[k : k + 1, :] * unit + (2.0 / centre) * eye)
        systems.append(jnp.concatenate(scaled, axis=1))
    inverses, rests = [], []
    for system in systems:
        rest = wide - system
        blocks = block_diagonal(rest, mask, group)
        (square,) = times_blocks([rest], blocks)
        (cube,) = times_blocks([square], blocks)
        inverses.append(wide + lead * (rest + square))
        rests.append(lead * cube - (lead - 1.0) * rest)
    for step in range(5):
        for at in range(len(systems)):
            blocks = block_diagonal(rests[at], mask, group)
            more, *rest = times_blocks([inverses[at], rests[at]][: 2 if step < 4 else 1], blocks)
            inverses[at] = inverses[at] + more
            rests[at] = rest[0] if rest else None
    for at in range(len(systems)):
        (product,) = times_blocks([inverses[at]], block_diagonal(systems[at], mask, group))
        blocks = block_diagonal(wide - product, mask, group)
        (more,) = times_blocks([inverses[at]], blocks)
        inverses[at] = inverses[at] + more
    for k in range(count):
        place = (k % group) * rank
        unit = 1.0 / (centre * rho[k : k + 1, :])
        inverse = inverses[k // group][:, place : place + rank] * unit
        inverse_ref[k] = left_triple(inverse)
        base_ref[k] = dot(
            inverse_ref[k],
            right_triple(
                rho[k : k + 1, :] * (aux_ref[k] - dual_s_ref[k] + coupled_ref[k] - dual_c_ref[k])
            ),
        )
        both = jnp.concatenate([inverse * weights[k : k + 1, :]] * 2, axis=1)
        side = lax.div(lax.broadcasted_iota(jnp.int32, both.shape, 1), rank)
        both = jnp.where(side == lax.rem(order_ref[k], 2), both, 0.0)
        high, low = split(both)
        pair, place = stored_place(order_ref, k, count, rank)
        mover_ref[pair, place, :] = jnp.concatenate([high, high, low], axis=1)


def cross_blocks(lefts, rights, rank):
    group = len(lefts)
    wide = group * rank
    left = jnp.concatenate(split(jnp.concatenate(lefts, axis=0)), axis=0)
    right = left
    if rights is not lefts:
        right = jnp.concatenate(split(jnp.concatenate(rights, axis=0)), axis=0)
    total = dot(left, right, NT)
    total = total[:wide, :wide] + total[:wide, wide:] + total[wide:, :wide]
    return diagonal_blocks(total, rank, group)


def summed(refs, at):
    total = refs[0][at]
    for ref in refs[1:]:
        total = total + ref[at]
    return total


def stored_place(order_ref, k, count, rank):
    stored = lax.rem(order_ref[k], count)
    return lax.div(stored, 2), pl.ds(pl.multiple_of(lax.rem(stored, 2) * rank, rank), rank)


def move(mover, projected):
    high, low = split(projected)
    return dot(mover, jnp.concatenate([high, low, high], axis=1), NT)


def move_kernel(mover_ref, *refs):
    *projected_refs, moved_ref, turned_ref = refs
    rows = moved_ref.shape[2]
    for pair in range(moved_ref.shape[0]):
        projected = summed(projected_refs, slice(pair * rows, (pair + 1) * rows))
        moved_ref[pair] = move(mover_ref[pair], projected)
        turned_ref[pair] = projected.T


def first_kernel(group, order_ref, *refs):
    base_ref, mover_ref, dual_s_ref, dual_c_ref, early_ref = refs[2:7]
    *projected_refs, tall_ref, target_ref, gram_ref, moved = refs[7:]
    count, rank, rows = base_ref.shape
    early = early_ref.shape[0]
    for pair in range(early):
        moved[pair] = early_ref[pair]
    for pair in range(early, count // 2):
        place = slice((pair - early) * rows, (pair - early + 1) * rows)
        moved[pair] = move(mover_ref[pair], summed(projected_refs, place))
    talls = []
    for k in range(count):
        pair, place = stored_place(order_ref, k, count, rank)
        evolving = base_ref[k] + moved[pair, place, :]
        target_ref[k] = evolving + dual_s_ref[k]
        tall = evolving + dual_c_ref[k]
        tall_ref[k] = tall
        talls.append(tall)
        if len(talls) == group:
            gram_ref[k // group] = cross_blocks(talls, talls, rank)
            talls = []


def smooth(odd, now, targets, rho, inside_ref, near_ref, far_ref):
    count = len(targets)
    width = SWEEPS
    share = {j: 2.0 * smooth_weight / (rho[j] + 4.0 * smooth_weight) for j in rho}
    pull = {j: (rho[j] / (rho[j] + 4.0 * smooth_weight)) * targets[j] for j in range(count)}
    now = {j: now[j] for j in range(count)}
    for sweep in range(width):
        later = {}
        for j in range(-sweep - 1, count + sweep + 1):
            beside = [now[i] for i in (j - 1, j + 1) if i in now]
            total = beside[0] if len(beside) == 1 else beside[0] + beside[1]
            total = share[j] * total
            later[j] = total + pull[j] if j in pull else total
        now = later
    for j in range(count):
        inside_ref[j] = now[j]
    rows = inside_ref.shape[2]
    for j in range(width):
        lanes = slice((j % 2) * rows, (j % 2 + 1) * rows)
        near_ref[j // 2, :, lanes] = jnp.where(odd == 1, now[j - width], now[count + j])
        far_ref[j // 2, :, lanes] = jnp.where(odd == 1, now[count + j], now[j - width])


def all_rho(before_ref, rho_ref, after_ref):
    count = rho_ref.shape[0]
    rho = {j: rho_ref[j : j + 1, 0:1] for j in range(count)}
    for j in range(SWEEPS):
        rho[j - SWEEPS] = before_ref[count - SWEEPS + j : count - SWEEPS + j + 1, 0:1]
        rho[count + j] = after_ref[j : j + 1, 0:1]
    return rho


def smooth_kernel(
    odd_ref, order_ref, aux_ref, target_ref, before_ref, rho_ref, after_ref, diagonal_ref,
    columns_ref, early_ref, *refs
):
    *projected_refs, side_ref, past_ref, next_ref, inside_ref, near_ref, far_ref, turned = refs
    count, rank, rows = aux_ref.shape
    for source, place in ((before_ref, past_ref), (after_ref, next_ref)):
        weights = source[...]
        rho = jnp.sum(weights * weights * diagonal_ref[...], axis=1, keepdims=True) / rank
        place[...] = jnp.broadcast_to(rho, place.shape)
    rho = all_rho(past_ref, rho_ref, next_ref)
    slices = range(count)
    smooth(
        odd_ref[0], [aux_ref[k] for k in slices], [target_ref[k] for k in slices], rho,
        inside_ref, near_ref, far_ref,
    )
    early = early_ref.shape[0]
    for pair in range(early):
        turned[pair] = early_ref[pair]
    for pair in range(early, count // 2):
        place = slice((pair - early) * rows, (pair - early + 1) * rows)
        turned[pair] = summed(projected_refs, place).T
    for k in slices:
        pair, place = stored_place(order_ref, k, count, rank)
        side_ref[k] = columns_ref[:, k : k + 1] * turned[pair, place, :]


def polar(grams, delta):
    rank, wide = grams[0].shape
    group = wide // rank
    mask = block_mask(rank, group)
    eye = wide_eye(rank, group)
    delta_wide = jnp.concatenate([delta] * group, axis=1)
    delta_blocks = block_diagonal(delta_wide, mask, group, NT)
    (across,) = from_left(delta.T, [delta_wide])
    traces = []
    for gram in grams:
        line = jnp.broadcast_to(jnp.sum(across * gram, axis=0, keepdims=True), (16, wide))
        high, low = split(line)
        rest = (line - high.astype(f32) - low.astype(f32)).astype(bf16)
        line = dot(high, mask) + dot(low, mask) + dot(rest, mask)
        traces.append(line[0:1] + eps_trace)
    rights = [times_blocks([gram], delta_blocks, NT)[0] for gram in grams]
    normals = from_left(delta, rights)
    currents = [normal / trace for normal, trace in zip(normals, traces)]
    scales = [1.0 / jnp.sqrt(trace) for trace in traces]
    roots = []
    for step in range(POLAR):
        for at in range(len(grams)):
            product = currents[at]
            blocks = block_diagonal(product, mask, group)
            if step == 0:
                roots.append(1.5 * eye - 0.5 * product)
                (square,) = times_blocks([product], blocks)
            elif step < POLAR - 1:
                square, more = times_blocks([product, roots[at]], blocks)
                roots[at] = 1.5 * roots[at] - 0.5 * more
            else:
                (more,) = times_blocks([roots[at]], blocks)
                roots[at] = 1.5 * roots[at] - 0.5 * more
            if step < POLAR - 1:
                half = 1.5 * product - 0.5 * square
                (more,) = times_blocks([half], blocks)
                currents[at] = 1.5 * half - 0.5 * more
    return roots, scales, rights


def mix(roots, scales, rights, delta, mixed_ref, partial_ref):
    rank, wide = roots[0].shape
    group = wide // rank
    mask = block_mask(rank, group)
    delta_blocks = block_diagonal(jnp.concatenate([delta] * group, axis=1), mask, group)
    left, right = [], []
    for at in range(len(roots)):
        high, low = split(roots[at] * scales[at])
        left += [high, high, low]
        high, low = split(rights[at])
        right += [high, low, high]
    partial = dot(jnp.concatenate(right, axis=1), jnp.concatenate(left, axis=1), NT)
    for at in range(len(roots)):
        (mixed,) = times_blocks([roots[at]], delta_blocks)
        mixed_ref[at] = mixed * scales[at]
    half = rank // 2
    partial_ref[...] = jnp.concatenate([partial[:half], partial[half:]], axis=1)


def first_polar_kernel(after_ref, delta_ref, *refs):
    *gram_refs, mixed_ref, partial_ref, gram_ref = refs
    grams = [summed(gram_refs, at) for at in range(gram_ref.shape[0])]
    for at in range(len(grams)):
        gram_ref[at] = grams[at]
    delta = delta_ref[...]
    mix(*polar(grams, delta), delta, mixed_ref, partial_ref)


def later_polar_kernel(last, after_ref, delta_ref, change_ref, old_ref, *refs):
    if last:
        *cross_refs, mixed_ref, partial_ref = refs
    else:
        *cross_refs, mixed_ref, partial_ref, gram_ref = refs
    groups, rank, wide = old_ref.shape
    group = wide // rank
    mask = block_mask(rank, group)
    grams = []
    for at in range(groups):
        cross = summed(cross_refs, at)
        change = change_ref[at]
        (onward,) = times_blocks([change], block_diagonal(old_ref[at], mask, group))
        onward = cross[:, :wide] + 0.5 * onward
        (one,) = times_blocks([onward], block_diagonal(change, mask, group, NT), NT)
        (other,) = times_blocks([change], block_diagonal(onward, mask, group, NT), NT)
        grams.append(cross[:, wide:] + one + other)
        if not last:
            gram_ref[at] = grams[at]
    delta = delta_ref[...]
    mix(*polar(grams, delta), delta, mixed_ref, partial_ref)


def ahead_kernel(
    group, odd_ref, after_ref, inside_ref, near_ref, far_ref, target_ref, tall_ref, side_ref, rho_ref,
    inverse_ref, known_ref, cross_ref, *kept
):
    count, rank, rows = inside_ref.shape
    width = SWEEPS
    knowns, talls = [], []
    for k in range(count):
        aux = inside_ref[k]
        for at, mine, other in ((k, near_ref, far_ref), (k - count + width, far_ref, near_ref)):
            if 0 <= at < width:
                lanes = slice((at % 2) * rows, (at % 2 + 1) * rows)
                aux = aux + jnp.where(
                    odd_ref[0] == 1, mine[at // 2, :, lanes], other[at // 2, :, lanes]
                )
        target, tall = target_ref[k], tall_ref[k]
        if kept:
            aux_ref, dual_ref = kept
            aux_ref[k] = aux
            dual_ref[k] = target - aux
        known = dot(
            inverse_ref[k],
            right_triple(side_ref[k] + rho_ref[k : k + 1, 0:1] * (2.0 * aux - target - tall)),
        )
        known_ref[k] = known
        talls.append(tall)
        knowns.append(known + tall)
        if len(talls) == group:
            cross_ref[k // group] = jnp.concatenate(
                [cross_blocks(knowns, talls, rank), cross_blocks(knowns, knowns, rank)], axis=1
            )
            knowns, talls = [], []


def add_kernel(unread, *refs):
    *term_refs, total_ref = refs[unread:]
    total = term_refs[0][...]
    for ref in term_refs[1:]:
        total = total + ref[...]
    total_ref[...] = total


def new_delta(sum_refs, total, rank):
    packed = sum_refs[0][...]
    for ref in sum_refs[1:]:
        packed = packed + ref[...]
    packed = packed / total
    return jnp.concatenate([packed[:, :rank], packed[:, rank:]], axis=0)


def mixer_kernel(total, mixed_ref, inverse_ref, rho_ref, *refs):
    *sum_refs, delta_ref, change_ref, forward_ref = refs
    groups, rank, wide = mixed_ref.shape
    group = wide // rank
    turned = new_delta(sum_refs, total, rank)
    delta_ref[...] = turned.T
    mixers = from_left(turned, [mixed_ref[at] for at in range(groups)])
    place = lax.div(lax.broadcasted_iota(jnp.int32, (1, wide), 1), rank)
    for at in range(groups):
        mixer = mixers[at]
        slices = range(at * group, (at + 1) * group)
        inverses = jnp.concatenate([inverse_ref[k] for k in slices], axis=0)
        onward = diagonal_blocks(dot(inverses, right_triple(mixer)), rank, group)
        rho = rho_ref[at * group : at * group + 1, 0:1]
        for k in slices[1:]:
            rho = jnp.where(place == k - at * group, rho_ref[k : k + 1, 0:1], rho)
        forward = 2.0 * rho * onward
        forward_ref[at] = forward
        change_ref[at] = forward - mixer


def rows_kernel(odd_ref, aux_ref, before_ref, rho_ref, after_ref, *refs):
    (change_ref, forward_ref, tall_ref, known_ref, dual_ref) = refs[:5]
    (next_ref, target_ref, inside_ref, near_ref, far_ref) = refs[5:]
    targets = new_rows(change_ref, forward_ref, tall_ref, known_ref, next_ref)
    count = len(targets)
    for k in range(count):
        targets[k] = targets[k] + dual_ref[k]
        target_ref[k] = targets[k]
    rho = all_rho(before_ref, rho_ref, after_ref)
    smooth(
        odd_ref[0], [aux_ref[k] for k in range(count)], targets, rho,
        inside_ref, near_ref, far_ref,
    )


def last_rows_kernel(mixed_ref, change_ref, forward_ref, tall_ref, known_ref, *outs):
    mixed_tall_ref, evolving_ref, next_ref = outs
    evolvings = new_rows(change_ref, forward_ref, tall_ref, known_ref, next_ref)
    groups, rank, wide = mixed_ref.shape
    group = wide // rank
    for k in range(len(evolvings)):
        evolving_ref[k] = evolvings[k]
        place = (k % group) * rank
        mixed = left_triple(mixed_ref[k // group][:, place : place + rank])
        mixed_tall_ref[k] = right_triple(dot(mixed, right_triple(next_ref[k])))


def new_rows(change_ref, forward_ref, tall_ref, known_ref, next_ref):
    groups, rank, wide = change_ref.shape
    group = wide // rank
    evolvings = []
    for k in range(groups * group):
        lanes = slice((k % group) * rank, (k % group + 1) * rank)
        change, forward = change_ref[k // group][:, lanes], forward_ref[k // group][:, lanes]
        left = jnp.concatenate([left_triple(change), left_triple(forward)], axis=0)
        tall, known = tall_ref[k], known_ref[k]
        both = dot(left, right_triple(tall))
        next_ref[k] = known + tall + both[:rank]
        evolvings.append(known + both[rank:])
    return evolvings


def last_kernel(total, mixed_tall_ref, *refs):
    *sum_refs, coupled_ref, delta_ref = refs
    turned = new_delta(sum_refs, total, delta_ref.shape[0])
    delta_ref[...] = turned.T
    delta_left = left_triple(turned)
    for k in range(coupled_ref.shape[0]):
        coupled_ref[k] = dot(delta_left, mixed_tall_ref[k])


per_microsecond = 1_100_000_000


def call(
    kernel, name, outs, *args, scalars=0, unread=0, microseconds=0.3, limit=16, scratch=()
):
    flops = int(microseconds * per_microsecond)
    specs = [pl.BlockSpec(memory_space=pltpu.SMEM)] * scalars
    specs += [pl.BlockSpec(memory_space=pl.ANY)] * unread
    specs += [pl.BlockSpec(memory_space=pltpu.VMEM)] * (len(args) - len(specs))
    shapes = [jax.ShapeDtypeStruct(shape, dtype) for shape, dtype in outs]
    moved = sum(arg.size * arg.dtype.itemsize for arg in args)
    moved += sum(shape.size * shape.dtype.itemsize for shape in shapes)
    return pl.pallas_call(
        kernel,
        out_shape=shapes,
        in_specs=specs,
        out_specs=[pl.BlockSpec(memory_space=pltpu.VMEM)] * len(shapes),
        scratch_shapes=list(scratch),
        compiler_params=pltpu.CompilerParams(vmem_limit_bytes=limit * 1024 * 1024),
        cost_estimate=pl.CostEstimate(flops=flops, bytes_accessed=moved, transcendentals=0),
        name=name,
    )(*args)


def rotated(value, axis, shift):
    count = lax.axis_size(axis)
    return lax.ppermute(value, axis, [(i, (i + shift) % count) for i in range(count)])


def swapped(value, axis, first):
    count = lax.axis_size(axis)
    pairs = [((i + first) % count, (i + first + 1) % count) for i in range(0, count, 2)]
    return lax.ppermute(value, axis, pairs + [(b, a) for a, b in pairs])


def from_others(value, axis):
    return [rotated(value, axis, shift) for shift in range(1, lax.axis_size(axis))]


def stage_sizes(count):
    sizes = []
    while count > 1:
        sizes.append(next(size for size in (4, 2, 3, 5, 7, count) if count % size == 0))
        count //= sizes[-1]
    return sizes


def in_stages(value, axis, beside=None):
    count = lax.axis_size(axis)
    stride = 1
    terms, firsts = [value], []
    for size in stage_sizes(count):
        value = terms[0]
        if len(terms) > 1:
            unread = [] if beside is None else [beside]
            (value,) = call(
                functools.partial(add_kernel, len(unread)),
                "add",
                [(value.shape, f32)],
                *unread, *terms,
                unread=len(unread),
            )
        terms = [value]
        for shift in range(1, size):
            moves = []
            for i in range(count):
                digit = (i // stride) % size
                other = digit ^ shift if size in (2, 4) else (digit + shift) % size
                moves.append((i, i + (other - digit) * stride))
            terms.append(lax.ppermute(value, axis, moves))
        stride *= size
        firsts = firsts or terms
    return terms, firsts


def body(
    data, order, chan_factor, slice_weights, smooth_aux, coupled, smooth_dual, coupling_dual, delta
):
    count, all_rows, channels = data.shape
    rank = chan_factor.shape[1]
    rows = smooth_aux.shape[1]
    parts = lax.axis_size("chan")
    total = count * lax.axis_size("cuts")
    group = group_size(count, rank)
    groups = count // group
    wide = group * rank
    flip = lambda value: jnp.swapaxes(value, 1, 2)
    aux, coup, dual_s, dual_c = map(flip, (smooth_aux, coupled, smooth_dual, coupling_dual))
    factor = chan_factor.T
    state = ((count, rank, rows), f32)
    quads = ((groups, rank, wide), f32)
    square = ((rank, rank), f32)
    halo = (((SWEEPS + 1) // 2, rank, 2 * rows), f32)
    lanes = lambda height: ((height, 128), f32)
    scale = ((groups, 8, wide), f32)

    me = lax.axis_index("chan").astype(jnp.int32).reshape(1)
    odd = lax.rem(lax.axis_index("cuts"), 2).astype(jnp.int32).reshape(1)
    early = count // 4
    own, received = [], []
    for first, pairs, lead in ((0, early, True), (2 * early, count // 2 - early, False)):
        height = pairs * rows + (rank // 2 if lead else 0)
        projected = call(
            functools.partial(project_kernel, first, pairs, rows, lead),
            "project",
            [((height, 2 * rank), f32)] * parts + [(factor.shape, factor.dtype)] * lead,
            me, data, factor,
            scalars=1, unread=1, limit=52,
            scratch=[
                pltpu.VMEM((2 * pairs, all_rows, channels), data.dtype),
                pltpu.SemaphoreType.DMA((4 * pairs,)),
            ],
        )
        if lead:
            *projected, factor = projected
        own.append(projected[0])
        received.append([rotated(projected[shift], "chan", shift) for shift in range(1, parts)])

    late_weights, _ = lax.optimization_barrier((slice_weights, own[-1]))
    before = rotated(late_weights, "cuts", 1)
    after = rotated(late_weights, "cuts", -1)
    inverse, mover, rho, diagonal, columns, base = call(
        functools.partial(setup_kernel, parts, early * rows, group),
        "setup",
        [
            ((count, rank, 3 * rank), bf16),
            ((count // 2, 2 * rank, 6 * rank), bf16),
            lanes(count),
            ((count, rank), f32),
            ((rank, count), f32),
            state,
        ],
        order, own[0], *received[0], slice_weights, aux, coup, dual_s, dual_c,
        scalars=1,
    )
    half_state = ((early, 2 * rank, rows), f32)
    moved, turned = call(
        move_kernel, "move", [half_state, half_state], mover, own[0], *received[0]
    )
    tall, target, gram = call(
        functools.partial(first_kernel, group),
        "first",
        [state, state, quads],
        order, before, after, base, mover, dual_s, dual_c, moved, own[1], *received[1],
        scalars=1, unread=2,
        scratch=[pltpu.VMEM((count // 2, 2 * rank, rows), f32)],
    )
    side, before, after, inside, to_near, to_far = call(
        smooth_kernel,
        "smooth",
        [state, lanes(count), lanes(count), state, halo, halo],
        odd, order, aux, target, before, rho, after, diagonal, columns, turned, own[1],
        *received[1],
        scalars=2,
        scratch=[pltpu.VMEM((count // 2, 2 * rank, rows), f32)],
    )
    polar_outs = [quads, ((rank // 2, 2 * rank), f32), quads]
    for inner in range(INNER):
        if inner == 0:
            mixed, partial, gram = call(
                first_polar_kernel,
                "polar",
                polar_outs,
                inside, delta, gram, *from_others(gram, "chan"),
                unread=1, microseconds=3,
            )
        else:
            last = inner == INNER - 1
            mixed, partial, *gram = call(
                functools.partial(later_polar_kernel, last),
                "polar",
                polar_outs[:2] if last else polar_outs,
                inside, delta, change, old, cross, *crosses,
                unread=1,
            )
            gram = gram[0] if gram else None
        if inner == INNER - 1:
            mixed_tall, evolving = call(
                last_rows_kernel,
                "rows",
                [((count, 3 * rank, rows), bf16), state],
                mixed, change, forward, tall, known,
                scratch=[pltpu.VMEM(state[0], f32)],
            )
            coup, delta = call(
                functools.partial(last_kernel, total),
                "last",
                [state, square],
                mixed_tall, *in_stages(partial, "cuts")[0],
            )
            continue
        near = swapped(to_near, "cuts", 0)
        far = swapped(to_far, "cuts", 1)
        known, cross, *kept = call(
            functools.partial(ahead_kernel, group),
            "ahead",
            [state, ((groups, rank, 2 * wide), f32)] + [state] * (2 if inner < INNER - 2 else 0),
            odd, partial, inside, near, far, target, tall, side, rho, inverse,
            scalars=1, unread=1,
        )
        sums, firsts = in_stages(partial, "cuts", beside=cross)
        _, cross = lax.optimization_barrier((firsts, cross))
        crosses = from_others(cross, "chan")
        old = gram
        delta, change, forward = call(
            functools.partial(mixer_kernel, total),
            "mixer",
            [square, quads, quads],
            mixed, inverse, rho, *sums,
        )
        if inner < INNER - 2:
            tall, target, inside, to_near, to_far = call(
                rows_kernel,
                "rows",
                [state, state, state, halo, halo],
                odd, kept[0], before, rho, after, change, forward, tall, known, kept[1],
                scalars=1,
            )
    return (flip(evolving), flip(coup), delta)


def solution(mesh):
    return jax.shard_map(
        body,
        mesh=mesh,
        in_specs=(
            P("cuts", None, "chan"),
            P("cuts"),
            P("chan", None),
            P("cuts", None),
            P("cuts", "chan", None),
            P("cuts", "chan", None),
            P("cuts", "chan", None),
            P("cuts", "chan", None),
            P(),
        ),
        out_specs=(P("cuts", "chan", None), P("cuts", "chan", None), P()),
        check_vma=False,
    )
```
